32 devices in a mesh: blk: 16 (over z, y, core), ij: 2 (over x).
Axes of the slice: x: 2, y: 2, z: 4, core: 2. Of those that a mesh axis runs over, the one named last changes fastest.
Arguments:
- density: float32 [16, 6, 256, 128], P('blk', None, 'ij'), may hold values from 0.8 to 1.2
- momentum: float32 [16, 3, 6, 256, 128], P('blk', None, None, 'ij'), may hold values from -2.5 to 2.5
- energy: float32 [16, 6, 256, 128], P('blk', None, 'ij'), may hold values from 2.5 to 4
- metrics: float32 [16, 4, 256, 128], P('blk', None, 'ij'), may hold values from -1 to 1
- volume: float32 [16, 256, 128], P('blk', 'ij'), may hold values from 0.5 to 2
- placed: int32 [16], replicated, may hold values from 0 to 15, each once
- neighbour: int32 [16, 2], replicated, may hold values from 0 to 15, as said below
- face: int32 [16, 2], replicated, may hold values from 0 to 1, as said below
- orient: int32 [16, 2], replicated, may hold values from 0 to 1, as said below
Outputs:
- next_density: float32 [16, 6, 256, 128], P('blk', None, 'ij')
- next_momentum: float32 [16, 3, 6, 256, 128], P('blk', None, None, 'ij')
- next_energy: float32 [16, 6, 256, 128], P('blk', None, 'ij')
The draws below stay inside these ranges and needn't reach their ends.
Inputs may be any that keep to these rules, and one draw needn't show every extreme that they name: If face f of block b meets face g of block c with orientation o, then face g of c meets face f of b with orientation o; every block id appears as a neighbour. `face`: consistent with neighbour as stated there. `orient`: consistent with neighbour as stated there.
All inputs are finite; a program needn't handle non-finite values.
Results may differ from the reference program's by a relative error of at most 0.00002.
Values sent between devices are 32-bit elements; how exact they have to be, the bound alone decides.
No kernel may reach another device: no remote copies, remote signals or barrier semaphores. Data moves between devices by JAX's collectives and lax.ppermute only.
A program may use at most 128 MiB of HBM per device.

```python
import math
import jax
import jax.numpy as jnp
from jax import lax

NI = 256
NJ = 128
PLANES = 6
BLOCKS = 16


def face_pairing(key):
    order = jax.random.permutation(jax.random.fold_in(key, 7), 2 * BLOCKS).astype(jnp.int32)
    first_half = order[0::2]
    second_half = order[1::2]
    partner = jnp.zeros((2 * BLOCKS,), jnp.int32).at[first_half].set(second_half).at[second_half].set(first_half)
    flips = jax.random.randint(jax.random.fold_in(key, 11), (BLOCKS,), 0, 2, dtype=jnp.int32)
    twisted = jnp.zeros((2 * BLOCKS,), jnp.int32).at[first_half].set(flips).at[second_half].set(flips)
    return (partner.reshape(BLOCKS, 2), twisted.reshape(BLOCKS, 2))


def draw_neighbour(key, part):
    partner, twisted = face_pairing(key)
    return partner // 2


def draw_face(key, part):
    partner, twisted = face_pairing(key)
    return partner % 2


def draw_orient(key, part):
    partner, twisted = face_pairing(key)
    return twisted


def shard_levels(key, dims, pieces, smallest, high):
    level, own = 1.0, jax.random.fold_in(key, 6)
    for dim, parts in pieces:
        heights = jnp.exp(jax.random.uniform(jax.random.fold_in(own, dim), (parts,), jnp.float32, smallest / len(pieces), high / len(pieces)))
        level = level * jnp.repeat(heights, dims[dim] // parts).reshape([-1 if axis == dim else 1 for axis in range(len(dims))])
    return level


def bell_draw(key, extent, width, most, pieces=(), kind=jnp.bfloat16):
    entries = jax.random.normal(key, extent, jnp.float32) * width
    if len(pieces) > 0:
        entries = shard_levels(key, extent, pieces, -0.22, 0.18) * entries
    return jnp.clip(entries, min=-most, max=most).astype(kind)


def setup_inputs(seed: int = 0) -> dict:
    streams_of = jax.random.split(jax.random.key(seed), 10)
    density = jnp.clip(0.8 + 0.40000004 * jax.random.uniform(streams_of[0], (BLOCKS, PLANES, NI, NJ), jnp.float32) ** shard_levels(streams_of[0], (BLOCKS, PLANES, NI, NJ), ((0, 16), (2, 2)), -0.2, 0.2), 0.8, 1.2)
    momentum = bell_draw(streams_of[1], (BLOCKS, 3, PLANES, NI, NJ), 0.3, 2.5, ((0, 16), (3, 2)), jnp.float32)
    energy = jnp.clip(2.5 + 1.5 * jax.random.uniform(streams_of[2], (BLOCKS, PLANES, NI, NJ), jnp.float32) ** shard_levels(streams_of[2], (BLOCKS, PLANES, NI, NJ), ((0, 16), (2, 2)), -0.2, 0.2), 2.5, 4.0)
    metrics = jnp.clip(jax.random.uniform(streams_of[3], (BLOCKS, 4, NI, NJ), jnp.float32, -1.0, 1.0) * shard_levels(streams_of[3], (BLOCKS, 4, NI, NJ), ((0, 16), (2, 2)), -0.4, 0.0), -1.0, 1.0)
    volume = jnp.clip(jnp.exp(math.log(2.0) - 1.3862944 * jax.random.uniform(streams_of[4], (BLOCKS, NI, NJ), jnp.float32) ** shard_levels(streams_of[4], (BLOCKS, NI, NJ), ((0, 16), (1, 2)), -0.2, 0.2)), 0.5, 2.0)
    placed = jax.random.permutation(streams_of[5], BLOCKS).astype(jnp.int32)
    neighbour = draw_neighbour(jax.random.fold_in(streams_of[9], 71), 0)
    face = draw_face(jax.random.fold_in(streams_of[9], 71), 0)
    orient = draw_orient(jax.random.fold_in(streams_of[9], 71), 0)
    return dict(density=density, momentum=momentum, energy=energy, metrics=metrics, volume=volume, placed=placed, neighbour=neighbour, face=face, orient=orient)


pressure_factor = 0.4
viscosity = 0.05
conduction = 0.1
time_step = 0.03


def slope_rows(f):
    return (f[..., 0:-4, 2:-2] - 8.0 * f[..., 1:-3, 2:-2] + 8.0 * f[..., 3:-1, 2:-2] - f[..., 4:, 2:-2]) / 12.0


def slope_cols(f):
    return (f[..., 2:-2, 0:-4] - 8.0 * f[..., 2:-2, 1:-3] + 8.0 * f[..., 2:-2, 3:-1] - f[..., 2:-2, 4:]) / 12.0


def slope_planes(f):
    return (jnp.roll(f, 2, -3) - 8.0 * jnp.roll(f, 1, -3) + 8.0 * jnp.roll(f, -1, -3) - jnp.roll(f, -2, -3)) / 12.0


def curve_rows(f):
    return (-f[..., 0:-4, 2:-2] + 16.0 * f[..., 1:-3, 2:-2] - 30.0 * f[..., 2:-2, 2:-2] + 16.0 * f[..., 3:-1, 2:-2] - f[..., 4:, 2:-2]) / 12.0


def curve_cols(f):
    return (-f[..., 2:-2, 0:-4] + 16.0 * f[..., 2:-2, 1:-3] - 30.0 * f[..., 2:-2, 2:-2] + 16.0 * f[..., 2:-2, 3:-1] - f[..., 2:-2, 4:]) / 12.0


def curve_planes(f):
    return (-jnp.roll(f, 2, -3) + 16.0 * jnp.roll(f, 1, -3) - 30.0 * f + 16.0 * jnp.roll(f, -1, -3) - jnp.roll(f, -2, -3)) / 12.0


def interior(f):
    return f[..., 2:-2, 2:-2]


def residual(ext):
    planes = ext.shape[1] - 1
    fields = ext[:, :planes]
    metric = ext[:, planes]
    dens = fields[0]
    moment = fields[1:4]
    energy_now = fields[4]
    velocity = moment / dens
    kinetic = 0.5 * jnp.sum(moment * velocity, axis=0)
    pressure = pressure_factor * (energy_now - kinetic)
    thermal = pressure / dens
    total_head = energy_now + pressure
    row_ax, row_ay, col_bx, col_by, cell_vol = metric[0], metric[1], metric[2], metric[3], metric[4]
    along_rows = row_ax * velocity[0] + row_ay * velocity[1]
    along_cols = col_bx * velocity[0] + col_by * velocity[1]
    flux_rows = cell_vol * jnp.stack([dens * along_rows, moment[0] * along_rows + row_ax * pressure,
                                      moment[1] * along_rows + row_ay * pressure, moment[2] * along_rows,
                                      total_head * along_rows])
    flux_cols = cell_vol * jnp.stack([dens * along_cols, moment[0] * along_cols + col_bx * pressure,
                                      moment[1] * along_cols + col_by * pressure, moment[2] * along_cols,
                                      total_head * along_cols])
    flux_planes = jnp.stack([moment[2], moment[0] * velocity[2], moment[1] * velocity[2],
                             moment[2] * velocity[2] + pressure, total_head * velocity[2]])
    inviscid = -(slope_rows(flux_rows) + slope_cols(flux_cols)) / interior(cell_vol) - slope_planes(interior(flux_planes))
    row_weight = interior(row_ax * row_ax + row_ay * row_ay)
    col_weight = interior(col_bx * col_bx + col_by * col_by)

    def laplace(w):
        return row_weight * curve_rows(w) + col_weight * curve_cols(w) + curve_planes(interior(w))

    half_speed = kinetic / dens
    diffuse = jnp.stack([jnp.zeros_like(inviscid[0]), viscosity * laplace(velocity[0]),
                         viscosity * laplace(velocity[1]), viscosity * laplace(velocity[2]),
                         viscosity * laplace(half_speed) + conduction * laplace(thermal)])
    return inviscid + diffuse


def wall_signs(planes):
    channel = jnp.arange(5)[:, None]
    plane_index = jnp.arange(planes)[None, :]
    flipped = (channel >= 1) & (channel <= 3) & (plane_index < planes - 1)
    return jnp.where(flipped, -1.0, 1.0)[:, :, None, None]


def ghost_factors(twisted, facing, planes):
    own_face = jnp.arange(2)[None, :]
    turn = jnp.where(twisted == 1, -1.0, 1.0)
    same = jnp.where(facing == own_face, -1.0, 1.0)
    channel = jnp.arange(5)[None, None, :]
    by_channel = jnp.where(channel < 2, turn[:, :, None], jnp.where(channel < 4, same[:, :, None], 1.0))
    metric_plane = (jnp.arange(planes) == planes - 1)[None, None, None, :]
    return jnp.where(metric_plane, by_channel[:, :, :, None], 1.0)


def locate(placed):
    blocks = placed.shape[0]
    slots = jnp.arange(blocks, dtype=jnp.int32)
    return jnp.sum(jnp.where(placed[:, None] == slots[None, :], slots[:, None], 0), axis=0).astype(jnp.int32)


def extend(base, placed, neighbour, face, orient):
    planes = base.shape[2]
    low_wall = base[:, :, :, 1::-1] * wall_signs(planes)
    high_wall = base[:, :, :, -1:-3:-1]
    rowed = jnp.concatenate([low_wall, base, high_wall], axis=3)
    strips = jnp.stack([base[..., 0:2], base[..., -1:-3:-1]], axis=1)
    position_of = locate(placed)
    next_ids = neighbour[placed]
    facing = face[placed]
    twisted = orient[placed]
    partner = position_of[next_ids]
    ghosts = strips[partner, facing]
    ghosts = jnp.where(twisted[:, :, None, None, None, None] == 1, ghosts[..., ::-1, :], ghosts)
    ghosts = ghosts * ghost_factors(twisted, facing, planes)[..., None, None]
    left = jnp.pad(ghosts[:, 0][..., ::-1], ((0, 0), (0, 0), (0, 0), (2, 2), (0, 0)), constant_values=1.0)
    right = jnp.pad(ghosts[:, 1], ((0, 0), (0, 0), (0, 0), (2, 2), (0, 0)), constant_values=1.0)
    return jnp.concatenate([left, rowed, right], axis=-1)


def reference(density, momentum, energy, metrics, volume, placed, neighbour, face, orient):
    fields = jnp.concatenate([density[:, None], momentum, energy[:, None]], axis=1)
    metric_plane = jnp.concatenate([metrics, volume[:, None]], axis=1)[:, :, None]

    def tendency(state):
        ext = extend(jnp.concatenate([state, metric_plane], axis=2), placed, neighbour, face, orient)
        return lax.map(residual, ext)

    section = fields + time_step * tendency(fields)
    result = 0.5 * fields + 0.5 * (section + time_step * tendency(section))
    return result[:, 0], result[:, 1:4], result[:, 4]
```

```python
import functools

import jax
import jax.numpy as jnp
from jax import lax
from jax.experimental import pallas as pl
from jax.experimental.pallas import tpu as pltpu
from jax.sharding import PartitionSpec as P

pressure_factor = 0.4
viscosity = 0.05
time_step = 0.03
unit = time_step / 12.0

LANES = 128
PAD = 8
DEPTH = 4
CH = 5
VMEM_LIMIT = 48 * 1024 * 1024


def turn(x, shift, axis):
    shift = shift % x.shape[axis]
    return x if shift == 0 else pltpu.roll(x, shift, axis)


def lanes_of(shape):
    return lax.broadcasted_iota(jnp.int32, shape, len(shape) - 1)


def rows_of(shape):
    return lax.broadcasted_iota(jnp.int32, shape, len(shape) - 2)


def plane_at(refs, c, k, rows):
    dens, mom, en, met, vol = refs
    if k == dens.shape[1]:
        return met[0, c, rows] if c < 4 else vol[0, rows]
    if c == 0:
        return dens[0, k, rows]
    if c == 4:
        return en[0, k, rows]
    return mom[0, c - 1, k, rows]


def point(f):
    rho, m1, m2, m3, e = f
    r = 1.0 / rho
    u1, u2, u3 = m1 * r, m2 * r, m3 * r
    kin = 0.5 * (m1 * u1 + m2 * u2 + m3 * u3)
    p = pressure_factor * (e - kin)
    return (u1, u2, u3, (kin + 2.0 * p) * r), p, e + p


def metric_terms(m):
    ax, ay, bx, by, v = m
    kv = viscosity * unit
    rw = kv * (ax * ax + ay * ay)
    cw = kv * (bx * bx + by * by)
    return v * ax, v * ay, v * bx, v * by, -unit / v, rw, cw, 30.0 * (rw + cw + kv)


def flux(f, w, p, h, gx, gy):
    rho, m1, m2, m3, _ = f
    u = gx * w[0] + gy * w[1]
    return (rho * u, m1 * u + gx * p, m2 * u + gy * p, m3 * u, h * u)


def flux_planes(f, w, p, h):
    u3 = w[2]
    return (f[3], f[1] * u3, f[2] * u3, f[3] * u3 + p, h * u3)


def slope(x, at):
    return 8.0 * (at(x, 1) - at(x, -1)) - (at(x, 2) - at(x, -2))


def curve(x, at):
    return 16.0 * (at(x, 1) + at(x, -1)) - (at(x, 2) + at(x, -2))


def along(axis):
    return lambda x, o: turn(x, -o, axis)


def plane_shift(x, o):
    o = o % x.shape[0]
    return jnp.concatenate([x[o:], x[:o]], axis=0)


def tile_rate(f, m, at_i, at_j):
    vax, vay, vbx, vby, niv, rw, cw, tw = metric_terms(m)
    kv = viscosity * unit
    w, p, h = point(f)
    fi = flux(f, w, p, h, vax, vay)
    fj = flux(f, w, p, h, vbx, vby)
    fk = flux_planes(f, w, p, h)
    out = []
    for c in range(CH):
        val = niv * (slope(fi[c], at_i) + slope(fj[c], at_j)) - unit * slope(fk[c], plane_shift)
        if c > 0:
            x = w[c - 1]
            val = val + (
                rw * curve(x, at_i) + cw * curve(x, at_j) + kv * curve(x, plane_shift) - tw * x
            )
        out.append(val)
    return out, fj, w, niv, cw


def edge_terms(fn, w, niv, cw):
    out = []
    for face in range(2):
        rows = rows_of(fn[face][0].shape)
        terms = []
        for c in range(CH):
            a, b = fn[face][c], fn[1 - face][c]
            first = 8.0 * (turn(a, -1, 1) + b) - (turn(a, -2, 1) + turn(b, 1, 1))
            second = -(turn(a, -2, 1) + turn(b, -1, 1))
            val = niv[face] * jnp.where(rows == 1, first, second)
            if c > 0:
                a, b = w[face][c - 1], w[1 - face][c - 1]
                first = 16.0 * (turn(a, -1, 1) - b) - (turn(a, -2, 1) - turn(b, 1, 1))
                second = -(turn(a, -2, 1) - turn(b, -1, 1))
                val = val + cw[face] * jnp.where(rows == 1, first, second)
            terms.append(val)
        out.append(terms)
    return out


def put_edges(ref, terms, planes, wide):
    for c in range(CH):
        for k in range(planes):
            at = (c * planes + k) * 4
            ref[at : at + 2, 0:wide] = terms[1][c][k, 0:2]
            ref[at + 2 : at + 3, 0:wide] = terms[0][c][k, 1:2]
            ref[at + 3 : at + 4, 0:wide] = terms[0][c][k, 0:1]


def edge_lanes(tile, index):
    lane = lanes_of(tile.shape)
    moved = turn(tile, LANES - 2 - 4 * index, 1)
    return jnp.where((lane < 2) | (lane >= LANES - 2), moved, 0.0)


def cut_kernel(halves, dens, mom, en, met, vol, placed, orient, send, own, *rest):
    edges, scratch = rest[:-1], rest[-1]
    refs = (dens, mom, en, met, vol)
    planes, rows = dens.shape[1], dens.shape[2]
    block = placed[lax.axis_index("blk")]
    half = lax.axis_index("ij")
    twist = [orient[block, 0] == 1, orient[block, 1] == 1]
    lane = lanes_of((rows, LANES))
    mirror = jnp.where(
        rows_of((LANES, LANES)) + lanes_of((LANES, LANES)) == rows - 1, 1.0, 0.0
    )
    row = rows_of((64, LANES))
    twisted = jnp.where(
        row % 8 < 4, jnp.where(twist[1], 1, 0), jnp.where(twist[0], 1, 0)
    ) == 1
    scratch[CH * 64 :] = jnp.zeros((3 * 64, LANES), jnp.float32)
    for c in range(CH):
        packed = jnp.zeros((rows, LANES), jnp.float32)
        for k in range(planes + 1):
            x = plane_at(refs, c, k, slice(None))
            packed = jnp.where(lane // 8 == k, turn(x, 8 * k + 4, 1), packed)
        if rows < LANES:
            packed = jnp.concatenate(
                [packed, jnp.zeros((LANES - rows, LANES), jnp.float32)], axis=0
            )
        strip = packed.T[0:64]
        if c in (2, 3):
            strip = jnp.where((row >= planes * 8) & (row % 8 >= 4), -strip, strip)
        own[c] = strip
        back = jnp.dot(
            strip,
            mirror,
            precision=lax.Precision.HIGHEST,
            preferred_element_type=jnp.float32,
        )
        if c < 2:
            back = jnp.where(row >= planes * 8, -back, back)
        scratch[c * 64 : c * 64 + 64] = jnp.where(twisted, back, strip)
    for k in range(planes + 1):
        for d in range(DEPTH):
            at = (k * DEPTH + d) * 16
            send[at : at + 8] = scratch[pl.ds(k * 8 + 4 + d, 8, stride=64)]
            send[at + 8 : at + 16] = scratch[pl.ds(k * 8 + 3 - d, 8, stride=64)]
    for c in range(CH):
        for k in range(planes + 1):
            low = plane_at(refs, c, k, slice(0, 4))
            high = plane_at(refs, c, k, slice(rows - 4, rows))
            if len(edges) == 1:
                edges[0][c, k * 4 : k * 4 + 4] = jnp.where(half == 0, high, low)
            else:
                edges[0][c, k * 4 : k * 4 + 4] = low
                edges[1][c, k * 4 : k * 4 + 4] = high


def relay_kernel(halves, rows, placed, neighbour, face, orient, got, send, ext, where_is):
    blocks = placed.shape[0]

    def note(slot, _):
        where_is[placed[slot]] = slot
        return 0

    lax.fori_loop(0, blocks, note, 0)
    lane = lanes_of((8, LANES))

    def pass_on(n, _):
        slot, f = n // 2, n % 2
        block = placed[slot]
        partner = where_is[neighbour[block, f]]
        side, turned = face[block, f], orient[block, f]
        for half in range(halves):

            def piece(h):
                h = jnp.where(turned == 1, halves - 1 - h, h)
                at = ((partner * halves + h) * 2 + side) * 8
                return got[pl.ds(pl.multiple_of(at, 8), 8)]

            at = pl.multiple_of(((slot * halves + half) * 2 + f) * 8, 8)
            send[pl.ds(at, 8)] = piece(half)
            low, high = piece(max(half - 1, 0)), piece(min(half + 1, halves - 1))
            ends = jnp.where(lane < 2, turn(low, 2 - rows, 1), turn(high, 2, 1))
            ext[pl.ds(at, 8)] = jnp.where(lane < 4, ends, 0.0)
        return 0

    lax.fori_loop(0, 2 * blocks, pass_on, 0)
    count = 2 * blocks * halves
    ends = ext[pl.ds(0, count, stride=8)]
    for c in range(1, CH):
        ends = ends + turn(ext[pl.ds(c, count, stride=8)], 4 * c, 1)
    send[pl.ds(5, count, stride=8)] = ends


def flux_chunk(get, mets, fi, w, r, rest=None):
    rows = pl.ds(r, 8)
    vax, vay, vbx, vby, niv, rw, cw, tw = [mets[j, rows] for j in range(8)]
    at_j = along(1)
    for k in range(fi.shape[1]):
        f = [get(c, k, r) for c in range(CH)]
        wk, p, h = point(f)
        for c, x in enumerate(flux(f, wk, p, h, vax, vay)):
            fi[c, k, rows] = x
        for c in range(4):
            w[c, k, rows] = wk[c]
        if rest is None:
            continue
        fk, acc = rest
        fj = flux(f, wk, p, h, vbx, vby)
        for c in range(CH):
            val = niv * slope(fj[c], at_j)
            if c > 0:
                val = val + (cw * curve(wk[c - 1], at_j) - tw * wk[c - 1])
            acc[c, k, rows] = val
        for c, x in enumerate(flux_planes(f, wk, p, h)):
            fk[c, k, rows] = x


def sum_chunk(mets, fi, w, fk, acc, r, emit):
    planes = fi.shape[1]
    kv = viscosity * unit
    rows = pl.ds(r, 8)
    niv, rw = mets[4, rows], mets[5, rows]
    for c in range(CH):
        t = [fk[c, k, rows] for k in range(planes)]
        x = [w[c - 1, k, rows] for k in range(planes)] if c > 0 else None
        for k in range(planes):

            def near(v, o):
                return v[(k + o) % planes]

            def at_i(v, o):
                return v[pl.ds(r + o, 8)]

            val = acc[c, k, rows] + niv * slope(fi.at[c, k], at_i) - unit * slope(t, near)
            if c > 0:
                val = val + (rw * curve(w.at[c - 1, k], at_i) + kv * curve(x, near))
            emit(c, k, r, val)


def chunks(count, body):
    def step(n, _):
        body(pl.multiple_of(n * 8, 8))
        return 0

    lax.fori_loop(0, count, step, 0)


def first_kernel(dens, mom, en, met, vol, part, mets, fi, w, fk, acc):
    refs = (dens, mom, en, met, vol)
    planes, rows = dens.shape[1], dens.shape[2]

    def terms(r):
        m = [plane_at(refs, c, planes, pl.ds(r, 8)) for c in range(CH)]
        for j, x in enumerate(metric_terms(m)):
            mets[j, pl.ds(r + PAD, 8)] = x

    def get(c, k, r):
        return plane_at(refs, c, k, pl.ds(r - PAD, 8))

    def fluxes(r):
        terms(r)
        flux_chunk(get, mets, fi, w, r + PAD, (fk, acc))

    def emit(c, k, r, val):
        part[c, k, pl.ds(r - PAD, 8)] = get(c, k, r) + val

    def sums(r):
        sum_chunk(mets, fi, w, fk, acc, r + PAD, emit)

    empty = jnp.zeros((PAD, LANES), jnp.float32)
    for k in range(planes):
        for c in range(CH):
            fi[c, k, 0:PAD] = empty
            fi[c, k, rows + PAD :] = empty
        for c in range(4):
            w[c, k, 0:PAD] = empty
            w[c, k, rows + PAD :] = empty
    chunks(rows // 8, fluxes)
    chunks(rows // 8, sums)


def last_kernel(
    halves, dens, mom, en, met, vol, placed, orient, own, below, above, got, part,
    next_dens, next_mom, next_en,
    tall, strips, turned, back, sec, mets, fi, w, fk, acc,
):
    refs = (dens, mom, en, met, vol)
    planes, rows = dens.shape[1], dens.shape[2]
    every = planes + 1
    half = lax.axis_index("ij")
    block = placed[lax.axis_index("blk")]
    low_wall, high_wall = half == 0, half == halves - 1
    low_flag, high_flag = jnp.where(low_wall, 1, 0), jnp.where(high_wall, 1, 0)

    for c in range(CH):
        for k in range(every):
            tall[0, c, k, 4:8] = plane_at(refs, c, k, slice(0, 4))
            tall[1, c, k, 0:4] = plane_at(refs, c, k, slice(rows - 4, rows))

    @pl.when(low_wall)
    def _():
        for c in range(CH):
            for k in range(every):
                sign = -1.0 if 1 <= c <= 3 and k < planes else 1.0
                for d in range(4):
                    tall[0, c, k, 3 - d : 4 - d] = sign * plane_at(refs, c, k, slice(d, d + 1))

    @pl.when(jnp.logical_not(low_wall))
    def _():
        for c in range(CH):
            for k in range(every):
                tall[0, c, k, 0:4] = below[c, k * 4 : k * 4 + 4]

    @pl.when(high_wall)
    def _():
        for c in range(CH):
            for k in range(every):
                for d in range(4):
                    tall[1, c, k, 4 + d : 5 + d] = plane_at(
                        refs, c, k, slice(rows - 1 - d, rows - d)
                    )

    @pl.when(jnp.logical_not(high_wall))
    def _():
        for c in range(CH):
            for k in range(every):
                tall[1, c, k, 4:8] = above[c, k * 4 : k * 4 + 4]

    lane8, row8 = lanes_of((8, LANES)), rows_of((8, LANES))
    stacked = []
    for c in range(CH):
        packed = jnp.zeros((8, LANES), jnp.float32)
        for k in range(every):
            x = jnp.where(row8 < 4, tall[0, c, k], tall[1, c, k])
            packed = jnp.where(lane8 // 8 == k, turn(x, 8 * k + 4, 1), packed)
        stacked.append(packed)
    stacked.append(jnp.zeros((LANES - 8 * CH, LANES), jnp.float32))
    ends = jnp.concatenate(stacked, axis=0).T[0:64]

    count = DEPTH * every
    lane = lanes_of((count, LANES))
    row = rows_of((count, LANES))
    is_field = row < planes * DEPTH
    lane64 = lanes_of((64, LANES))

    def set_strip(c, f, first, second, rows_at):
        for k in range(every):
            for at, start, size in rows_at(k):
                strips[c, f, k, at : at + size, 0:LANES] = first[start : start + size]
                strips[c, f, k, at : at + size, LANES:] = second[start : start + size]

    def spread(main, outer, lane):
        if rows == LANES:
            return main, outer
        return jnp.where((lane == rows) | (lane == rows + 1), turn(outer, rows, 1), main), outer

    for c in range(CH):
        outer = turn(ends, -(8 * c + 4), 1)
        if c in (2, 3):
            r64 = rows_of((64, LANES))
            outer = jnp.where((r64 >= planes * 8) & (r64 % 8 >= 4), -outer, outer)
        first, second = spread(own[c], outer, lane64)
        set_strip(c, 1, first, second, lambda k: ((0, k * 8 + 2, 2),))
        set_strip(c, 0, first, second, lambda k: ((0, k * 8 + 5, 1), (1, k * 8 + 4, 1)))
        for f in range(2):
            twist = jnp.where(orient[block, f] == 1, 1, 0)
            main = got[pl.ds(f * 8 + c, count, stride=16)]
            outer = turn(got[pl.ds(f * 8 + 5, count, stride=16)], LANES - 2 - 4 * c, 1)
            if c in (2, 3):
                main = jnp.where(is_field, main, -main)
                outer = jnp.where(is_field, outer, -outer)
            low = jnp.where(lane == LANES - 2, turn(main, LANES - 3, 1), turn(main, LANES - 1, 1))
            high = jnp.where(lane == 0, turn(main, 1 - rows, 1), turn(main, 3 - rows, 1))
            if 1 <= c <= 3:
                low = jnp.where(is_field & (twist == 0), -low, low)
                high = jnp.where(is_field & (twist == 1), -high, high)
            outer = jnp.where((lane >= LANES // 2) & (low_flag == 1), low, outer)
            outer = jnp.where((lane < LANES // 2) & (high_flag == 1), high, outer)
            first, second = spread(main, outer, lane)
            set_strip(c, f, first, second, lambda k: ((2, k * DEPTH, DEPTH),))
            for k in range(every):
                strips[c, f, k, 6:8] = jnp.ones((2, 2 * LANES), jnp.float32)

    fn, ws, nivs, cws = [], [], [], []
    for f in range(2):
        fields = [strips[c, f, 0:planes] for c in range(CH)]
        m = [strips[c, f, planes] for c in range(CH)]
        rate, flux_n, wn, niv, cw = tile_rate(fields, m, along(2), along(1))
        for c in range(CH):
            strips[c, f, 0:planes] = fields[c] + rate[c]
        fn.append(flux_n)
        ws.append(wn)
        nivs.append(niv)
        cws.append(cw)
    turned[...] = jnp.zeros((LANES, 2 * LANES), jnp.float32)
    put_edges(turned, edge_terms(fn, ws, nivs, cws), planes, 2 * LANES)
    back[PAD : PAD + LANES] = turned[:, 0:LANES].T
    back[PAD + LANES : PAD + 2 * LANES] = turned[:, LANES:].T
    back[0:PAD] = back[2 * LANES : 2 * LANES + PAD]

    def finish(r):
        tile = back[pl.ds(r + PAD, 8)]
        for c in range(CH):
            for k in range(planes):
                sec[c, k, pl.ds(r + PAD, 8)] = part[c, k, pl.ds(r, 8)] + edge_lanes(
                    tile, c * planes + k
                )

    chunks(rows // 8, finish)
    sub = rows_of((planes, 8, LANES))
    for end in range(2):
        start = -4 if end == 0 else rows - 4
        fields = [tall[end, c, 0:planes] for c in range(CH)]
        m = [tall[end, c, planes] for c in range(CH)]
        rate = tile_rate(fields, m, along(1), along(2))[0]
        tile = back[PAD + start : PAD + start + 8]
        for c in range(CH):
            extra = jnp.stack([edge_lanes(tile, c * planes + k) for k in range(planes)])
            x = fields[c] + rate[c] + extra
            if end == 0:
                sign = -1.0 if 1 <= c <= 3 else 1.0
                wall = sign * jnp.where(sub == 2, turn(x, -3, 1), turn(x, -1, 1))
                x = jnp.where((sub < 4) & (low_flag == 1), wall, x)
            else:
                wall = jnp.where(sub == 4, turn(x, 1, 1), turn(x, 3, 1))
                x = jnp.where((sub >= 4) & (high_flag == 1), wall, x)
            for k in range(planes):
                sec[c, k, PAD + start + 2 : PAD + start + 6] = x[k, 2:6]

    if rows < LANES:
        back[...] = jnp.zeros(back.shape, jnp.float32)

    def pack(r):
        packed = jnp.zeros((8, LANES), jnp.float32)
        for c in range(CH):
            for k in range(planes):
                index = c * planes + k
                x = turn(sec[c, k, pl.ds(r + PAD, 8)], 4 * index + 2, 1)
                packed = jnp.where(lane8 // 4 == index, x, packed)
        back[pl.ds(r, 8)] = packed

    chunks(rows // 8, pack)
    columns = back[0:LANES].T
    fn, ws = [], []
    for c in range(CH):
        for k in range(planes):
            at = (c * planes + k) * 4
            strips[c, 1, k, 0:2, 0:LANES] = columns[at : at + 2]
            strips[c, 0, k, 0:1, 0:LANES] = columns[at + 3 : at + 4]
            strips[c, 0, k, 1:2, 0:LANES] = columns[at + 2 : at + 3]
    for f in range(2):
        fields = [strips[c, f, 0:planes, :, 0:LANES] for c in range(CH)]
        m = [strips[c, f, planes, :, 0:LANES] for c in range(CH)]
        _, _, vbx, vby, _, _, _, _ = metric_terms(m)
        wn, p, h = point(fields)
        fn.append(flux(fields, wn, p, h, vbx, vby))
        ws.append(wn)
    nivs = [x[:, 0:LANES] for x in nivs]
    cws = [x[:, 0:LANES] for x in cws]
    put_edges(turned, edge_terms(fn, ws, nivs, cws), planes, LANES)
    back[0:LANES] = turned[:, 0:LANES].T

    def terms(r):
        m = [plane_at(refs, c, planes, pl.ds(r, 8)) for c in range(CH)]
        for j, x in enumerate(metric_terms(m)):
            mets[j, pl.ds(r + PAD, 8)] = x

    for end, at in ((0, PAD - 4), (1, PAD + rows - 4)):
        m = [tall[end, c, planes] for c in range(CH)]
        for j, x in enumerate(metric_terms(m)):
            mets[j, at : at + 8] = x

    def get(c, k, r):
        return sec[c, k, pl.ds(r, 8)]

    def fluxes(r):
        terms(r)
        flux_chunk(get, mets, fi, w, r + PAD, (fk, acc))

    def emit(c, k, r, val):
        at = pl.ds(r - PAD, 8)
        extra = edge_lanes(back[at], c * planes + k)
        x = 0.5 * (plane_at(refs, c, k, at) + (get(c, k, r) + (val + extra)))
        if c == 0:
            next_dens[0, k, at] = x
        elif c == 4:
            next_en[0, k, at] = x
        else:
            next_mom[0, c - 1, k, at] = x

    def sums(r):
        sum_chunk(mets, fi, w, fk, acc, r + PAD, emit)

    flux_chunk(get, mets, fi, w, 0)
    flux_chunk(get, mets, fi, w, rows + PAD)
    chunks(rows // 8, fluxes)
    chunks(rows // 8, sums)


def local(mesh_shape, density, momentum, energy, metrics, volume, placed, neighbour, face, orient):
    halves = mesh_shape["ij"]
    devices = mesh_shape["blk"] * halves
    planes, rows = density.shape[1], density.shape[2]
    fields = (density, momentum, energy, metrics, volume)
    f32 = jnp.float32
    vmem = pl.BlockSpec(memory_space=pltpu.VMEM)
    smem = pl.BlockSpec(memory_space=pltpu.SMEM)
    params = pltpu.CompilerParams(vmem_limit_bytes=VMEM_LIMIT)
    piece = jax.ShapeDtypeStruct((devices * 16, LANES), f32)
    edge = jax.ShapeDtypeStruct((CH, 4 * (planes + 1), LANES), f32)
    edges = 1 if halves == 2 else 2

    sent, own, *halo = pl.pallas_call(
        functools.partial(cut_kernel, halves),
        out_shape=[piece, jax.ShapeDtypeStruct((CH, 64, LANES), f32)] + [edge] * edges,
        in_specs=[vmem] * 5 + [smem] * 2,
        out_specs=[vmem] * (2 + edges),
        scratch_shapes=[pltpu.VMEM((8 * 64, LANES), f32)],
        compiler_params=params,
        name="cut",
    )(*fields, placed, orient)

    def swap(x):
        x = x.reshape(devices, 16, LANES)
        x = lax.all_to_all(x, ("blk", "ij"), 0, 0, tiled=True)
        return x.reshape(devices * 16, LANES)

    if edges == 1:
        below = above = lax.ppermute(halo[0], "ij", [(0, 1), (1, 0)])
    else:
        below = lax.ppermute(halo[1], "ij", [(i, i + 1) for i in range(halves - 1)])
        above = lax.ppermute(halo[0], "ij", [(i + 1, i) for i in range(halves - 1)])
    got = swap(sent)
    relayed = pl.pallas_call(
        functools.partial(relay_kernel, halves, rows),
        out_shape=piece,
        in_specs=[smem] * 4 + [vmem],
        out_specs=vmem,
        scratch_shapes=[
            pltpu.VMEM((devices * 16, LANES), f32),
            pltpu.SMEM((placed.shape[0],), jnp.int32),
        ],
        compiler_params=params,
        name="relay",
    )(placed, neighbour, face, orient, got)
    ghosts = swap(relayed)

    tall = rows + 2 * PAD
    stage = [
        pltpu.VMEM((8, tall, LANES), f32),
        pltpu.VMEM((CH, planes, tall, LANES), f32),
        pltpu.VMEM((4, planes, tall, LANES), f32),
        pltpu.VMEM((CH, planes, tall, LANES), f32),
        pltpu.VMEM((CH, planes, tall, LANES), f32),
    ]
    part = pl.pallas_call(
        first_kernel,
        out_shape=jax.ShapeDtypeStruct((CH, planes, rows, LANES), f32),
        in_specs=[vmem] * 5,
        out_specs=vmem,
        scratch_shapes=stage,
        compiler_params=params,
        name="first_section",
    )(*fields)

    return pl.pallas_call(
        functools.partial(last_kernel, halves),
        out_shape=[
            jax.ShapeDtypeStruct(density.shape, f32),
            jax.ShapeDtypeStruct(momentum.shape, f32),
            jax.ShapeDtypeStruct(energy.shape, f32),
        ],
        in_specs=[vmem] * 5 + [smem] * 2 + [vmem] * 5,
        out_specs=[vmem] * 3,
        scratch_shapes=[
            pltpu.VMEM((2, CH, planes + 1, 8, LANES), f32),
            pltpu.VMEM((CH, 2, planes + 1, 8, 2 * LANES), f32),
            pltpu.VMEM((LANES, 2 * LANES), f32),
            pltpu.VMEM((2 * LANES + PAD, LANES), f32),
            pltpu.VMEM((CH, planes, tall, LANES), f32),
        ]
        + stage,
        compiler_params=params,
        name="second_section",
    )(*fields, placed, orient, own, below, above, ghosts, part)


def solution(mesh):
    return jax.shard_map(
        functools.partial(local, dict(mesh.shape)),
        mesh=mesh,
        in_specs=(
            P("blk", None, "ij", None),
            P("blk", None, None, "ij", None),
            P("blk", None, "ij", None),
            P("blk", None, "ij", None),
            P("blk", "ij", None),
            P(),
            P(),
            P(),
            P(),
        ),
        out_specs=(
            P("blk", None, "ij", None),
            P("blk", None, None, "ij", None),
            P("blk", None, "ij", None),
        ),
        check_vma=False,
    )
```

```python
import functools

import jax
import jax.numpy as jnp
from jax import lax
from jax.experimental import pallas as pl
from jax.experimental.pallas import tpu as pltpu
from jax.sharding import PartitionSpec as P

pressure_factor = 0.4
viscosity = 0.05
time_step = 0.03
unit = time_step / 12.0

LANES = 128
PAD = 8
DEPTH = 4
CH = 5
SENT = 2 * CH
PASSED = 2 * CH + 1
FIRST = 4


def turn(x, shift, axis):
    shift = shift % x.shape[axis]
    return x if shift == 0 else pltpu.roll(x, shift, axis)


def lanes_of(shape):
    return lax.broadcasted_iota(jnp.int32, shape, len(shape) - 1)


def rows_of(shape):
    return lax.broadcasted_iota(jnp.int32, shape, len(shape) - 2)


def plane_at(refs, c, k, rows):
    dens, mom, en, met, vol = refs
    if k == dens.shape[1]:
        return met[0, c, rows] if c < 4 else vol[0, rows]
    if c == 0:
        return dens[0, k, rows]
    if c == 4:
        return en[0, k, rows]
    return mom[0, c - 1, k, rows]


def point(f):
    rho, m1, m2, m3, e = f
    r = 1.0 / rho
    u1, u2, u3 = m1 * r, m2 * r, m3 * r
    kin = 0.5 * (m1 * u1 + m2 * u2 + m3 * u3)
    p = pressure_factor * (e - kin)
    return (u1, u2, u3, (kin + 2.0 * p) * r), p, e + p


def metric_terms(m):
    ax, ay, bx, by, v = m
    kv = viscosity * unit
    rw = kv * (ax * ax + ay * ay)
    cw = kv * (bx * bx + by * by)
    return v * ax, v * ay, v * bx, v * by, -unit / v, rw, cw, 30.0 * (rw + cw + kv)


def flux(f, w, p, h, gx, gy):
    rho, m1, m2, m3, _ = f
    u = gx * w[0] + gy * w[1]
    return (rho * u, m1 * u + gx * p, m2 * u + gy * p, m3 * u, h * u)


def flux_planes(f, w, p, h):
    u3 = w[2]
    return (f[3], f[1] * u3, f[2] * u3, f[3] * u3 + p, h * u3)


def slope(x, at):
    return 8.0 * (at(x, 1) - at(x, -1)) - (at(x, 2) - at(x, -2))


def curve(x, at):
    return 16.0 * (at(x, 1) + at(x, -1)) - (at(x, 2) + at(x, -2))


def along(axis):
    return lambda x, o: turn(x, -o, axis)


def plane_shift(x, o):
    o = o % x.shape[0]
    return jnp.concatenate([x[o:], x[:o]], axis=0)


def tile_rate(f, m, at_i, at_j):
    vax, vay, vbx, vby, niv, rw, cw, tw = metric_terms(m)
    kv = viscosity * unit
    w, p, h = point(f)
    fi = flux(f, w, p, h, vax, vay)
    fj = flux(f, w, p, h, vbx, vby)
    fk = flux_planes(f, w, p, h)
    out = []
    for c in range(CH):
        val = niv * (slope(fi[c], at_i) + slope(fj[c], at_j)) - unit * slope(fk[c], plane_shift)
        if c > 0:
            x = w[c - 1]
            val = val + (
                rw * curve(x, at_i) + cw * curve(x, at_j) + kv * curve(x, plane_shift) - tw * x
            )
        out.append(val)
    return out, fj, w, niv, cw


def pack_columns(x, k, low_from, high_from, packed):
    lane = lanes_of(x.shape)
    if (high_from - low_from) % LANES == 4:
        return jnp.where(lane // 8 == k, turn(x, 8 * k - low_from, 1), packed)
    packed = jnp.where(lane // 4 == 2 * k, turn(x, 8 * k - low_from, 1), packed)
    return jnp.where(lane // 4 == 2 * k + 1, turn(x, 8 * k + 4 - high_from, 1), packed)


def across(x):
    if x.shape[0] < LANES:
        x = jnp.concatenate([x, jnp.zeros((LANES - x.shape[0], LANES), jnp.float32)], axis=0)
    return x.T


def cut_kernel(halves, dens, mom, en, met, vol, placed, face, orient, send, own, *rest):
    edges, (scratch, *held, sems) = rest[:-7], rest[-7:]
    planes, rows = dens.shape[1], dens.shape[2]
    copies = [
        pltpu.make_async_copy(src, dst, sems.at[n])
        for n, (src, dst) in enumerate(zip((dens, mom, en, met, vol), held))
    ]
    for n in (3, 4, 0, 1, 2):
        copies[n].start()
    block = placed[lax.axis_index("blk")]
    half = lax.axis_index("ij")
    row = rows_of((64, LANES))
    high_side = row % 8 < 4
    mirror = jnp.where(
        rows_of((LANES, LANES)) + lanes_of((LANES, LANES)) == rows - 1, 1.0, 0.0
    )
    flip = [jnp.where(orient[block, f] == 1, -1.0, 1.0) for f in range(2)]
    same = [jnp.where(face[block, f] == f, -1.0, 1.0) for f in range(2)]
    rising = [face[block, f] == 1 for f in range(2)]
    turned = jnp.where(high_side, flip[1], flip[0])
    facing = jnp.where(high_side, same[1], same[0])
    for n in (3, 4):
        copies[n].wait()
    for c in range(CH):
        if c == 0:
            copies[0].wait()
        elif c == 1:
            copies[1].wait()
        elif c == 4:
            copies[2].wait()
        packed = jnp.zeros((rows, LANES), jnp.float32)
        for k in range(planes + 1):
            x = plane_at(held, c, k, slice(None))
            packed = pack_columns(x, k, LANES - 4, 0, packed)
        strip = across(packed)[0:64]
        own[c] = strip
        back = jnp.dot(
            strip,
            mirror,
            precision=lax.Precision.HIGHEST,
            preferred_element_type=jnp.float32,
        )
        moved = jnp.where(turned < 0.0, back, strip)
        if c < 4:
            moved = jnp.where(row >= planes * 8, moved * (turned if c < 2 else facing), moved)
        scratch[c * 64 : c * 64 + 64] = moved
    for k in range(planes + 1):
        for e in range(DEPTH):
            at = (FIRST + k * DEPTH + e) * SENT
            low = k * 8 + 4 + jnp.where(rising[0], e, 3 - e)
            high = k * 8 + jnp.where(rising[1], 3 - e, e)
            send[at : at + CH] = scratch[pl.ds(low, CH, stride=64)]
            send[at + CH : at + SENT] = scratch[pl.ds(high, CH, stride=64)]
    for c in range(CH):
        for k in range(planes + 1):
            low = plane_at(held, c, k, slice(0, 4))
            high = plane_at(held, c, k, slice(rows - 4, rows))
            if len(edges) == 1:
                edges[0][c, k * 4 : k * 4 + 4] = jnp.where(half == 0, high, low)
            else:
                edges[0][c, k * 4 : k * 4 + 4] = low
                edges[1][c, k * 4 : k * 4 + 4] = high


def relay_kernel(
    halves, rows, planes, placed, neighbour, face, orient, got, part,
    send, below, above, signs, where_is,
):
    del part
    blocks = placed.shape[0]
    devices = blocks * halves
    me = lax.axis_index("blk") * halves + lax.axis_index("ij")
    is_field = (me >= FIRST) & (me < FIRST + DEPTH * planes)

    def note(slot, _):
        where_is[placed[slot]] = slot
        return 0

    lax.fori_loop(0, blocks, note, 0, unroll=True)

    def pass_on(slot, _):
        block = placed[slot]
        for f in range(2):
            partner = where_is[neighbour[block, f]]
            side, turned = face[block, f], orient[block, f]
            sign = jnp.where(turned == 1, -1.0, 1.0)

            def piece(h):
                h = jnp.where(turned == 1, halves - 1 - h, h)
                return got[pl.ds((partner * halves + h) * SENT + side * CH, CH)]

            pieces = [piece(h) for h in range(halves)]
            for half in range(halves):
                at = slot * halves + half
                send[pl.ds(at * PASSED + f * CH, CH)] = pieces[half]
                below[pl.ds((f * devices + at) * 8, CH)] = pieces[max(half - 1, 0)]
                above[pl.ds((f * devices + at) * 8, CH)] = pieces[min(half + 1, halves - 1)]
                signs[pl.ds(f * devices + at, 1)] = jnp.full((1, LANES), sign, jnp.float32)
        return 0

    lax.fori_loop(0, blocks, pass_on, 0, unroll=4)
    count = 2 * devices
    lane = lanes_of((count, LANES))
    half = rows_of((count, LANES)) % halves
    sign = signs[...]
    ends = jnp.zeros((count, LANES), jnp.float32)
    for c in range(CH):
        low, high = below[pl.ds(c, count, stride=8)], above[pl.ds(c, count, stride=8)]
        at = 4 * c
        low_wall = jnp.where(lane == at, turn(low, at - 1, 1), turn(low, at + 1, 1))
        high_wall = jnp.where(
            lane == at + 2, turn(high, at + 3 - rows, 1), turn(high, at + 5 - rows, 1)
        )
        if 1 <= c <= 3:
            low_wall = jnp.where(is_field, -sign * low_wall, low_wall)
            high_wall = jnp.where(is_field, sign * high_wall, high_wall)
        low = jnp.where(half == 0, low_wall, turn(low, at + 2 - rows, 1))
        high = jnp.where(half == halves - 1, high_wall, turn(high, at + 2, 1))
        ends = jnp.where(lane // 2 == 2 * c, low, jnp.where(lane // 2 == 2 * c + 1, high, ends))
    send[pl.ds(2 * CH, devices, stride=PASSED)] = ends[0:devices] + turn(
        ends[devices:], 4 * CH, 1
    )


def flux_chunk(get, mets, fi, w, r, rest=None):
    rows = pl.ds(r, 8)
    vax, vay, vbx, vby, niv, rw, cw, tw = [mets[j, rows] for j in range(8)]
    at_j = along(1)
    for k in range(fi.shape[1]):
        f = [get(c, k, r) for c in range(CH)]
        wk, p, h = point(f)
        for c, x in enumerate(flux(f, wk, p, h, vax, vay)):
            fi[c, k, rows] = x
        for c in range(4):
            w[c, k, rows] = wk[c]
        if rest is None:
            continue
        fk, acc = rest
        fj = flux(f, wk, p, h, vbx, vby)
        for c in range(CH):
            val = niv * slope(fj[c], at_j)
            if c > 0:
                val = val + (cw * curve(wk[c - 1], at_j) - tw * wk[c - 1])
            acc[c, k, rows] = val
        for c, x in enumerate(flux_planes(f, wk, p, h)):
            fk[c, k, rows] = x


def sum_chunk(mets, fi, w, fk, acc, r, emit):
    planes = fi.shape[1]
    kv = viscosity * unit
    rows = pl.ds(r, 8)
    niv, rw = mets[4, rows], mets[5, rows]
    for c in range(CH):
        t = [fk[c, k, rows] for k in range(planes)]
        x = [w[c - 1, k, rows] for k in range(planes)] if c > 0 else None
        for k in range(planes):

            def near(v, o):
                return v[(k + o) % planes]

            def at_i(v, o):
                return v[pl.ds(r + o, 8)]

            val = acc[c, k, rows] + niv * slope(fi.at[c, k], at_i) - unit * slope(t, near)
            if c > 0:
                val = val + (rw * curve(w.at[c - 1, k], at_i) + kv * curve(x, near))
            emit(c, k, r, val)


def chunks(count, body):
    def step(n, _):
        body(pl.multiple_of(n * 8, 8))
        return 0

    lax.fori_loop(0, count, step, 0)


def first_kernel(dens, mom, en, met, vol, part, mets, fi, w, fk, acc):
    refs = (dens, mom, en, met, vol)
    planes, rows = dens.shape[1], dens.shape[2]

    def terms(r):
        m = [plane_at(refs, c, planes, pl.ds(r, 8)) for c in range(CH)]
        for j, x in enumerate(metric_terms(m)):
            mets[j, pl.ds(r + PAD, 8)] = x

    def get(c, k, r):
        return plane_at(refs, c, k, pl.ds(r - PAD, 8))

    def fluxes(r):
        terms(r)
        flux_chunk(get, mets, fi, w, r + PAD, (fk, acc))

    def emit(c, k, r, val):
        part[c, k, pl.ds(r - PAD, 8)] = get(c, k, r) + val

    def sums(r):
        sum_chunk(mets, fi, w, fk, acc, r + PAD, emit)

    empty = jnp.zeros((PAD, LANES), jnp.float32)
    for k in range(planes):
        for c in range(CH):
            fi[c, k, 0:PAD] = empty
            fi[c, k, rows + PAD :] = empty
        for c in range(4):
            w[c, k, 0:PAD] = empty
            w[c, k, rows + PAD :] = empty
    chunks(rows // 8, fluxes)
    chunks(rows // 8, sums)


def pack_ends(tall, count):
    row8, lane8 = rows_of((8, LANES)), lanes_of((8, LANES))
    stacked = []
    for c in range(CH):
        packed = jnp.zeros((8, LANES), jnp.float32)
        for k in range(count):
            x = jnp.where(row8 < 4, tall[0, c, k], tall[1, c, k])
            packed = pack_columns(x, k, LANES - 4, 0, packed)
        stacked.append(packed)
    ends = across(jnp.concatenate(stacked, axis=0))
    out = []
    for c in range(CH):
        x = jnp.zeros((8, LANES), jnp.float32)
        for k in range(count):
            moved = turn(ends[k * 8 : k * 8 + 8], 4 * k - (8 * c + 2), 1)
            x = jnp.where(lane8 // 4 == k, moved, x)
        out.append(x)
    return out


def second_kernel(
    halves, dens, mom, en, met, vol, below, above, part,
    out, ends_base, ends_sec, inner,
    tall, sec, mets, fi, w, fk, acc,
):
    refs = (dens, mom, en, met, vol)
    planes, rows = dens.shape[1], dens.shape[2]
    every = planes + 1
    half = lax.axis_index("ij")
    low_wall, high_wall = half == 0, half == halves - 1
    low_flag, high_flag = jnp.where(low_wall, 1, 0), jnp.where(high_wall, 1, 0)

    for c in range(CH):
        for k in range(every):
            tall[0, c, k, 4:8] = plane_at(refs, c, k, slice(0, 4))
            tall[1, c, k, 0:4] = plane_at(refs, c, k, slice(rows - 4, rows))

    @pl.when(low_wall)
    def _():
        for c in range(CH):
            for k in range(every):
                sign = -1.0 if 1 <= c <= 3 and k < planes else 1.0
                for d in range(4):
                    tall[0, c, k, 3 - d : 4 - d] = sign * plane_at(refs, c, k, slice(d, d + 1))

    @pl.when(jnp.logical_not(low_wall))
    def _():
        for c in range(CH):
            for k in range(every):
                tall[0, c, k, 0:4] = below[c, k * 4 : k * 4 + 4]

    @pl.when(high_wall)
    def _():
        for c in range(CH):
            for k in range(every):
                for d in range(4):
                    tall[1, c, k, 4 + d : 5 + d] = plane_at(
                        refs, c, k, slice(rows - 1 - d, rows - d)
                    )

    @pl.when(jnp.logical_not(high_wall))
    def _():
        for c in range(CH):
            for k in range(every):
                tall[1, c, k, 4:8] = above[c, k * 4 : k * 4 + 4]

    for c, x in enumerate(pack_ends(tall, every)):
        ends_base[c] = x

    def terms(r):
        m = [plane_at(refs, c, planes, pl.ds(r, 8)) for c in range(CH)]
        for j, x in enumerate(metric_terms(m)):
            mets[j, pl.ds(r + PAD, 8)] = x

    for end, at in ((0, PAD - 4), (1, PAD + rows - 4)):
        m = [tall[end, c, planes] for c in range(CH)]
        for j, x in enumerate(metric_terms(m)):
            mets[j, at : at + 8] = x

    def finish(r):
        for c in range(CH):
            for k in range(planes):
                sec[c, k, pl.ds(r + PAD, 8)] = part[c, k, pl.ds(r, 8)]

    chunks(rows // 8, finish)
    sub = rows_of((planes, 8, LANES))
    for end in range(2):
        start = -4 if end == 0 else rows - 4
        fields = [tall[end, c, 0:planes] for c in range(CH)]
        m = [tall[end, c, planes] for c in range(CH)]
        rate = tile_rate(fields, m, along(1), along(2))[0]
        for c in range(CH):
            x = fields[c] + rate[c]
            tall[end, c, 0:planes] = x
            if end == 0:
                sign = -1.0 if 1 <= c <= 3 else 1.0
                wall = sign * jnp.where(sub == 2, turn(x, -3, 1), turn(x, -1, 1))
                x = jnp.where((sub < 4) & (low_flag == 1), wall, x)
            else:
                wall = jnp.where(sub == 4, turn(x, 1, 1), turn(x, 3, 1))
                x = jnp.where((sub >= 4) & (high_flag == 1), wall, x)
            for k in range(planes):
                sec[c, k, PAD + start + 2 : PAD + start + 6] = x[k, 2:6]
    for c, x in enumerate(pack_ends(tall, planes)):
        ends_sec[c] = x
    for c in range(CH):
        packed = jnp.zeros((rows, LANES), jnp.float32)
        for k in range(every):
            x = sec[c, k, PAD : PAD + rows] if k < planes else plane_at(refs, c, k, slice(None))
            packed = pack_columns(x, k, LANES - 6, 2, packed)
        inner[c] = across(packed)[0:64]

    def get(c, k, r):
        return sec[c, k, pl.ds(r, 8)]

    def fluxes(r):
        terms(r)
        flux_chunk(get, mets, fi, w, r + PAD, (fk, acc))

    def emit(c, k, r, val):
        at = pl.ds(r - PAD, 8)
        out[c, k, at] = 0.5 * (plane_at(refs, c, k, at) + (get(c, k, r) + val))

    def sums(r):
        sum_chunk(mets, fi, w, fk, acc, r + PAD, emit)

    flux_chunk(get, mets, fi, w, 0)
    flux_chunk(get, mets, fi, w, rows + PAD)
    chunks(rows // 8, fluxes)
    chunks(rows // 8, sums)


def beyond(packed, f, k, rows):
    base = 4 * (7 * f + k)
    low = turn(packed, LANES - 2 - base, 1)
    top = rows % LANES
    high = low if top == 0 else turn(packed, top - 2 - base, 1)
    lane = lanes_of(packed.shape)

    def at(x, o):
        if o < 0:
            x = jnp.where(lane >= LANES + o, low, x)
        else:
            x = jnp.where((lane >= top) & (lane < top + o), high, x)
        return turn(x, -o, 1)

    return at


def strip_stage(rows, planes, fields, mets, ends, ends_gx, ends_gy, hold, done):
    kv = viscosity * unit
    fk, ws, acc = hold
    at_j = along(0)
    wx, px, hx = point(ends)
    fx = flux(ends, wx, px, hx, ends_gx, ends_gy)
    for f in range(2):
        vax, vay, vbx, vby, niv, rw, cw, tw = mets[f]
        for k in range(planes):
            x = [fields(c, f, k) for c in range(CH)]
            w, p, h = point(x)
            fi, fj = flux(x, w, p, h, vax, vay), flux(x, w, p, h, vbx, vby)
            for c in range(CH):
                val = niv * (slope(fi[c], beyond(fx[c], f, k, rows)) + slope(fj[c], at_j))
                if c > 0:
                    v = w[c - 1]
                    ext = beyond(wx[c - 1], f, k, rows)
                    val = val + (rw * curve(v, ext) + cw * curve(v, at_j) - tw * v)
                    ws[c - 1, f, k] = v
                acc[c, f, k] = x[c] + val
            for c, v in enumerate(flux_planes(x, w, p, h)):
                fk[c, f, k] = v
        for c in range(CH):
            t = [fk[c, f, k] for k in range(planes)]
            v = [ws[c - 1, f, k] for k in range(planes)] if c > 0 else None
            for k in range(planes):

                def near(y, o):
                    return y[(k + o) % planes]

                val = acc[c, f, k] - unit * slope(t, near)
                if c > 0:
                    val = val + kv * curve(v, near)
                done(c, f, k, val)


def last_kernel(
    halves, rows, planes, own, ends_base, ends_sec, inner, got, out,
    next_dens, next_mom, next_en,
    base, sec, fk, ws, acc, turned, back, full, sems,
):
    half = lax.axis_index("ij")
    low_wall, high_wall = half == 0, half == halves - 1
    sub, lane = rows_of((8, LANES)), lanes_of((8, LANES))

    def ghost(row, f, k):
        if f == 1:
            return got[pl.ds(DEPTH * k * PASSED + row, 8, stride=PASSED)]
        if k < planes:
            return got[pl.ds((FIRST + DEPTH * k) * PASSED + row, 8, stride=PASSED)]
        return turn(got[pl.ds(DEPTH * k * PASSED + row, 8, stride=PASSED)], 4, 0)

    def mix(f, mine, others):
        return jnp.where((sub < 4) == (f == 1), mine, others)

    for c in range(CH):
        for k in range(planes + 1):
            mine = own[c, k * 8 : k * 8 + 8]
            for f in range(2):
                base[c, f, k] = mix(f, mine, ghost(f * CH + c, f, k))
    mets = [metric_terms([base[c, f, planes] for c in range(CH)]) for f in range(2)]

    arrived = [[ghost(2 * CH, f, k) for k in range(planes + 1)] for f in range(2)]
    twice, ends = [], []
    for c in range(CH):
        mine = jnp.where(lane < 28, ends_base[c], turn(ends_base[c], 28, 1))
        others = jnp.zeros((8, LANES), jnp.float32)
        for f in range(2):
            for k in range(planes + 1):
                to = 28 * f + 4 * k
                moved = turn(arrived[f][k], to - 4 * CH * f - 4 * c, 1)
                others = jnp.where(lane // 4 == to // 4, moved, others)
        twice.append(mine)
        ends.append(jnp.where((lane < 28) == (sub >= 4), mine, others))

    def spread(x):
        y = x
        for k in range(planes):
            y = jnp.where((lane % 28) // 4 == k, turn(x, 4 * (k - planes), 1), y)
        return y

    vax, vay, vbx, vby, niv, rw, cw, tw = [spread(x) for x in metric_terms(ends)]
    wrapped = [spread(x) for x in metric_terms(twice)[2:4]]

    def keep(c, f, k, val):
        sec[c, f, k] = val

    strip_stage(
        rows, planes, lambda c, f, k: base[c, f, k], mets, ends, vax, vay, (fk, ws, acc), keep
    )

    for c in range(CH):
        for k in range(planes + 1):
            mine = inner[c, k * 8 : k * 8 + 8]
            for f in range(2):
                x = sec[c, f, k] if k < planes else base[c, f, k]
                sec[c, f, k] = mix(f, mine, turn(x, 2 if f == 1 else -2, 0))

    def shifted(x):
        return jnp.where(lane < 28, turn(x, -2, 0), turn(x, 2, 0))

    w1, p1, h1 = point(ends)
    w0, p0, h0 = point(twice)
    new, old = flux(ends, w1, p1, h1, vbx, vby), flux(twice, w0, p0, h0, *wrapped)
    at_j = along(0)
    touched = jnp.where(lane < 28, (sub - 4) // 2, (sub - 2) // 2) == 0
    second = []
    for c in range(CH):
        add = niv * slope(new[c] - old[c], at_j)
        if c > 0:
            add = add + cw * curve(w1[c - 1] - w0[c - 1], at_j)
        x = jnp.where(lane < 28, ends_sec[c], turn(ends_sec[c], 28, 1))
        x = shifted(x + jnp.where(touched, add, 0.0))
        for f in range(2):
            for k in range(planes):
                to = 28 * f + 4 * k
                first = jnp.where(low_wall, to, to + 2)
                one = pltpu.roll(
                    sec[c, f, k], jnp.where(low_wall, (to - 1) % LANES, (to + 3 - rows) % LANES), 1
                )
                two = pltpu.roll(
                    sec[c, f, k], jnp.where(low_wall, (to + 1) % LANES, (to + 5 - rows) % LANES), 1
                )
                if 1 <= c <= 3:
                    sign = jnp.where(low_wall, -1.0, 1.0)
                    one, two = sign * one, sign * two
                at = jnp.where(low_wall | high_wall, lane - first, -1)
                x = jnp.where(at == 0, one, jnp.where(at == 1, two, x))
        second.append(x)
    mets = [metric_terms([sec[c, f, planes] for c in range(CH)]) for f in range(2)]
    strip_stage(
        rows, planes, lambda c, f, k: sec[c, f, k], mets, second, shifted(vax), shifted(vay),
        (fk, ws, acc), keep,
    )

    per = LANES // 8
    for c in range(CH):
        for k in range(planes):
            x = jnp.where(sub < 4, turn(sec[c, 1, k], -2, 0), turn(sec[c, 0, k], 2, 0))
            at = (c * planes + k) * 8
            turned[at : at + 8] = 0.5 * (own[c, k * 8 : k * 8 + 8] + x)
    blocks = turned.shape[0] // LANES
    for n in range(blocks):
        back[n] = turned[n * LANES : (n + 1) * LANES].T
    copies = []
    for c in range(CH):

        def merge(r, c=c):
            at = pl.ds(r, 8)
            for k in range(planes):
                index = c * planes + k
                moved = turn(back[index // per, at], LANES - 4 - 8 * (index % per), 1)
                inside = (lane >= 4) & (lane < LANES - 4)
                full[c, k, at] = jnp.where(inside, out[c, k, at], moved)

        chunks(rows // 8, merge)
        dst = next_dens.at[0] if c == 0 else next_en.at[0] if c == 4 else next_mom.at[0, c - 1]
        copies.append(pltpu.make_async_copy(full.at[c], dst, sems.at[c]))
        copies[-1].start()
    for copy in copies:
        copy.wait()


def local(mesh_shape, density, momentum, energy, metrics, volume, placed, neighbour, face, orient):
    halves = mesh_shape["ij"]
    devices = mesh_shape["blk"] * halves
    planes, rows = density.shape[1], density.shape[2]
    every = planes + 1
    fields = (density, momentum, energy, metrics, volume)
    f32 = jnp.float32
    vmem = pl.BlockSpec(memory_space=pltpu.VMEM)
    smem = pl.BlockSpec(memory_space=pltpu.SMEM)
    hbm = pl.BlockSpec(memory_space=pltpu.HBM)

    def call(kernel, name, outs, ins, out_specs, scratch, mib, cost=None):
        return pl.pallas_call(
            kernel,
            out_shape=outs,
            in_specs=ins,
            out_specs=out_specs,
            scratch_shapes=scratch,
            compiler_params=pltpu.CompilerParams(vmem_limit_bytes=mib * 1024 * 1024),
            cost_estimate=cost,
            name=name,
        )

    def shape(*dims):
        return jax.ShapeDtypeStruct(dims, f32)

    edge = shape(CH, 4 * every, LANES)
    edges = 1 if halves == 2 else 2
    sent, own, *halo = call(
        functools.partial(cut_kernel, halves),
        "cut",
        [shape(devices * SENT, LANES), shape(CH, 64, LANES)] + [edge] * edges,
        [hbm] * 5 + [smem] * 3,
        [vmem] * (2 + edges),
        [pltpu.VMEM((CH * 64, LANES), f32)]
        + [pltpu.VMEM(x.shape, f32) for x in fields]
        + [pltpu.SemaphoreType.DMA((5,))],
        16,
    )(*fields, placed, face, orient)

    def swap(x):
        x = x.reshape(devices, x.shape[0] // devices, 1, LANES)
        x = lax.all_to_all(x, ("blk", "ij"), 0, 0, tiled=True)
        return x.reshape(x.shape[0] * x.shape[1], LANES)

    got = swap(sent)
    if edges == 1:
        below = above = lax.ppermute(halo[0], "ij", [(0, 1), (1, 0)])
    else:
        below = lax.ppermute(halo[1], "ij", [(i, i + 1) for i in range(halves - 1)])
        above = lax.ppermute(halo[0], "ij", [(i + 1, i) for i in range(halves - 1)])

    tall = rows + 2 * PAD
    block = shape(CH, planes, rows, LANES)
    stage = [
        pltpu.VMEM((8, tall, LANES), f32),
        pltpu.VMEM((CH, planes, tall, LANES), f32),
        pltpu.VMEM((4, planes, tall, LANES), f32),
        pltpu.VMEM((CH, planes, tall, LANES), f32),
        pltpu.VMEM((CH, planes, tall, LANES), f32),
    ]
    work = planes * rows * LANES
    cost = pl.CostEstimate(flops=300 * work, bytes_accessed=150 * work, transcendentals=work)
    part = call(
        first_kernel, "first_section", block, [vmem] * 5, vmem, stage, 24, cost
    )(*fields)
    relayed = call(
        functools.partial(relay_kernel, halves, rows, planes),
        "relay",
        shape(devices * PASSED, LANES),
        [smem] * 4 + [vmem, pl.BlockSpec(memory_space=pl.ANY)],
        vmem,
        [
            pltpu.VMEM((devices * 16, LANES), f32),
            pltpu.VMEM((devices * 16, LANES), f32),
            pltpu.VMEM((devices * 2, LANES), f32),
            pltpu.SMEM((placed.shape[0],), jnp.int32),
        ],
        16,
    )(placed, neighbour, face, orient, got, part)
    ghosts = swap(relayed)
    out, ends_base, ends_sec, inner = call(
        functools.partial(second_kernel, halves),
        "second_section",
        [block, shape(CH, 8, LANES), shape(CH, 8, LANES), shape(CH, 64, LANES)],
        [vmem] * 8,
        [vmem] * 4,
        [
            pltpu.VMEM((2, CH, every, 8, LANES), f32),
            pltpu.VMEM((CH, planes, tall, LANES), f32),
        ]
        + stage,
        32,
        cost,
    )(*fields, below, above, part)
    strip = pltpu.VMEM((CH, 2, every, 8, LANES), f32)
    flat = -(-CH * planes * 8 // LANES)
    return call(
        functools.partial(last_kernel, halves, rows, planes),
        "strips",
        [shape(*density.shape), shape(*momentum.shape), shape(*energy.shape)],
        [vmem] * 6,
        [hbm] * 3,
        [strip] * 5
        + [
            pltpu.VMEM((flat * LANES, LANES), f32),
            pltpu.VMEM((flat, LANES, LANES), f32),
            pltpu.VMEM((CH, planes, rows, LANES), f32),
            pltpu.SemaphoreType.DMA((CH,)),
        ],
        16,
    )(own, ends_base, ends_sec, inner, ghosts, out)


def solution(mesh):
    return jax.shard_map(
        functools.partial(local, dict(mesh.shape)),
        mesh=mesh,
        in_specs=(
            P("blk", None, "ij", None),
            P("blk", None, None, "ij", None),
            P("blk", None, "ij", None),
            P("blk", None, "ij", None),
            P("blk", "ij", None),
            P(),
            P(),
            P(),
            P(),
        ),
        out_specs=(
            P("blk", None, "ij", None),
            P("blk", None, None, "ij", None),
            P("blk", None, "ij", None),
        ),
        check_vma=False,
    )
```

```python
import functools

import jax
import jax.numpy as jnp
from jax import lax
from jax.experimental import pallas as pl
from jax.experimental.pallas import tpu as pltpu
from jax.sharding import PartitionSpec as P

pressure_factor = 0.4
viscosity = 0.05
time_step = 0.03
unit = time_step / 12.0

LANES = 128
PAD = 8
DEPTH = 4
CH = 5
VMEM_LIMIT = 60 * 1024 * 1024
SENT = 2 * CH
PASSED = 2 * CH + 1
FIRST = 4


def turn(x, shift, axis):
    shift = shift % x.shape[axis]
    return x if shift == 0 else pltpu.roll(x, shift, axis)


def lanes_of(shape):
    return lax.broadcasted_iota(jnp.int32, shape, len(shape) - 1)


def rows_of(shape):
    return lax.broadcasted_iota(jnp.int32, shape, len(shape) - 2)


def metric_at(refs, c, rows):
    return refs[3][0, c, rows] if c < 4 else refs[4][0, rows]


def field_at(refs, c, k, rows):
    dens, mom, en, _, _ = refs
    if c == 0:
        return dens[0, k, rows]
    if c == 4:
        return en[0, k, rows]
    return mom[0, c - 1, k, rows]


def point(f):
    rho, m1, m2, m3, e = f
    r = 1.0 / rho
    u1, u2, u3 = m1 * r, m2 * r, m3 * r
    kin = 0.5 * (m1 * u1 + m2 * u2 + m3 * u3)
    p = pressure_factor * (e - kin)
    return (u1, u2, u3, (kin + 2.0 * p) * r), p, e + p


def metric_terms(m):
    ax, ay, bx, by, v = m
    kv = viscosity * unit
    rw = kv * (ax * ax + ay * ay)
    cw = kv * (bx * bx + by * by)
    return v * ax, v * ay, v * bx, v * by, -unit / v, rw, cw, 30.0 * (rw + cw + kv)


def flux(f, w, p, h, gx, gy):
    rho, m1, m2, m3, _ = f
    u = gx * w[0] + gy * w[1]
    return (rho * u, m1 * u + gx * p, m2 * u + gy * p, m3 * u, h * u)


def flux_planes(f, w, p, h):
    u3 = w[2]
    return (f[3], f[1] * u3, f[2] * u3, f[3] * u3 + p, h * u3)


def slope(x, at):
    return 8.0 * (at(x, 1) - at(x, -1)) - (at(x, 2) - at(x, -2))


def curve(x, at):
    return 16.0 * (at(x, 1) + at(x, -1)) - (at(x, 2) + at(x, -2))


def along(axis):
    return lambda x, o: turn(x, -o, axis)


def within(lane, start, size):
    return (lane >= start) & (lane < start + size)


def roll_by(x, shift, axis=1):
    size = x.shape[axis]
    return pltpu.roll(x, lax.rem(shift + 4 * size, size), axis)


def across(x):
    if x.shape[0] < LANES:
        x = jnp.concatenate([x, jnp.zeros((LANES - x.shape[0], LANES), jnp.float32)], axis=0)
    return x.T


def loop(count, body, start=None, unroll=1):
    if start is None:

        def step(n, _):
            body(n)
            return 0

        lax.fori_loop(0, count, step, 0, unroll=unroll)
        return None
    return lax.fori_loop(0, count, body, start, unroll=unroll)


def fetch(sources, targets, sems):
    copies = [
        pltpu.make_async_copy(src, dst, sems.at[n])
        for n, (src, dst) in enumerate(zip(sources, targets))
    ]
    for copy in copies:
        copy.start()
    return copies


def tile_stage(planes, load, mets, shift_i, shift_j, hold, done):
    kv = viscosity * unit
    fk, ws, acc = hold

    def spread(k):
        for s in range(2):
            vax, vay, vbx, vby, niv, rw, cw, tw = mets[s]
            x = [load(c, s, k) for c in range(CH)]
            w, p, h = point(x)
            fi, fj = flux(x, w, p, h, vax, vay), flux(x, w, p, h, vbx, vby)
            for c in range(CH):
                val = niv * (slope(fi[c], shift_i(0, c, s, k)) + slope(fj[c], shift_j))
                if c > 0:
                    v = w[c - 1]
                    val = val + (
                        rw * curve(v, shift_i(1, c - 1, s, k)) + cw * curve(v, shift_j) - tw * v
                    )
                    ws[c - 1, s, k] = v
                acc[c, s, k] = x[c] + val
            for c, v in enumerate(flux_planes(x, w, p, h)):
                fk[c, s, k] = v

    def gather(k):
        at = {o: lax.rem(k + o + planes, planes) for o in (-2, -1, 0, 1, 2)}
        for s in range(2):
            for c in range(CH):
                val = acc[c, s, k] - unit * slope(0, lambda _, o: fk[c, s, at[o]])
                if c > 0:
                    val = val + kv * curve(0, lambda _, o: ws[c - 1, s, at[o]])
                done(c, s, k, val)

    loop(planes, spread)
    loop(planes, gather)


def cut_kernel(
    halves, dens, mom, en, met, vol, placed, face, orient, send, own, *rest
):
    edges, (packed, strips, *held, sems) = rest[:-8], rest[-8:]
    copies = fetch((dens, mom, en, met, vol), held, sems)
    planes, rows = dens.shape[1], dens.shape[2]
    block = placed[lax.axis_index("blk")]
    half = lax.axis_index("ij")
    row, lane = rows_of((64, LANES)), lanes_of((8, LANES))
    high_side = row % 8 < 4
    mirror = jnp.where(
        rows_of((LANES, LANES)) + lanes_of((LANES, LANES)) == rows - 1, 1.0, 0.0
    )
    flip = [jnp.where(orient[f, block] == 1, -1.0, 1.0) for f in range(2)]
    same = [jnp.where(face[f, block] == f, -1.0, 1.0) for f in range(2)]
    rising = [face[f, block] == 1 for f in range(2)]
    turned = jnp.where(high_side, flip[1], flip[0])
    facing = jnp.where(high_side, same[1], same[0])
    for copy in copies:
        copy.wait()
    if rows < LANES:
        packed[...] = jnp.zeros(packed.shape, jnp.float32)

    def pack(r):
        for c in range(CH):
            out = turn(metric_at(held, c, pl.ds(r, 8)), 8 * planes + 4, 1)
            for k in range(planes):
                x = turn(field_at(held, c, k, pl.ds(r, 8)), 8 * k + 4, 1)
                out = jnp.where(within(lane, 8 * k, 8), x, out)
            packed[c, pl.ds(r, 8)] = out

    chunks(rows // 8, pack)

    def orient_strip(c):
        strip = packed[c].T[0:64]
        own[c] = strip
        back = jnp.dot(
            strip,
            mirror,
            precision=lax.Precision.HIGHEST,
            preferred_element_type=jnp.float32,
        )
        moved = jnp.where(turned < 0.0, back, strip)
        sign = jnp.where(c < 2, turned, jnp.where(c < 4, facing, 1.0))
        moved = jnp.where(row >= planes * 8, moved * sign, moved)
        strips[pl.ds(pl.multiple_of(c * 64, 64), 64)] = moved

    loop(CH, orient_strip)

    def put(n):
        k, e = n >> 2, n & 3
        at = (FIRST + n) * SENT
        low = k * 8 + 4 + jnp.where(rising[0], e, 3 - e)
        high = k * 8 + jnp.where(rising[1], 3 - e, e)
        send[pl.ds(at, CH)] = strips[pl.ds(low, CH, stride=64)]
        send[pl.ds(at + CH, CH)] = strips[pl.ds(high, CH, stride=64)]

    loop(DEPTH * (planes + 1), put, unroll=4)

    def edge(c, at, low, high):
        if len(edges) == 1:
            edges[0][c, pl.ds(at, 4)] = jnp.where(half == 0, high, low)
        else:
            edges[0][c, pl.ds(at, 4)] = low
            edges[1][c, pl.ds(at, 4)] = high

    def cut_ends(k):
        for c in range(CH):
            low = field_at(held, c, k, slice(0, 4))
            edge(c, k * 4, low, field_at(held, c, k, slice(rows - 4, rows)))

    loop(planes, cut_ends)
    for c in range(CH):
        low = metric_at(held, c, slice(0, 4))
        edge(c, planes * 4, low, metric_at(held, c, slice(rows - 4, rows)))


def relay_kernel(
    halves, rows, planes, placed, neighbour, face, orient, got, part,
    send, below, above, signs, where_is,
):
    del part
    blocks = placed.shape[0]
    devices = blocks * halves
    me = lax.axis_index("blk") * halves + lax.axis_index("ij")
    is_field = (me >= FIRST) & (me < FIRST + DEPTH * planes)

    def note(slot, _):
        where_is[placed[slot]] = slot
        return 0

    lax.fori_loop(0, blocks, note, 0, unroll=True)

    def pass_on(slot, _):
        block = placed[slot]
        for f in range(2):
            partner = where_is[neighbour[f, block]]
            side, turned = face[f, block], orient[f, block]
            sign = jnp.where(turned == 1, -1.0, 1.0)

            def piece(h):
                h = jnp.where(turned == 1, halves - 1 - h, h)
                return got[pl.ds((partner * halves + h) * SENT + side * CH, CH)]

            pieces = [piece(h) for h in range(halves)]
            for half in range(halves):
                at = slot * halves + half
                send[pl.ds(at * PASSED + f * CH, CH)] = pieces[half]
                below[pl.ds((f * devices + at) * 8, CH)] = pieces[max(half - 1, 0)]
                above[pl.ds((f * devices + at) * 8, CH)] = pieces[min(half + 1, halves - 1)]
                signs[pl.ds(f * devices + at, 1)] = jnp.full((1, LANES), sign, jnp.float32)
        return 0

    lax.fori_loop(0, blocks, pass_on, 0, unroll=4)
    count = 2 * devices
    lane = lanes_of((count, LANES))
    half = rows_of((count, LANES)) % halves
    sign = signs[...]
    ends = jnp.zeros((count, LANES), jnp.float32)
    for c in range(CH):
        low, high = below[pl.ds(c, count, stride=8)], above[pl.ds(c, count, stride=8)]
        at = 4 * c
        low_wall = jnp.where(lane == at, turn(low, at - 1, 1), turn(low, at + 1, 1))
        high_wall = jnp.where(
            lane == at + 2, turn(high, at + 3 - rows, 1), turn(high, at + 5 - rows, 1)
        )
        if 1 <= c <= 3:
            low_wall = jnp.where(is_field, -sign * low_wall, low_wall)
            high_wall = jnp.where(is_field, sign * high_wall, high_wall)
        low = jnp.where(half == 0, low_wall, turn(low, at + 2 - rows, 1))
        high = jnp.where(half == halves - 1, high_wall, turn(high, at + 2, 1))
        ends = jnp.where(within(lane, at, 2), low, jnp.where(within(lane, at + 2, 2), high, ends))
    send[pl.ds(2 * CH, devices, stride=PASSED)] = ends[0:devices] + turn(
        ends[devices:], 4 * CH, 1
    )


def flux_chunk(get, mets, fi, w, fk, acc, r):
    rows = pl.ds(r, 8)
    vax, vay, vbx, vby, niv, rw, cw, tw = [mets[j, rows] for j in range(8)]
    at_j = along(1)
    for k in range(fi.shape[1]):
        f = [get(c, k, r) for c in range(CH)]
        wk, p, h = point(f)
        for c, x in enumerate(flux(f, wk, p, h, vax, vay)):
            fi[c, k, rows] = x
        for c in range(4):
            w[c, k, rows] = wk[c]
        fj = flux(f, wk, p, h, vbx, vby)
        for c in range(CH):
            val = niv * slope(fj[c], at_j)
            if c > 0:
                val = val + (cw * curve(wk[c - 1], at_j) - tw * wk[c - 1])
            acc[c, k, rows] = val
        for c, x in enumerate(flux_planes(f, wk, p, h)):
            fk[c, k, rows] = x


def sum_chunk(mets, fi, w, fk, acc, r, emit):
    planes = fi.shape[1]
    kv = viscosity * unit
    rows = pl.ds(r, 8)
    niv, rw = mets[4, rows], mets[5, rows]
    for c in range(CH):
        t = [fk[c, k, rows] for k in range(planes)]
        x = [w[c - 1, k, rows] for k in range(planes)] if c > 0 else None
        for k in range(planes):

            def near(v, o):
                return v[(k + o) % planes]

            def at_i(v, o):
                return v[pl.ds(r + o, 8)]

            val = acc[c, k, rows] + niv * slope(fi.at[c, k], at_i) - unit * slope(t, near)
            if c > 0:
                val = val + (rw * curve(w.at[c - 1, k], at_i) + kv * curve(x, near))
            emit(c, k, r, val)


def chunks(count, body):
    def step(n, _):
        body(pl.multiple_of(n * 8, 8))
        return 0

    lax.fori_loop(0, count, step, 0)


def first_kernel(
    dens, mom, en, met, vol, part, d, m, e, t, v, full, mets, fi, w, fk, acc, sems, out_sems
):
    held = (d, m, e, t, v)
    copies = fetch((dens, mom, en, met, vol), held, sems)
    planes, rows = dens.shape[1], dens.shape[2]
    for copy in copies:
        copy.wait()

    def get(c, k, r):
        return field_at(held, c, k, pl.ds(r - PAD, 8))

    def fluxes(r):
        terms = metric_terms([metric_at(held, c, pl.ds(r, 8)) for c in range(CH)])
        for j, x in enumerate(terms):
            mets[j, pl.ds(r + PAD, 8)] = x
        flux_chunk(get, mets, fi, w, fk, acc, r + PAD)

    def emit(c, k, r, val):
        full[c, k, pl.ds(r - PAD, 8)] = get(c, k, r) + val

    def leave(r):
        at = pl.ds(r, 8)
        return pltpu.make_async_copy(full.at[:, :, at], part.at[:, :, at], out_sems.at[r // 8])

    def sums(r):
        sum_chunk(mets, fi, w, fk, acc, r + PAD, emit)
        leave(r).start()

    chunks(rows // 8, fluxes)
    chunks(rows // 8, sums)
    chunks(rows // 8, lambda r: leave(r).wait())


def pack_ends(tall, scratch, planes, extra):
    sub, lane = rows_of((8, LANES)), lanes_of((8, LANES))
    count = planes + extra

    def first(k, packed):
        out = []
        for c in range(CH):
            x = roll_by(jnp.where(sub < 4, tall[0, c, k], tall[1, c, k]), 8 * k + 4)
            out.append(jnp.where(within(lane, 8 * k, 8), x, packed[c]))
        return tuple(out)

    empty = jnp.zeros((8, LANES), jnp.float32)
    packed = loop(count, first, (empty,) * CH)
    scratch[...] = across(jnp.concatenate(packed, axis=0))

    def second(k, packed):
        x = scratch[pl.ds(pl.multiple_of(8 * k, 8), 8)]
        return tuple(
            jnp.where(within(lane, 4 * k, 4), roll_by(x, 4 * k - (8 * c + 2)), packed[c])
            for c in range(CH)
        )

    return loop(count, second, (empty,) * CH)


def second_kernel(
    halves, dens, mom, en, met, vol, below, above, part,
    out, ends_base, ends_sec, inner,
    d, m, e, t, v, tall, packed, tile_fk, tile_w, tile_acc,
    sec, full, mets, fi, w, fk, acc, sems, out_sems,
):
    held = (d, m, e, t, v)
    planes, rows = dens.shape[1], dens.shape[2]
    copies = fetch((dens, mom, en, met, vol), held, sems)
    arrive = pltpu.make_async_copy(part, sec.at[:, :, PAD : PAD + rows], sems.at[5])
    arrive.start()
    half = lax.axis_index("ij")
    low_wall, high_wall = half == 0, half == halves - 1
    low_flag, high_flag = jnp.where(low_wall, 1, 0), jnp.where(high_wall, 1, 0)
    sub, lane = rows_of((8, LANES)), lanes_of((8, LANES))
    for copy in copies:
        copy.wait()

    def ends_of(c, k, low, high, others, sign):
        tall[0, c, k, 4:8] = low
        tall[1, c, k, 0:4] = high
        for n in range(4):
            near = jnp.where(low_wall, sign * low[3 - n : 4 - n], others[0][n : n + 1])
            far = jnp.where(high_wall, high[3 - n : 4 - n], others[1][n : n + 1])
            tall[0, c, k, n : n + 1] = near
            tall[1, c, k, 4 + n : 5 + n] = far

    def set_ends(k):
        for c in range(CH):
            low, high = (
                field_at(held, c, k, slice(0, 4)),
                field_at(held, c, k, slice(rows - 4, rows)),
            )
            others = (below[c, pl.ds(4 * k, 4)], above[c, pl.ds(4 * k, 4)])
            ends_of(c, k, low, high, others, -1.0 if 1 <= c <= 3 else 1.0)

    loop(planes, set_ends)
    for c in range(CH):
        low, high = metric_at(held, c, slice(0, 4)), metric_at(held, c, slice(rows - 4, rows))
        others = (below[c, 4 * planes : 4 * planes + 4], above[c, 4 * planes : 4 * planes + 4])
        ends_of(c, planes, low, high, others, 1.0)
    for c, x in enumerate(pack_ends(tall, packed.at[0], planes, 1)):
        ends_base[c] = x

    def terms(r):
        out = metric_terms([metric_at(held, c, pl.ds(r, 8)) for c in range(CH)])
        for j, x in enumerate(out):
            mets[j, pl.ds(r + PAD, 8)] = x

    chunks(rows // 8, terms)
    tall_mets = [metric_terms([tall[s, c, planes] for c in range(CH)]) for s in range(2)]
    for s, at in ((0, PAD - 4), (1, PAD + rows - 4)):
        for j, x in enumerate(tall_mets[s]):
            mets[j, at : at + 8] = x

    arrive.wait()

    def done(c, s, k, x):
        tall[s, c, k] = x
        if s == 0:
            sign = -1.0 if 1 <= c <= 3 else 1.0
            wall = sign * jnp.where(sub == 2, turn(x, -3, 0), turn(x, -1, 0))
            x = jnp.where((sub < 4) & (low_flag == 1), wall, x)
        else:
            wall = jnp.where(sub == 4, turn(x, 1, 0), turn(x, 3, 0))
            x = jnp.where((sub >= 4) & (high_flag == 1), wall, x)
        start = PAD - 2 if s == 0 else PAD + rows - 2
        sec[c, k, start : start + 4] = x[2:6]

    tile_stage(
        planes, lambda c, s, k: tall[s, c, k], tall_mets, lambda *_: along(0), along(1),
        (tile_fk, tile_w, tile_acc), done,
    )
    for c, x in enumerate(pack_ends(tall, packed.at[0], planes, 0)):
        ends_sec[c] = x

    if rows < LANES:
        packed[...] = jnp.zeros(packed.shape, jnp.float32)

    def pack(r):
        for c in range(CH):
            x = metric_at(held, c, pl.ds(r, 8))
            at = 8 * planes
            out = jnp.where(lane < at + 4, turn(x, at + 6, 1), turn(x, at + 2, 1))
            for k in range(planes):
                x = sec[c, k, pl.ds(r + PAD, 8)]
                at = 8 * k
                out = jnp.where(within(lane, at, 4), turn(x, at + 6, 1), out)
                out = jnp.where(within(lane, at + 4, 4), turn(x, at + 2, 1), out)
            packed[c, pl.ds(r, 8)] = out

    chunks(rows // 8, pack)

    def flip(c):
        inner[c] = packed[c].T[0:64]

    loop(CH, flip)

    def get(c, k, r):
        return sec[c, k, pl.ds(r, 8)]

    def emit(c, k, r, val):
        at = pl.ds(r - PAD, 8)
        full[c, k, at] = 0.5 * (field_at(held, c, k, at) + (get(c, k, r) + val))

    def leave(r):
        at = pl.ds(r, 8)
        return pltpu.make_async_copy(full.at[:, :, at], out.at[:, :, at], out_sems.at[r // 8])

    def sums(r):
        sum_chunk(mets, fi, w, fk, acc, r + PAD, emit)
        leave(r).start()

    chunks(rows // 8 + 2, lambda r: flux_chunk(get, mets, fi, w, fk, acc, r))
    chunks(rows // 8, sums)
    chunks(rows // 8, lambda r: leave(r).wait())


def beyond(packed, f, k, rows):
    base = 28 * f + 4 * k
    low = roll_by(packed, LANES - 2 - base)
    top = rows % LANES
    high = low if top == 0 else roll_by(packed, top - 2 - base)
    lane = lanes_of(packed.shape)

    def at(x, o):
        if o < 0:
            x = jnp.where(lane >= LANES + o, low, x)
        else:
            x = jnp.where(within(lane, top, o), high, x)
        return turn(x, -o, 1)

    return at


def last_kernel(
    halves, rows, planes, own, ends_base, ends_sec, inner, got, out,
    next_dens, next_mom, next_en,
    base, sec, fk, ws, acc, turned, back, full, sems,
):
    arrive = pltpu.make_async_copy(out, full, sems.at[CH])
    arrive.start()
    half = lax.axis_index("ij")
    low_wall, high_wall = half == 0, half == halves - 1
    sub, lane = rows_of((8, LANES)), lanes_of((8, LANES))

    def mix(f, mine, others):
        return jnp.where((sub < 4) == (f == 1), mine, others)

    def gather(k, others):
        start = DEPTH * k * PASSED

        def ghost(row, f):
            x = got[pl.ds(start + row, 8, stride=PASSED)]
            return x if f == 1 else turn(x, 4, 0)

        others = list(others)
        for f in range(2):
            arrived = ghost(2 * CH, f)
            to = 28 * f + 4 * k
            for c in range(CH):
                mine = own[c, pl.ds(pl.multiple_of(k * 8, 8), 8)]
                base[c, f, k] = mix(f, mine, ghost(f * CH + c, f))
                moved = roll_by(arrived, to - 4 * CH * f - 4 * c)
                others[c] = jnp.where(within(lane, to, 4), moved, others[c])
        return tuple(others)

    empty = jnp.zeros((8, LANES), jnp.float32)
    others = loop(planes + 1, gather, (empty,) * CH)
    low_lanes = lane < 28
    twice = [jnp.where(low_lanes, ends_base[c], turn(ends_base[c], 28, 1)) for c in range(CH)]
    ends = [jnp.where(low_lanes == (sub >= 4), twice[c], others[c]) for c in range(CH)]
    slot = jnp.where(low_lanes, lane, lane - 28)

    def spread(k, kept):
        shift, hit = 4 * (k - planes), within(slot, 4 * k, 4)
        return tuple((x, jnp.where(hit, roll_by(x, shift), y)) for x, y in kept)

    kept = metric_terms(ends)[0:5] + metric_terms(ends)[6:7] + metric_terms(twice)[2:4]
    kept = loop(planes, spread, tuple((x, x) for x in kept))
    vax, vay, vbx, vby, niv, cw, *wrapped = [y for _, y in kept]

    def keep(c, f, k, val):
        sec[c, f, k] = val

    def stage(held, ends, gx, gy):
        mets = [metric_terms([held[c, f, planes] for c in range(CH)]) for f in range(2)]
        w, p, h = point(ends)
        rims = (flux(ends, w, p, h, gx, gy), w)
        tile_stage(
            planes,
            lambda c, f, k: held[c, f, k],
            mets,
            lambda kind, c, f, k: beyond(rims[kind][c], f, k, rows),
            along(0),
            (fk, ws, acc),
            keep,
        )

    stage(base, ends, vax, vay)

    def move(k, source):
        for c in range(CH):
            mine = inner[c, pl.ds(pl.multiple_of(k * 8, 8), 8)]
            for f in range(2):
                sec[c, f, k] = mix(f, mine, turn(source[c, f, k], 2 if f == 1 else -2, 0))

    loop(planes, lambda k: move(k, sec))
    move(jnp.int32(planes), base)

    def shifted(x):
        return jnp.where(low_lanes, turn(x, -2, 0), turn(x, 2, 0))

    w1, p1, h1 = point(ends)
    w0, p0, h0 = point(twice)
    new, old = flux(ends, w1, p1, h1, vbx, vby), flux(twice, w0, p0, h0, *wrapped)
    at_j = along(0)
    touched = within(sub, jnp.where(low_lanes, 4, 2), 2)
    second = []
    for c in range(CH):
        add = niv * slope(new[c] - old[c], at_j)
        if c > 0:
            add = add + cw * curve(w1[c - 1] - w0[c - 1], at_j)
        x = jnp.where(low_lanes, ends_sec[c], turn(ends_sec[c], 28, 1))
        second.append(shifted(x + jnp.where(touched, add, 0.0)))
    walled = low_wall | high_wall

    def reflect(k, second):
        second = list(second)
        for f in range(2):
            to = 28 * f + 4 * k
            first = jnp.where(walled, jnp.where(low_wall, to, to + 2), -8)
            shift = jnp.where(low_wall, to - 1, to + 3 - rows)
            for c in range(CH):
                x = sec[c, f, k]
                one, two = roll_by(x, shift), roll_by(x, shift + 2)
                if 1 <= c <= 3:
                    sign = jnp.where(low_wall, -1.0, 1.0)
                    one, two = sign * one, sign * two
                x = jnp.where(lane == first, one, second[c])
                second[c] = jnp.where(lane == first + 1, two, x)
        return tuple(second)

    second = loop(planes, reflect, tuple(second))
    stage(sec, second, shifted(vax), shifted(vay))

    per = LANES // 8

    def finish(k):
        for c in range(CH):
            x = jnp.where(sub < 4, turn(sec[c, 1, k], -2, 0), turn(sec[c, 0, k], 2, 0))
            at = pl.multiple_of((c * planes + k) * 8, 8)
            mine = own[c, pl.ds(pl.multiple_of(k * 8, 8), 8)]
            turned[pl.ds(at, 8)] = 0.5 * (mine + x)

    loop(planes, finish)

    def flip(n):
        back[n] = turned[pl.ds(pl.multiple_of(n * LANES, LANES), LANES)].T

    loop(turned.shape[0] // LANES, flip)
    arrive.wait()
    inside = within(lane, 4, LANES - 8)
    copies = []
    for c in range(CH):

        def merge(k, c=c):
            index = c * planes + k
            which, place = index // per, lax.rem(index, per)
            for r in range(0, rows, 8):
                moved = roll_by(back[which, r : r + 8], LANES - 4 - 8 * place)
                full[c, k, r : r + 8] = jnp.where(inside, full[c, k, r : r + 8], moved)

        loop(planes, merge)
        dst = next_dens.at[0] if c == 0 else next_en.at[0] if c == 4 else next_mom.at[0, c - 1]
        copies.append(pltpu.make_async_copy(full.at[c], dst, sems.at[c]))
        copies[-1].start()
    for copy in copies:
        copy.wait()


def local(mesh_shape, density, momentum, energy, metrics, volume, placed, neighbour, face, orient):
    halves = mesh_shape["ij"]
    devices = mesh_shape["blk"] * halves
    planes, rows = density.shape[1], density.shape[2]
    every = planes + 1
    fields = (density, momentum, energy, metrics, volume)
    f32 = jnp.float32
    vmem = pl.BlockSpec(memory_space=pltpu.VMEM)
    smem = pl.BlockSpec(memory_space=pltpu.SMEM)
    hbm = pl.BlockSpec(memory_space=pltpu.HBM)

    def call(kernel, name, outs, ins, out_specs, scratch, cost=None):
        return pl.pallas_call(
            kernel,
            out_shape=outs,
            in_specs=ins,
            out_specs=out_specs,
            scratch_shapes=scratch,
            compiler_params=pltpu.CompilerParams(vmem_limit_bytes=VMEM_LIMIT),
            cost_estimate=cost,
            name=name,
        )

    def shape(*dims):
        return jax.ShapeDtypeStruct(dims, f32)

    neighbour, face, orient = neighbour.T, face.T, orient.T
    strip = pltpu.VMEM((CH, 2, every, 8, LANES), f32)
    held = [pltpu.VMEM(x.shape, f32) for x in fields]
    edge = shape(CH, 4 * every, LANES)
    edges = 1 if halves == 2 else 2
    sent, own, *halo = call(
        functools.partial(cut_kernel, halves),
        "cut",
        [shape(devices * SENT, LANES), shape(CH, 64, LANES)] + [edge] * edges,
        [hbm] * 5 + [smem] * 3,
        [vmem] * (2 + edges),
        [pltpu.VMEM((CH, LANES, LANES), f32), pltpu.VMEM((CH * 64, LANES), f32)]
        + held
        + [pltpu.SemaphoreType.DMA((5,))],
    )(*fields, placed, face, orient)

    def swap(x):
        x = x.reshape(devices, x.shape[0] // devices, 1, LANES)
        x = lax.all_to_all(x, ("blk", "ij"), 0, 0, tiled=True)
        return x.reshape(x.shape[0] * x.shape[1], LANES)

    got = swap(sent)
    if edges == 1:
        below = above = lax.ppermute(halo[0], "ij", [(0, 1), (1, 0)])
    else:
        below = lax.ppermute(halo[1], "ij", [(i, i + 1) for i in range(halves - 1)])
        above = lax.ppermute(halo[0], "ij", [(i + 1, i) for i in range(halves - 1)])

    tall = rows + 2 * PAD
    block = shape(CH, planes, rows, LANES)
    stage = [
        pltpu.VMEM((CH, planes, rows, LANES), f32),
        pltpu.VMEM((8, tall, LANES), f32),
        pltpu.VMEM((CH, planes, tall, LANES), f32),
        pltpu.VMEM((4, planes, tall, LANES), f32),
        pltpu.VMEM((CH, planes, tall, LANES), f32),
        pltpu.VMEM((CH, planes, tall, LANES), f32),
    ]
    work = planes * rows * LANES
    cost = pl.CostEstimate(flops=300 * work, bytes_accessed=150 * work, transcendentals=work)
    leaving = pltpu.SemaphoreType.DMA((rows // 8,))
    part = call(
        first_kernel,
        "first_section",
        block,
        [hbm] * 5,
        hbm,
        held + stage + [pltpu.SemaphoreType.DMA((5,)), leaving],
        cost,
    )(*fields)
    relayed = call(
        functools.partial(relay_kernel, halves, rows, planes),
        "relay",
        shape(devices * PASSED, LANES),
        [smem] * 4 + [vmem, hbm],
        vmem,
        [
            pltpu.VMEM((devices * 16, LANES), f32),
            pltpu.VMEM((devices * 16, LANES), f32),
            pltpu.VMEM((devices * 2, LANES), f32),
            pltpu.SMEM((placed.shape[0],), jnp.int32),
        ],
    )(placed, neighbour, face, orient, got, part)
    ghosts = swap(relayed)
    out, ends_base, ends_sec, inner = call(
        functools.partial(second_kernel, halves),
        "second_section",
        [block, shape(CH, 8, LANES), shape(CH, 8, LANES), shape(CH, 64, LANES)],
        [hbm] * 5 + [vmem] * 2 + [hbm],
        [hbm] + [vmem] * 3,
        held
        + [
            pltpu.VMEM((2, CH, every, 8, LANES), f32),
            pltpu.VMEM((CH, LANES, LANES), f32),
            strip,
            strip,
            strip,
            pltpu.VMEM((CH, planes, tall, LANES), f32),
        ]
        + stage
        + [pltpu.SemaphoreType.DMA((6,)), leaving],
        cost,
    )(*fields, below, above, part)
    flat = -(-CH * planes * 8 // LANES)
    return call(
        functools.partial(last_kernel, halves, rows, planes),
        "strips",
        [shape(*density.shape), shape(*momentum.shape), shape(*energy.shape)],
        [vmem] * 5 + [hbm],
        [hbm] * 3,
        [strip] * 5
        + [
            pltpu.VMEM((flat * LANES, LANES), f32),
            pltpu.VMEM((flat, LANES, LANES), f32),
            pltpu.VMEM((CH, planes, rows, LANES), f32),
            pltpu.SemaphoreType.DMA((CH + 1,)),
        ],
    )(own, ends_base, ends_sec, inner, ghosts, out)


def solution(mesh):
    return jax.shard_map(
        functools.partial(local, dict(mesh.shape)),
        mesh=mesh,
        in_specs=(
            P("blk", None, "ij", None),
            P("blk", None, None, "ij", None),
            P("blk", None, "ij", None),
            P("blk", None, "ij", None),
            P("blk", "ij", None),
            P(),
            P(),
            P(),
            P(),
        ),
        out_specs=(
            P("blk", None, "ij", None),
            P("blk", None, None, "ij", None),
            P("blk", None, "ij", None),
        ),
        check_vma=False,
    )
```

```python
import functools

import jax
import jax.numpy as jnp
from jax import lax
from jax.experimental import pallas as pl
from jax.experimental.pallas import tpu as pltpu
from jax.sharding import PartitionSpec as P

pressure_factor = 0.4
viscosity = 0.05
time_step = 0.03
unit = time_step / 12.0

LANES = 128
PAD = 16
DEPTH = 4
CH = 5
VMEM_LIMIT = 63 * 1024 * 1024
SENT = 2 * CH
PASSED = 2 * CH + 1
FIRST = 4


def turn(x, shift, axis):
    shift = shift % x.shape[axis]
    return x if shift == 0 else pltpu.roll(x, shift, axis)


def lanes_of(shape):
    return lax.broadcasted_iota(jnp.int32, shape, len(shape) - 1)


def rows_of(shape):
    return lax.broadcasted_iota(jnp.int32, shape, len(shape) - 2)


def point(f):
    rho, m1, m2, m3, e = f
    r = 1.0 / rho
    u1, u2, u3 = m1 * r, m2 * r, m3 * r
    kin = 0.5 * (m1 * u1 + m2 * u2 + m3 * u3)
    p = pressure_factor * (e - kin)
    return (u1, u2, u3, (kin + 2.0 * p) * r), p, e + p


def metric_terms(m):
    ax, ay, bx, by, v = m
    kv = viscosity * unit
    rw = kv * (ax * ax + ay * ay)
    cw = kv * (bx * bx + by * by)
    return v * ax, v * ay, v * bx, v * by, -unit / v, rw, cw, 30.0 * (rw + cw + kv)


def flux(f, w, p, h, gx, gy):
    rho, m1, m2, m3, _ = f
    u = gx * w[0] + gy * w[1]
    return (rho * u, m1 * u + gx * p, m2 * u + gy * p, m3 * u, h * u)


def flux_planes(f, w, p, h):
    u3 = w[2]
    return (f[3], f[1] * u3, f[2] * u3, f[3] * u3 + p, h * u3)


def slope(x, at):
    return 8.0 * (at(x, 1) - at(x, -1)) - (at(x, 2) - at(x, -2))


def curve(x, at):
    return 16.0 * (at(x, 1) + at(x, -1)) - (at(x, 2) + at(x, -2))


def along(axis):
    return lambda x, o: turn(x, -o, axis)


def within(lane, start, size):
    return (lane >= start) & (lane < start + size)


def roll_by(x, shift, axis=1):
    size = x.shape[axis]
    return pltpu.roll(x, lax.rem(shift + 4 * size, size), axis)


def across(x):
    if x.shape[0] < LANES:
        x = jnp.concatenate([x, jnp.zeros((LANES - x.shape[0], LANES), jnp.float32)], axis=0)
    return x.T


def loop(count, body, start=None, unroll=1):
    if start is None:

        def step(n, _):
            body(n)
            return 0

        lax.fori_loop(0, count, step, 0, unroll=unroll)
        return None
    return lax.fori_loop(0, count, body, start, unroll=unroll)


def copy_all(pairs, sems, first=0):
    copies = [
        pltpu.make_async_copy(src, dst, sems.at[first + n]) for n, (src, dst) in enumerate(pairs)
    ]
    for copy in copies:
        copy.start()
    return copies


def state_pairs(fields, state, planes, rows):
    dens, mom, en, met, vol = fields
    return [
        (dens.at[0], state.at[0, 0:planes, rows]),
        (mom.at[0], state.at[1:4, 0:planes, rows]),
        (en.at[0], state.at[4, 0:planes, rows]),
        (met.at[0], state.at[0:4, planes, rows]),
        (vol.at[0], state.at[4, planes, rows]),
    ]


def wait_all(copies):
    for copy in copies:
        copy.wait()


def tile_stage(planes, load, mets, shift_i, shift_j, hold, done):
    kv = viscosity * unit
    fk, ws, acc = hold

    def spread(k):
        for s in range(2):
            vax, vay, vbx, vby, niv, rw, cw, tw = mets[s]
            x = [load(c, s, k) for c in range(CH)]
            w, p, h = point(x)
            fi, fj = flux(x, w, p, h, vax, vay), flux(x, w, p, h, vbx, vby)
            for c in range(CH):
                val = niv * (slope(fi[c], shift_i(0, c, s, k)) + slope(fj[c], shift_j))
                if c > 0:
                    v = w[c - 1]
                    val = val + (
                        rw * curve(v, shift_i(1, c - 1, s, k)) + cw * curve(v, shift_j) - tw * v
                    )
                    ws[c - 1, s, k] = v
                acc[c, s, k] = x[c] + val
            for c, v in enumerate(flux_planes(x, w, p, h)):
                fk[c, s, k] = v

    def gather(k):
        at = {o: lax.rem(k + o + planes, planes) for o in (-2, -1, 0, 1, 2)}
        for s in range(2):
            for c in range(CH):
                val = acc[c, s, k] - unit * slope(0, lambda _, o: fk[c, s, at[o]])
                if c > 0:
                    val = val + kv * curve(0, lambda _, o: ws[c - 1, s, at[o]])
                done(c, s, k, val)

    loop(planes, spread)
    loop(planes, gather)


def cut_kernel(halves, dens, mom, en, met, vol, placed, face, orient, send, own, *rest):
    edges, rest = rest[: -7 - (1 if halves == 2 else 2)], rest[-7 - (1 if halves == 2 else 2) :]
    held_send, held_own, *held_edges = rest[: 2 + len(edges)]
    state, packed, strips, sems, out_sems = rest[2 + len(edges) :]
    planes, rows = dens.shape[1], dens.shape[2]
    copies = copy_all(
        state_pairs((dens, mom, en, met, vol), state, planes, slice(None)), sems
    )
    block = placed[lax.axis_index("blk")]
    half = lax.axis_index("ij")
    row, lane = rows_of((64, LANES)), lanes_of((8, LANES))
    high_side = row % 8 < 4
    mirror = jnp.where(
        rows_of((LANES, LANES)) + lanes_of((LANES, LANES)) == rows - 1, 1.0, 0.0
    )
    flip = [jnp.where(orient[f, block] == 1, -1.0, 1.0) for f in range(2)]
    same = [jnp.where(face[f, block] == f, -1.0, 1.0) for f in range(2)]
    rising = [face[f, block] == 1 for f in range(2)]
    turned = jnp.where(high_side, flip[1], flip[0])
    facing = jnp.where(high_side, same[1], same[0])
    if rows < LANES:
        packed[...] = jnp.zeros(packed.shape, jnp.float32)
    wait_all(copies)

    def cut_ends(k):
        for c in range(CH):
            low, high = state[c, k, 0:4], state[c, k, rows - 4 : rows]
            if len(edges) == 1:
                held_edges[0][c, pl.ds(k * 4, 4)] = jnp.where(half == 0, high, low)
            else:
                held_edges[0][c, pl.ds(k * 4, 4)] = low
                held_edges[1][c, pl.ds(k * 4, 4)] = high

    loop(planes + 1, cut_ends)
    out = copy_all(list(zip(held_edges, edges)), out_sems, 2)

    def pack(r):
        for c in range(CH):
            packs = jnp.zeros((8, LANES), jnp.float32)
            for k in range(planes + 1):
                x = turn(state[c, k, pl.ds(r, 8)], 8 * k + 4, 1)
                packs = jnp.where(within(lane, 8 * k, 8), x, packs)
            packed[c, pl.ds(r, 8)] = packs

    chunks(rows // 8, pack)

    def orient_strip(c):
        strip = packed[c].T[0:64]
        held_own[c] = strip
        back = jnp.dot(
            strip,
            mirror,
            precision=lax.Precision.HIGHEST,
            preferred_element_type=jnp.float32,
        )
        moved = jnp.where(turned < 0.0, back, strip)
        sign = jnp.where(c < 2, turned, jnp.where(c < 4, facing, 1.0))
        moved = jnp.where(row >= planes * 8, moved * sign, moved)
        strips[pl.ds(pl.multiple_of(c * 64, 64), 64)] = moved

    loop(CH, orient_strip)
    out += copy_all([(held_own, own)], out_sems, 1)

    def put(n):
        k, e = n >> 2, n & 3
        at = (FIRST + n) * SENT
        low = k * 8 + 4 + jnp.where(rising[0], e, 3 - e)
        high = k * 8 + jnp.where(rising[1], 3 - e, e)
        held_send[pl.ds(at, CH)] = strips[pl.ds(low, CH, stride=64)]
        held_send[pl.ds(at + CH, CH)] = strips[pl.ds(high, CH, stride=64)]

    loop(DEPTH * (planes + 1), put, unroll=4)
    wait_all(out + copy_all([(held_send, send)], out_sems, 0))


def relay_kernel(
    halves, rows, planes, devices, route, got, send,
    held_got, held_send, below, above, signs, sems,
):
    arrive = copy_all([(got, held_got)], sems)
    me = lax.axis_index("blk") * halves + lax.axis_index("ij")
    is_field = (me >= FIRST) & (me < FIRST + DEPTH * planes)
    arrive[0].wait()

    def pass_on(slot):
        for f in range(2):
            code = route[2 * slot + f]
            partner, side, turned = code >> 2, (code >> 1) & 1, code & 1
            sign = jnp.where(turned == 1, -1.0, 1.0)

            def piece(h):
                h = jnp.where(turned == 1, halves - 1 - h, h)
                return held_got[pl.ds((partner * halves + h) * SENT + side * CH, CH)]

            pieces = [piece(h) for h in range(halves)]
            for half in range(halves):
                at = slot * halves + half
                held_send[pl.ds(at * PASSED + f * CH, CH)] = pieces[half]
                below[pl.ds((f * devices + at) * 8, CH)] = pieces[max(half - 1, 0)]
                above[pl.ds((f * devices + at) * 8, CH)] = pieces[min(half + 1, halves - 1)]
                signs[pl.ds(f * devices + at, 1)] = jnp.full((1, LANES), sign, jnp.float32)

    loop(devices // halves, pass_on, unroll=4)
    count = 2 * devices
    lane = lanes_of((count, LANES))
    half = rows_of((count, LANES)) % halves
    sign = signs[...]
    ends = jnp.zeros((count, LANES), jnp.float32)
    for c in range(CH):
        low, high = below[pl.ds(c, count, stride=8)], above[pl.ds(c, count, stride=8)]
        at = 4 * c
        low_wall = jnp.where(lane == at, turn(low, at - 1, 1), turn(low, at + 1, 1))
        high_wall = jnp.where(
            lane == at + 2, turn(high, at + 3 - rows, 1), turn(high, at + 5 - rows, 1)
        )
        if 1 <= c <= 3:
            low_wall = jnp.where(is_field, -sign * low_wall, low_wall)
            high_wall = jnp.where(is_field, sign * high_wall, high_wall)
        low = jnp.where(half == 0, low_wall, turn(low, at + 2 - rows, 1))
        high = jnp.where(half == halves - 1, high_wall, turn(high, at + 2, 1))
        ends = jnp.where(within(lane, at, 2), low, jnp.where(within(lane, at + 2, 2), high, ends))
    held_send[pl.ds(2 * CH, devices, stride=PASSED)] = ends[0:devices] + turn(
        ends[devices:], 4 * CH, 1
    )
    wait_all(copy_all([(held_send, send)], sems, 1))


def flux_chunk(get, mets, fi, w, fk, acc, r):
    rows = pl.ds(r, 8)
    vax, vay, vbx, vby, niv, rw, cw, tw = [mets[j, rows] for j in range(8)]
    at_j = along(1)
    for k in range(fi.shape[1]):
        f = [get(c, k, r) for c in range(CH)]
        wk, p, h = point(f)
        for c, x in enumerate(flux(f, wk, p, h, vax, vay)):
            fi[c, k, rows] = x
        for c in range(4):
            w[c, k, rows] = wk[c]
        fj = flux(f, wk, p, h, vbx, vby)
        for c in range(CH):
            val = niv * slope(fj[c], at_j)
            if c > 0:
                val = val + (cw * curve(wk[c - 1], at_j) - tw * wk[c - 1])
            acc[c, k, rows] = val
        for c, x in enumerate(flux_planes(f, wk, p, h)):
            fk[c, k, rows] = x


def sum_chunk(mets, fi, w, fk, acc, r, emit):
    planes = fi.shape[1]
    kv = viscosity * unit
    rows = pl.ds(r, 8)
    niv, rw = mets[4, rows], mets[5, rows]
    for c in range(CH):
        t = [fk[c, k, rows] for k in range(planes)]
        x = [w[c - 1, k, rows] for k in range(planes)] if c > 0 else None
        for k in range(planes):

            def near(v, o):
                return v[(k + o) % planes]

            def at_i(v, o):
                return v[pl.ds(r + o, 8)]

            val = acc[c, k, rows] + niv * slope(fi.at[c, k], at_i) - unit * slope(t, near)
            if c > 0:
                val = val + (rw * curve(w.at[c - 1, k], at_i) + kv * curve(x, near))
            emit(c, k, r, val)


def chunks(count, body):
    def step(n, _):
        body(pl.multiple_of(n * 8, 8))
        return 0

    lax.fori_loop(0, count, step, 0)


def pack_ends(arr, rows, scratch, planes):
    sub, lane = rows_of((8, LANES)), lanes_of((8, LANES))

    def first(k, packed):
        out = []
        for c in range(CH):
            low, high = arr[c, k, PAD - 4 : PAD + 4], arr[c, k, PAD + rows - 4 : PAD + rows + 4]
            x = roll_by(jnp.where(sub < 4, low, high), 8 * k + 4)
            out.append(jnp.where(within(lane, 8 * k, 8), x, packed[c]))
        return tuple(out)

    empty = jnp.zeros((8, LANES), jnp.float32)
    packed = loop(planes, first, (empty,) * CH)
    scratch[...] = across(jnp.concatenate(packed, axis=0))

    def second(k, packed):
        x = scratch[pl.ds(pl.multiple_of(8 * k, 8), 8)]
        return tuple(
            jnp.where(within(lane, 4 * k, 4), roll_by(x, 4 * k - (8 * c + 2)), packed[c])
            for c in range(CH)
        )

    return loop(planes, second, (empty,) * CH)


def at_walls(halves, arr, rows, planes, fields):
    half = lax.axis_index("ij")

    @pl.when(half == 0)
    def _():
        def low(k):
            sign = jnp.where(k < fields, -1.0, 1.0)
            for c in range(CH):
                for n in range(2):
                    x = arr[c, k, PAD + n : PAD + n + 1]
                    arr[c, k, PAD - 1 - n : PAD - n] = sign * x if 1 <= c <= 3 else x

        loop(planes, low)

    @pl.when(half == halves - 1)
    def _():
        def high(k):
            for c in range(CH):
                for n in range(2):
                    at = PAD + rows + n
                    arr[c, k, at : at + 1] = arr[c, k, PAD + rows - 1 - n : PAD + rows - n]

        loop(planes, high)


def first_kernel(
    halves, dens, mom, en, met, vol, below, above, placed, neighbour, face, orient,
    part, terms_out, ends_base, route,
    state, low, high, sec, mets, fi, w, fk, acc, ends, scratch, where_is, sems, out_sems,
):
    planes, rows = dens.shape[1], dens.shape[2]
    inside = slice(PAD, PAD + rows)
    pairs = state_pairs((dens, mom, en, met, vol), state, planes, inside)
    copies = copy_all(pairs + [(below, low), (above, high)], sems)
    blocks = placed.shape[0]

    def note(slot):
        where_is[placed[slot]] = slot

    def direct(slot):
        block = placed[slot]
        for f in range(2):
            partner = where_is[neighbour[f, block]]
            route[2 * slot + f] = partner * 4 + face[f, block] * 2 + orient[f, block]

    loop(blocks, note)
    loop(blocks, direct)
    wait_all(copies)
    half = lax.axis_index("ij")

    @pl.when(half > 0)
    def _():
        def fill(k):
            for c in range(CH):
                state[c, k, PAD - 4 : PAD] = low[c, pl.ds(4 * k, 4)]

        loop(planes + 1, fill)

    @pl.when(half < halves - 1)
    def _():
        def fill(k):
            for c in range(CH):
                state[c, k, PAD + rows : PAD + rows + 4] = high[c, pl.ds(4 * k, 4)]

        loop(planes + 1, fill)

    at_walls(halves, state, rows, planes + 1, planes)
    for c, x in enumerate(pack_ends(state, rows, scratch, planes + 1)):
        ends[c] = x
    out = copy_all([(ends, ends_base)], out_sems, 0)

    def get(c, k, r):
        return state[c, k, pl.ds(r, 8)]

    def fluxes(n):
        r = n + PAD - 8
        at = pl.ds(r, 8)
        for j, x in enumerate(metric_terms([state[c, planes, at] for c in range(CH)])):
            mets[j, at] = x
        flux_chunk(get, mets, fi, w, fk, acc, r)

    chunks(rows // 8 + 2, fluxes)
    out += copy_all([(mets.at[:, PAD - 8 : PAD + rows + 8], terms_out)], out_sems, 1)

    def emit(c, k, r, val):
        sec[c, k, pl.ds(r, 8)] = get(c, k, r) + val

    chunks(rows // 8 + 2, lambda n: sum_chunk(mets, fi, w, fk, acc, n + PAD - 8, emit))
    at_walls(halves, sec, rows, planes, planes)
    wait_all(out + copy_all([(sec.at[:, :, PAD - 8 : PAD + rows + 8], part)], out_sems, 2))


def second_kernel(
    dens, mom, en, met, vol, part, terms, out, ends_sec, inner,
    state, sec, full, mets, fi, w, fk, acc, packed, scratch, ends, strips, sems, out_sems,
):
    planes, rows = dens.shape[1], dens.shape[2]
    tall = slice(PAD - 8, PAD + rows + 8)
    early = copy_all([(part, sec.at[:, :, tall]), (terms, mets.at[:, tall])], sems)
    pairs = state_pairs((dens, mom, en, met, vol), state, planes, slice(None))
    late = copy_all(pairs, sems, 2)
    lane = lanes_of((8, LANES))
    wait_all(early)

    def get(c, k, r):
        return sec[c, k, pl.ds(r, 8)]

    chunks(rows // 8 + 2, lambda n: flux_chunk(get, mets, fi, w, fk, acc, n + PAD - 8))
    wait_all(late)

    def emit(c, k, r, val):
        at = pl.ds(r - PAD, 8)
        full[c, k, at] = 0.5 * (state[c, k, at] + (get(c, k, r) + val))

    def leave(n):
        at = pl.ds(n, 8)
        return pltpu.make_async_copy(full.at[:, :, at], out.at[:, :, at], out_sems.at[n // 8])

    def sums(n):
        sum_chunk(mets, fi, w, fk, acc, n + PAD, emit)
        leave(n).start()

    chunks(rows // 8, sums)

    for c, x in enumerate(pack_ends(sec, rows, scratch, planes)):
        ends[c] = x
    if rows < LANES:
        packed[...] = jnp.zeros(packed.shape, jnp.float32)

    def pack(n):
        for c in range(CH):
            x = state[c, planes, pl.ds(n, 8)]
            at = 8 * planes
            packs = jnp.where(lane < at + 4, turn(x, at + 6, 1), turn(x, at + 2, 1))
            for k in range(planes):
                x = sec[c, k, pl.ds(n + PAD, 8)]
                at = 8 * k
                packs = jnp.where(within(lane, at, 4), turn(x, at + 6, 1), packs)
                packs = jnp.where(within(lane, at + 4, 4), turn(x, at + 2, 1), packs)
            packed[c, pl.ds(n, 8)] = packs

    chunks(rows // 8, pack)

    def flip(c):
        strips[c] = packed[c].T[0:64]

    loop(CH, flip)
    last = copy_all([(ends, ends_sec), (strips, inner)], out_sems, rows // 8)
    chunks(rows // 8, lambda n: leave(n).wait())
    wait_all(last)


def beyond(packed, f, k, rows):
    base = 28 * f + 4 * k
    low = roll_by(packed, LANES - 2 - base)
    top = rows % LANES
    high = low if top == 0 else roll_by(packed, top - 2 - base)
    lane = lanes_of(packed.shape)

    def at(x, o):
        if o < 0:
            x = jnp.where(lane >= LANES + o, low, x)
        else:
            x = jnp.where(within(lane, top, o), high, x)
        return turn(x, -o, 1)

    return at


def last_kernel(
    halves, rows, planes, own_at, ends_base_at, ends_sec_at, inner_at, got_at, out,
    next_dens, next_mom, next_en,
    own, ends_base, ends_sec, inner, got, base, sec, fk, ws, acc, turned, back, full, sems,
):
    late = copy_all([(inner_at, inner), (ends_sec_at, ends_sec), (out, full)], sems)
    early = copy_all([(got_at, got), (own_at, own), (ends_base_at, ends_base)], sems, 3)
    half = lax.axis_index("ij")
    low_wall, high_wall = half == 0, half == halves - 1
    sub, lane = rows_of((8, LANES)), lanes_of((8, LANES))

    def mix(f, mine, others):
        return jnp.where((sub < 4) == (f == 1), mine, others)

    wait_all(early)

    def gather(k, others):
        start = DEPTH * k * PASSED

        def ghost(row, f):
            x = got[pl.ds(start + row, 8, stride=PASSED)]
            return x if f == 1 else turn(x, 4, 0)

        others = list(others)
        for f in range(2):
            arrived = ghost(2 * CH, f)
            to = 28 * f + 4 * k
            for c in range(CH):
                mine = own[c, pl.ds(pl.multiple_of(k * 8, 8), 8)]
                base[c, f, k] = mix(f, mine, ghost(f * CH + c, f))
                moved = roll_by(arrived, to - 4 * CH * f - 4 * c)
                others[c] = jnp.where(within(lane, to, 4), moved, others[c])
        return tuple(others)

    empty = jnp.zeros((8, LANES), jnp.float32)
    others = loop(planes + 1, gather, (empty,) * CH)
    low_lanes = lane < 28
    twice = [jnp.where(low_lanes, ends_base[c], turn(ends_base[c], 28, 1)) for c in range(CH)]
    ends = [jnp.where(low_lanes == (sub >= 4), twice[c], others[c]) for c in range(CH)]
    slot = jnp.where(low_lanes, lane, lane - 28)

    def spread(k, kept):
        shift, hit = 4 * (k - planes), within(slot, 4 * k, 4)
        return tuple((x, jnp.where(hit, roll_by(x, shift), y)) for x, y in kept)

    kept = metric_terms(ends)[0:5] + metric_terms(ends)[6:7] + metric_terms(twice)[2:4]
    kept = loop(planes, spread, tuple((x, x) for x in kept))
    vax, vay, vbx, vby, niv, cw, *wrapped = [y for _, y in kept]

    def keep(c, f, k, val):
        sec[c, f, k] = val

    def stage(held, ends, gx, gy):
        mets = [metric_terms([held[c, f, planes] for c in range(CH)]) for f in range(2)]
        w, p, h = point(ends)
        rims = (flux(ends, w, p, h, gx, gy), w)
        tile_stage(
            planes,
            lambda c, f, k: held[c, f, k],
            mets,
            lambda kind, c, f, k: beyond(rims[kind][c], f, k, rows),
            along(0),
            (fk, ws, acc),
            keep,
        )

    stage(base, ends, vax, vay)
    wait_all(late[0:2])

    def move(k, source):
        for c in range(CH):
            mine = inner[c, pl.ds(pl.multiple_of(k * 8, 8), 8)]
            for f in range(2):
                sec[c, f, k] = mix(f, mine, turn(source[c, f, k], 2 if f == 1 else -2, 0))

    loop(planes, lambda k: move(k, sec))
    move(jnp.int32(planes), base)

    def shifted(x):
        return jnp.where(low_lanes, turn(x, -2, 0), turn(x, 2, 0))

    w1, p1, h1 = point(ends)
    w0, p0, h0 = point(twice)
    new, old = flux(ends, w1, p1, h1, vbx, vby), flux(twice, w0, p0, h0, *wrapped)
    at_j = along(0)
    touched = within(sub, jnp.where(low_lanes, 4, 2), 2)
    second = []
    for c in range(CH):
        add = niv * slope(new[c] - old[c], at_j)
        if c > 0:
            add = add + cw * curve(w1[c - 1] - w0[c - 1], at_j)
        x = jnp.where(low_lanes, ends_sec[c], turn(ends_sec[c], 28, 1))
        second.append(shifted(x + jnp.where(touched, add, 0.0)))
    walled = low_wall | high_wall

    def reflect(k, second):
        second = list(second)
        for f in range(2):
            to = 28 * f + 4 * k
            first = jnp.where(walled, jnp.where(low_wall, to, to + 2), -8)
            shift = jnp.where(low_wall, to - 1, to + 3 - rows)
            for c in range(CH):
                x = sec[c, f, k]
                one, two = roll_by(x, shift), roll_by(x, shift + 2)
                if 1 <= c <= 3:
                    sign = jnp.where(low_wall, -1.0, 1.0)
                    one, two = sign * one, sign * two
                x = jnp.where(lane == first, one, second[c])
                second[c] = jnp.where(lane == first + 1, two, x)
        return tuple(second)

    second = loop(planes, reflect, tuple(second))
    stage(sec, second, shifted(vax), shifted(vay))

    per = LANES // 8

    def finish(k):
        for c in range(CH):
            x = jnp.where(sub < 4, turn(sec[c, 1, k], -2, 0), turn(sec[c, 0, k], 2, 0))
            at = pl.multiple_of((c * planes + k) * 8, 8)
            mine = own[c, pl.ds(pl.multiple_of(k * 8, 8), 8)]
            turned[pl.ds(at, 8)] = 0.5 * (mine + x)

    loop(planes, finish)

    def flip(n):
        back[n] = turned[pl.ds(pl.multiple_of(n * LANES, LANES), LANES)].T

    loop(turned.shape[0] // LANES, flip)
    late[2].wait()
    inside = within(lane, 4, LANES - 8)
    copies = []
    for c in range(CH):

        def merge(k, c=c):
            index = c * planes + k
            which, place = index // per, lax.rem(index, per)
            for r in range(0, rows, 8):
                moved = roll_by(back[which, r : r + 8], LANES - 4 - 8 * place)
                full[c, k, r : r + 8] = jnp.where(inside, full[c, k, r : r + 8], moved)

        loop(planes, merge)
        dst = next_dens.at[0] if c == 0 else next_en.at[0] if c == 4 else next_mom.at[0, c - 1]
        copies.append(pltpu.make_async_copy(full.at[c], dst, sems.at[6 + c]))
        copies[-1].start()
    for copy in copies:
        copy.wait()


def local(mesh_shape, density, momentum, energy, metrics, volume, placed, neighbour, face, orient):
    halves = mesh_shape["ij"]
    blocks = mesh_shape["blk"]
    devices = blocks * halves
    planes, rows = density.shape[1], density.shape[2]
    every = planes + 1
    fields = (density, momentum, energy, metrics, volume)
    neighbour, face, orient = neighbour.T, face.T, orient.T
    smem = pl.BlockSpec(memory_space=pltpu.SMEM)
    hbm = pl.BlockSpec(memory_space=pltpu.HBM)

    def call(kernel, name, outs, ins, out_specs, scratch, cost=None):
        return pl.pallas_call(
            kernel,
            out_shape=outs,
            in_specs=ins,
            out_specs=out_specs,
            scratch_shapes=scratch,
            compiler_params=pltpu.CompilerParams(vmem_limit_bytes=VMEM_LIMIT),
            cost_estimate=cost,
            name=name,
        )

    def shape(*dims):
        return jax.ShapeDtypeStruct(dims, jnp.float32)

    def vmem(x):
        return pltpu.VMEM(x.shape, jnp.float32)

    def sems(count):
        return pltpu.SemaphoreType.DMA((count,))

    sent, passed = shape(devices * SENT, LANES), shape(devices * PASSED, LANES)
    strip, rim = shape(CH, 64, LANES), shape(CH, 8, LANES)
    edge = shape(CH, 4 * every, LANES)
    edges = 1 if halves == 2 else 2
    square = shape(LANES, LANES)
    state = shape(CH, every, rows, LANES)
    outs = [sent, strip] + [edge] * edges
    to_send, own, *halo = call(
        functools.partial(cut_kernel, halves),
        "cut",
        outs,
        [hbm] * 5 + [smem] * 3,
        [hbm] * (2 + edges),
        [vmem(x) for x in outs]
        + [
            vmem(state),
            pltpu.VMEM((CH, LANES, LANES), jnp.float32),
            pltpu.VMEM((CH * 64, LANES), jnp.float32),
            sems(5),
            sems(2 + edges),
        ],
    )(*fields, placed, face, orient)

    def swap(x):
        x = x.reshape(devices, x.shape[0] // devices, 1, LANES)
        x = lax.all_to_all(x, ("blk", "ij"), 0, 0, tiled=True)
        return x.reshape(x.shape[0] * x.shape[1], LANES)

    if edges == 1:
        below = above = lax.ppermute(halo[0], "ij", [(0, 1), (1, 0)])
    else:
        below = lax.ppermute(halo[1], "ij", [(i, i + 1) for i in range(halves - 1)])
        above = lax.ppermute(halo[0], "ij", [(i + 1, i) for i in range(halves - 1)])
    got = swap(to_send)

    tall = rows + 2 * PAD
    block = shape(CH, planes, rows, LANES)
    high = shape(CH, planes, rows + 16, LANES)
    terms = shape(8, rows + 16, LANES)
    padded = shape(CH, planes, tall, LANES)
    stage = [
        vmem(shape(8, tall, LANES)),
        vmem(padded),
        vmem(shape(4, planes, tall, LANES)),
        vmem(padded),
        vmem(padded),
    ]
    work = planes * rows * LANES
    cost = pl.CostEstimate(flops=300 * work, bytes_accessed=150 * work, transcendentals=work)
    part, kept, ends_base, route = call(
        functools.partial(first_kernel, halves),
        "first_section",
        [high, terms, rim, jax.ShapeDtypeStruct((2 * blocks,), jnp.int32)],
        [hbm] * 7 + [smem] * 4,
        [hbm] * 3 + [smem],
        [vmem(shape(CH, every, tall, LANES)), vmem(edge), vmem(edge), vmem(padded)]
        + stage
        + [vmem(rim), vmem(square), pltpu.SMEM((blocks,), jnp.int32), sems(7), sems(3)],
        cost,
    )(*fields, below, above, placed, neighbour, face, orient)
    relayed = call(
        functools.partial(relay_kernel, halves, rows, planes, devices),
        "relay",
        passed,
        [smem, hbm],
        hbm,
        [
            vmem(sent),
            vmem(passed),
            vmem(shape(devices * 16, LANES)),
            vmem(shape(devices * 16, LANES)),
            vmem(shape(devices * 2, LANES)),
            sems(2),
        ],
    )(route, got)
    ghosts = swap(relayed)
    out, ends_sec, inner = call(
        second_kernel,
        "second_section",
        [block, rim, strip],
        [hbm] * 7,
        [hbm] * 3,
        [vmem(state), vmem(padded), vmem(block)]
        + stage
        + [
            pltpu.VMEM((CH, LANES, LANES), jnp.float32),
            vmem(square),
            vmem(rim),
            vmem(strip),
            sems(7),
            sems(rows // 8 + 2),
        ],
        cost,
    )(*fields, part, kept)
    tiles = shape(CH, 2, every, 8, LANES)
    flat = -(-CH * planes * 8 // LANES)
    return call(
        functools.partial(last_kernel, halves, rows, planes),
        "strips",
        [shape(*density.shape), shape(*momentum.shape), shape(*energy.shape)],
        [hbm] * 6,
        [hbm] * 3,
        [vmem(x) for x in (strip, rim, rim, strip, passed)]
        + [vmem(tiles)] * 5
        + [
            vmem(shape(flat * LANES, LANES)),
            vmem(shape(flat, LANES, LANES)),
            vmem(block),
            sems(6 + CH),
        ],
    )(own, ends_base, ends_sec, inner, ghosts, out)


def solution(mesh):
    return jax.shard_map(
        functools.partial(local, dict(mesh.shape)),
        mesh=mesh,
        in_specs=(
            P("blk", None, "ij", None),
            P("blk", None, None, "ij", None),
            P("blk", None, "ij", None),
            P("blk", None, "ij", None),
            P("blk", "ij", None),
            P(),
            P(),
            P(),
            P(),
        ),
        out_specs=(
            P("blk", None, "ij", None),
            P("blk", None, None, "ij", None),
            P("blk", None, "ij", None),
        ),
        check_vma=False,
    )
```

```python
import functools

import jax
import jax.numpy as jnp
from jax import lax
from jax.experimental import pallas as pl
from jax.experimental.pallas import tpu as pltpu
from jax.sharding import PartitionSpec as P

pressure_factor = 0.4
viscosity = 0.05
time_step = 0.03
unit = time_step / 12.0

LANES = 128
PAD = 8
PIECES = 4
DEPTH = 4
CH = 5
VMEM_MIB = 63
SENT = 2 * CH
PASSED = 2 * CH + 1
FIRST = 4


def turn(x, shift, axis):
    shift = shift % x.shape[axis]
    return x if shift == 0 else pltpu.roll(x, shift, axis)


def lanes_of(shape):
    return lax.broadcasted_iota(jnp.int32, shape, len(shape) - 1)


def rows_of(shape):
    return lax.broadcasted_iota(jnp.int32, shape, len(shape) - 2)


def point(f):
    rho, m1, m2, m3, e = f
    r = 1.0 / rho
    u1, u2, u3 = m1 * r, m2 * r, m3 * r
    kin = 0.5 * (m1 * u1 + m2 * u2 + m3 * u3)
    p = pressure_factor * (e - kin)
    return (u1, u2, u3, (kin + 2.0 * p) * r), p, e + p


def metric_terms(m):
    ax, ay, bx, by, v = m
    kv = viscosity * unit
    rw = kv * (ax * ax + ay * ay)
    cw = kv * (bx * bx + by * by)
    return v * ax, v * ay, v * bx, v * by, -unit / v, rw, cw, 30.0 * (rw + cw + kv)


def flux(f, w, p, h, gx, gy):
    rho, m1, m2, m3, _ = f
    u = gx * w[0] + gy * w[1]
    return (rho * u, m1 * u + gx * p, m2 * u + gy * p, m3 * u, h * u)


def flux_planes(f, w, p, h):
    u3 = w[2]
    return (f[3], f[1] * u3, f[2] * u3, f[3] * u3 + p, h * u3)


def slope(x, at):
    return 8.0 * (at(x, 1) - at(x, -1)) - (at(x, 2) - at(x, -2))


def curve(x, at):
    return 16.0 * (at(x, 1) + at(x, -1)) - (at(x, 2) + at(x, -2))


def along(axis):
    return lambda x, o: turn(x, -o, axis)


def within(lane, start, size):
    return (lane >= start) & (lane < start + size)


def roll_by(x, shift, axis=1):
    size = x.shape[axis]
    return pltpu.roll(x, lax.rem(shift + 4 * size, size), axis)


def across(x):
    if x.shape[0] < LANES:
        x = jnp.concatenate([x, jnp.zeros((LANES - x.shape[0], LANES), jnp.float32)], axis=0)
    return x.T


def loop(count, body, unroll=1):
    def step(n, _):
        body(n)
        return 0

    lax.fori_loop(0, count, step, 0, unroll=unroll)


def copy_all(pairs, sems, first=0):
    copies = [
        pltpu.make_async_copy(src, dst, sems.at[first + n]) for n, (src, dst) in enumerate(pairs)
    ]
    for copy in copies:
        copy.start()
    return copies


def state_pairs(fields, state, planes, start, size):
    dens, mom, en, met, vol = fields
    at = pl.ds(start, size)
    return [
        (dens.at[0, :, at], state.at[0, 0:planes, at]),
        (mom.at[0, :, :, at], state.at[1:4, 0:planes, at]),
        (en.at[0, :, at], state.at[4, 0:planes, at]),
        (met.at[0, :, at], state.at[0:4, planes, at]),
        (vol.at[0, at], state.at[4, planes, at]),
    ]


def arrive_in_pieces(fields, state, sems):
    planes, rows = fields[0].shape[1], fields[0].shape[2]
    size = max(8, rows // PIECES)
    for n in range(rows // size):
        copy_all(state_pairs(fields, state, planes, n * size, size), sems, 5 * n)

    def expect(start):
        @pl.when(lax.rem(start, size) == 0)
        def _():
            for n, (src, dst) in enumerate(state_pairs(fields, state, planes, start, size)):
                pltpu.make_async_copy(src, dst, sems.at[5 * (start // size) + n]).wait()

    return expect


def wait_all(copies):
    for copy in copies:
        copy.wait()


def tile_stage(planes, load, mets, shift_i, shift_j, hold, done):
    kv = viscosity * unit
    fk, ws, acc = hold

    def spread(k):
        for s in range(2):
            vax, vay, vbx, vby, niv, rw, cw, tw = mets[s]
            x = [load(c, s, k) for c in range(CH)]
            w, p, h = point(x)
            fi, fj = flux(x, w, p, h, vax, vay), flux(x, w, p, h, vbx, vby)
            for c in range(CH):
                val = niv * (slope(fi[c], shift_i(0, c, s, k)) + slope(fj[c], shift_j))
                if c > 0:
                    v = w[c - 1]
                    val = val + (
                        rw * curve(v, shift_i(1, c - 1, s, k)) + cw * curve(v, shift_j) - tw * v
                    )
                    ws[c - 1, s, k] = v
                acc[c, s, k] = x[c] + val
            for c, v in enumerate(flux_planes(x, w, p, h)):
                fk[c, s, k] = v

    def gather(k):
        at = {o: lax.rem(k + o + planes, planes) for o in (-2, -1, 0, 1, 2)}
        for s in range(2):
            for c in range(CH):
                val = acc[c, s, k] - unit * slope(0, lambda _, o: fk[c, s, at[o]])
                if c > 0:
                    val = val + kv * curve(0, lambda _, o: ws[c - 1, s, at[o]])
                done(c, s, k, val)

    loop(planes, spread, unroll=2)
    loop(planes, gather, unroll=2)


def cut_kernel(halves, dens, mom, en, met, vol, placed, face, orient, send, own, *rest):
    edges, rest = rest[: -7 - (1 if halves == 2 else 2)], rest[-7 - (1 if halves == 2 else 2) :]
    held_send, held_own, *held_edges = rest[: 2 + len(edges)]
    state, packed, strips, sems, out_sems = rest[2 + len(edges) :]
    planes, rows = dens.shape[1], dens.shape[2]
    expect = arrive_in_pieces((dens, mom, en, met, vol), state, sems)
    block = placed[lax.axis_index("blk")]
    half = lax.axis_index("ij")
    row, lane = rows_of((64, LANES)), lanes_of((8, LANES))
    high_side = row % 8 < 4
    mirror = jnp.where(
        rows_of((LANES, LANES)) + lanes_of((LANES, LANES)) == rows - 1, 1.0, 0.0
    )
    flip = [jnp.where(orient[f, block] == 1, -1.0, 1.0) for f in range(2)]
    same = [jnp.where(face[f, block] == f, -1.0, 1.0) for f in range(2)]
    rising = [face[f, block] == 1 for f in range(2)]
    turned = jnp.where(high_side, flip[1], flip[0])
    facing = jnp.where(high_side, same[1], same[0])
    if rows < LANES:
        packed[...] = jnp.zeros(packed.shape, jnp.float32)
    def pack(r):
        expect(r)
        for c in range(CH):
            packs = jnp.zeros((8, LANES), jnp.float32)
            for k in range(planes + 1):
                x = turn(state[c, k, pl.ds(r, 8)], 8 * k + 4, 1)
                packs = jnp.where(within(lane, 8 * k, 8), x, packs)
            packed[c, pl.ds(r, 8)] = packs

    chunks(rows // 8, pack)

    def cut_ends(k):
        for c in range(CH):
            low, high = state[c, k, 0:4], state[c, k, rows - 4 : rows]
            if len(edges) == 1:
                held_edges[0][c, k * 4 : k * 4 + 4] = jnp.where(half == 0, high, low)
            else:
                held_edges[0][c, k * 4 : k * 4 + 4] = low
                held_edges[1][c, k * 4 : k * 4 + 4] = high

    for k in range(planes + 1):
        cut_ends(k)
    out = copy_all(list(zip(held_edges, edges)), out_sems, 2)

    def orient_strip(c):
        strip = packed[c].T[0:64]
        held_own[c] = strip
        back = jnp.dot(
            strip,
            mirror,
            precision=lax.Precision.HIGHEST,
            preferred_element_type=jnp.float32,
        )
        moved = jnp.where(turned < 0.0, back, strip)
        sign = jnp.where(c < 2, turned, jnp.where(c < 4, facing, 1.0))
        moved = jnp.where(row >= planes * 8, moved * sign, moved)
        strips[pl.ds(pl.multiple_of(c * 64, 64), 64)] = moved

    loop(CH, orient_strip)
    out += copy_all([(held_own, own)], out_sems, 1)

    def put(n):
        k, e = n >> 2, n & 3
        at = (FIRST + n) * SENT
        low = k * 8 + 4 + jnp.where(rising[0], e, 3 - e)
        high = k * 8 + jnp.where(rising[1], 3 - e, e)
        held_send[pl.ds(at, CH)] = strips[pl.ds(low, CH, stride=64)]
        held_send[pl.ds(at + CH, CH)] = strips[pl.ds(high, CH, stride=64)]

    loop(DEPTH * (planes + 1), put, unroll=4)
    wait_all(out + copy_all([(held_send, send)], out_sems, 0))


def relay_kernel(
    halves, rows, planes, devices, route, halo, held_got, send,
    held_send, below, above, signs, sems,
):
    del halo
    me = lax.axis_index("blk") * halves + lax.axis_index("ij")
    is_field = (me >= FIRST) & (me < FIRST + DEPTH * planes)

    def pass_on(slot):
        for f in range(2):
            code = route[2 * slot + f]
            partner, side, turned = code >> 2, (code >> 1) & 1, code & 1
            sign = jnp.where(turned == 1, -1.0, 1.0)

            def piece(h):
                h = jnp.where(turned == 1, halves - 1 - h, h)
                return held_got[pl.ds((partner * halves + h) * SENT + side * CH, CH)]

            pieces = [piece(h) for h in range(halves)]
            for half in range(halves):
                at = slot * halves + half
                held_send[pl.ds(at * PASSED + f * CH, CH)] = pieces[half]
                below[pl.ds((f * devices + at) * 8, CH)] = pieces[max(half - 1, 0)]
                above[pl.ds((f * devices + at) * 8, CH)] = pieces[min(half + 1, halves - 1)]
                signs[pl.ds(f * devices + at, 1)] = jnp.full((1, LANES), sign, jnp.float32)

    loop(devices // halves, pass_on, unroll=4)
    count = 2 * devices
    lane = lanes_of((count, LANES))
    half = rows_of((count, LANES)) % halves
    sign = signs[...]
    ends = jnp.zeros((count, LANES), jnp.float32)
    for c in range(CH):
        low, high = below[pl.ds(c, count, stride=8)], above[pl.ds(c, count, stride=8)]
        at = 4 * c
        low_wall = jnp.where(lane == at, turn(low, at - 1, 1), turn(low, at + 1, 1))
        high_wall = jnp.where(
            lane == at + 2, turn(high, at + 3 - rows, 1), turn(high, at + 5 - rows, 1)
        )
        if 1 <= c <= 3:
            low_wall = jnp.where(is_field, -sign * low_wall, low_wall)
            high_wall = jnp.where(is_field, sign * high_wall, high_wall)
        low = jnp.where(half == 0, low_wall, turn(low, at + 2 - rows, 1))
        high = jnp.where(half == halves - 1, high_wall, turn(high, at + 2, 1))
        ends = jnp.where(within(lane, at, 2), low, jnp.where(within(lane, at + 2, 2), high, ends))
    held_send[pl.ds(2 * CH, devices, stride=PASSED)] = ends[0:devices] + turn(
        ends[devices:], 4 * CH, 1
    )
    wait_all(copy_all([(held_send, send)], sems))


def flux_chunk(get, mets, fi, w, fk, acc, r):
    rows = pl.ds(r, 8)
    vax, vay, vbx, vby, niv, rw, cw, tw = [mets[j, rows] for j in range(8)]
    at_j = along(1)
    for k in range(fi.shape[1]):
        f = [get(c, k, r) for c in range(CH)]
        wk, p, h = point(f)
        for c, x in enumerate(flux(f, wk, p, h, vax, vay)):
            fi[c, k, rows] = x
        for c in range(4):
            w[c, k, rows] = wk[c]
        fj = flux(f, wk, p, h, vbx, vby)
        for c in range(CH):
            val = niv * slope(fj[c], at_j)
            if c > 0:
                val = val + (cw * curve(wk[c - 1], at_j) - tw * wk[c - 1])
            acc[c, k, rows] = val
        for c, x in enumerate(flux_planes(f, wk, p, h)):
            fk[c, k, rows] = x


def sum_chunk(mets, fi, w, fk, acc, r, emit):
    planes = fi.shape[1]
    kv = viscosity * unit
    rows = pl.ds(r, 8)
    niv, rw = mets[4, rows], mets[5, rows]
    for c in range(CH):
        t = [fk[c, k, rows] for k in range(planes)]
        x = [w[c - 1, k, rows] for k in range(planes)] if c > 0 else None
        for k in range(planes):

            def near(v, o):
                return v[(k + o) % planes]

            def at_i(v, o):
                return v[pl.ds(r + o, 8)]

            val = acc[c, k, rows] + niv * slope(fi.at[c, k], at_i) - unit * slope(t, near)
            if c > 0:
                val = val + (rw * curve(w.at[c - 1, k], at_i) + kv * curve(x, near))
            emit(c, k, r, val)


def chunks(count, body):
    def step(n, _):
        body(pl.multiple_of(n * 8, 8))
        return 0

    lax.fori_loop(0, count, step, 0)


def first_kernel(
    dens, mom, en, met, vol, placed, neighbour, face, orient, part, route,
    state, full, mets, fi, w, fk, acc, where_is, sems, out_sems,
):
    planes, rows = dens.shape[1], dens.shape[2]
    expect = arrive_in_pieces((dens, mom, en, met, vol), state, sems)
    blocks = placed.shape[0]

    def note(slot):
        where_is[placed[slot]] = slot

    def direct(slot):
        block = placed[slot]
        for f in range(2):
            partner = where_is[neighbour[f, block]]
            route[2 * slot + f] = partner * 4 + face[f, block] * 2 + orient[f, block]

    loop(blocks, note, unroll=8)
    loop(blocks, direct, unroll=4)

    def get(c, k, r):
        return state[c, k, pl.ds(r - PAD, 8)]

    def fluxes(n):
        expect(n)
        m = [state[c, planes, pl.ds(n, 8)] for c in range(CH)]
        for j, x in enumerate(metric_terms(m)):
            mets[j, pl.ds(n + PAD, 8)] = x
        flux_chunk(get, mets, fi, w, fk, acc, n + PAD)

    def emit(c, k, r, val):
        full[c, k, pl.ds(r - PAD, 8)] = get(c, k, r) + val

    leave = leaving(full, part, out_sems)

    def sums(n):
        sum_chunk(mets, fi, w, fk, acc, n + PAD, emit)
        leave(n).start()

    chunks(rows // 8, fluxes)
    chunks(rows // 8, sums)
    chunks(rows // 8, lambda n: leave(n).wait())


def leaving(full, out, sems):
    def leave(n):
        at = pl.ds(n, 8)
        return pltpu.make_async_copy(full.at[:, :, at], out.at[:, :, at], sems.at[n // 8])

    return leave


def pack_ends(tall, planes):
    sub, lane = rows_of((8, LANES)), lanes_of((8, LANES))
    stacked = []
    for c in range(CH):
        packed = jnp.zeros((8, LANES), jnp.float32)
        for k in range(planes):
            x = turn(jnp.where(sub < 4, tall[0, c, k], tall[1, c, k]), 8 * k + 4, 1)
            packed = jnp.where(within(lane, 8 * k, 8), x, packed)
        stacked.append(packed)
    ends = across(jnp.concatenate(stacked, axis=0))
    out = []
    for c in range(CH):
        packed = jnp.zeros((8, LANES), jnp.float32)
        for k in range(planes):
            x = turn(ends[k * 8 : k * 8 + 8], 4 * k - (8 * c + 2), 1)
            packed = jnp.where(within(lane, 4 * k, 4), x, packed)
        out.append(packed)
    return out


def second_kernel(
    halves, dens, mom, en, met, vol, below, above, part,
    out, ends_base, ends_sec, inner,
    state, low, high, tall, tile_fk, tile_w, tile_acc, packed, ends, strips,
    sec, full, mets, fi, w, fk, acc, sems, out_sems,
):
    planes, rows = dens.shape[1], dens.shape[2]
    every = planes + 1
    halo = copy_all([(below, low), (above, high)], sems, 5 * PIECES)
    expect = arrive_in_pieces((dens, mom, en, met, vol), state, sems)
    arrive = copy_all([(part, sec.at[:, :, PAD : PAD + rows])], sems, 5 * PIECES + 2)
    half = lax.axis_index("ij")
    low_wall, high_wall = half == 0, half == halves - 1
    low_flag, high_flag = jnp.where(low_wall, 1, 0), jnp.where(high_wall, 1, 0)
    sub, lane = rows_of((8, LANES)), lanes_of((8, LANES))
    wait_all(halo)
    loop(min(PIECES, rows // 8), lambda n: expect(n * max(8, rows // PIECES)))

    for c in range(CH):
        for k in range(every):
            tall[0, c, k, 4:8] = state[c, k, 0:4]
            tall[1, c, k, 0:4] = state[c, k, rows - 4 : rows]

    @pl.when(low_wall)
    def _():
        for c in range(CH):
            for k in range(every):
                for n in range(2):
                    x = state[c, k, n : n + 1]
                    tall[0, c, k, 3 - n : 4 - n] = -x if 1 <= c <= 3 and k < planes else x

    @pl.when(jnp.logical_not(low_wall))
    def _():
        for c in range(CH):
            for k in range(every):
                tall[0, c, k, 0:4] = low[c, 4 * k : 4 * k + 4]

    @pl.when(high_wall)
    def _():
        for c in range(CH):
            for k in range(every):
                for n in range(2):
                    tall[1, c, k, 4 + n : 5 + n] = state[c, k, rows - 1 - n : rows - n]

    @pl.when(jnp.logical_not(high_wall))
    def _():
        for c in range(CH):
            for k in range(every):
                tall[1, c, k, 4:8] = high[c, 4 * k : 4 * k + 4]

    for c, x in enumerate(pack_ends(tall, every)):
        ends[0, c] = x

    def terms(n):
        m = [state[c, planes, pl.ds(n, 8)] for c in range(CH)]
        for j, x in enumerate(metric_terms(m)):
            mets[j, pl.ds(n + PAD, 8)] = x

    chunks(rows // 8, terms)
    tall_mets = [metric_terms([tall[s, c, planes] for c in range(CH)]) for s in range(2)]
    for s, at in ((0, PAD - 4), (1, PAD + rows - 4)):
        for j, x in enumerate(tall_mets[s]):
            mets[j, at : at + 8] = x

    wait_all(arrive)

    def done(c, s, k, x):
        tall[s, c, k] = x
        if s == 0:
            sign = -1.0 if 1 <= c <= 3 else 1.0
            wall = sign * jnp.where(sub == 2, turn(x, -3, 0), turn(x, -1, 0))
            x = jnp.where((sub < 4) & (low_flag == 1), wall, x)
        else:
            wall = jnp.where(sub == 4, turn(x, 1, 0), turn(x, 3, 0))
            x = jnp.where((sub >= 4) & (high_flag == 1), wall, x)
        start = PAD - 2 if s == 0 else PAD + rows - 2
        sec[c, k, start : start + 4] = x[2:6]

    tile_stage(
        planes, lambda c, s, k: tall[s, c, k], tall_mets, lambda *_: along(0), along(1),
        (tile_fk, tile_w, tile_acc), done,
    )
    for c, x in enumerate(pack_ends(tall, planes)):
        ends[1, c] = x
    last = copy_all([(ends.at[0], ends_base), (ends.at[1], ends_sec)], out_sems, rows // 8)

    if rows < LANES:
        packed[...] = jnp.zeros(packed.shape, jnp.float32)

    def pack(n):
        for c in range(CH):
            x = state[c, planes, pl.ds(n, 8)]
            at = 8 * planes
            packs = jnp.where(lane < at + 4, turn(x, at + 6, 1), turn(x, at + 2, 1))
            for k in range(planes):
                x = sec[c, k, pl.ds(n + PAD, 8)]
                at = 8 * k
                packs = jnp.where(within(lane, at, 4), turn(x, at + 6, 1), packs)
                packs = jnp.where(within(lane, at + 4, 4), turn(x, at + 2, 1), packs)
            packed[c, pl.ds(n, 8)] = packs

    chunks(rows // 8, pack)
    for c in range(CH):
        strips[c] = packed[c].T[0:64]
    last += copy_all([(strips, inner)], out_sems, rows // 8 + 2)

    def get(c, k, r):
        return sec[c, k, pl.ds(r, 8)]

    def emit(c, k, r, val):
        at = pl.ds(r - PAD, 8)
        full[c, k, at] = 0.5 * (state[c, k, at] + (get(c, k, r) + val))

    leave = leaving(full, out, out_sems)

    def sums(n):
        sum_chunk(mets, fi, w, fk, acc, n + PAD, emit)
        leave(n).start()

    chunks(rows // 8 + 2, lambda r: flux_chunk(get, mets, fi, w, fk, acc, r))
    chunks(rows // 8, sums)
    chunks(rows // 8, lambda n: leave(n).wait())
    wait_all(last)


def beyond(packed, f, k, rows):
    base = 28 * f + 4 * k
    low = roll_by(packed, LANES - 2 - base)
    top = rows % LANES
    high = low if top == 0 else roll_by(packed, top - 2 - base)
    lane = lanes_of(packed.shape)

    def at(x, o):
        if o < 0:
            x = jnp.where(lane >= LANES + o, low, x)
        else:
            x = jnp.where(within(lane, top, o), high, x)
        return turn(x, -o, 1)

    return at


def last_kernel(
    halves, rows, planes, own_at, ends_base_at, ends_sec_at, inner_at, got_at, out,
    next_dens, next_mom, next_en,
    own, ends_base, ends_sec, inner, got, base, sec, fk, ws, acc, turned, back, full, sems,
):
    late = copy_all([(inner_at, inner), (ends_sec_at, ends_sec), (out, full)], sems)
    early = copy_all([(got_at, got), (own_at, own), (ends_base_at, ends_base)], sems, 3)
    half = lax.axis_index("ij")
    low_wall, high_wall = half == 0, half == halves - 1
    sub, lane = rows_of((8, LANES)), lanes_of((8, LANES))

    def mix(f, mine, others):
        return jnp.where((sub < 4) == (f == 1), mine, others)

    wait_all(early)

    others = [jnp.zeros((8, LANES), jnp.float32)] * CH
    for k in range(planes + 1):
        start = DEPTH * k * PASSED
        for f in range(2):

            def ghost(row):
                x = got[pl.ds(start + row, 8, stride=PASSED)]
                return x if f == 1 else turn(x, 4, 0)

            arrived = ghost(2 * CH)
            to = 28 * f + 4 * k
            for c in range(CH):
                base[c, f, k] = mix(f, own[c, k * 8 : k * 8 + 8], ghost(f * CH + c))
                moved = turn(arrived, to - 4 * CH * f - 4 * c, 1)
                others[c] = jnp.where(within(lane, to, 4), moved, others[c])

    low_lanes = lane < 28
    twice = [jnp.where(low_lanes, ends_base[c], turn(ends_base[c], 28, 1)) for c in range(CH)]
    ends = [jnp.where(low_lanes == (sub >= 4), twice[c], others[c]) for c in range(CH)]
    slot = jnp.where(low_lanes, lane, lane - 28)

    def spread(x):
        y = x
        for k in range(planes):
            y = jnp.where(within(slot, 4 * k, 4), turn(x, 4 * (k - planes), 1), y)
        return y

    vax, vay, vbx, vby, niv, _, cw, _ = [spread(x) for x in metric_terms(ends)]
    wrapped = [spread(x) for x in metric_terms(twice)[2:4]]

    def keep(c, f, k, val):
        sec[c, f, k] = val

    def stage(held, ends, gx, gy):
        mets = [metric_terms([held[c, f, planes] for c in range(CH)]) for f in range(2)]
        w, p, h = point(ends)
        rims = (flux(ends, w, p, h, gx, gy), w)
        tile_stage(
            planes,
            lambda c, f, k: held[c, f, k],
            mets,
            lambda kind, c, f, k: beyond(rims[kind][c], f, k, rows),
            along(0),
            (fk, ws, acc),
            keep,
        )

    stage(base, ends, vax, vay)
    wait_all(late[0:2])

    def move(k, source):
        for c in range(CH):
            mine = inner[c, k * 8 : k * 8 + 8]
            for f in range(2):
                sec[c, f, k] = mix(f, mine, turn(source[c, f, k], 2 if f == 1 else -2, 0))

    for k in range(planes):
        move(k, sec)
    move(planes, base)

    def shifted(x):
        return jnp.where(low_lanes, turn(x, -2, 0), turn(x, 2, 0))

    w1, p1, h1 = point(ends)
    w0, p0, h0 = point(twice)
    new, old = flux(ends, w1, p1, h1, vbx, vby), flux(twice, w0, p0, h0, *wrapped)
    at_j = along(0)
    touched = within(sub, jnp.where(low_lanes, 4, 2), 2)
    second = []
    for c in range(CH):
        add = niv * slope(new[c] - old[c], at_j)
        if c > 0:
            add = add + cw * curve(w1[c - 1] - w0[c - 1], at_j)
        x = jnp.where(low_lanes, ends_sec[c], turn(ends_sec[c], 28, 1))
        second.append(shifted(x + jnp.where(touched, add, 0.0)))
    walled = low_wall | high_wall

    for k in range(planes):
        for f in range(2):
            to = 28 * f + 4 * k
            first = jnp.where(walled, jnp.where(low_wall, to, to + 2), -8)
            shift = jnp.where(low_wall, (to - 1) % LANES, (to + 3 - rows) % LANES)
            next_shift = jnp.where(low_wall, (to + 1) % LANES, (to + 5 - rows) % LANES)
            for c in range(CH):
                x = sec[c, f, k]
                one, two = pltpu.roll(x, shift, 1), pltpu.roll(x, next_shift, 1)
                x = jnp.where(lane == first, one, two)
                if 1 <= c <= 3:
                    x = jnp.where(low_wall, -1.0, 1.0) * x
                second[c] = jnp.where(within(lane, first, 2), x, second[c])
    stage(sec, second, shifted(vax), shifted(vay))

    per = LANES // 8

    for k in range(planes):
        for c in range(CH):
            x = jnp.where(sub < 4, turn(sec[c, 1, k], -2, 0), turn(sec[c, 0, k], 2, 0))
            at = (c * planes + k) * 8
            turned[at : at + 8] = 0.5 * (own[c, k * 8 : k * 8 + 8] + x)
    for n in range(turned.shape[0] // LANES):
        back[n] = turned[n * LANES : (n + 1) * LANES].T
    wait_all(late[2:])
    inside = within(lane, 4, LANES - 8)
    size = max(8, rows // PIECES)

    def leave(start):
        at = pl.ds(start, size)
        targets = [next_dens.at[0, :, at], next_en.at[0, :, at], next_mom.at[0, :, :, at]]
        sources = [full.at[0, :, at], full.at[4, :, at], full.at[1:4, :, at]]
        first = 6 + 3 * (start // size)
        return [
            pltpu.make_async_copy(src, dst, sems.at[first + n])
            for n, (src, dst) in enumerate(zip(sources, targets))
        ]

    def merge(r):
        at = pl.ds(r, 8)
        for c in range(CH):
            for k in range(planes):
                index = c * planes + k
                moved = turn(back[index // per, at], LANES - 4 - 8 * (index % per), 1)
                full[c, k, at] = jnp.where(inside, full[c, k, at], moved)

        @pl.when(lax.rem(r + 8, size) == 0)
        def _():
            for copy in leave(pl.multiple_of(r + 8 - size, 8)):
                copy.start()

    chunks(rows // 8, merge)
    for n in range(rows // size):
        wait_all(leave(n * size))


def local(mesh_shape, density, momentum, energy, metrics, volume, placed, neighbour, face, orient):
    halves = mesh_shape["ij"]
    blocks = mesh_shape["blk"]
    devices = blocks * halves
    planes, rows = density.shape[1], density.shape[2]
    every = planes + 1
    fields = (density, momentum, energy, metrics, volume)
    neighbour, face, orient = neighbour.T, face.T, orient.T
    smem = pl.BlockSpec(memory_space=pltpu.SMEM)
    hbm = pl.BlockSpec(memory_space=pltpu.HBM)

    def call(kernel, name, outs, ins, out_specs, scratch, cost=None, mib=VMEM_MIB):
        return pl.pallas_call(
            kernel,
            out_shape=outs,
            in_specs=ins,
            out_specs=out_specs,
            scratch_shapes=scratch,
            compiler_params=pltpu.CompilerParams(vmem_limit_bytes=mib * 1024 * 1024),
            cost_estimate=cost,
            name=name,
        )

    def shape(*dims):
        return jax.ShapeDtypeStruct(dims, jnp.float32)

    def vmem(x):
        return pltpu.VMEM(x.shape, jnp.float32)

    def sems(count):
        return pltpu.SemaphoreType.DMA((count,))

    sent, passed = shape(devices * SENT, LANES), shape(devices * PASSED, LANES)
    strip, rim = shape(CH, 64, LANES), shape(CH, 8, LANES)
    edge = shape(CH, 4 * every, LANES)
    edges = 1 if halves == 2 else 2
    square = shape(LANES, LANES)
    state = shape(CH, every, rows, LANES)
    outs = [sent, strip] + [edge] * edges
    to_send, own, *halo = call(
        functools.partial(cut_kernel, halves),
        "cut",
        outs,
        [hbm] * 5 + [smem] * 3,
        [hbm] * (2 + edges),
        [vmem(x) for x in outs]
        + [
            vmem(state),
            pltpu.VMEM((CH, LANES, LANES), jnp.float32),
            pltpu.VMEM((CH * 64, LANES), jnp.float32),
            sems(5 * PIECES),
            sems(2 + edges),
        ],
    )(*fields, placed, face, orient)

    def swap(x):
        x = x.reshape(devices, x.shape[0] // devices, 1, LANES)
        x = lax.all_to_all(x, ("blk", "ij"), 0, 0, tiled=True)
        return x.reshape(x.shape[0] * x.shape[1], LANES)

    if edges == 1:
        below = above = lax.ppermute(halo[0], "ij", [(0, 1), (1, 0)])
    else:
        below = lax.ppermute(halo[1], "ij", [(i, i + 1) for i in range(halves - 1)])
        above = lax.ppermute(halo[0], "ij", [(i + 1, i) for i in range(halves - 1)])
    got = swap(to_send)

    tall = rows + 2 * PAD
    block = shape(CH, planes, rows, LANES)
    padded = shape(CH, planes, tall, LANES)
    stage = [
        vmem(shape(8, tall, LANES)),
        vmem(padded),
        vmem(shape(4, planes, tall, LANES)),
        vmem(padded),
        vmem(padded),
    ]
    work = planes * rows * LANES
    cost = pl.CostEstimate(flops=300 * work, bytes_accessed=150 * work, transcendentals=work)
    leave = sems(rows // 8 + 3)
    part, route = call(
        first_kernel,
        "first_section",
        [block, jax.ShapeDtypeStruct((2 * blocks,), jnp.int32)],
        [hbm] * 5 + [smem] * 4,
        [hbm, smem],
        [vmem(state), vmem(block)]
        + stage
        + [pltpu.SMEM((blocks,), jnp.int32), sems(5 * PIECES), leave],
        cost,
    )(*fields, placed, neighbour, face, orient)
    relayed = call(
        functools.partial(relay_kernel, halves, rows, planes, devices),
        "relay",
        passed,
        [smem, hbm, pl.BlockSpec(memory_space=pltpu.VMEM)],
        hbm,
        [
            vmem(passed),
            vmem(shape(devices * 16, LANES)),
            vmem(shape(devices * 16, LANES)),
            vmem(shape(devices * 2, LANES)),
            sems(1),
        ],
        mib=16,
    )(route, below, got)
    ghosts = swap(relayed)
    tiles = shape(CH, 2, every, 8, LANES)
    flat = -(-CH * planes * 8 // LANES)
    out, ends_base, ends_sec, inner = call(
        functools.partial(second_kernel, halves),
        "second_section",
        [block, rim, rim, strip],
        [hbm] * 8,
        [hbm] * 4,
        [vmem(state), vmem(edge), vmem(edge), vmem(shape(2, CH, every, 8, LANES))]
        + [vmem(tiles)] * 3
        + [
            pltpu.VMEM((CH, LANES, LANES), jnp.float32),
            vmem(shape(2, CH, 8, LANES)),
            vmem(strip),
            vmem(padded),
            vmem(block),
        ]
        + stage
        + [sems(5 * PIECES + 3), leave],
        cost,
    )(*fields, below, above, part)
    return call(
        functools.partial(last_kernel, halves, rows, planes),
        "strips",
        [shape(*density.shape), shape(*momentum.shape), shape(*energy.shape)],
        [hbm] * 6,
        [hbm] * 3,
        [vmem(x) for x in (strip, rim, rim, strip, passed)]
        + [vmem(tiles)] * 5
        + [
            vmem(shape(flat * LANES, LANES)),
            vmem(shape(flat, LANES, LANES)),
            vmem(block),
            sems(6 + 3 * PIECES),
        ],
    )(own, ends_base, ends_sec, inner, ghosts, out)


def solution(mesh):
    return jax.shard_map(
        functools.partial(local, dict(mesh.shape)),
        mesh=mesh,
        in_specs=(
            P("blk", None, "ij", None),
            P("blk", None, None, "ij", None),
            P("blk", None, "ij", None),
            P("blk", None, "ij", None),
            P("blk", "ij", None),
            P(),
            P(),
            P(),
            P(),
        ),
        out_specs=(
            P("blk", None, "ij", None),
            P("blk", None, None, "ij", None),
            P("blk", None, "ij", None),
        ),
        check_vma=False,
    )
```

```python
import functools

import jax
import jax.numpy as jnp
from jax import lax
from jax.experimental import pallas as pl
from jax.experimental.pallas import tpu as pltpu
from jax.sharding import PartitionSpec as P

pressure_factor = 0.4
viscosity = 0.05
time_step = 0.03
unit = time_step / 12.0

LANES = 128
PAD = 8
PIECES = 4
DEPTH = 4
CH = 5
VMEM_MIB = 32
SENT = 2 * CH
PASSED = 2 * CH + 1
FIRST = 4


def turn(x, shift, axis):
    shift = shift % x.shape[axis]
    return x if shift == 0 else pltpu.roll(x, shift, axis)


def lanes_of(shape):
    return lax.broadcasted_iota(jnp.int32, shape, len(shape) - 1)


def rows_of(shape):
    return lax.broadcasted_iota(jnp.int32, shape, len(shape) - 2)


def point(f):
    rho, m1, m2, m3, e = f
    r = 1.0 / rho
    u1, u2, u3 = m1 * r, m2 * r, m3 * r
    kin = 0.5 * (m1 * u1 + m2 * u2 + m3 * u3)
    p = pressure_factor * (e - kin)
    return (u1, u2, u3, (kin + 2.0 * p) * r), p, e + p


def metric_terms(m):
    ax, ay, bx, by, v = m
    kv = viscosity * unit
    rw = kv * (ax * ax + ay * ay)
    cw = kv * (bx * bx + by * by)
    return v * ax, v * ay, v * bx, v * by, -unit / v, rw, cw, 30.0 * (rw + cw + kv)


def flux(f, w, p, h, gx, gy):
    rho, m1, m2, m3, _ = f
    u = gx * w[0] + gy * w[1]
    return (rho * u, m1 * u + gx * p, m2 * u + gy * p, m3 * u, h * u)


def flux_planes(f, w, p, h):
    u3 = w[2]
    return (f[3], f[1] * u3, f[2] * u3, f[3] * u3 + p, h * u3)


def slope(x, at):
    return 8.0 * (at(x, 1) - at(x, -1)) - (at(x, 2) - at(x, -2))


def curve(x, at):
    return 16.0 * (at(x, 1) + at(x, -1)) - (at(x, 2) + at(x, -2))


def along(axis):
    return lambda x, o: turn(x, -o, axis)


def within(lane, start, size):
    return (lane >= start) & (lane < start + size)


def roll_by(x, shift, axis=1):
    size = x.shape[axis]
    return pltpu.roll(x, lax.rem(shift + 4 * size, size), axis)


def across(x):
    if x.shape[0] < LANES:
        x = jnp.concatenate([x, jnp.zeros((LANES - x.shape[0], LANES), jnp.float32)], axis=0)
    return x.T


def loop(count, body, unroll=1):
    def step(n, _):
        body(n)
        return 0

    lax.fori_loop(0, count, step, 0, unroll=unroll)


def copy_all(pairs, sems, first=0):
    copies = [
        pltpu.make_async_copy(src, dst, sems.at[first + n]) for n, (src, dst) in enumerate(pairs)
    ]
    for copy in copies:
        copy.start()
    return copies


def state_pairs(fields, state, planes, start, size):
    dens, mom, en, met, vol = fields
    at = pl.ds(start, size)
    return [
        (dens.at[0, :, at], state.at[0, 0:planes, at]),
        (mom.at[0, :, :, at], state.at[1:4, 0:planes, at]),
        (en.at[0, :, at], state.at[4, 0:planes, at]),
        (met.at[0, :, at], state.at[0:4, planes, at]),
        (vol.at[0, at], state.at[4, planes, at]),
    ]


def arrive_in_pieces(fields, state, sems):
    planes, rows = fields[0].shape[1], fields[0].shape[2]
    size = max(8, rows // PIECES)
    for n in range(rows // size):
        copy_all(state_pairs(fields, state, planes, n * size, size), sems, 5 * n)

    def expect(start):
        @pl.when(lax.rem(start, size) == 0)
        def _():
            for n, (src, dst) in enumerate(state_pairs(fields, state, planes, start, size)):
                pltpu.make_async_copy(src, dst, sems.at[5 * (start // size) + n]).wait()

    return expect


def wait_all(copies):
    for copy in copies:
        copy.wait()


def tile_stage(planes, load, mets, shift_i, shift_j, hold, done):
    kv = viscosity * unit
    fk, ws, acc = hold

    def spread(k):
        for s in range(2):
            vax, vay, vbx, vby, niv, rw, cw, tw = mets[s]
            x = [load(c, s, k) for c in range(CH)]
            w, p, h = point(x)
            fi, fj = flux(x, w, p, h, vax, vay), flux(x, w, p, h, vbx, vby)
            for c in range(CH):
                val = niv * (slope(fi[c], shift_i(0, c, s, k)) + slope(fj[c], shift_j))
                if c > 0:
                    v = w[c - 1]
                    val = val + (
                        rw * curve(v, shift_i(1, c - 1, s, k)) + cw * curve(v, shift_j) - tw * v
                    )
                    ws[c - 1, s, k] = v
                acc[c, s, k] = x[c] + val
            for c, v in enumerate(flux_planes(x, w, p, h)):
                fk[c, s, k] = v

    def gather(k):
        at = {o: lax.rem(k + o + planes, planes) for o in (-2, -1, 0, 1, 2)}
        for s in range(2):
            for c in range(CH):
                val = acc[c, s, k] - unit * slope(0, lambda _, o: fk[c, s, at[o]])
                if c > 0:
                    val = val + kv * curve(0, lambda _, o: ws[c - 1, s, at[o]])
                done(c, s, k, val)

    loop(planes, spread, unroll=2)
    loop(planes, gather, unroll=2)


def cut_kernel(
    halves, dens, mom, en, met, vol, placed_at, face_at, orient_at, send, own, state, *rest
):
    edges, rest = rest[: 1 if halves == 2 else 2], rest[1 if halves == 2 else 2 :]
    held_send, packed, strips, placed, face, orient, sems, table_sems, out_sems = rest
    tables = copy_all(
        [(placed_at, placed), (face_at, face), (orient_at, orient)], table_sems
    )
    planes, rows = dens.shape[1], dens.shape[2]
    expect = arrive_in_pieces((dens, mom, en, met, vol), state, sems)
    half = lax.axis_index("ij")
    lane = lanes_of((8, LANES))
    if rows < LANES:
        packed[...] = jnp.zeros(packed.shape, jnp.float32)
    def pack(r):
        expect(r)
        for c in range(CH):
            packs = jnp.zeros((8, LANES), jnp.float32)
            for k in range(planes + 1):
                x = turn(state[c, k, pl.ds(r, 8)], 8 * k + 4, 1)
                packs = jnp.where(within(lane, 8 * k, 8), x, packs)
            packed[c, pl.ds(r, 8)] = packs

    chunks(rows // 8, pack)

    def cut_ends(k):
        for c in range(CH):
            low, high = state[c, k, 0:4], state[c, k, rows - 4 : rows]
            if len(edges) == 1:
                edges[0][c, k * 4 : k * 4 + 4] = jnp.where(half == 0, high, low)
            else:
                edges[0][c, k * 4 : k * 4 + 4] = low
                edges[1][c, k * 4 : k * 4 + 4] = high

    for k in range(planes + 1):
        cut_ends(k)

    wait_all(tables)
    block = placed[lax.axis_index("blk")]
    row = rows_of((64, LANES))
    high_side = row % 8 < 4
    mirror = jnp.where(
        rows_of((LANES, LANES)) + lanes_of((LANES, LANES)) == rows - 1, 1.0, 0.0
    )
    flip = [jnp.where(orient[f, block] == 1, -1.0, 1.0) for f in range(2)]
    same = [jnp.where(face[f, block] == f, -1.0, 1.0) for f in range(2)]
    rising = [face[f, block] == 1 for f in range(2)]
    turned = jnp.where(high_side, flip[1], flip[0])
    facing = jnp.where(high_side, same[1], same[0])

    def orient_strip(c):
        strip = packed[c].T[0:64]
        own[c] = strip
        back = jnp.dot(
            strip,
            mirror,
            precision=lax.Precision.HIGHEST,
            preferred_element_type=jnp.float32,
        )
        moved = jnp.where(turned < 0.0, back, strip)
        sign = jnp.where(c < 2, turned, jnp.where(c < 4, facing, 1.0))
        moved = jnp.where(row >= planes * 8, moved * sign, moved)
        strips[pl.ds(pl.multiple_of(c * 64, 64), 64)] = moved

    loop(CH, orient_strip)

    def put(n):
        k, e = n >> 2, n & 3
        at = (FIRST + n) * SENT
        low = k * 8 + 4 + jnp.where(rising[0], e, 3 - e)
        high = k * 8 + jnp.where(rising[1], 3 - e, e)
        held_send[pl.ds(at, CH)] = strips[pl.ds(low, CH, stride=64)]
        held_send[pl.ds(at + CH, CH)] = strips[pl.ds(high, CH, stride=64)]

    loop(DEPTH * (planes + 1), put, unroll=4)
    wait_all(copy_all([(held_send, send)], out_sems))


def relay_kernel(
    halves, rows, planes, devices, route_at, halo, held_got, send,
    held_send, below, above, signs, route, sems,
):
    del halo
    wait_all(copy_all([(route_at, route)], sems, 1))
    me = lax.axis_index("blk") * halves + lax.axis_index("ij")
    is_field = (me >= FIRST) & (me < FIRST + DEPTH * planes)

    def pass_on(slot):
        for f in range(2):
            code = route[2 * slot + f]
            partner, side, turned = code >> 2, (code >> 1) & 1, code & 1
            sign = jnp.where(turned == 1, -1.0, 1.0)

            def piece(h):
                h = jnp.where(turned == 1, halves - 1 - h, h)
                return held_got[pl.ds((partner * halves + h) * SENT + side * CH, CH)]

            pieces = [piece(h) for h in range(halves)]
            for half in range(halves):
                at = slot * halves + half
                held_send[pl.ds(at * PASSED + f * CH, CH)] = pieces[half]
                below[pl.ds((f * devices + at) * 8, CH)] = pieces[max(half - 1, 0)]
                above[pl.ds((f * devices + at) * 8, CH)] = pieces[min(half + 1, halves - 1)]
                signs[pl.ds(f * devices + at, 1)] = jnp.full((1, LANES), sign, jnp.float32)

    loop(devices // halves, pass_on, unroll=4)
    count = 2 * devices
    lane = lanes_of((count, LANES))
    half = rows_of((count, LANES)) % halves
    sign = signs[...]
    ends = jnp.zeros((count, LANES), jnp.float32)
    for c in range(CH):
        low, high = below[pl.ds(c, count, stride=8)], above[pl.ds(c, count, stride=8)]
        at = 4 * c
        low_wall = jnp.where(lane == at, turn(low, at - 1, 1), turn(low, at + 1, 1))
        high_wall = jnp.where(
            lane == at + 2, turn(high, at + 3 - rows, 1), turn(high, at + 5 - rows, 1)
        )
        if 1 <= c <= 3:
            low_wall = jnp.where(is_field, -sign * low_wall, low_wall)
            high_wall = jnp.where(is_field, sign * high_wall, high_wall)
        low = jnp.where(half == 0, low_wall, turn(low, at + 2 - rows, 1))
        high = jnp.where(half == halves - 1, high_wall, turn(high, at + 2, 1))
        ends = jnp.where(within(lane, at, 2), low, jnp.where(within(lane, at + 2, 2), high, ends))
    held_send[pl.ds(2 * CH, devices, stride=PASSED)] = ends[0:devices] + turn(
        ends[devices:], 4 * CH, 1
    )
    wait_all(copy_all([(held_send, send)], sems))


def flux_chunk(get, mets, fi, w, fk, acc, r):
    rows = pl.ds(r, 8)
    vax, vay, vbx, vby, niv, rw, cw, tw = [mets[j, rows] for j in range(8)]
    at_j = along(1)
    for k in range(fi.shape[1]):
        f = [get(c, k, r) for c in range(CH)]
        wk, p, h = point(f)
        for c, x in enumerate(flux(f, wk, p, h, vax, vay)):
            fi[c, k, rows] = x
        for c in range(4):
            w[c, k, rows] = wk[c]
        fj = flux(f, wk, p, h, vbx, vby)
        for c in range(CH):
            val = niv * slope(fj[c], at_j)
            if c > 0:
                val = val + (cw * curve(wk[c - 1], at_j) - tw * wk[c - 1])
            acc[c, k, rows] = val
        for c, x in enumerate(flux_planes(f, wk, p, h)):
            fk[c, k, rows] = x


def sum_chunk(mets, fi, w, fk, acc, r, emit):
    planes = fi.shape[1]
    kv = viscosity * unit
    rows = pl.ds(r, 8)
    niv, rw = mets[4, rows], mets[5, rows]
    for c in range(CH):
        t = [fk[c, k, rows] for k in range(planes)]
        x = [w[c - 1, k, rows] for k in range(planes)] if c > 0 else None
        for k in range(planes):

            def near(v, o):
                return v[(k + o) % planes]

            def at_i(v, o):
                return v[pl.ds(r + o, 8)]

            val = acc[c, k, rows] + niv * slope(fi.at[c, k], at_i) - unit * slope(t, near)
            if c > 0:
                val = val + (rw * curve(w.at[c - 1, k], at_i) + kv * curve(x, near))
            emit(c, k, r, val)


def chunks(count, body):
    def step(n, _):
        body(pl.multiple_of(n * 8, 8))
        return 0

    lax.fori_loop(0, count, step, 0)


def first_kernel(
    state, placed_at, neighbour_at, face_at, orient_at, part, route,
    mets, fi, w, fk, acc, placed, neighbour, face, orient, where_is, sems,
):
    planes, rows = part.shape[1], part.shape[2]
    pairs = zip((placed_at, neighbour_at, face_at, orient_at), (placed, neighbour, face, orient))
    tables = copy_all(list(pairs), sems)

    def get(c, k, r):
        return state[c, k, pl.ds(r - PAD, 8)]

    def fluxes(n):
        m = [state[c, planes, pl.ds(n, 8)] for c in range(CH)]
        for j, x in enumerate(metric_terms(m)):
            mets[j, pl.ds(n + PAD, 8)] = x
        flux_chunk(get, mets, fi, w, fk, acc, n + PAD)

    def emit(c, k, r, val):
        part[c, k, pl.ds(r - PAD, 8)] = get(c, k, r) + val

    chunks(rows // 8, fluxes)
    chunks(rows // 8, lambda n: sum_chunk(mets, fi, w, fk, acc, n + PAD, emit))
    wait_all(tables)
    blocks = placed.shape[0]

    def note(slot):
        where_is[placed[slot]] = slot

    def direct(slot):
        block = placed[slot]
        for f in range(2):
            partner = where_is[neighbour[f, block]]
            route[2 * slot + f] = partner * 4 + face[f, block] * 2 + orient[f, block]

    loop(blocks, note, unroll=8)
    loop(blocks, direct, unroll=4)


def pack_ends(tall, planes):
    sub, lane = rows_of((8, LANES)), lanes_of((8, LANES))
    stacked = []
    for c in range(CH):
        packed = jnp.zeros((8, LANES), jnp.float32)
        for k in range(planes):
            x = turn(jnp.where(sub < 4, tall[0, c, k], tall[1, c, k]), 8 * k + 4, 1)
            packed = jnp.where(within(lane, 8 * k, 8), x, packed)
        stacked.append(packed)
    ends = across(jnp.concatenate(stacked, axis=0))
    out = []
    for c in range(CH):
        packed = jnp.zeros((8, LANES), jnp.float32)
        for k in range(planes):
            x = turn(ends[k * 8 : k * 8 + 8], 4 * k - (8 * c + 2), 1)
            packed = jnp.where(within(lane, 4 * k, 4), x, packed)
        out.append(packed)
    return out


def second_kernel(
    halves, state, low, high, part, out, ends_base, ends_sec, strips,
    tall, tile_fk, tile_w, tile_acc, packed, sec, mets, fi, w, fk, acc, sems,
):
    planes, rows = part.shape[1], part.shape[2]
    every = planes + 1
    arrive = copy_all([(part, sec.at[:, :, PAD : PAD + rows])], sems)
    half = lax.axis_index("ij")
    low_wall, high_wall = half == 0, half == halves - 1
    low_flag, high_flag = jnp.where(low_wall, 1, 0), jnp.where(high_wall, 1, 0)
    sub, lane = rows_of((8, LANES)), lanes_of((8, LANES))

    for c in range(CH):
        for k in range(every):
            tall[0, c, k, 4:8] = state[c, k, 0:4]
            tall[1, c, k, 0:4] = state[c, k, rows - 4 : rows]

    @pl.when(low_wall)
    def _():
        for c in range(CH):
            for k in range(every):
                for n in range(2):
                    x = state[c, k, n : n + 1]
                    tall[0, c, k, 3 - n : 4 - n] = -x if 1 <= c <= 3 and k < planes else x

    @pl.when(jnp.logical_not(low_wall))
    def _():
        for c in range(CH):
            for k in range(every):
                tall[0, c, k, 0:4] = low[c, 4 * k : 4 * k + 4]

    @pl.when(high_wall)
    def _():
        for c in range(CH):
            for k in range(every):
                for n in range(2):
                    tall[1, c, k, 4 + n : 5 + n] = state[c, k, rows - 1 - n : rows - n]

    @pl.when(jnp.logical_not(high_wall))
    def _():
        for c in range(CH):
            for k in range(every):
                tall[1, c, k, 4:8] = high[c, 4 * k : 4 * k + 4]

    for c, x in enumerate(pack_ends(tall, every)):
        ends_base[c] = x

    def terms(n):
        m = [state[c, planes, pl.ds(n, 8)] for c in range(CH)]
        for j, x in enumerate(metric_terms(m)):
            mets[j, pl.ds(n + PAD, 8)] = x

    chunks(rows // 8, terms)
    tall_mets = [metric_terms([tall[s, c, planes] for c in range(CH)]) for s in range(2)]
    for s, at in ((0, PAD - 4), (1, PAD + rows - 4)):
        for j, x in enumerate(tall_mets[s]):
            mets[j, at : at + 8] = x

    wait_all(arrive)

    def done(c, s, k, x):
        tall[s, c, k] = x
        if s == 0:
            sign = -1.0 if 1 <= c <= 3 else 1.0
            wall = sign * jnp.where(sub == 2, turn(x, -3, 0), turn(x, -1, 0))
            x = jnp.where((sub < 4) & (low_flag == 1), wall, x)
        else:
            wall = jnp.where(sub == 4, turn(x, 1, 0), turn(x, 3, 0))
            x = jnp.where((sub >= 4) & (high_flag == 1), wall, x)
        start = PAD - 2 if s == 0 else PAD + rows - 2
        sec[c, k, start : start + 4] = x[2:6]

    tile_stage(
        planes, lambda c, s, k: tall[s, c, k], tall_mets, lambda *_: along(0), along(1),
        (tile_fk, tile_w, tile_acc), done,
    )
    for c, x in enumerate(pack_ends(tall, planes)):
        ends_sec[c] = x

    if rows < LANES:
        packed[...] = jnp.zeros(packed.shape, jnp.float32)

    def pack(n):
        for c in range(CH):
            x = state[c, planes, pl.ds(n, 8)]
            at = 8 * planes
            packs = jnp.where(lane < at + 4, turn(x, at + 6, 1), turn(x, at + 2, 1))
            for k in range(planes):
                x = sec[c, k, pl.ds(n + PAD, 8)]
                at = 8 * k
                packs = jnp.where(within(lane, at, 4), turn(x, at + 6, 1), packs)
                packs = jnp.where(within(lane, at + 4, 4), turn(x, at + 2, 1), packs)
            packed[c, pl.ds(n, 8)] = packs

    chunks(rows // 8, pack)
    for c in range(CH):
        strips[c] = packed[c].T[0:64]

    def get(c, k, r):
        return sec[c, k, pl.ds(r, 8)]

    def emit(c, k, r, val):
        at = pl.ds(r - PAD, 8)
        out[c, k, at] = 0.5 * (state[c, k, at] + (get(c, k, r) + val))

    chunks(rows // 8 + 2, lambda r: flux_chunk(get, mets, fi, w, fk, acc, r))
    chunks(rows // 8, lambda n: sum_chunk(mets, fi, w, fk, acc, n + PAD, emit))


def beyond(packed, f, k, rows):
    base = 28 * f + 4 * k
    low = roll_by(packed, LANES - 2 - base)
    top = rows % LANES
    high = low if top == 0 else roll_by(packed, top - 2 - base)
    lane = lanes_of(packed.shape)

    def at(x, o):
        if o < 0:
            x = jnp.where(lane >= LANES + o, low, x)
        else:
            x = jnp.where(within(lane, top, o), high, x)
        return turn(x, -o, 1)

    return at


def last_kernel(
    halves, rows, planes, own, ends_base, ends_sec, inner, got, out,
    next_dens, next_mom, next_en,
    base, sec, fk, ws, acc, turned, back, full, sems,
):
    half = lax.axis_index("ij")
    low_wall, high_wall = half == 0, half == halves - 1
    sub, lane = rows_of((8, LANES)), lanes_of((8, LANES))

    def mix(f, mine, others):
        return jnp.where((sub < 4) == (f == 1), mine, others)

    others = [jnp.zeros((8, LANES), jnp.float32)] * CH
    for k in range(planes + 1):
        start = DEPTH * k * PASSED
        for f in range(2):

            def ghost(row):
                x = got[pl.ds(start + row, 8, stride=PASSED)]
                return x if f == 1 else turn(x, 4, 0)

            arrived = ghost(2 * CH)
            to = 28 * f + 4 * k
            for c in range(CH):
                base[c, f, k] = mix(f, own[c, k * 8 : k * 8 + 8], ghost(f * CH + c))
                moved = turn(arrived, to - 4 * CH * f - 4 * c, 1)
                others[c] = jnp.where(within(lane, to, 4), moved, others[c])

    low_lanes = lane < 28
    twice = [jnp.where(low_lanes, ends_base[c], turn(ends_base[c], 28, 1)) for c in range(CH)]
    ends = [jnp.where(low_lanes == (sub >= 4), twice[c], others[c]) for c in range(CH)]
    slot = jnp.where(low_lanes, lane, lane - 28)

    def spread(x):
        y = x
        for k in range(planes):
            y = jnp.where(within(slot, 4 * k, 4), turn(x, 4 * (k - planes), 1), y)
        return y

    vax, vay, vbx, vby, niv, _, cw, _ = [spread(x) for x in metric_terms(ends)]
    wrapped = [spread(x) for x in metric_terms(twice)[2:4]]

    def keep(c, f, k, val):
        sec[c, f, k] = val

    def stage(held, ends, gx, gy):
        mets = [metric_terms([held[c, f, planes] for c in range(CH)]) for f in range(2)]
        w, p, h = point(ends)
        rims = (flux(ends, w, p, h, gx, gy), w)
        tile_stage(
            planes,
            lambda c, f, k: held[c, f, k],
            mets,
            lambda kind, c, f, k: beyond(rims[kind][c], f, k, rows),
            along(0),
            (fk, ws, acc),
            keep,
        )

    stage(base, ends, vax, vay)

    def move(k, source):
        for c in range(CH):
            mine = inner[c, k * 8 : k * 8 + 8]
            for f in range(2):
                sec[c, f, k] = mix(f, mine, turn(source[c, f, k], 2 if f == 1 else -2, 0))

    for k in range(planes):
        move(k, sec)
    move(planes, base)

    def shifted(x):
        return jnp.where(low_lanes, turn(x, -2, 0), turn(x, 2, 0))

    w1, p1, h1 = point(ends)
    w0, p0, h0 = point(twice)
    new, old = flux(ends, w1, p1, h1, vbx, vby), flux(twice, w0, p0, h0, *wrapped)
    at_j = along(0)
    touched = within(sub, jnp.where(low_lanes, 4, 2), 2)
    second = []
    for c in range(CH):
        add = niv * slope(new[c] - old[c], at_j)
        if c > 0:
            add = add + cw * curve(w1[c - 1] - w0[c - 1], at_j)
        x = jnp.where(low_lanes, ends_sec[c], turn(ends_sec[c], 28, 1))
        second.append(shifted(x + jnp.where(touched, add, 0.0)))
    walled = low_wall | high_wall

    for k in range(planes):
        for f in range(2):
            to = 28 * f + 4 * k
            first = jnp.where(walled, jnp.where(low_wall, to, to + 2), -8)
            shift = jnp.where(low_wall, (to - 1) % LANES, (to + 3 - rows) % LANES)
            next_shift = jnp.where(low_wall, (to + 1) % LANES, (to + 5 - rows) % LANES)
            for c in range(CH):
                x = sec[c, f, k]
                one, two = pltpu.roll(x, shift, 1), pltpu.roll(x, next_shift, 1)
                x = jnp.where(lane == first, one, two)
                if 1 <= c <= 3:
                    x = jnp.where(low_wall, -1.0, 1.0) * x
                second[c] = jnp.where(within(lane, first, 2), x, second[c])
    stage(sec, second, shifted(vax), shifted(vay))

    per = LANES // 8

    for k in range(planes):
        for c in range(CH):
            x = jnp.where(sub < 4, turn(sec[c, 1, k], -2, 0), turn(sec[c, 0, k], 2, 0))
            at = (c * planes + k) * 8
            turned[at : at + 8] = 0.5 * (own[c, k * 8 : k * 8 + 8] + x)
    for n in range(turned.shape[0] // LANES):
        back[n] = turned[n * LANES : (n + 1) * LANES].T
    inside = within(lane, 4, LANES - 8)
    size = max(8, rows // PIECES)

    def leave(start):
        at = pl.ds(start, size)
        targets = [next_dens.at[0, :, at], next_en.at[0, :, at], next_mom.at[0, :, :, at]]
        sources = [full.at[0, :, at], full.at[4, :, at], full.at[1:4, :, at]]
        first = 3 * (start // size)
        return [
            pltpu.make_async_copy(src, dst, sems.at[first + n])
            for n, (src, dst) in enumerate(zip(sources, targets))
        ]

    def merge(r):
        at = pl.ds(r, 8)
        for c in range(CH):
            for k in range(planes):
                index = c * planes + k
                moved = turn(back[index // per, at], LANES - 4 - 8 * (index % per), 1)
                full[c, k, at] = jnp.where(inside, out[c, k, at], moved)

        @pl.when(lax.rem(r + 8, size) == 0)
        def _():
            for copy in leave(pl.multiple_of(r + 8 - size, 8)):
                copy.start()

    chunks(rows // 8, merge)
    for n in range(rows // size):
        wait_all(leave(n * size))


def local(mesh_shape, density, momentum, energy, metrics, volume, placed, neighbour, face, orient):
    halves = mesh_shape["ij"]
    blocks = mesh_shape["blk"]
    devices = blocks * halves
    planes, rows = density.shape[1], density.shape[2]
    every = planes + 1
    fields = (density, momentum, energy, metrics, volume)
    neighbour, face, orient = neighbour.T, face.T, orient.T
    vmem = pl.BlockSpec(memory_space=pltpu.VMEM)
    smem = pl.BlockSpec(memory_space=pltpu.SMEM)
    hbm = pl.BlockSpec(memory_space=pltpu.HBM)
    anywhere = pl.BlockSpec(memory_space=pl.ANY)

    def call(kernel, name, outs, ins, out_specs, scratch, cost=None):
        run = pl.pallas_call(
            kernel,
            out_shape=[
                held(x) if spec is vmem else far(x) if spec is hbm else x
                for x, spec in zip(outs, out_specs)
            ],
            in_specs=ins,
            out_specs=out_specs,
            scratch_shapes=scratch,
            compiler_params=pltpu.CompilerParams(vmem_limit_bytes=VMEM_MIB * 1024 * 1024),
            cost_estimate=cost,
            name=name,
        )

        def keep(*operands):
            return run(
                *[
                    x
                    if spec not in (vmem, hbm)
                    else pltpu.with_memory_space_constraint(x, spec.memory_space)
                    for x, spec in zip(operands, ins)
                ]
            )

        return keep

    def shape(*dims):
        return jax.ShapeDtypeStruct(dims, jnp.float32)

    def held(x):
        return pltpu.VMEM(x.shape, x.dtype)

    def far(x):
        return pltpu.HBM(x.shape, x.dtype)

    def table(x):
        return pltpu.SMEM(x.shape, jnp.int32)

    def sems(count):
        return pltpu.SemaphoreType.DMA((count,))

    sent, passed = shape(devices * SENT, LANES), shape(devices * PASSED, LANES)
    strip, rim = shape(CH, 64, LANES), shape(CH, 8, LANES)
    edge = shape(CH, 4 * every, LANES)
    edges = 1 if halves == 2 else 2
    square = shape(CH, LANES, LANES)
    to_send, own, state, *halo = call(
        functools.partial(cut_kernel, halves),
        "cut",
        [sent, strip, shape(CH, every, rows, LANES)] + [edge] * edges,
        [hbm] * 8,
        [hbm] + [vmem] * (2 + edges),
        [
            held(sent),
            held(square),
            held(shape(CH * 64, LANES)),
            table(placed),
            table(face),
            table(orient),
            sems(5 * PIECES),
            sems(3),
            sems(1),
        ],
    )(*fields, placed, face, orient)

    def swap(x):
        x = x.reshape(devices, x.shape[0] // devices, 1, LANES)
        x = lax.all_to_all(x, ("blk", "ij"), 0, 0, tiled=True)
        return x.reshape(x.shape[0] * x.shape[1], LANES)

    if edges == 1:
        below = above = lax.ppermute(halo[0], "ij", [(0, 1), (1, 0)])
    else:
        below = lax.ppermute(halo[1], "ij", [(i, i + 1) for i in range(halves - 1)])
        above = lax.ppermute(halo[0], "ij", [(i + 1, i) for i in range(halves - 1)])
    got = swap(to_send)

    tall = rows + 2 * PAD
    block = shape(CH, planes, rows, LANES)
    padded = held(shape(CH, planes, tall, LANES))
    stage = [
        held(shape(8, tall, LANES)),
        padded,
        held(shape(4, planes, tall, LANES)),
        padded,
        padded,
    ]
    work = planes * rows * LANES
    cost = pl.CostEstimate(flops=300 * work, bytes_accessed=150 * work, transcendentals=work)
    route = jax.ShapeDtypeStruct((2 * blocks,), jnp.int32)
    part, route_out = call(
        first_kernel,
        "first_section",
        [block, route],
        [vmem] + [hbm] * 4,
        [vmem, smem],
        stage + [table(x) for x in (placed, neighbour, face, orient, placed)] + [sems(4)],
        cost,
    )(state, placed, neighbour, face, orient)
    (relayed,) = call(
        functools.partial(relay_kernel, halves, rows, planes, devices),
        "relay",
        [passed],
        [anywhere, anywhere, vmem],
        [hbm],
        [
            held(passed),
            held(shape(devices * 16, LANES)),
            held(shape(devices * 16, LANES)),
            held(shape(devices * 2, LANES)),
            table(route),
            sems(2),
        ],
    )(route_out, below, got)
    ghosts = swap(relayed)
    tiles = held(shape(CH, 2, every, 8, LANES))
    flat = -(-CH * planes * 8 // LANES)
    out, ends_base, ends_sec, inner = call(
        functools.partial(second_kernel, halves),
        "second_section",
        [block, rim, rim, strip],
        [vmem] * 4,
        [vmem] * 4,
        [held(shape(2, CH, every, 8, LANES))]
        + [tiles] * 3
        + [held(square), padded]
        + stage
        + [sems(1)],
        cost,
    )(state, below, above, part)
    return call(
        functools.partial(last_kernel, halves, rows, planes),
        "strips",
        [shape(*density.shape), shape(*momentum.shape), shape(*energy.shape)],
        [vmem] * 6,
        [hbm] * 3,
        [tiles] * 5
        + [
            held(shape(flat * LANES, LANES)),
            held(shape(flat, LANES, LANES)),
            held(block),
            sems(3 * PIECES),
        ],
    )(own, ends_base, ends_sec, inner, ghosts, out)


def solution(mesh):
    return jax.shard_map(
        functools.partial(local, dict(mesh.shape)),
        mesh=mesh,
        in_specs=(
            P("blk", None, "ij", None),
            P("blk", None, None, "ij", None),
            P("blk", None, "ij", None),
            P("blk", None, "ij", None),
            P("blk", "ij", None),
            P(),
            P(),
            P(),
            P(),
        ),
        out_specs=(
            P("blk", None, "ij", None),
            P("blk", None, None, "ij", None),
            P("blk", None, "ij", None),
        ),
        check_vma=False,
    )
```

```python
import functools

import jax
import jax.numpy as jnp
from jax import lax
from jax.experimental import pallas as pl
from jax.experimental.pallas import tpu as pltpu
from jax.sharding import PartitionSpec as P

pressure_factor = 0.4
viscosity = 0.05
time_step = 0.03
unit = time_step / 12.0

LANES = 128
PAD = 8
PIECES = 4
DEPTH = 4
CH = 5
VMEM_MIB = 32
SENT = 2 * CH
PASSED = 2 * CH + 1
FIRST = 4


def turn(x, shift, axis):
    shift = shift % x.shape[axis]
    return x if shift == 0 else pltpu.roll(x, shift, axis)


def lanes_of(shape):
    return lax.broadcasted_iota(jnp.int32, shape, len(shape) - 1)


def rows_of(shape):
    return lax.broadcasted_iota(jnp.int32, shape, len(shape) - 2)


def point(f):
    rho, m1, m2, m3, e = f
    r = 1.0 / rho
    u1, u2, u3 = m1 * r, m2 * r, m3 * r
    kin = 0.5 * (m1 * u1 + m2 * u2 + m3 * u3)
    p = pressure_factor * (e - kin)
    return (u1, u2, u3, (kin + 2.0 * p) * r), p, e + p


def metric_terms(m):
    ax, ay, bx, by, v = m
    kv = viscosity * unit
    rw = kv * (ax * ax + ay * ay)
    cw = kv * (bx * bx + by * by)
    return v * ax, v * ay, v * bx, v * by, -unit / v, rw, cw, 30.0 * (rw + cw + kv)


def flux(f, w, p, h, gx, gy):
    rho, m1, m2, m3, _ = f
    u = gx * w[0] + gy * w[1]
    return (rho * u, m1 * u + gx * p, m2 * u + gy * p, m3 * u, h * u)


def flux_planes(f, w, p, h):
    u3 = w[2]
    return (f[3], f[1] * u3, f[2] * u3, f[3] * u3 + p, h * u3)


def slope(x, at):
    return 8.0 * (at(x, 1) - at(x, -1)) - (at(x, 2) - at(x, -2))


def curve(x, at):
    return 16.0 * (at(x, 1) + at(x, -1)) - (at(x, 2) + at(x, -2))


def along(axis):
    return lambda x, o: turn(x, -o, axis)


def within(lane, start, size):
    return (lane >= start) & (lane < start + size)


def roll_by(x, shift, axis=1):
    size = x.shape[axis]
    return pltpu.roll(x, lax.rem(shift + 4 * size, size), axis)


def across(x):
    if x.shape[0] < LANES:
        x = jnp.concatenate([x, jnp.zeros((LANES - x.shape[0], LANES), jnp.float32)], axis=0)
    return x.T


def loop(count, body, unroll=1):
    def step(n, _):
        body(n)
        return 0

    lax.fori_loop(0, count, step, 0, unroll=unroll)


def copy_all(pairs, sems, first=0):
    copies = [
        pltpu.make_async_copy(src, dst, sems.at[first + n]) for n, (src, dst) in enumerate(pairs)
    ]
    for copy in copies:
        copy.start()
    return copies


def state_pairs(fields, state, planes, start, size):
    dens, mom, en, met, vol = fields
    at = pl.ds(start, size)
    return [
        (dens.at[0, :, at], state.at[0, 0:planes, at]),
        (mom.at[0, :, :, at], state.at[1:4, 0:planes, at]),
        (en.at[0, :, at], state.at[4, 0:planes, at]),
        (met.at[0, :, at], state.at[0:4, planes, at]),
        (vol.at[0, at], state.at[4, planes, at]),
    ]


def arrive_in_pieces(fields, state, sems):
    planes, rows = fields[0].shape[1], fields[0].shape[2]
    size = max(8, rows // PIECES)
    for n in range(rows // size):
        copy_all(state_pairs(fields, state, planes, n * size, size), sems, 5 * n)

    def expect(start):
        @pl.when(lax.rem(start, size) == 0)
        def _():
            for n, (src, dst) in enumerate(state_pairs(fields, state, planes, start, size)):
                pltpu.make_async_copy(src, dst, sems.at[5 * (start // size) + n]).wait()

    return expect


def wait_all(copies):
    for copy in copies:
        copy.wait()


def tile_stage(planes, load, mets, shift_i, shift_j, hold, done):
    kv = viscosity * unit
    fk, ws, acc = hold

    def spread(k):
        for s in range(2):
            vax, vay, vbx, vby, niv, rw, cw, tw = mets[s]
            x = [load(c, s, k) for c in range(CH)]
            w, p, h = point(x)
            fi, fj = flux(x, w, p, h, vax, vay), flux(x, w, p, h, vbx, vby)
            for c in range(CH):
                val = niv * (slope(fi[c], shift_i(0, c, s, k)) + slope(fj[c], shift_j))
                if c > 0:
                    v = w[c - 1]
                    val = val + (
                        rw * curve(v, shift_i(1, c - 1, s, k)) + cw * curve(v, shift_j) - tw * v
                    )
                    ws[c - 1, s, k] = v
                acc[c, s, k] = x[c] + val
            for c, v in enumerate(flux_planes(x, w, p, h)):
                fk[c, s, k] = v

    def gather(k):
        at = {o: lax.rem(k + o + planes, planes) for o in (-2, -1, 0, 1, 2)}
        for s in range(2):
            for c in range(CH):
                val = acc[c, s, k] - unit * slope(0, lambda _, o: fk[c, s, at[o]])
                if c > 0:
                    val = val + kv * curve(0, lambda _, o: ws[c - 1, s, at[o]])
                done(c, s, k, val)

    loop(planes, spread, unroll=2)
    loop(planes, gather, unroll=2)


def cut_kernel(
    halves, dens, mom, en, met, vol, placed_at, face_at, orient_at, send, own, state, *rest
):
    edges, rest = rest[: 1 if halves == 2 else 2], rest[1 if halves == 2 else 2 :]
    held_send, packed, strips, placed, face, orient, sems, table_sems, out_sems = rest
    tables = copy_all(
        [(placed_at, placed), (face_at, face), (orient_at, orient)], table_sems
    )
    planes, rows = dens.shape[1], dens.shape[2]
    expect = arrive_in_pieces((dens, mom, en, met, vol), state, sems)
    half = lax.axis_index("ij")
    lane = lanes_of((8, LANES))
    if rows < LANES:
        packed[...] = jnp.zeros(packed.shape, jnp.float32)
    def pack(r):
        expect(r)
        for c in range(CH):
            packs = jnp.zeros((8, LANES), jnp.float32)
            for k in range(planes + 1):
                x = turn(state[c, k, pl.ds(r, 8)], 8 * k + 4, 1)
                packs = jnp.where(within(lane, 8 * k, 8), x, packs)
            packed[c, pl.ds(r, 8)] = packs

    chunks(rows // 8, pack, unroll=2)

    def cut_ends(k):
        for c in range(CH):
            low, high = state[c, k, 0:4], state[c, k, rows - 4 : rows]
            if len(edges) == 1:
                edges[0][c, k * 4 : k * 4 + 4] = jnp.where(half == 0, high, low)
            else:
                edges[0][c, k * 4 : k * 4 + 4] = low
                edges[1][c, k * 4 : k * 4 + 4] = high

    for k in range(planes + 1):
        cut_ends(k)

    wait_all(tables)
    block = placed[lax.axis_index("blk")]
    row = rows_of((64, LANES))
    high_side = row % 8 < 4
    mirror = jnp.where(
        rows_of((LANES, LANES)) + lanes_of((LANES, LANES)) == rows - 1, 1.0, 0.0
    )
    flip = [jnp.where(orient[f, block] == 1, -1.0, 1.0) for f in range(2)]
    same = [jnp.where(face[f, block] == f, -1.0, 1.0) for f in range(2)]
    rising = [face[f, block] == 1 for f in range(2)]
    turned = jnp.where(high_side, flip[1], flip[0])
    facing = jnp.where(high_side, same[1], same[0])

    def orient_strip(c):
        strip = packed[c].T[0:64]
        own[c] = strip
        back = jnp.dot(
            strip,
            mirror,
            precision=lax.Precision.HIGHEST,
            preferred_element_type=jnp.float32,
        )
        moved = jnp.where(turned < 0.0, back, strip)
        sign = jnp.where(c < 2, turned, jnp.where(c < 4, facing, 1.0))
        moved = jnp.where(row >= planes * 8, moved * sign, moved)
        strips[pl.ds(pl.multiple_of(c * 64, 64), 64)] = moved

    loop(CH, orient_strip)

    def put(n):
        k, e = n >> 2, n & 3
        at = (FIRST + n) * SENT
        low = k * 8 + 4 + jnp.where(rising[0], e, 3 - e)
        high = k * 8 + jnp.where(rising[1], 3 - e, e)
        held_send[pl.ds(at, CH)] = strips[pl.ds(low, CH, stride=64)]
        held_send[pl.ds(at + CH, CH)] = strips[pl.ds(high, CH, stride=64)]

    loop(DEPTH * (planes + 1), put, unroll=4)
    wait_all(copy_all([(held_send, send)], out_sems))


def relay_kernel(
    halves, rows, planes, devices, route_at, halo, part, held_got, send,
    held_send, below, above, signs, route, sems,
):
    del halo, part
    wait_all(copy_all([(route_at, route)], sems, 1))
    me = lax.axis_index("blk") * halves + lax.axis_index("ij")
    is_field = (me >= FIRST) & (me < FIRST + DEPTH * planes)

    def pass_on(slot):
        for f in range(2):
            code = route[2 * slot + f]
            partner, side, turned = code >> 2, (code >> 1) & 1, code & 1
            sign = jnp.where(turned == 1, -1.0, 1.0)

            def piece(h):
                h = jnp.where(turned == 1, halves - 1 - h, h)
                return held_got[pl.ds((partner * halves + h) * SENT + side * CH, CH)]

            pieces = [piece(h) for h in range(halves)]
            for half in range(halves):
                at = slot * halves + half
                held_send[pl.ds(at * PASSED + f * CH, CH)] = pieces[half]
                below[pl.ds((f * devices + at) * 8, CH)] = pieces[max(half - 1, 0)]
                above[pl.ds((f * devices + at) * 8, CH)] = pieces[min(half + 1, halves - 1)]
                signs[pl.ds(f * devices + at, 1)] = jnp.full((1, LANES), sign, jnp.float32)

    loop(devices // halves, pass_on, unroll=4)
    count = 2 * devices
    lane = lanes_of((count, LANES))
    half = rows_of((count, LANES)) % halves
    sign = signs[...]
    ends = jnp.zeros((count, LANES), jnp.float32)
    for c in range(CH):
        low, high = below[pl.ds(c, count, stride=8)], above[pl.ds(c, count, stride=8)]
        at = 4 * c
        low_wall = jnp.where(lane == at, turn(low, at - 1, 1), turn(low, at + 1, 1))
        high_wall = jnp.where(
            lane == at + 2, turn(high, at + 3 - rows, 1), turn(high, at + 5 - rows, 1)
        )
        if 1 <= c <= 3:
            low_wall = jnp.where(is_field, -sign * low_wall, low_wall)
            high_wall = jnp.where(is_field, sign * high_wall, high_wall)
        low = jnp.where(half == 0, low_wall, turn(low, at + 2 - rows, 1))
        high = jnp.where(half == halves - 1, high_wall, turn(high, at + 2, 1))
        ends = jnp.where(within(lane, at, 2), low, jnp.where(within(lane, at + 2, 2), high, ends))
    held_send[pl.ds(2 * CH, devices, stride=PASSED)] = ends[0:devices] + turn(
        ends[devices:], 4 * CH, 1
    )
    wait_all(copy_all([(held_send, send)], sems))


def flux_chunk(get, mets, fi, w, fk, acc, r):
    rows = pl.ds(r, 8)
    vax, vay, vbx, vby, niv, rw, cw, tw = [mets[j, rows] for j in range(8)]
    at_j = along(1)
    for k in range(fi.shape[1]):
        f = [get(c, k, r) for c in range(CH)]
        wk, p, h = point(f)
        for c, x in enumerate(flux(f, wk, p, h, vax, vay)):
            fi[c, k, rows] = x
        for c in range(4):
            w[c, k, rows] = wk[c]
        fj = flux(f, wk, p, h, vbx, vby)
        for c in range(CH):
            val = niv * slope(fj[c], at_j)
            if c > 0:
                val = val + (cw * curve(wk[c - 1], at_j) - tw * wk[c - 1])
            acc[c, k, rows] = val
        for c, x in enumerate(flux_planes(f, wk, p, h)):
            fk[c, k, rows] = x


def sum_chunk(mets, fi, w, fk, acc, r, emit):
    planes = fi.shape[1]
    kv = viscosity * unit
    rows = pl.ds(r, 8)
    niv, rw = mets[4, rows], mets[5, rows]
    for c in range(CH):
        t = [fk[c, k, rows] for k in range(planes)]
        x = [w[c - 1, k, rows] for k in range(planes)] if c > 0 else None
        for k in range(planes):

            def near(v, o):
                return v[(k + o) % planes]

            def at_i(v, o):
                return v[pl.ds(r + o, 8)]

            val = acc[c, k, rows] + niv * slope(fi.at[c, k], at_i) - unit * slope(t, near)
            if c > 0:
                val = val + (rw * curve(w.at[c - 1, k], at_i) + kv * curve(x, near))
            emit(c, k, r, val)


def chunks(count, body, unroll=1):
    def step(n, _):
        body(pl.multiple_of(n * 8, 8))
        return 0

    lax.fori_loop(0, count, step, 0, unroll=unroll)


def first_kernel(
    state, placed_at, neighbour_at, face_at, orient_at, part, route,
    mets, fi, w, fk, acc, placed, neighbour, face, orient, where_is, sems,
):
    planes, rows = part.shape[1], part.shape[2]
    pairs = zip((placed_at, neighbour_at, face_at, orient_at), (placed, neighbour, face, orient))
    wait_all(copy_all(list(pairs), sems))
    count = rows // 8
    blocks = placed.shape[0]
    share = -(-blocks // count)

    def slots(n):
        return [jnp.minimum((n // 8) * share + i, blocks - 1) for i in range(share)]

    def get(c, k, r):
        return state[c, k, pl.ds(r - PAD, 8)]

    def fluxes(n):
        for slot in slots(n):
            where_is[placed[slot]] = slot
        m = [state[c, planes, pl.ds(n, 8)] for c in range(CH)]
        for j, x in enumerate(metric_terms(m)):
            mets[j, pl.ds(n + PAD, 8)] = x
        flux_chunk(get, mets, fi, w, fk, acc, n + PAD)

    def emit(c, k, r, val):
        part[c, k, pl.ds(r - PAD, 8)] = get(c, k, r) + val

    def sums(n):
        for slot in slots(n):
            block = placed[slot]
            for f in range(2):
                partner = where_is[neighbour[f, block]]
                route[2 * slot + f] = partner * 4 + face[f, block] * 2 + orient[f, block]
        sum_chunk(mets, fi, w, fk, acc, n + PAD, emit)

    chunks(count, fluxes, unroll=2)
    chunks(count, sums, unroll=2)


def pack_ends(tall, planes):
    sub, lane = rows_of((8, LANES)), lanes_of((8, LANES))
    stacked = []
    for c in range(CH):
        packed = jnp.zeros((8, LANES), jnp.float32)
        for k in range(planes):
            x = turn(jnp.where(sub < 4, tall[0, c, k], tall[1, c, k]), 8 * k + 4, 1)
            packed = jnp.where(within(lane, 8 * k, 8), x, packed)
        stacked.append(packed)
    ends = across(jnp.concatenate(stacked, axis=0))
    out = []
    for c in range(CH):
        packed = jnp.zeros((8, LANES), jnp.float32)
        for k in range(planes):
            x = turn(ends[k * 8 : k * 8 + 8], 4 * k - (8 * c + 2), 1)
            packed = jnp.where(within(lane, 4 * k, 4), x, packed)
        out.append(packed)
    return out


def second_kernel(
    halves, state, low, high, part, out, ends_base, ends_sec, inner,
    tall, tile_fk, tile_w, tile_acc, packed, sec, mets, fi, w, fk, acc, sems,
):
    planes, rows = part.shape[1], part.shape[2]
    every = planes + 1
    arrive = copy_all([(part, sec.at[:, :, PAD : PAD + rows])], sems)
    half = lax.axis_index("ij")
    low_wall, high_wall = half == 0, half == halves - 1
    low_flag, high_flag = jnp.where(low_wall, 1, 0), jnp.where(high_wall, 1, 0)
    sub, lane = rows_of((8, LANES)), lanes_of((8, LANES))

    for c in range(CH):
        for k in range(every):
            tall[0, c, k, 4:8] = state[c, k, 0:4]
            tall[1, c, k, 0:4] = state[c, k, rows - 4 : rows]

    @pl.when(low_wall)
    def _():
        for c in range(CH):
            for k in range(every):
                for n in range(2):
                    x = state[c, k, n : n + 1]
                    tall[0, c, k, 3 - n : 4 - n] = -x if 1 <= c <= 3 and k < planes else x

    @pl.when(jnp.logical_not(low_wall))
    def _():
        for c in range(CH):
            for k in range(every):
                tall[0, c, k, 0:4] = low[c, 4 * k : 4 * k + 4]

    @pl.when(high_wall)
    def _():
        for c in range(CH):
            for k in range(every):
                for n in range(2):
                    tall[1, c, k, 4 + n : 5 + n] = state[c, k, rows - 1 - n : rows - n]

    @pl.when(jnp.logical_not(high_wall))
    def _():
        for c in range(CH):
            for k in range(every):
                tall[1, c, k, 4:8] = high[c, 4 * k : 4 * k + 4]

    for c, x in enumerate(pack_ends(tall, every)):
        ends_base[c] = x

    def terms(n):
        m = [state[c, planes, pl.ds(n, 8)] for c in range(CH)]
        for j, x in enumerate(metric_terms(m)):
            mets[j, pl.ds(n + PAD, 8)] = x

    chunks(rows // 8, terms)
    tall_mets = [metric_terms([tall[s, c, planes] for c in range(CH)]) for s in range(2)]
    for s, at in ((0, PAD - 4), (1, PAD + rows - 4)):
        for j, x in enumerate(tall_mets[s]):
            mets[j, at : at + 8] = x

    wait_all(arrive)

    def done(c, s, k, x):
        tall[s, c, k] = x
        if s == 0:
            sign = -1.0 if 1 <= c <= 3 else 1.0
            wall = sign * jnp.where(sub == 2, turn(x, -3, 0), turn(x, -1, 0))
            x = jnp.where((sub < 4) & (low_flag == 1), wall, x)
        else:
            wall = jnp.where(sub == 4, turn(x, 1, 0), turn(x, 3, 0))
            x = jnp.where((sub >= 4) & (high_flag == 1), wall, x)
        start = PAD - 2 if s == 0 else PAD + rows - 2
        sec[c, k, start : start + 4] = x[2:6]

    tile_stage(
        planes, lambda c, s, k: tall[s, c, k], tall_mets, lambda *_: along(0), along(1),
        (tile_fk, tile_w, tile_acc), done,
    )
    for c, x in enumerate(pack_ends(tall, planes)):
        ends_sec[c] = x

    if rows < LANES:
        packed[...] = jnp.zeros(packed.shape, jnp.float32)

    def pack(n):
        for c in range(CH):
            packs = turn(state[c, planes, pl.ds(n, 8)], 12 * planes + 6, 1)
            for k in range(planes):
                x = turn(sec[c, k, pl.ds(n + PAD, 8)], 12 * k + 6, 1)
                packs = jnp.where(within(lane, 12 * k, 12), x, packs)
            packed[c, pl.ds(n, 8)] = packs

    chunks(rows // 8, pack, unroll=2)
    for c in range(CH):
        inner[c] = packed[c].T[0 : inner.shape[1]]

    def get(c, k, r):
        return sec[c, k, pl.ds(r, 8)]

    def emit(c, k, r, val):
        at = pl.ds(r - PAD, 8)
        out[c, k, at] = 0.5 * (state[c, k, at] + (get(c, k, r) + val))

    chunks(rows // 8 + 2, lambda r: flux_chunk(get, mets, fi, w, fk, acc, r), unroll=2)
    chunks(rows // 8, lambda n: sum_chunk(mets, fi, w, fk, acc, n + PAD, emit), unroll=2)


def beyond(packed, f, k, rows):
    base = 28 * f + 4 * k
    low = roll_by(packed, LANES - 2 - base)
    top = rows % LANES
    high = low if top == 0 else roll_by(packed, top - 2 - base)
    lane = lanes_of(packed.shape)

    def at(x, o):
        if o < 0:
            x = jnp.where(lane >= LANES + o, low, x)
        else:
            x = jnp.where(within(lane, top, o), high, x)
        return turn(x, -o, 1)

    return at


def last_kernel(
    halves, rows, planes, own, ends_base, ends_sec, inner, got, out,
    next_dens, next_mom, next_en,
    base, sec, fk, ws, acc, turned, back, full, sems,
):
    half = lax.axis_index("ij")
    low_wall, high_wall = half == 0, half == halves - 1
    sub, lane = rows_of((8, LANES)), lanes_of((8, LANES))

    def mix(f, mine, others):
        return jnp.where((sub < 4) == (f == 1), mine, others)

    others = [jnp.zeros((8, LANES), jnp.float32)] * CH
    for k in range(planes + 1):
        start = DEPTH * k * PASSED
        for f in range(2):

            def ghost(row):
                x = got[pl.ds(start + row, 8, stride=PASSED)]
                return x if f == 1 else turn(x, 4, 0)

            arrived = ghost(2 * CH)
            to = 28 * f + 4 * k
            for c in range(CH):
                base[c, f, k] = mix(f, own[c, k * 8 : k * 8 + 8], ghost(f * CH + c))
                moved = turn(arrived, to - 4 * CH * f - 4 * c, 1)
                others[c] = jnp.where(within(lane, to, 4), moved, others[c])

    low_lanes = lane < 28
    twice = [jnp.where(low_lanes, ends_base[c], turn(ends_base[c], 28, 1)) for c in range(CH)]
    ends = [jnp.where(low_lanes == (sub >= 4), twice[c], others[c]) for c in range(CH)]
    slot = jnp.where(low_lanes, lane, lane - 28)

    def spread(x):
        y = x
        for k in range(planes):
            y = jnp.where(within(slot, 4 * k, 4), turn(x, 4 * (k - planes), 1), y)
        return y

    vax, vay, vbx, vby, niv, _, cw, _ = [spread(x) for x in metric_terms(ends)]
    wrapped = [spread(x) for x in metric_terms(twice)[2:4]]

    def keep(c, f, k, val):
        sec[c, f, k] = val

    def stage(held, ends, gx, gy):
        mets = [metric_terms([held[c, f, planes] for c in range(CH)]) for f in range(2)]
        w, p, h = point(ends)
        rims = (flux(ends, w, p, h, gx, gy), w)
        tile_stage(
            planes,
            lambda c, f, k: held[c, f, k],
            mets,
            lambda kind, c, f, k: beyond(rims[kind][c], f, k, rows),
            along(0),
            (fk, ws, acc),
            keep,
        )

    stage(base, ends, vax, vay)

    def move(k, source):
        for c in range(CH):
            at = 12 * k
            mine = jnp.where(sub < 4, inner[c, at : at + 8], inner[c, at + 4 : at + 12])
            for f in range(2):
                sec[c, f, k] = mix(f, mine, turn(source[c, f, k], 2 if f == 1 else -2, 0))

    for k in range(planes):
        move(k, sec)
    move(planes, base)

    def shifted(x):
        return jnp.where(low_lanes, turn(x, -2, 0), turn(x, 2, 0))

    w1, p1, h1 = point(ends)
    w0, p0, h0 = point(twice)
    new, old = flux(ends, w1, p1, h1, vbx, vby), flux(twice, w0, p0, h0, *wrapped)
    at_j = along(0)
    touched = within(sub, jnp.where(low_lanes, 4, 2), 2)
    second = []
    for c in range(CH):
        add = niv * slope(new[c] - old[c], at_j)
        if c > 0:
            add = add + cw * curve(w1[c - 1] - w0[c - 1], at_j)
        x = jnp.where(low_lanes, ends_sec[c], turn(ends_sec[c], 28, 1))
        second.append(shifted(x + jnp.where(touched, add, 0.0)))
    walled = low_wall | high_wall

    for k in range(planes):
        for f in range(2):
            to = 28 * f + 4 * k
            first = jnp.where(walled, jnp.where(low_wall, to, to + 2), -8)
            shift = jnp.where(low_wall, (to - 1) % LANES, (to + 3 - rows) % LANES)
            next_shift = jnp.where(low_wall, (to + 1) % LANES, (to + 5 - rows) % LANES)
            for c in range(CH):
                x = sec[c, f, k]
                one, two = pltpu.roll(x, shift, 1), pltpu.roll(x, next_shift, 1)
                x = jnp.where(lane == first, one, two)
                if 1 <= c <= 3:
                    x = jnp.where(low_wall, -1.0, 1.0) * x
                second[c] = jnp.where(within(lane, first, 2), x, second[c])
    stage(sec, second, shifted(vax), shifted(vay))

    per = LANES // 8

    for k in range(planes):
        for c in range(CH):
            x = jnp.where(sub < 4, turn(sec[c, 1, k], -2, 0), turn(sec[c, 0, k], 2, 0))
            at = (c * planes + k) * 8
            turned[at : at + 8] = 0.5 * (own[c, k * 8 : k * 8 + 8] + x)
    for n in range(turned.shape[0] // LANES):
        back[n] = turned[n * LANES : (n + 1) * LANES].T
    inside = within(lane, 4, LANES - 8)
    size = max(8, rows // PIECES)

    def leave(start):
        at = pl.ds(start, size)
        targets = [next_dens.at[0, :, at], next_en.at[0, :, at], next_mom.at[0, :, :, at]]
        sources = [full.at[0, :, at], full.at[4, :, at], full.at[1:4, :, at]]
        first = 3 * (start // size)
        return [
            pltpu.make_async_copy(src, dst, sems.at[first + n])
            for n, (src, dst) in enumerate(zip(sources, targets))
        ]

    def merge(r):
        at = pl.ds(r, 8)
        for c in range(CH):
            for k in range(planes):
                index = c * planes + k
                moved = turn(back[index // per, at], LANES - 4 - 8 * (index % per), 1)
                full[c, k, at] = jnp.where(inside, out[c, k, at], moved)

        @pl.when(lax.rem(r + 8, size) == 0)
        def _():
            for copy in leave(pl.multiple_of(r + 8 - size, 8)):
                copy.start()

    chunks(rows // 8, merge)
    for n in range(rows // size):
        wait_all(leave(n * size))


def local(mesh_shape, density, momentum, energy, metrics, volume, placed, neighbour, face, orient):
    halves = mesh_shape["ij"]
    blocks = mesh_shape["blk"]
    devices = blocks * halves
    planes, rows = density.shape[1], density.shape[2]
    every = planes + 1
    fields = (density, momentum, energy, metrics, volume)
    neighbour, face, orient = neighbour.T, face.T, orient.T
    vmem = pl.BlockSpec(memory_space=pltpu.VMEM)
    smem = pl.BlockSpec(memory_space=pltpu.SMEM)
    hbm = pl.BlockSpec(memory_space=pltpu.HBM)
    anywhere = pl.BlockSpec(memory_space=pl.ANY)

    def call(kernel, name, outs, ins, out_specs, scratch, cost=None, alias=None):
        run = pl.pallas_call(
            kernel,
            out_shape=[
                held(x) if spec is vmem else far(x) if spec is hbm else x
                for x, spec in zip(outs, out_specs)
            ],
            in_specs=ins,
            out_specs=out_specs,
            scratch_shapes=scratch,
            compiler_params=pltpu.CompilerParams(vmem_limit_bytes=VMEM_MIB * 1024 * 1024),
            cost_estimate=cost,
            input_output_aliases=alias or {},
            name=name,
        )

        def keep(*operands):
            return run(
                *[
                    x
                    if spec not in (vmem, hbm)
                    else pltpu.with_memory_space_constraint(x, spec.memory_space)
                    for x, spec in zip(operands, ins)
                ]
            )

        return keep

    def shape(*dims):
        return jax.ShapeDtypeStruct(dims, jnp.float32)

    def held(x):
        return pltpu.VMEM(x.shape, x.dtype)

    def far(x):
        return pltpu.HBM(x.shape, x.dtype)

    def table(x):
        return pltpu.SMEM(x.shape, jnp.int32)

    def sems(count):
        return pltpu.SemaphoreType.DMA((count,))

    sent, passed = shape(devices * SENT, LANES), shape(devices * PASSED, LANES)
    strip, rim = shape(CH, 64, LANES), shape(CH, 8, LANES)
    edge = shape(CH, 4 * every, LANES)
    edges = 1 if halves == 2 else 2
    square = shape(CH, LANES, LANES)
    whole = shape(CH, every, rows, LANES)
    to_send, own, state, *halo = call(
        functools.partial(cut_kernel, halves),
        "cut",
        [sent, strip, whole] + [edge] * edges,
        [hbm] * 8,
        [hbm] + [vmem] * (2 + edges),
        [
            held(sent),
            held(square),
            held(shape(CH * 64, LANES)),
            table(placed),
            table(face),
            table(orient),
            sems(5 * PIECES),
            sems(3),
            sems(1),
        ],
    )(*fields, placed, face, orient)

    def swap(x):
        x = x.reshape(devices, x.shape[0] // devices, 1, LANES)
        x = lax.all_to_all(x, ("blk", "ij"), 0, 0, tiled=True)
        return x.reshape(x.shape[0] * x.shape[1], LANES)

    if edges == 1:
        below = above = lax.ppermute(halo[0], "ij", [(0, 1), (1, 0)])
    else:
        below = lax.ppermute(halo[1], "ij", [(i, i + 1) for i in range(halves - 1)])
        above = lax.ppermute(halo[0], "ij", [(i + 1, i) for i in range(halves - 1)])
    got = swap(to_send)

    tall = rows + 2 * PAD
    block = shape(CH, planes, rows, LANES)
    padded = held(shape(CH, planes, tall, LANES))
    stage = [
        held(shape(8, tall, LANES)),
        padded,
        held(shape(4, planes, tall, LANES)),
        padded,
        padded,
    ]
    work = planes * rows * LANES
    cost = pl.CostEstimate(flops=300 * work, bytes_accessed=150 * work, transcendentals=work)
    route = jax.ShapeDtypeStruct((2 * blocks,), jnp.int32)
    part, route_out = call(
        first_kernel,
        "first_section",
        [block, route],
        [vmem] + [hbm] * 4,
        [vmem, smem],
        stage + [table(x) for x in (placed, neighbour, face, orient, placed)] + [sems(4)],
        cost,
    )(state, placed, neighbour, face, orient)
    (relayed,) = call(
        functools.partial(relay_kernel, halves, rows, planes, devices),
        "relay",
        [passed],
        [anywhere, anywhere, anywhere, vmem],
        [hbm],
        [
            held(passed),
            held(shape(devices * 16, LANES)),
            held(shape(devices * 16, LANES)),
            held(shape(devices * 2, LANES)),
            table(route),
            sems(2),
        ],
    )(route_out, below, part, got)
    ghosts = swap(relayed)
    tiles = held(shape(CH, 2, every, 8, LANES))
    flat = -(-CH * planes * 8 // LANES)
    out, ends_base, ends_sec, inner = call(
        functools.partial(second_kernel, halves),
        "second_section",
        [whole, rim, rim, shape(CH, 12 * every + 4, LANES)],
        [vmem] * 4,
        [vmem] * 4,
        [held(shape(2, CH, every, 8, LANES))]
        + [tiles] * 3
        + [held(square), padded]
        + stage
        + [sems(1)],
        cost,
        {0: 0},
    )(state, below, above, part)
    return call(
        functools.partial(last_kernel, halves, rows, planes),
        "strips",
        [shape(*density.shape), shape(*momentum.shape), shape(*energy.shape)],
        [vmem] * 6,
        [hbm] * 3,
        [tiles] * 5
        + [
            held(shape(flat * LANES, LANES)),
            held(shape(flat, LANES, LANES)),
            held(block),
            sems(3 * PIECES),
        ],
    )(own, ends_base, ends_sec, inner, ghosts, out)


def solution(mesh):
    return jax.shard_map(
        functools.partial(local, dict(mesh.shape)),
        mesh=mesh,
        in_specs=(
            P("blk", None, "ij", None),
            P("blk", None, None, "ij", None),
            P("blk", None, "ij", None),
            P("blk", None, "ij", None),
            P("blk", "ij", None),
            P(),
            P(),
            P(),
            P(),
        ),
        out_specs=(
            P("blk", None, "ij", None),
            P("blk", None, None, "ij", None),
            P("blk", None, "ij", None),
        ),
        check_vma=False,
    )
```

```python
import functools

import jax
import jax.numpy as jnp
from jax import lax
from jax.experimental import pallas as pl
from jax.experimental.pallas import tpu as pltpu
from jax.sharding import PartitionSpec as P

pressure_factor = 0.4
viscosity = 0.05
time_step = 0.03
unit = time_step / 12.0

LANES = 128
PAD = 8
PIECES = 4
DEPTH = 4
CH = 5
VMEM_MIB = 32
SENT = 2 * CH
PASSED = 2 * CH + 1
FIRST = 4


def turn(x, shift, axis):
    shift = shift % x.shape[axis]
    return x if shift == 0 else pltpu.roll(x, shift, axis)


def lanes_of(shape):
    return lax.broadcasted_iota(jnp.int32, shape, len(shape) - 1)


def rows_of(shape):
    return lax.broadcasted_iota(jnp.int32, shape, len(shape) - 2)


def point(f):
    rho, m1, m2, m3, e = f
    r = 1.0 / rho
    u1, u2, u3 = m1 * r, m2 * r, m3 * r
    kin = 0.5 * (m1 * u1 + m2 * u2 + m3 * u3)
    p = pressure_factor * (e - kin)
    return (u1, u2, u3, (kin + 2.0 * p) * r), p, e + p


def metric_terms(m):
    ax, ay, bx, by, v = m
    kv = viscosity * unit
    rw = kv * (ax * ax + ay * ay)
    cw = kv * (bx * bx + by * by)
    return v * ax, v * ay, v * bx, v * by, -unit / v, rw, cw, 30.0 * (rw + cw + kv)


def flux(f, w, p, h, gx, gy):
    rho, m1, m2, m3, _ = f
    u = gx * w[0] + gy * w[1]
    return (rho * u, m1 * u + gx * p, m2 * u + gy * p, m3 * u, h * u)


def flux_planes(f, w, p, h):
    u3 = w[2]
    return (f[3], f[1] * u3, f[2] * u3, f[3] * u3 + p, h * u3)


def slope(x, at):
    return 8.0 * (at(x, 1) - at(x, -1)) - (at(x, 2) - at(x, -2))


def curve(x, at):
    return 16.0 * (at(x, 1) + at(x, -1)) - (at(x, 2) + at(x, -2))


def along(axis):
    return lambda x, o: turn(x, -o, axis)


def within(lane, start, size):
    return (lane >= start) & (lane < start + size)


def roll_by(x, shift, axis=1):
    size = x.shape[axis]
    return pltpu.roll(x, lax.rem(shift + 4 * size, size), axis)


def across(x):
    if x.shape[0] < LANES:
        x = jnp.concatenate([x, jnp.zeros((LANES - x.shape[0], LANES), jnp.float32)], axis=0)
    return x.T


def loop(count, body, unroll=1):
    def step(n, _):
        body(n)
        return 0

    lax.fori_loop(0, count, step, 0, unroll=unroll)


def copy_all(pairs, sems, first=0):
    copies = [
        pltpu.make_async_copy(src, dst, sems.at[first + n]) for n, (src, dst) in enumerate(pairs)
    ]
    for copy in copies:
        copy.start()
    return copies


def state_pairs(fields, state, planes, start, size):
    dens, mom, en, met, vol = fields
    at, to = pl.ds(start, size), pl.ds(start + PAD, size)
    return [
        (dens.at[0, :, at], state.at[0, 0:planes, to]),
        (mom.at[0, :, :, at], state.at[1:4, 0:planes, to]),
        (en.at[0, :, at], state.at[4, 0:planes, to]),
        (met.at[0, :, at], state.at[0:4, planes, to]),
        (vol.at[0, at], state.at[4, planes, to]),
    ]


def arrive_in_pieces(fields, state, sems):
    planes, rows = fields[0].shape[1], fields[0].shape[2]
    size = max(8, rows // PIECES)
    for n in range(rows // size):
        copy_all(state_pairs(fields, state, planes, n * size, size), sems, 5 * n)

    def expect(start):
        @pl.when(lax.rem(start, size) == 0)
        def _():
            for n, (src, dst) in enumerate(state_pairs(fields, state, planes, start, size)):
                pltpu.make_async_copy(src, dst, sems.at[5 * (start // size) + n]).wait()

    return expect


def wait_all(copies):
    for copy in copies:
        copy.wait()


def tile_stage(planes, load, mets, shift_i, shift_j, hold, done):
    kv = viscosity * unit
    fk, ws, acc = hold

    def spread(k):
        for s in range(2):
            vax, vay, vbx, vby, niv, rw, cw, tw = mets[s]
            x = [load(c, s, k) for c in range(CH)]
            w, p, h = point(x)
            fi, fj = flux(x, w, p, h, vax, vay), flux(x, w, p, h, vbx, vby)
            for c in range(CH):
                val = niv * (slope(fi[c], shift_i(0, c, s, k)) + slope(fj[c], shift_j))
                if c > 0:
                    v = w[c - 1]
                    val = val + (
                        rw * curve(v, shift_i(1, c - 1, s, k)) + cw * curve(v, shift_j) - tw * v
                    )
                    ws[c - 1, s, k] = v
                acc[c, s, k] = x[c] + val
            for c, v in enumerate(flux_planes(x, w, p, h)):
                fk[c, s, k] = v

    def gather(k):
        at = {o: lax.rem(k + o + planes, planes) for o in (-2, -1, 0, 1, 2)}
        for s in range(2):
            for c in range(CH):
                val = acc[c, s, k] - unit * slope(0, lambda _, o: fk[c, s, at[o]])
                if c > 0:
                    val = val + kv * curve(0, lambda _, o: ws[c - 1, s, at[o]])
                done(c, s, k, val)

    loop(planes, spread, unroll=2)
    loop(planes, gather, unroll=2)


def cut_kernel(
    halves, dens, mom, en, met, vol, placed_at, face_at, orient_at, send, own, state, *rest
):
    edges, rest = rest[: 1 if halves == 2 else 2], rest[1 if halves == 2 else 2 :]
    held_send, packed, strips, placed, face, orient, sems, table_sems, out_sems = rest
    tables = copy_all(
        [(placed_at, placed), (face_at, face), (orient_at, orient)], table_sems
    )
    planes, rows = dens.shape[1], dens.shape[2]
    expect = arrive_in_pieces((dens, mom, en, met, vol), state, sems)
    half = lax.axis_index("ij")
    lane = lanes_of((8, LANES))
    if rows < LANES:
        packed[...] = jnp.zeros(packed.shape, jnp.float32)
    def pack(r):
        expect(r)
        for c in range(CH):
            packs = jnp.zeros((8, LANES), jnp.float32)
            for k in range(planes + 1):
                x = turn(state[c, k, pl.ds(r + PAD, 8)], 8 * k + 4, 1)
                packs = jnp.where(within(lane, 8 * k, 8), x, packs)
            packed[c, pl.ds(r, 8)] = packs

    chunks(rows // 8, pack, unroll=2)

    def cut_ends(k):
        for c in range(CH):
            low, high = state[c, k, PAD : PAD + 4], state[c, k, PAD + rows - 4 : PAD + rows]
            if len(edges) == 1:
                edges[0][c, k * 4 : k * 4 + 4] = jnp.where(half == 0, high, low)
            else:
                edges[0][c, k * 4 : k * 4 + 4] = low
                edges[1][c, k * 4 : k * 4 + 4] = high

    for k in range(planes + 1):
        cut_ends(k)

    wait_all(tables)
    block = placed[lax.axis_index("blk")]
    row = rows_of((64, LANES))
    high_side = row % 8 < 4
    mirror = jnp.where(
        rows_of((LANES, LANES)) + lanes_of((LANES, LANES)) == rows - 1, 1.0, 0.0
    )
    flip = [jnp.where(orient[f, block] == 1, -1.0, 1.0) for f in range(2)]
    same = [jnp.where(face[f, block] == f, -1.0, 1.0) for f in range(2)]
    rising = [face[f, block] == 1 for f in range(2)]
    turned = jnp.where(high_side, flip[1], flip[0])
    facing = jnp.where(high_side, same[1], same[0])

    def orient_strip(c):
        strip = packed[c].T[0:64]
        own[c] = strip
        back = jnp.dot(
            strip,
            mirror,
            precision=lax.Precision.HIGHEST,
            preferred_element_type=jnp.float32,
        )
        moved = jnp.where(turned < 0.0, back, strip)
        sign = jnp.where(c < 2, turned, jnp.where(c < 4, facing, 1.0))
        moved = jnp.where(row >= planes * 8, moved * sign, moved)
        strips[pl.ds(pl.multiple_of(c * 64, 64), 64)] = moved

    loop(CH, orient_strip, unroll=CH)

    def put(n):
        k, e = n >> 2, n & 3
        at = (FIRST + n) * SENT
        low = k * 8 + 4 + jnp.where(rising[0], e, 3 - e)
        high = k * 8 + jnp.where(rising[1], 3 - e, e)
        held_send[pl.ds(at, CH)] = strips[pl.ds(low, CH, stride=64)]
        held_send[pl.ds(at + CH, CH)] = strips[pl.ds(high, CH, stride=64)]

    loop(DEPTH * (planes + 1), put, unroll=4)
    wait_all(copy_all([(held_send, send)], out_sems))


def relay_kernel(
    halves, rows, planes, slots, route_at, after, *rest,
):
    del after
    sources, (send, held_send, below, above, signs, route, sems) = rest[:-7], rest[-7:]
    wait_all(copy_all([(route_at, route)], sems, 1))
    blocks = route.shape[0] // 2
    per = slots // blocks
    half = lax.axis_index("ij")
    first = lax.axis_index("blk") * per - FIRST

    def pass_on(slot):
        for f in range(2):
            code = route[2 * slot + f]
            partner, side, turned = code >> 2, (code >> 1) & 1, code & 1
            sign = jnp.where(turned == 1, -1.0, 1.0)
            for i in range(per):

                def piece(offset):
                    part = jnp.clip(half + offset, 0, halves - 1)
                    part = jnp.where(turned == 1, halves - 1 - part, part)
                    at = (partner * per + i) * SENT + side * CH
                    if len(sources) == 1:
                        return sources[0][pl.ds(part * (slots * SENT) + at, CH)]
                    mine, others = (x[pl.ds(at, CH)] for x in sources)
                    return jnp.where(part == half, mine, others)

                at = slot * per + i
                held_send[pl.ds(at * PASSED + f * CH, CH)] = piece(0)
                below[pl.ds((f * slots + at) * 8, CH)] = piece(-1)
                above[pl.ds((f * slots + at) * 8, CH)] = piece(1)
                signs[pl.ds(f * slots + at, 1)] = jnp.full((1, LANES), sign, jnp.float32)

    loop(blocks, pass_on, unroll=4)
    count = 2 * slots
    lane = lanes_of((count, LANES))
    piece_at = first + lax.rem(rows_of((count, LANES)), per)
    is_field = (piece_at >= 0) & (piece_at < DEPTH * planes)
    sign = signs[...]
    low_end, high_end = half == 0, half == halves - 1
    low_sign = jnp.where(is_field, -sign, 1.0)
    high_sign = jnp.where(is_field, sign, 1.0)
    ends = jnp.zeros((count, LANES), jnp.float32)
    for c in range(CH):
        low, high = below[pl.ds(c, count, stride=8)], above[pl.ds(c, count, stride=8)]
        at = 4 * c
        low_wall = jnp.where(lane == at, turn(low, at - 1, 1), turn(low, at + 1, 1))
        high_wall = jnp.where(
            lane == at + 2, turn(high, at + 3 - rows, 1), turn(high, at + 5 - rows, 1)
        )
        if 1 <= c <= 3:
            low_wall, high_wall = low_sign * low_wall, high_sign * high_wall
        low = jnp.where(low_end, low_wall, turn(low, at + 2 - rows, 1))
        high = jnp.where(high_end, high_wall, turn(high, at + 2, 1))
        ends = jnp.where(within(lane, at, 2), low, jnp.where(within(lane, at + 2, 2), high, ends))
    held_send[pl.ds(2 * CH, slots, stride=PASSED)] = ends[0:slots] + turn(
        ends[slots:], 4 * CH, 1
    )
    wait_all(copy_all([(held_send, send)], sems))


def flux_chunk(get, mets, fi, w, fk, acc, r):
    rows = pl.ds(r, 8)
    vax, vay, vbx, vby, niv, rw, cw, tw = [mets[j, rows] for j in range(8)]
    at_j = along(1)
    for k in range(fi.shape[1]):
        f = [get(c, k, r) for c in range(CH)]
        wk, p, h = point(f)
        for c, x in enumerate(flux(f, wk, p, h, vax, vay)):
            fi[c, k, rows] = x
        for c in range(4):
            w[c, k, rows] = wk[c]
        fj = flux(f, wk, p, h, vbx, vby)
        for c in range(CH):
            val = niv * slope(fj[c], at_j)
            if c > 0:
                val = val + (cw * curve(wk[c - 1], at_j) - tw * wk[c - 1])
            acc[c, k, rows] = val
        for c, x in enumerate(flux_planes(f, wk, p, h)):
            fk[c, k, rows] = x


def sum_chunk(mets, fi, w, fk, acc, r, emit):
    planes = fi.shape[1]
    kv = viscosity * unit
    rows = pl.ds(r, 8)
    niv, rw = mets[4, rows], mets[5, rows]
    for c in range(CH):
        t = [fk[c, k, rows] for k in range(planes)]
        x = [w[c - 1, k, rows] for k in range(planes)] if c > 0 else None
        for k in range(planes):

            def near(v, o):
                return v[(k + o) % planes]

            def at_i(v, o):
                return v[pl.ds(r + o, 8)]

            val = acc[c, k, rows] + niv * slope(fi.at[c, k], at_i) - unit * slope(t, near)
            if c > 0:
                val = val + (rw * curve(w.at[c - 1, k], at_i) + kv * curve(x, near))
            emit(c, k, r, val)


def chunks(count, body, unroll=1):
    def step(n, _):
        body(pl.multiple_of(n * 8, 8))
        return 0

    lax.fori_loop(0, count, step, 0, unroll=unroll)


def first_kernel(
    state_in, placed_at, neighbour_at, face_at, orient_at, state, route,
    mets, fi, w, fk, acc, placed, neighbour, face, orient, where_is, sems,
):
    del state_in
    planes, rows = fi.shape[1], fi.shape[2] - 2 * PAD
    pairs = zip((placed_at, neighbour_at, face_at, orient_at), (placed, neighbour, face, orient))
    wait_all(copy_all(list(pairs), sems))
    count = rows // 8
    blocks = placed.shape[0]
    share = -(-blocks // count)

    def slots(n):
        return [jnp.minimum((n // 8) * share + i, blocks - 1) for i in range(share)]

    def get(c, k, r):
        return state[c, k, pl.ds(r, 8)]

    def fluxes(n):
        for slot in slots(n):
            where_is[placed[slot]] = slot
        at = pl.ds(n + PAD, 8)
        for j, x in enumerate(metric_terms([state[c, planes, at] for c in range(CH)])):
            mets[j, at] = x
        flux_chunk(get, mets, fi, w, fk, acc, n + PAD)

    def emit(c, k, r, val):
        state[c, planes + 1 + k, pl.ds(r, 8)] = get(c, k, r) + val

    def sums(n):
        for slot in slots(n):
            block = placed[slot]
            for f in range(2):
                partner = where_is[neighbour[f, block]]
                route[2 * slot + f] = partner * 4 + face[f, block] * 2 + orient[f, block]
        sum_chunk(mets, fi, w, fk, acc, n + PAD, emit)

    chunks(count, fluxes)
    chunks(count, sums)


def pack_ends(tall, planes):
    sub, lane = rows_of((8, LANES)), lanes_of((8, LANES))
    stacked = []
    for c in range(CH):
        packed = jnp.zeros((8, LANES), jnp.float32)
        for k in range(planes):
            x = turn(jnp.where(sub < 4, tall[0, c, k], tall[1, c, k]), 8 * k + 4, 1)
            packed = jnp.where(within(lane, 8 * k, 8), x, packed)
        stacked.append(packed)
    ends = across(jnp.concatenate(stacked, axis=0))
    out = []
    for c in range(CH):
        packed = jnp.zeros((8, LANES), jnp.float32)
        for k in range(planes):
            x = turn(ends[k * 8 : k * 8 + 8], 4 * k - (8 * c + 2), 1)
            packed = jnp.where(within(lane, 4 * k, 4), x, packed)
        out.append(packed)
    return out


def ends_kernel(
    halves, state_in, low, high, state, ends_base, ends_sec, inner,
    tall, tile_fk, tile_w, tile_acc, packed,
):
    del state_in
    planes, rows = tall.shape[2] - 1, state.shape[2] - 2 * PAD
    every = planes + 1
    half = lax.axis_index("ij")
    low_wall, high_wall = half == 0, half == halves - 1
    low_flag, high_flag = jnp.where(low_wall, 1, 0), jnp.where(high_wall, 1, 0)
    sub, lane = rows_of((8, LANES)), lanes_of((8, LANES))
    top = PAD + rows

    for c in range(CH):
        for k in range(every):
            tall[0, c, k, 4:8] = state[c, k, PAD : PAD + 4]
            tall[1, c, k, 0:4] = state[c, k, top - 4 : top]

    @pl.when(low_wall)
    def _():
        for c in range(CH):
            for k in range(every):
                for n in range(2):
                    x = state[c, k, PAD + n : PAD + n + 1]
                    tall[0, c, k, 3 - n : 4 - n] = -x if 1 <= c <= 3 and k < planes else x

    @pl.when(jnp.logical_not(low_wall))
    def _():
        for c in range(CH):
            for k in range(every):
                tall[0, c, k, 0:4] = low[c, 4 * k : 4 * k + 4]

    @pl.when(high_wall)
    def _():
        for c in range(CH):
            for k in range(every):
                for n in range(2):
                    tall[1, c, k, 4 + n : 5 + n] = state[c, k, top - 1 - n : top - n]

    @pl.when(jnp.logical_not(high_wall))
    def _():
        for c in range(CH):
            for k in range(every):
                tall[1, c, k, 4:8] = high[c, 4 * k : 4 * k + 4]

    for c, x in enumerate(pack_ends(tall, every)):
        ends_base[c] = x
    for c in range(CH):
        state[c, planes, PAD - 4 : PAD] = tall[0, c, planes, 0:4]
        state[c, planes, top : top + 4] = tall[1, c, planes, 4:8]
    mets = [metric_terms([tall[s, c, planes] for c in range(CH)]) for s in range(2)]

    def done(c, s, k, x):
        tall[s, c, k] = x
        if s == 0:
            sign = -1.0 if 1 <= c <= 3 else 1.0
            wall = sign * jnp.where(sub == 2, turn(x, -3, 0), turn(x, -1, 0))
            x = jnp.where((sub < 4) & (low_flag == 1), wall, x)
        else:
            wall = jnp.where(sub == 4, turn(x, 1, 0), turn(x, 3, 0))
            x = jnp.where((sub >= 4) & (high_flag == 1), wall, x)
        start = PAD - 2 if s == 0 else top - 2
        state[c, every + k, start : start + 4] = x[2:6]

    tile_stage(
        planes, lambda c, s, k: tall[s, c, k], mets, lambda *_: along(0), along(1),
        (tile_fk, tile_w, tile_acc), done,
    )
    for c, x in enumerate(pack_ends(tall, planes)):
        ends_sec[c] = x

    if rows < LANES:
        packed[...] = jnp.zeros(packed.shape, jnp.float32)

    def pack(n):
        at = pl.ds(n + PAD, 8)
        for c in range(CH):
            packs = turn(state[c, planes, at], 12 * planes + 6, 1)
            for k in range(planes):
                x = turn(state[c, every + k, at], 12 * k + 6, 1)
                packs = jnp.where(within(lane, 12 * k, 12), x, packs)
            packed[c, pl.ds(n, 8)] = packs

    chunks(rows // 8, pack, unroll=2)
    for c in range(CH):
        inner[c] = packed[c].T[0 : inner.shape[1]]


def second_kernel(state_in, after, state, mets, fi, w, fk, acc):
    del state_in, after
    planes, rows = fi.shape[1], fi.shape[2] - 2 * PAD

    def get(c, k, r):
        return state[c, planes + 1 + k, pl.ds(r, 8)]

    def fluxes(n):
        at = pl.ds(n, 8)
        for j, x in enumerate(metric_terms([state[c, planes, at] for c in range(CH)])):
            mets[j, at] = x
        flux_chunk(get, mets, fi, w, fk, acc, n)

    def emit(c, k, r, val):
        at = pl.ds(r, 8)
        state[c, k, at] = 0.5 * (state[c, k, at] + (get(c, k, r) + val))

    chunks(rows // 8 + 2, fluxes)
    chunks(rows // 8, lambda n: sum_chunk(mets, fi, w, fk, acc, n + PAD, emit))


def beyond(packed, f, k, rows):
    base = 28 * f + 4 * k
    low = roll_by(packed, LANES - 2 - base)
    top = rows % LANES
    high = low if top == 0 else roll_by(packed, top - 2 - base)
    lane = lanes_of(packed.shape)

    def at(x, o):
        if o < 0:
            x = jnp.where(lane >= LANES + o, low, x)
        else:
            x = jnp.where(within(lane, top, o), high, x)
        return turn(x, -o, 1)

    return at


def last_kernel(
    halves, rows, planes, own, ends_base, ends_sec, inner, got, out,
    next_dens, next_mom, next_en,
    base, sec, fk, ws, acc, turned, back, full, sems,
):
    half = lax.axis_index("ij")
    low_wall, high_wall = half == 0, half == halves - 1
    sub, lane = rows_of((8, LANES)), lanes_of((8, LANES))

    def mix(f, mine, others):
        return jnp.where((sub < 4) == (f == 1), mine, others)

    others = [jnp.zeros((8, LANES), jnp.float32)] * CH
    for k in range(planes + 1):
        start = DEPTH * k * PASSED
        for f in range(2):

            def ghost(row):
                x = got[pl.ds(start + row, 8, stride=PASSED)]
                return x if f == 1 else turn(x, 4, 0)

            arrived = ghost(2 * CH)
            to = 28 * f + 4 * k
            for c in range(CH):
                base[c, f, k] = mix(f, own[c, k * 8 : k * 8 + 8], ghost(f * CH + c))
                moved = turn(arrived, to - 4 * CH * f - 4 * c, 1)
                others[c] = jnp.where(within(lane, to, 4), moved, others[c])

    low_lanes = lane < 28
    twice = [jnp.where(low_lanes, ends_base[c], turn(ends_base[c], 28, 1)) for c in range(CH)]
    ends = [jnp.where(low_lanes == (sub >= 4), twice[c], others[c]) for c in range(CH)]
    slot = jnp.where(low_lanes, lane, lane - 28)

    def spread(x):
        y = x
        for k in range(planes):
            y = jnp.where(within(slot, 4 * k, 4), turn(x, 4 * (k - planes), 1), y)
        return y

    vax, vay, vbx, vby, niv, _, cw, _ = [spread(x) for x in metric_terms(ends)]
    wrapped = [spread(x) for x in metric_terms(twice)[2:4]]

    def keep(c, f, k, val):
        sec[c, f, k] = val

    def stage(held, ends, gx, gy):
        mets = [metric_terms([held[c, f, planes] for c in range(CH)]) for f in range(2)]
        w, p, h = point(ends)
        rims = (flux(ends, w, p, h, gx, gy), w)
        tile_stage(
            planes,
            lambda c, f, k: held[c, f, k],
            mets,
            lambda kind, c, f, k: beyond(rims[kind][c], f, k, rows),
            along(0),
            (fk, ws, acc),
            keep,
        )

    stage(base, ends, vax, vay)

    def move(k, source):
        for c in range(CH):
            at = 12 * k
            mine = jnp.where(sub < 4, inner[c, at : at + 8], inner[c, at + 4 : at + 12])
            for f in range(2):
                sec[c, f, k] = mix(f, mine, turn(source[c, f, k], 2 if f == 1 else -2, 0))

    for k in range(planes):
        move(k, sec)
    move(planes, base)

    def shifted(x):
        return jnp.where(low_lanes, turn(x, -2, 0), turn(x, 2, 0))

    w1, p1, h1 = point(ends)
    w0, p0, h0 = point(twice)
    new, old = flux(ends, w1, p1, h1, vbx, vby), flux(twice, w0, p0, h0, *wrapped)
    at_j = along(0)
    touched = within(sub, jnp.where(low_lanes, 4, 2), 2)
    second = []
    for c in range(CH):
        add = niv * slope(new[c] - old[c], at_j)
        if c > 0:
            add = add + cw * curve(w1[c - 1] - w0[c - 1], at_j)
        x = jnp.where(low_lanes, ends_sec[c], turn(ends_sec[c], 28, 1))
        second.append(shifted(x + jnp.where(touched, add, 0.0)))
    walled = low_wall | high_wall

    for k in range(planes):
        for f in range(2):
            to = 28 * f + 4 * k
            first = jnp.where(walled, jnp.where(low_wall, to, to + 2), -8)
            shift = jnp.where(low_wall, (to - 1) % LANES, (to + 3 - rows) % LANES)
            next_shift = jnp.where(low_wall, (to + 1) % LANES, (to + 5 - rows) % LANES)
            for c in range(CH):
                x = sec[c, f, k]
                one, two = pltpu.roll(x, shift, 1), pltpu.roll(x, next_shift, 1)
                x = jnp.where(lane == first, one, two)
                if 1 <= c <= 3:
                    x = jnp.where(low_wall, -1.0, 1.0) * x
                second[c] = jnp.where(within(lane, first, 2), x, second[c])
    stage(sec, second, shifted(vax), shifted(vay))

    per = LANES // 8

    for k in range(planes):
        for c in range(CH):
            x = jnp.where(sub < 4, turn(sec[c, 1, k], -2, 0), turn(sec[c, 0, k], 2, 0))
            at = (c * planes + k) * 8
            turned[at : at + 8] = 0.5 * (own[c, k * 8 : k * 8 + 8] + x)
    for n in range(turned.shape[0] // LANES):
        back[n] = turned[n * LANES : (n + 1) * LANES].T
    inside = within(lane, 4, LANES - 8)
    size = max(8, rows // PIECES)

    def leave(start):
        at = pl.ds(start, size)
        targets = [next_dens.at[0, :, at], next_en.at[0, :, at], next_mom.at[0, :, :, at]]
        sources = [full.at[0, :, at], full.at[4, :, at], full.at[1:4, :, at]]
        first = 3 * (start // size)
        return [
            pltpu.make_async_copy(src, dst, sems.at[first + n])
            for n, (src, dst) in enumerate(zip(sources, targets))
        ]

    def merge(r):
        at = pl.ds(r, 8)
        for c in range(CH):
            for k in range(planes):
                index = c * planes + k
                moved = turn(back[index // per, at], LANES - 4 - 8 * (index % per), 1)
                full[c, k, at] = jnp.where(inside, out[c, k, pl.ds(r + PAD, 8)], moved)

        @pl.when(lax.rem(r + 8, size) == 0)
        def _():
            for copy in leave(pl.multiple_of(r + 8 - size, 8)):
                copy.start()

    chunks(rows // 8, merge, unroll=2)
    for n in range(rows // size):
        wait_all(leave(n * size))


def local(mesh_shape, density, momentum, energy, metrics, volume, placed, neighbour, face, orient):
    halves = mesh_shape["ij"]
    blocks = mesh_shape["blk"]
    planes, rows = density.shape[1], density.shape[2]
    every = planes + 1
    fields = (density, momentum, energy, metrics, volume)
    neighbour, face, orient = neighbour.T, face.T, orient.T
    vmem = pl.BlockSpec(memory_space=pltpu.VMEM)
    smem = pl.BlockSpec(memory_space=pltpu.SMEM)
    hbm = pl.BlockSpec(memory_space=pltpu.HBM)
    anywhere = pl.BlockSpec(memory_space=pl.ANY)

    def call(kernel, name, outs, ins, out_specs, scratch, cost=None, alias=None):
        run = pl.pallas_call(
            kernel,
            out_shape=[
                held(x) if spec is vmem else far(x) if spec is hbm else x
                for x, spec in zip(outs, out_specs)
            ],
            in_specs=ins,
            out_specs=out_specs,
            scratch_shapes=scratch,
            compiler_params=pltpu.CompilerParams(vmem_limit_bytes=VMEM_MIB * 1024 * 1024),
            cost_estimate=cost,
            input_output_aliases=alias or {},
            name=name,
        )

        def keep(*operands):
            return run(
                *[
                    x
                    if spec not in (vmem, hbm)
                    else pltpu.with_memory_space_constraint(x, spec.memory_space)
                    for x, spec in zip(operands, ins)
                ]
            )

        return keep

    def shape(*dims):
        return jax.ShapeDtypeStruct(dims, jnp.float32)

    def held(x):
        return pltpu.VMEM(x.shape, x.dtype)

    def far(x):
        return pltpu.HBM(x.shape, x.dtype)

    def table(x):
        return pltpu.SMEM(x.shape, jnp.int32)

    def sems(count):
        return pltpu.SemaphoreType.DMA((count,))

    slots = max(FIRST + DEPTH * every, blocks)
    slots = -(-slots // blocks) * blocks
    sent, passed = shape(slots * SENT, LANES), shape(slots * PASSED, LANES)
    strip, rim = shape(CH, 64, LANES), shape(CH, 8, LANES)
    edge = shape(CH, 4 * every, LANES)
    edges = 1 if halves == 2 else 2
    square = held(shape(CH, LANES, LANES))
    tall = rows + 2 * PAD
    whole = shape(CH, every + planes, tall, LANES)
    to_send, own, state, *halo = call(
        functools.partial(cut_kernel, halves),
        "cut",
        [sent, strip, whole] + [edge] * edges,
        [hbm] * 8,
        [hbm] + [vmem] * (2 + edges),
        [
            held(sent),
            square,
            held(shape(CH * 64, LANES)),
            table(placed),
            table(face),
            table(orient),
            sems(5 * PIECES),
            sems(3),
            sems(1),
        ],
    )(*fields, placed, face, orient)

    def swap(x):
        x = x.reshape(blocks, x.shape[0] // blocks, 1, LANES)
        x = lax.all_to_all(x, "blk", 0, 0, tiled=True)
        return x.reshape(x.shape[0] * x.shape[1], LANES)

    if edges == 1:
        below = above = lax.ppermute(halo[0], "ij", [(0, 1), (1, 0)])
    else:
        below = lax.ppermute(halo[1], "ij", [(i, i + 1) for i in range(halves - 1)])
        above = lax.ppermute(halo[0], "ij", [(i + 1, i) for i in range(halves - 1)])
    got = swap(to_send)

    padded = held(shape(CH, planes, tall, LANES))
    stage = [
        held(shape(8, tall, LANES)),
        padded,
        held(shape(4, planes, tall, LANES)),
        padded,
        padded,
    ]
    work = planes * rows * LANES
    cost = pl.CostEstimate(flops=300 * work, bytes_accessed=150 * work, transcendentals=work)
    route = jax.ShapeDtypeStruct((2 * blocks,), jnp.int32)
    state, route_out = call(
        first_kernel,
        "first_section",
        [whole, route],
        [vmem] + [hbm] * 4,
        [vmem, smem],
        stage + [table(x) for x in (placed, neighbour, face, orient, placed)] + [sems(4)],
        cost,
        {0: 0},
    )(state, placed, neighbour, face, orient)
    if halves == 2:
        sources = [got, lax.ppermute(got, "ij", [(0, 1), (1, 0)])]
    else:
        sources = [lax.all_gather(got, "ij", axis=0, tiled=True)]
    tiles = held(shape(CH, 2, every, 8, LANES))
    state, ends_base, ends_sec, inner = call(
        functools.partial(ends_kernel, halves),
        "ends",
        [whole, rim, rim, shape(CH, 12 * every + 4, LANES)],
        [vmem] * 3,
        [vmem] * 4,
        [held(shape(2, CH, every, 8, LANES))] + [tiles] * 3 + [square],
        cost,
        {0: 0},
    )(state, below, above)
    (relayed,) = call(
        functools.partial(relay_kernel, halves, rows, planes, slots),
        "relay",
        [passed],
        [anywhere] * 2 + [vmem] * len(sources),
        [hbm],
        [
            held(passed),
            held(shape(slots * 16, LANES)),
            held(shape(slots * 16, LANES)),
            held(shape(slots * 2, LANES)),
            table(route),
            sems(2),
        ],
    )(route_out, ends_sec, *sources)
    ghosts = swap(relayed)
    (state,) = call(
        second_kernel,
        "second_section",
        [whole],
        [vmem, hbm],
        [vmem],
        stage,
        cost,
        {0: 0},
    )(state, relayed)
    flat = -(-CH * planes * 8 // LANES)
    return call(
        functools.partial(last_kernel, halves, rows, planes),
        "strips",
        [shape(*density.shape), shape(*momentum.shape), shape(*energy.shape)],
        [vmem] * 6,
        [hbm] * 3,
        [tiles] * 5
        + [
            held(shape(flat * LANES, LANES)),
            held(shape(flat, LANES, LANES)),
            held(shape(CH, planes, rows, LANES)),
            sems(3 * PIECES),
        ],
    )(own, ends_base, ends_sec, inner, ghosts, state)


def solution(mesh):
    return jax.shard_map(
        functools.partial(local, dict(mesh.shape)),
        mesh=mesh,
        in_specs=(
            P("blk", None, "ij", None),
            P("blk", None, None, "ij", None),
            P("blk", None, "ij", None),
            P("blk", None, "ij", None),
            P("blk", "ij", None),
            P(),
            P(),
            P(),
            P(),
        ),
        out_specs=(
            P("blk", None, "ij", None),
            P("blk", None, None, "ij", None),
            P("blk", None, "ij", None),
        ),
        check_vma=False,
    )
```

```python
import functools

import jax
import jax.numpy as jnp
from jax import lax
from jax.experimental import pallas as pl
from jax.experimental.pallas import tpu as pltpu
from jax.sharding import PartitionSpec as P

pressure_factor = 0.4
viscosity = 0.05
time_step = 0.03
unit = time_step / 12.0

LANES = 128
PAD = 8
PIECES = 4
DEPTH = 4
CH = 5
VMEM_MIB = 32
SENT = 2 * CH
PASSED = 2 * CH + 1
FIRST = 4


def turn(x, shift, axis):
    shift = shift % x.shape[axis]
    return x if shift == 0 else pltpu.roll(x, shift, axis)


def lanes_of(shape):
    return lax.broadcasted_iota(jnp.int32, shape, len(shape) - 1)


def rows_of(shape):
    return lax.broadcasted_iota(jnp.int32, shape, len(shape) - 2)


def point(f):
    rho, m1, m2, m3, e = f
    r = 1.0 / rho
    u1, u2, u3 = m1 * r, m2 * r, m3 * r
    kin = 0.5 * (m1 * u1 + m2 * u2 + m3 * u3)
    p = pressure_factor * (e - kin)
    return (u1, u2, u3, (kin + 2.0 * p) * r), p, e + p


def metric_terms(m):
    ax, ay, bx, by, v = m
    kv = viscosity * unit
    rw = kv * (ax * ax + ay * ay)
    cw = kv * (bx * bx + by * by)
    return v * ax, v * ay, v * bx, v * by, -unit / v, rw, cw, 30.0 * (rw + cw + kv)


def flux(f, w, p, h, gx, gy):
    rho, m1, m2, m3, _ = f
    u = gx * w[0] + gy * w[1]
    return (rho * u, m1 * u + gx * p, m2 * u + gy * p, m3 * u, h * u)


def flux_planes(f, w, p, h):
    u3 = w[2]
    return (f[3], f[1] * u3, f[2] * u3, f[3] * u3 + p, h * u3)


def slope(x, at):
    return 8.0 * (at(x, 1) - at(x, -1)) - (at(x, 2) - at(x, -2))


def curve(x, at):
    return 16.0 * (at(x, 1) + at(x, -1)) - (at(x, 2) + at(x, -2))


def along(axis):
    return lambda x, o: turn(x, -o, axis)


def within(lane, start, size):
    return (lane >= start) & (lane < start + size)


def roll_by(x, shift, axis=1):
    size = x.shape[axis]
    return pltpu.roll(x, lax.rem(shift + 4 * size, size), axis)


def across(x):
    if x.shape[0] < LANES:
        x = jnp.concatenate([x, jnp.zeros((LANES - x.shape[0], LANES), jnp.float32)], axis=0)
    return x.T


def loop(count, body, unroll=1):
    def step(n, _):
        body(n)
        return 0

    lax.fori_loop(0, count, step, 0, unroll=unroll)


def copy_all(pairs, sems, first=0):
    copies = [
        pltpu.make_async_copy(src, dst, sems.at[first + n]) for n, (src, dst) in enumerate(pairs)
    ]
    for copy in copies:
        copy.start()
    return copies


def state_pairs(fields, state, planes, start, size):
    dens, mom, en, met, vol = fields
    at, to = pl.ds(start, size), pl.ds(start + PAD, size)
    return [
        (dens.at[0, :, at], state.at[0, 0:planes, to]),
        (mom.at[0, :, :, at], state.at[1:4, 0:planes, to]),
        (en.at[0, :, at], state.at[4, 0:planes, to]),
        (met.at[0, :, at], state.at[0:4, planes, to]),
        (vol.at[0, at], state.at[4, planes, to]),
    ]


def arrive_in_pieces(fields, state, sems):
    planes, rows = fields[0].shape[1], fields[0].shape[2]
    size = max(8, rows // PIECES)
    for n in range(rows // size):
        copy_all(state_pairs(fields, state, planes, n * size, size), sems, 5 * n)

    def expect(start):
        @pl.when(lax.rem(start, size) == 0)
        def _():
            for n, (src, dst) in enumerate(state_pairs(fields, state, planes, start, size)):
                pltpu.make_async_copy(src, dst, sems.at[5 * (start // size) + n]).wait()

    return expect


def wait_all(copies):
    for copy in copies:
        copy.wait()


def tile_stage(planes, load, mets, shift_i, shift_j, hold, done):
    kv = viscosity * unit
    fk, ws, acc = hold

    def spread(k):
        for s in range(2):
            vax, vay, vbx, vby, niv, rw, cw, tw = mets[s]
            x = [load(c, s, k) for c in range(CH)]
            w, p, h = point(x)
            fi, fj = flux(x, w, p, h, vax, vay), flux(x, w, p, h, vbx, vby)
            for c in range(CH):
                val = niv * (slope(fi[c], shift_i(0, c, s, k)) + slope(fj[c], shift_j))
                if c > 0:
                    v = w[c - 1]
                    val = val + (
                        rw * curve(v, shift_i(1, c - 1, s, k)) + cw * curve(v, shift_j) - tw * v
                    )
                    ws[c - 1, s, k] = v
                acc[c, s, k] = x[c] + val
            for c, v in enumerate(flux_planes(x, w, p, h)):
                fk[c, s, k] = v

    def gather(k):
        at = {o: lax.rem(k + o + planes, planes) for o in (-2, -1, 0, 1, 2)}
        for s in range(2):
            for c in range(CH):
                val = acc[c, s, k] - unit * slope(0, lambda _, o: fk[c, s, at[o]])
                if c > 0:
                    val = val + kv * curve(0, lambda _, o: ws[c - 1, s, at[o]])
                done(c, s, k, val)

    loop(planes, spread, unroll=2)
    loop(planes, gather, unroll=2)


def cut_kernel(
    halves, dens, mom, en, met, vol, placed_at, face_at, orient_at, send, own, tall, state, *rest
):
    edges, rest = rest[: 1 if halves == 2 else 2], rest[1 if halves == 2 else 2 :]
    held_send, packed, strips, placed, face, orient, sems, table_sems, out_sems = rest
    tables = copy_all(
        [(placed_at, placed), (face_at, face), (orient_at, orient)], table_sems
    )
    planes, rows = dens.shape[1], dens.shape[2]
    expect = arrive_in_pieces((dens, mom, en, met, vol), state, sems)
    half = lax.axis_index("ij")
    lane = lanes_of((8, LANES))
    if rows < LANES:
        packed[...] = jnp.zeros(packed.shape, jnp.float32)
    def pack(r):
        expect(r)
        for c in range(CH):
            packs = jnp.zeros((8, LANES), jnp.float32)
            for k in range(planes + 1):
                x = turn(state[c, k, pl.ds(r + PAD, 8)], 8 * k + 4, 1)
                packs = jnp.where(within(lane, 8 * k, 8), x, packs)
            packed[c, pl.ds(r, 8)] = packs

    chunks(rows // 8, pack, unroll=2)

    def cut_ends(k):
        for c in range(CH):
            low, high = state[c, k, PAD : PAD + 4], state[c, k, PAD + rows - 4 : PAD + rows]
            tall[0, c, k, 4:8] = low
            tall[1, c, k, 0:4] = high
            if len(edges) == 1:
                edges[0][c, k * 4 : k * 4 + 4] = jnp.where(half == 0, high, low)
            else:
                edges[0][c, k * 4 : k * 4 + 4] = low
                edges[1][c, k * 4 : k * 4 + 4] = high

    for k in range(planes + 1):
        cut_ends(k)

    wait_all(tables)
    block = placed[lax.axis_index("blk")]
    row = rows_of((64, LANES))
    high_side = row % 8 < 4
    mirror = jnp.where(
        rows_of((LANES, LANES)) + lanes_of((LANES, LANES)) == rows - 1, 1.0, 0.0
    )
    flip = [jnp.where(orient[f, block] == 1, -1.0, 1.0) for f in range(2)]
    same = [jnp.where(face[f, block] == f, -1.0, 1.0) for f in range(2)]
    rising = [face[f, block] == 1 for f in range(2)]
    turned = jnp.where(high_side, flip[1], flip[0])
    facing = jnp.where(high_side, same[1], same[0])

    def orient_strip(c):
        strip = packed[c].T[0:64]
        own[c] = strip
        back = jnp.dot(
            strip,
            mirror,
            precision=lax.Precision.HIGHEST,
            preferred_element_type=jnp.float32,
        )
        moved = jnp.where(turned < 0.0, back, strip)
        sign = jnp.where(c < 2, turned, jnp.where(c < 4, facing, 1.0))
        moved = jnp.where(row >= planes * 8, moved * sign, moved)
        strips[pl.ds(pl.multiple_of(c * 64, 64), 64)] = moved

    loop(CH, orient_strip, unroll=CH)

    def put(n):
        k, e = n >> 2, n & 3
        at = (FIRST + n) * SENT
        low = k * 8 + 4 + jnp.where(rising[0], e, 3 - e)
        high = k * 8 + jnp.where(rising[1], 3 - e, e)
        held_send[pl.ds(at, CH)] = strips[pl.ds(low, CH, stride=64)]
        held_send[pl.ds(at + CH, CH)] = strips[pl.ds(high, CH, stride=64)]

    loop(DEPTH * (planes + 1), put, unroll=4)
    wait_all(copy_all([(held_send, send)], out_sems))


def relay_kernel(
    halves, rows, planes, slots, route_at, after, *rest,
):
    del after
    sources, (send, held_send, below, above, signs, route, sems) = rest[:-7], rest[-7:]
    wait_all(copy_all([(route_at, route)], sems, 1))
    blocks = route.shape[0] // 2
    per = slots // blocks
    half = lax.axis_index("ij")
    first = lax.axis_index("blk") * per - FIRST

    def pass_on(slot):
        for f in range(2):
            code = route[2 * slot + f]
            partner, side, turned = code >> 2, (code >> 1) & 1, code & 1
            sign = jnp.where(turned == 1, -1.0, 1.0)
            for i in range(per):

                def piece(offset):
                    part = jnp.clip(half + offset, 0, halves - 1)
                    part = jnp.where(turned == 1, halves - 1 - part, part)
                    at = (partner * per + i) * SENT + side * CH
                    if len(sources) == 1:
                        return sources[0][pl.ds(part * (slots * SENT) + at, CH)]
                    mine, others = (x[pl.ds(at, CH)] for x in sources)
                    return jnp.where(part == half, mine, others)

                at = slot * per + i
                held_send[pl.ds(at * PASSED + f * CH, CH)] = piece(0)
                below[pl.ds((f * slots + at) * 8, CH)] = piece(-1)
                above[pl.ds((f * slots + at) * 8, CH)] = piece(1)
                signs[pl.ds(f * slots + at, 1)] = jnp.full((1, LANES), sign, jnp.float32)

    loop(blocks, pass_on, unroll=4)
    count = 2 * slots
    lane = lanes_of((count, LANES))
    piece_at = first + lax.rem(rows_of((count, LANES)), per)
    is_field = (piece_at >= 0) & (piece_at < DEPTH * planes)
    sign = signs[...]
    low_end, high_end = half == 0, half == halves - 1
    low_sign = jnp.where(is_field, -sign, 1.0)
    high_sign = jnp.where(is_field, sign, 1.0)
    ends = jnp.zeros((count, LANES), jnp.float32)
    for c in range(CH):
        low, high = below[pl.ds(c, count, stride=8)], above[pl.ds(c, count, stride=8)]
        at = 4 * c
        low_wall = jnp.where(lane == at, turn(low, at - 1, 1), turn(low, at + 1, 1))
        high_wall = jnp.where(
            lane == at + 2, turn(high, at + 3 - rows, 1), turn(high, at + 5 - rows, 1)
        )
        if 1 <= c <= 3:
            low_wall, high_wall = low_sign * low_wall, high_sign * high_wall
        low = jnp.where(low_end, low_wall, turn(low, at + 2 - rows, 1))
        high = jnp.where(high_end, high_wall, turn(high, at + 2, 1))
        ends = jnp.where(within(lane, at, 2), low, jnp.where(within(lane, at + 2, 2), high, ends))
    held_send[pl.ds(2 * CH, slots, stride=PASSED)] = ends[0:slots] + turn(
        ends[slots:], 4 * CH, 1
    )
    wait_all(copy_all([(held_send, send)], sems))


def flux_chunk(get, mets, fi, w, fk, acc, r):
    rows = pl.ds(r, 8)
    vax, vay, vbx, vby, niv, rw, cw, tw = [mets[j, rows] for j in range(8)]
    at_j = along(1)
    for k in range(fi.shape[1]):
        f = [get(c, k, r) for c in range(CH)]
        wk, p, h = point(f)
        for c, x in enumerate(flux(f, wk, p, h, vax, vay)):
            fi[c, k, rows] = x
        for c in range(4):
            w[c, k, rows] = wk[c]
        fj = flux(f, wk, p, h, vbx, vby)
        for c in range(CH):
            val = niv * slope(fj[c], at_j)
            if c > 0:
                val = val + (cw * curve(wk[c - 1], at_j) - tw * wk[c - 1])
            acc[c, k, rows] = val
        for c, x in enumerate(flux_planes(f, wk, p, h)):
            fk[c, k, rows] = x


def sum_chunk(mets, fi, w, fk, acc, r, emit):
    planes = fi.shape[1]
    kv = viscosity * unit
    rows = pl.ds(r, 8)
    niv, rw = mets[4, rows], mets[5, rows]
    for c in range(CH):
        t = [fk[c, k, rows] for k in range(planes)]
        x = [w[c - 1, k, rows] for k in range(planes)] if c > 0 else None
        for k in range(planes):

            def near(v, o):
                return v[(k + o) % planes]

            def at_i(v, o):
                return v[pl.ds(r + o, 8)]

            val = acc[c, k, rows] + niv * slope(fi.at[c, k], at_i) - unit * slope(t, near)
            if c > 0:
                val = val + (rw * curve(w.at[c - 1, k], at_i) + kv * curve(x, near))
            emit(c, k, r, val)


def chunks(count, body, unroll=1):
    def step(n, _):
        body(pl.multiple_of(n * 8, 8))
        return 0

    lax.fori_loop(0, count, step, 0, unroll=unroll)


def first_kernel(
    state_in, placed_at, neighbour_at, face_at, orient_at, state, route,
    mets, fi, w, fk, acc, placed, neighbour, face, orient, where_is, sems,
):
    del state_in
    planes, rows = fi.shape[1], fi.shape[2] - 2 * PAD
    pairs = zip((placed_at, neighbour_at, face_at, orient_at), (placed, neighbour, face, orient))
    tables = copy_all(list(pairs), sems)
    count = rows // 8
    blocks = placed.shape[0]
    share = -(-blocks // count)

    def slots(n):
        return [jnp.minimum((n // 8) * share + i, blocks - 1) for i in range(share)]

    def get(c, k, r):
        return state[c, k, pl.ds(r, 8)]

    def fluxes(n):
        at = pl.ds(n + PAD, 8)
        for j, x in enumerate(metric_terms([state[c, planes, at] for c in range(CH)])):
            mets[j, at] = x
        flux_chunk(get, mets, fi, w, fk, acc, n + PAD)

    def emit(c, k, r, val):
        state[c, k, pl.ds(r, 8)] = get(c, k, r) + val

    def sums(n):
        for slot in slots(n):
            block = placed[slot]
            for f in range(2):
                partner = where_is[neighbour[f, block]]
                route[2 * slot + f] = partner * 4 + face[f, block] * 2 + orient[f, block]
        sum_chunk(mets, fi, w, fk, acc, n + PAD, emit)

    def note(slot):
        where_is[placed[slot]] = slot

    chunks(count, fluxes, unroll=2)
    wait_all(tables)
    loop(blocks, note, unroll=8)
    chunks(count, sums, unroll=2)


def pack_ends(tall, planes):
    sub, lane = rows_of((8, LANES)), lanes_of((8, LANES))
    stacked = []
    for c in range(CH):
        packed = jnp.zeros((8, LANES), jnp.float32)
        for k in range(planes):
            x = turn(jnp.where(sub < 4, tall[0, c, k], tall[1, c, k]), 8 * k + 4, 1)
            packed = jnp.where(within(lane, 8 * k, 8), x, packed)
        stacked.append(packed)
    ends = across(jnp.concatenate(stacked, axis=0))
    out = []
    for c in range(CH):
        packed = jnp.zeros((8, LANES), jnp.float32)
        for k in range(planes):
            x = turn(ends[k * 8 : k * 8 + 8], 4 * k - (8 * c + 2), 1)
            packed = jnp.where(within(lane, 4 * k, 4), x, packed)
        out.append(packed)
    return out


def ends_kernel(
    halves, state_in, tall_in, low, high, state, tall, ends_base, ends_sec, inner,
    tile_fk, tile_w, tile_acc, packed,
):
    del state_in, tall_in
    planes, rows = tall.shape[2] - 1, state.shape[2] - 2 * PAD
    every = planes + 1
    half = lax.axis_index("ij")
    low_wall, high_wall = half == 0, half == halves - 1
    low_flag, high_flag = jnp.where(low_wall, 1, 0), jnp.where(high_wall, 1, 0)
    sub, lane = rows_of((8, LANES)), lanes_of((8, LANES))
    top = PAD + rows

    @pl.when(low_wall)
    def _():
        for c in range(CH):
            for k in range(every):
                for n in range(2):
                    x = tall[0, c, k, 4 + n : 5 + n]
                    tall[0, c, k, 3 - n : 4 - n] = -x if 1 <= c <= 3 and k < planes else x

    @pl.when(jnp.logical_not(low_wall))
    def _():
        for c in range(CH):
            for k in range(every):
                tall[0, c, k, 0:4] = low[c, 4 * k : 4 * k + 4]

    @pl.when(high_wall)
    def _():
        for c in range(CH):
            for k in range(every):
                for n in range(2):
                    tall[1, c, k, 4 + n : 5 + n] = tall[1, c, k, 3 - n : 4 - n]

    @pl.when(jnp.logical_not(high_wall))
    def _():
        for c in range(CH):
            for k in range(every):
                tall[1, c, k, 4:8] = high[c, 4 * k : 4 * k + 4]

    for c, x in enumerate(pack_ends(tall, every)):
        ends_base[c] = x
    for c in range(CH):
        state[c, planes, PAD - 4 : PAD] = tall[0, c, planes, 0:4]
        state[c, planes, top : top + 4] = tall[1, c, planes, 4:8]
    mets = [metric_terms([tall[s, c, planes] for c in range(CH)]) for s in range(2)]

    def done(c, s, k, x):
        tall[s, c, k] = x
        if s == 0:
            sign = -1.0 if 1 <= c <= 3 else 1.0
            wall = sign * jnp.where(sub == 2, turn(x, -3, 0), turn(x, -1, 0))
            x = jnp.where((sub < 4) & (low_flag == 1), wall, x)
        else:
            wall = jnp.where(sub == 4, turn(x, 1, 0), turn(x, 3, 0))
            x = jnp.where((sub >= 4) & (high_flag == 1), wall, x)
        start = PAD - 2 if s == 0 else top - 2
        state[c, k, start : start + 4] = x[2:6]

    tile_stage(
        planes, lambda c, s, k: tall[s, c, k], mets, lambda *_: along(0), along(1),
        (tile_fk, tile_w, tile_acc), done,
    )
    for c, x in enumerate(pack_ends(tall, planes)):
        ends_sec[c] = x

    if rows < LANES:
        packed[...] = jnp.zeros(packed.shape, jnp.float32)

    def pack(n):
        at = pl.ds(n + PAD, 8)
        for c in range(CH):
            packs = turn(state[c, planes, at], 12 * planes + 6, 1)
            for k in range(planes):
                x = turn(state[c, k, at], 12 * k + 6, 1)
                packs = jnp.where(within(lane, 12 * k, 12), x, packs)
            packed[c, pl.ds(n, 8)] = packs

    chunks(rows // 8, pack, unroll=2)
    for c in range(CH):
        inner[c] = packed[c].T[0 : inner.shape[1]]


def second_kernel(
    state_in, after, dens, mom, en, state, fields, mets, fi, w, fk, acc, sems
):
    del state_in, after
    planes, rows = fields.shape[1:3]
    pairs = [(dens.at[0], fields.at[0]), (mom.at[0], fields.at[1:4]), (en.at[0], fields.at[4])]
    copies = copy_all(pairs, sems)

    def get(c, k, r):
        return state[c, k, pl.ds(r, 8)]

    def fluxes(n):
        at = pl.ds(n, 8)
        for j, x in enumerate(metric_terms([state[c, planes, at] for c in range(CH)])):
            mets[j, at] = x
        flux_chunk(get, mets, fi, w, fk, acc, n)

    def emit(c, k, r, val):
        x = 0.5 * (fields[c, k, pl.ds(r - PAD, 8)] + (get(c, k, r) + val))
        state[c, k, pl.ds(r, 8)] = x

    chunks(rows // 8 + 2, fluxes, unroll=2)
    wait_all(copies)
    chunks(rows // 8, lambda n: sum_chunk(mets, fi, w, fk, acc, n + PAD, emit), unroll=2)


def beyond(packed, f, k, rows):
    base = 28 * f + 4 * k
    low = roll_by(packed, LANES - 2 - base)
    top = rows % LANES
    high = low if top == 0 else roll_by(packed, top - 2 - base)
    lane = lanes_of(packed.shape)

    def at(x, o):
        if o < 0:
            x = jnp.where(lane >= LANES + o, low, x)
        else:
            x = jnp.where(within(lane, top, o), high, x)
        return turn(x, -o, 1)

    return at


def last_kernel(
    halves, rows, planes, own, ends_base, ends_sec, inner, got, out,
    next_dens, next_mom, next_en,
    base, sec, fk, ws, acc, turned, back, full, sems,
):
    half = lax.axis_index("ij")
    low_wall, high_wall = half == 0, half == halves - 1
    sub, lane = rows_of((8, LANES)), lanes_of((8, LANES))

    def mix(f, mine, others):
        return jnp.where((sub < 4) == (f == 1), mine, others)

    others = [jnp.zeros((8, LANES), jnp.float32)] * CH
    for k in range(planes + 1):
        start = DEPTH * k * PASSED
        for f in range(2):

            def ghost(row):
                x = got[pl.ds(start + row, 8, stride=PASSED)]
                return x if f == 1 else turn(x, 4, 0)

            arrived = ghost(2 * CH)
            to = 28 * f + 4 * k
            for c in range(CH):
                base[c, f, k] = mix(f, own[c, k * 8 : k * 8 + 8], ghost(f * CH + c))
                moved = turn(arrived, to - 4 * CH * f - 4 * c, 1)
                others[c] = jnp.where(within(lane, to, 4), moved, others[c])

    low_lanes = lane < 28
    twice = [jnp.where(low_lanes, ends_base[c], turn(ends_base[c], 28, 1)) for c in range(CH)]
    ends = [jnp.where(low_lanes == (sub >= 4), twice[c], others[c]) for c in range(CH)]
    slot = jnp.where(low_lanes, lane, lane - 28)

    def spread(x):
        y = x
        for k in range(planes):
            y = jnp.where(within(slot, 4 * k, 4), turn(x, 4 * (k - planes), 1), y)
        return y

    vax, vay, vbx, vby, niv, _, cw, _ = [spread(x) for x in metric_terms(ends)]
    wrapped = [spread(x) for x in metric_terms(twice)[2:4]]

    def keep(c, f, k, val):
        sec[c, f, k] = val

    def stage(held, ends, gx, gy):
        mets = [metric_terms([held[c, f, planes] for c in range(CH)]) for f in range(2)]
        w, p, h = point(ends)
        rims = (flux(ends, w, p, h, gx, gy), w)
        tile_stage(
            planes,
            lambda c, f, k: held[c, f, k],
            mets,
            lambda kind, c, f, k: beyond(rims[kind][c], f, k, rows),
            along(0),
            (fk, ws, acc),
            keep,
        )

    stage(base, ends, vax, vay)

    def move(k, source):
        for c in range(CH):
            at = 12 * k
            mine = jnp.where(sub < 4, inner[c, at : at + 8], inner[c, at + 4 : at + 12])
            for f in range(2):
                sec[c, f, k] = mix(f, mine, turn(source[c, f, k], 2 if f == 1 else -2, 0))

    for k in range(planes):
        move(k, sec)
    move(planes, base)

    def shifted(x):
        return jnp.where(low_lanes, turn(x, -2, 0), turn(x, 2, 0))

    w1, p1, h1 = point(ends)
    w0, p0, h0 = point(twice)
    new, old = flux(ends, w1, p1, h1, vbx, vby), flux(twice, w0, p0, h0, *wrapped)
    at_j = along(0)
    touched = within(sub, jnp.where(low_lanes, 4, 2), 2)
    second = []
    for c in range(CH):
        add = niv * slope(new[c] - old[c], at_j)
        if c > 0:
            add = add + cw * curve(w1[c - 1] - w0[c - 1], at_j)
        x = jnp.where(low_lanes, ends_sec[c], turn(ends_sec[c], 28, 1))
        second.append(shifted(x + jnp.where(touched, add, 0.0)))
    walled = low_wall | high_wall

    for k in range(planes):
        for f in range(2):
            to = 28 * f + 4 * k
            first = jnp.where(walled, jnp.where(low_wall, to, to + 2), -8)
            shift = jnp.where(low_wall, (to - 1) % LANES, (to + 3 - rows) % LANES)
            next_shift = jnp.where(low_wall, (to + 1) % LANES, (to + 5 - rows) % LANES)
            for c in range(CH):
                x = sec[c, f, k]
                one, two = pltpu.roll(x, shift, 1), pltpu.roll(x, next_shift, 1)
                x = jnp.where(lane == first, one, two)
                if 1 <= c <= 3:
                    x = jnp.where(low_wall, -1.0, 1.0) * x
                second[c] = jnp.where(within(lane, first, 2), x, second[c])
    stage(sec, second, shifted(vax), shifted(vay))

    per = LANES // 8

    for k in range(planes):
        for c in range(CH):
            x = jnp.where(sub < 4, turn(sec[c, 1, k], -2, 0), turn(sec[c, 0, k], 2, 0))
            at = (c * planes + k) * 8
            turned[at : at + 8] = 0.5 * (own[c, k * 8 : k * 8 + 8] + x)
    for n in range(turned.shape[0] // LANES):
        back[n] = turned[n * LANES : (n + 1) * LANES].T
    inside = within(lane, 4, LANES - 8)
    size = max(8, rows // PIECES)

    def leave(start):
        at = pl.ds(start, size)
        targets = [next_dens.at[0, :, at], next_en.at[0, :, at], next_mom.at[0, :, :, at]]
        sources = [full.at[0, :, at], full.at[4, :, at], full.at[1:4, :, at]]
        first = 3 * (start // size)
        return [
            pltpu.make_async_copy(src, dst, sems.at[first + n])
            for n, (src, dst) in enumerate(zip(sources, targets))
        ]

    def merge(r):
        at = pl.ds(r, 8)
        for c in range(CH):
            for k in range(planes):
                index = c * planes + k
                moved = turn(back[index // per, at], LANES - 4 - 8 * (index % per), 1)
                full[c, k, at] = jnp.where(inside, out[c, k, pl.ds(r + PAD, 8)], moved)

        @pl.when(lax.rem(r + 8, size) == 0)
        def _():
            for copy in leave(pl.multiple_of(r + 8 - size, 8)):
                copy.start()

    chunks(rows // 8, merge, unroll=2)
    for n in range(rows // size):
        wait_all(leave(n * size))


def local(mesh_shape, density, momentum, energy, metrics, volume, placed, neighbour, face, orient):
    halves = mesh_shape["ij"]
    blocks = mesh_shape["blk"]
    planes, rows = density.shape[1], density.shape[2]
    every = planes + 1
    fields = (density, momentum, energy, metrics, volume)
    neighbour, face, orient = neighbour.T, face.T, orient.T
    vmem = pl.BlockSpec(memory_space=pltpu.VMEM)
    smem = pl.BlockSpec(memory_space=pltpu.SMEM)
    hbm = pl.BlockSpec(memory_space=pltpu.HBM)
    anywhere = pl.BlockSpec(memory_space=pl.ANY)

    def call(kernel, name, outs, ins, out_specs, scratch, cost=None, alias=None):
        run = pl.pallas_call(
            kernel,
            out_shape=[
                held(x) if spec is vmem else far(x) if spec is hbm else x
                for x, spec in zip(outs, out_specs)
            ],
            in_specs=ins,
            out_specs=out_specs,
            scratch_shapes=scratch,
            compiler_params=pltpu.CompilerParams(vmem_limit_bytes=VMEM_MIB * 1024 * 1024),
            cost_estimate=cost,
            input_output_aliases=alias or {},
            name=name,
        )

        def keep(*operands):
            return run(
                *[
                    x
                    if spec not in (vmem, hbm)
                    else pltpu.with_memory_space_constraint(x, spec.memory_space)
                    for x, spec in zip(operands, ins)
                ]
            )

        return keep

    def shape(*dims):
        return jax.ShapeDtypeStruct(dims, jnp.float32)

    def held(x):
        return pltpu.VMEM(x.shape, x.dtype)

    def far(x):
        return pltpu.HBM(x.shape, x.dtype)

    def table(x):
        return pltpu.SMEM(x.shape, jnp.int32)

    def sems(count):
        return pltpu.SemaphoreType.DMA((count,))

    slots = max(FIRST + DEPTH * every, blocks)
    slots = -(-slots // blocks) * blocks
    sent, passed = shape(slots * SENT, LANES), shape(slots * PASSED, LANES)
    strip, rim = shape(CH, 64, LANES), shape(CH, 8, LANES)
    edge = shape(CH, 4 * every, LANES)
    edges = 1 if halves == 2 else 2
    square = held(shape(CH, LANES, LANES))
    tall = rows + 2 * PAD
    whole = shape(CH, every, tall, LANES)
    rows_about = shape(2, CH, every, 8, LANES)
    to_send, own, about, state, *halo = call(
        functools.partial(cut_kernel, halves),
        "cut",
        [sent, strip, rows_about, whole] + [edge] * edges,
        [hbm] * 8,
        [hbm] + [vmem] * (3 + edges),
        [
            held(sent),
            square,
            held(shape(CH * 64, LANES)),
            table(placed),
            table(face),
            table(orient),
            sems(5 * PIECES),
            sems(3),
            sems(1),
        ],
    )(*fields, placed, face, orient)

    def swap(x):
        x = x.reshape(blocks, x.shape[0] // blocks, 1, LANES)
        x = lax.all_to_all(x, "blk", 0, 0, tiled=True)
        return x.reshape(x.shape[0] * x.shape[1], LANES)

    if edges == 1:
        below = above = lax.ppermute(halo[0], "ij", [(0, 1), (1, 0)])
    else:
        below = lax.ppermute(halo[1], "ij", [(i, i + 1) for i in range(halves - 1)])
        above = lax.ppermute(halo[0], "ij", [(i + 1, i) for i in range(halves - 1)])
    got = swap(to_send)

    padded = held(shape(CH, planes, tall, LANES))
    stage = [
        held(shape(8, tall, LANES)),
        padded,
        held(shape(4, planes, tall, LANES)),
        padded,
        padded,
    ]
    work = planes * rows * LANES
    cost = pl.CostEstimate(flops=300 * work, bytes_accessed=150 * work, transcendentals=work)
    route = jax.ShapeDtypeStruct((2 * blocks,), jnp.int32)
    state, route_out = call(
        first_kernel,
        "first_section",
        [whole, route],
        [vmem] + [hbm] * 4,
        [vmem, smem],
        stage + [table(x) for x in (placed, neighbour, face, orient, placed)] + [sems(4)],
        cost,
        {0: 0},
    )(state, placed, neighbour, face, orient)
    got, route_out, below, above = lax.optimization_barrier((got, route_out, below, above))
    if halves == 2:
        sources = [got, lax.ppermute(got, "ij", [(0, 1), (1, 0)])]
    else:
        sources = [lax.all_gather(got, "ij", axis=0, tiled=True)]
    tiles = held(shape(CH, 2, every, 8, LANES))
    state, _, ends_base, ends_sec, inner = call(
        functools.partial(ends_kernel, halves),
        "ends",
        [whole, rows_about, rim, rim, shape(CH, 12 * every + 4, LANES)],
        [vmem] * 4,
        [vmem] * 5,
        [tiles] * 3 + [square],
        cost,
        {0: 0, 1: 1},
    )(state, about, below, above)
    (relayed,) = call(
        functools.partial(relay_kernel, halves, rows, planes, slots),
        "relay",
        [passed],
        [anywhere] * 2 + [vmem] * len(sources),
        [hbm],
        [
            held(passed),
            held(shape(slots * 16, LANES)),
            held(shape(slots * 16, LANES)),
            held(shape(slots * 2, LANES)),
            table(route),
            sems(2),
        ],
    )(route_out, ends_sec, *sources)
    ghosts = swap(relayed)
    (state,) = call(
        second_kernel,
        "second_section",
        [whole],
        [vmem] + [hbm] * 4,
        [vmem],
        [held(shape(CH, planes, rows, LANES))] + stage + [sems(3)],
        cost,
        {0: 0},
    )(state, relayed, density, momentum, energy)
    flat = -(-CH * planes * 8 // LANES)
    return call(
        functools.partial(last_kernel, halves, rows, planes),
        "strips",
        [shape(*density.shape), shape(*momentum.shape), shape(*energy.shape)],
        [vmem] * 6,
        [hbm] * 3,
        [tiles] * 5
        + [
            held(shape(flat * LANES, LANES)),
            held(shape(flat, LANES, LANES)),
            held(shape(CH, planes, rows, LANES)),
            sems(3 * PIECES),
        ],
    )(own, ends_base, ends_sec, inner, ghosts, state)


def solution(mesh):
    return jax.shard_map(
        functools.partial(local, dict(mesh.shape)),
        mesh=mesh,
        in_specs=(
            P("blk", None, "ij", None),
            P("blk", None, None, "ij", None),
            P("blk", None, "ij", None),
            P("blk", None, "ij", None),
            P("blk", "ij", None),
            P(),
            P(),
            P(),
            P(),
        ),
        out_specs=(
            P("blk", None, "ij", None),
            P("blk", None, None, "ij", None),
            P("blk", None, "ij", None),
        ),
        check_vma=False,
    )
```

```python
import functools

import jax
import jax.numpy as jnp
from jax import lax
from jax.experimental import pallas as pl
from jax.experimental.pallas import tpu as pltpu
from jax.sharding import PartitionSpec as P

pressure_factor = 0.4
viscosity = 0.05
time_step = 0.03
unit = time_step / 12.0

LANES = 128
PAD = 8
PIECES = 4
DEPTH = 4
CH = 5
VMEM_MIB = 32
SENT = 2 * CH
PASSED = 2 * CH + 1
FIRST = 4


def turn(x, shift, axis):
    shift = shift % x.shape[axis]
    return x if shift == 0 else pltpu.roll(x, shift, axis)


def lanes_of(shape):
    return lax.broadcasted_iota(jnp.int32, shape, len(shape) - 1)


def rows_of(shape):
    return lax.broadcasted_iota(jnp.int32, shape, len(shape) - 2)


def point(f):
    rho, m1, m2, m3, e = f
    r = 1.0 / rho
    u1, u2, u3 = m1 * r, m2 * r, m3 * r
    kin = 0.5 * (m1 * u1 + m2 * u2 + m3 * u3)
    p = pressure_factor * (e - kin)
    return (u1, u2, u3, (kin + 2.0 * p) * r), p, e + p


def metric_terms(m):
    ax, ay, bx, by, v = m
    kv = viscosity * unit
    rw = kv * (ax * ax + ay * ay)
    cw = kv * (bx * bx + by * by)
    return v * ax, v * ay, v * bx, v * by, -unit / v, rw, cw, 30.0 * (rw + cw + kv)


def flux(f, w, p, h, gx, gy):
    rho, m1, m2, m3, _ = f
    u = gx * w[0] + gy * w[1]
    return (rho * u, m1 * u + gx * p, m2 * u + gy * p, m3 * u, h * u)


def flux_planes(f, w, p, h):
    u3 = w[2]
    return (f[3], f[1] * u3, f[2] * u3, f[3] * u3 + p, h * u3)


def slope(x, at):
    return 8.0 * (at(x, 1) - at(x, -1)) - (at(x, 2) - at(x, -2))


def curve(x, at):
    return 16.0 * (at(x, 1) + at(x, -1)) - (at(x, 2) + at(x, -2))


def along(axis):
    return lambda x, o: turn(x, -o, axis)


def within(lane, start, size):
    return (lane >= start) & (lane < start + size)


def roll_by(x, shift, axis=1):
    size = x.shape[axis]
    return pltpu.roll(x, lax.rem(shift + 4 * size, size), axis)


def across(x):
    if x.shape[0] < LANES:
        x = jnp.concatenate([x, jnp.zeros((LANES - x.shape[0], LANES), jnp.float32)], axis=0)
    return x.T


def loop(count, body, unroll=1):
    def step(n, _):
        body(n)
        return 0

    lax.fori_loop(0, count, step, 0, unroll=unroll)


def copy_all(pairs, sems, first=0):
    copies = [
        pltpu.make_async_copy(src, dst, sems.at[first + n]) for n, (src, dst) in enumerate(pairs)
    ]
    for copy in copies:
        copy.start()
    return copies


def state_pairs(fields, state, planes, start, size):
    dens, mom, en, met, vol = fields
    at, to = pl.ds(start, size), pl.ds(start + PAD, size)
    return [
        (dens.at[0, :, at], state.at[0, 0:planes, to]),
        (mom.at[0, :, :, at], state.at[1:4, 0:planes, to]),
        (en.at[0, :, at], state.at[4, 0:planes, to]),
        (met.at[0, :, at], state.at[0:4, planes, to]),
        (vol.at[0, at], state.at[4, planes, to]),
    ]


def arrive_in_pieces(fields, state, sems):
    planes, rows = fields[0].shape[1], fields[0].shape[2]
    size = max(8, rows // PIECES)
    for n in range(rows // size):
        copy_all(state_pairs(fields, state, planes, n * size, size), sems, 5 * n)

    def expect(start):
        @pl.when(lax.rem(start, size) == 0)
        def _():
            for n, (src, dst) in enumerate(state_pairs(fields, state, planes, start, size)):
                pltpu.make_async_copy(src, dst, sems.at[5 * (start // size) + n]).wait()

    return expect


def wait_all(copies):
    for copy in copies:
        copy.wait()


def tile_stage(planes, load, mets, shift_i, shift_j, hold, done):
    kv = viscosity * unit
    fk, ws, acc = hold

    def spread(k):
        for s in range(2):
            vax, vay, vbx, vby, niv, rw, cw, tw = mets[s]
            x = [load(c, s, k) for c in range(CH)]
            w, p, h = point(x)
            fi, fj = flux(x, w, p, h, vax, vay), flux(x, w, p, h, vbx, vby)
            for c in range(CH):
                val = niv * (slope(fi[c], shift_i(0, c, s, k)) + slope(fj[c], shift_j))
                if c > 0:
                    v = w[c - 1]
                    val = val + (
                        rw * curve(v, shift_i(1, c - 1, s, k)) + cw * curve(v, shift_j) - tw * v
                    )
                    ws[c - 1, s, k] = v
                acc[c, s, k] = x[c] + val
            for c, v in enumerate(flux_planes(x, w, p, h)):
                fk[c, s, k] = v

    def gather(k):
        at = {o: lax.rem(k + o + planes, planes) for o in (-2, -1, 0, 1, 2)}
        for s in range(2):
            for c in range(CH):
                val = acc[c, s, k] - unit * slope(0, lambda _, o: fk[c, s, at[o]])
                if c > 0:
                    val = val + kv * curve(0, lambda _, o: ws[c - 1, s, at[o]])
                done(c, s, k, val)

    loop(planes, spread, unroll=2)
    loop(planes, gather, unroll=2)


def cut_kernel(
    halves, dens, mom, en, met, vol, placed_at, face_at, orient_at, send, own, tall, state, *rest
):
    edges, rest = rest[: 1 if halves == 2 else 2], rest[1 if halves == 2 else 2 :]
    held_send, packed, strips, placed, face, orient, sems, table_sems, out_sems = rest
    tables = copy_all(
        [(placed_at, placed), (face_at, face), (orient_at, orient)], table_sems
    )
    planes, rows = dens.shape[1], dens.shape[2]
    expect = arrive_in_pieces((dens, mom, en, met, vol), state, sems)
    half = lax.axis_index("ij")
    lane = lanes_of((8, LANES))
    if rows < LANES:
        packed[...] = jnp.zeros(packed.shape, jnp.float32)
    def pack(r):
        expect(r)
        for c in range(CH):
            packs = jnp.zeros((8, LANES), jnp.float32)
            for k in range(planes + 1):
                x = turn(state[c, k, pl.ds(r + PAD, 8)], 8 * k + 4, 1)
                packs = jnp.where(within(lane, 8 * k, 8), x, packs)
            packed[c, pl.ds(r, 8)] = packs

    chunks(rows // 8, pack, unroll=2)

    def cut_ends(k):
        for c in range(CH):
            low, high = state[c, k, PAD : PAD + 4], state[c, k, PAD + rows - 4 : PAD + rows]
            tall[0, c, k, 4:8] = low
            tall[1, c, k, 0:4] = high
            if len(edges) == 1:
                edges[0][c, k * 4 : k * 4 + 4] = jnp.where(half == 0, high, low)
            else:
                edges[0][c, k * 4 : k * 4 + 4] = low
                edges[1][c, k * 4 : k * 4 + 4] = high

    for k in range(planes + 1):
        cut_ends(k)

    wait_all(tables)
    block = placed[lax.axis_index("blk")]
    row = rows_of((64, LANES))
    high_side = row % 8 < 4
    mirror = jnp.where(
        rows_of((LANES, LANES)) + lanes_of((LANES, LANES)) == rows - 1, 1.0, 0.0
    )
    flip = [jnp.where(orient[f, block] == 1, -1.0, 1.0) for f in range(2)]
    same = [jnp.where(face[f, block] == f, -1.0, 1.0) for f in range(2)]
    rising = [face[f, block] == 1 for f in range(2)]
    turned = jnp.where(high_side, flip[1], flip[0])
    facing = jnp.where(high_side, same[1], same[0])

    def orient_strip(c):
        strip = packed[c].T[0:64]
        own[c] = strip
        back = jnp.dot(
            strip,
            mirror,
            precision=lax.Precision.HIGHEST,
            preferred_element_type=jnp.float32,
        )
        moved = jnp.where(turned < 0.0, back, strip)
        sign = jnp.where(c < 2, turned, jnp.where(c < 4, facing, 1.0))
        moved = jnp.where(row >= planes * 8, moved * sign, moved)
        strips[pl.ds(pl.multiple_of(c * 64, 64), 64)] = moved

    loop(CH, orient_strip, unroll=CH)

    def put(n):
        k, e = n >> 2, n & 3
        at = (FIRST + n) * SENT
        low = k * 8 + 4 + jnp.where(rising[0], e, 3 - e)
        high = k * 8 + jnp.where(rising[1], 3 - e, e)
        held_send[pl.ds(at, CH)] = strips[pl.ds(low, CH, stride=64)]
        held_send[pl.ds(at + CH, CH)] = strips[pl.ds(high, CH, stride=64)]

    loop(DEPTH * (planes + 1), put, unroll=4)
    wait_all(copy_all([(held_send, send)], out_sems))


def relay_kernel(
    halves, rows, planes, devices, route_at, halo, held_got, send,
    held_send, below, above, signs, route, sems,
):
    del halo
    wait_all(copy_all([(route_at, route)], sems, 1))
    me = lax.axis_index("blk") * halves + lax.axis_index("ij")
    is_field = (me >= FIRST) & (me < FIRST + DEPTH * planes)

    def pass_on(slot):
        for f in range(2):
            code = route[2 * slot + f]
            partner, side, turned = code >> 2, (code >> 1) & 1, code & 1
            sign = jnp.where(turned == 1, -1.0, 1.0)

            def piece(h):
                h = jnp.where(turned == 1, halves - 1 - h, h)
                return held_got[pl.ds((partner * halves + h) * SENT + side * CH, CH)]

            pieces = [piece(h) for h in range(halves)]
            for half in range(halves):
                at = slot * halves + half
                held_send[pl.ds(at * PASSED + f * CH, CH)] = pieces[half]
                below[pl.ds((f * devices + at) * 8, CH)] = pieces[max(half - 1, 0)]
                above[pl.ds((f * devices + at) * 8, CH)] = pieces[min(half + 1, halves - 1)]
                signs[pl.ds(f * devices + at, 1)] = jnp.full((1, LANES), sign, jnp.float32)

    loop(devices // halves, pass_on, unroll=4)
    count = 2 * devices
    lane = lanes_of((count, LANES))
    half = rows_of((count, LANES)) % halves
    sign = signs[...]
    ends = jnp.zeros((count, LANES), jnp.float32)
    for c in range(CH):
        low, high = below[pl.ds(c, count, stride=8)], above[pl.ds(c, count, stride=8)]
        at = 4 * c
        low_wall = jnp.where(lane == at, turn(low, at - 1, 1), turn(low, at + 1, 1))
        high_wall = jnp.where(
            lane == at + 2, turn(high, at + 3 - rows, 1), turn(high, at + 5 - rows, 1)
        )
        if 1 <= c <= 3:
            low_wall = jnp.where(is_field, -sign * low_wall, low_wall)
            high_wall = jnp.where(is_field, sign * high_wall, high_wall)
        low = jnp.where(half == 0, low_wall, turn(low, at + 2 - rows, 1))
        high = jnp.where(half == halves - 1, high_wall, turn(high, at + 2, 1))
        ends = jnp.where(within(lane, at, 2), low, jnp.where(within(lane, at + 2, 2), high, ends))
    held_send[pl.ds(2 * CH, devices, stride=PASSED)] = ends[0:devices] + turn(
        ends[devices:], 4 * CH, 1
    )
    wait_all(copy_all([(held_send, send)], sems))


def flux_chunk(get, mets, fi, w, fk, acc, r):
    rows = pl.ds(r, 8)
    vax, vay, vbx, vby, niv, rw, cw, tw = [mets[j, rows] for j in range(8)]
    at_j = along(1)
    for k in range(fi.shape[1]):
        f = [get(c, k, r) for c in range(CH)]
        wk, p, h = point(f)
        for c, x in enumerate(flux(f, wk, p, h, vax, vay)):
            fi[c, k, rows] = x
        for c in range(4):
            w[c, k, rows] = wk[c]
        fj = flux(f, wk, p, h, vbx, vby)
        for c in range(CH):
            val = niv * slope(fj[c], at_j)
            if c > 0:
                val = val + (cw * curve(wk[c - 1], at_j) - tw * wk[c - 1])
            acc[c, k, rows] = val
        for c, x in enumerate(flux_planes(f, wk, p, h)):
            fk[c, k, rows] = x


def sum_chunk(mets, fi, w, fk, acc, r, emit):
    planes = fi.shape[1]
    kv = viscosity * unit
    rows = pl.ds(r, 8)
    niv, rw = mets[4, rows], mets[5, rows]
    for c in range(CH):
        t = [fk[c, k, rows] for k in range(planes)]
        x = [w[c - 1, k, rows] for k in range(planes)] if c > 0 else None
        for k in range(planes):

            def near(v, o):
                return v[(k + o) % planes]

            def at_i(v, o):
                return v[pl.ds(r + o, 8)]

            val = acc[c, k, rows] + niv * slope(fi.at[c, k], at_i) - unit * slope(t, near)
            if c > 0:
                val = val + (rw * curve(w.at[c - 1, k], at_i) + kv * curve(x, near))
            emit(c, k, r, val)


def chunks(count, body, unroll=1):
    def step(n, _):
        body(pl.multiple_of(n * 8, 8))
        return 0

    lax.fori_loop(0, count, step, 0, unroll=unroll)


def first_kernel(
    state_in, placed_at, neighbour_at, face_at, orient_at, state, route,
    mets, fi, w, fk, acc, placed, neighbour, face, orient, where_is, sems,
):
    del state_in
    planes, rows = fi.shape[1], fi.shape[2] - 2 * PAD
    pairs = zip((placed_at, neighbour_at, face_at, orient_at), (placed, neighbour, face, orient))
    tables = copy_all(list(pairs), sems)
    count = rows // 8
    blocks = placed.shape[0]
    share = -(-blocks // count)

    def slots(n):
        return [jnp.minimum((n // 8) * share + i, blocks - 1) for i in range(share)]

    def get(c, k, r):
        return state[c, k, pl.ds(r, 8)]

    def fluxes(n):
        at = pl.ds(n + PAD, 8)
        for j, x in enumerate(metric_terms([state[c, planes, at] for c in range(CH)])):
            mets[j, at] = x
        flux_chunk(get, mets, fi, w, fk, acc, n + PAD)

    def emit(c, k, r, val):
        state[c, k, pl.ds(r, 8)] = get(c, k, r) + val

    def sums(n):
        for slot in slots(n):
            block = placed[slot]
            for f in range(2):
                partner = where_is[neighbour[f, block]]
                route[2 * slot + f] = partner * 4 + face[f, block] * 2 + orient[f, block]
        sum_chunk(mets, fi, w, fk, acc, n + PAD, emit)

    def note(slot):
        where_is[placed[slot]] = slot

    chunks(count, fluxes, unroll=2)
    wait_all(tables)
    loop(blocks, note, unroll=8)
    chunks(count, sums, unroll=2)


def pack_ends(tall, planes):
    sub, lane = rows_of((8, LANES)), lanes_of((8, LANES))
    stacked = []
    for c in range(CH):
        packed = jnp.zeros((8, LANES), jnp.float32)
        for k in range(planes):
            x = turn(jnp.where(sub < 4, tall[0, c, k], tall[1, c, k]), 8 * k + 4, 1)
            packed = jnp.where(within(lane, 8 * k, 8), x, packed)
        stacked.append(packed)
    ends = across(jnp.concatenate(stacked, axis=0))
    out = []
    for c in range(CH):
        packed = jnp.zeros((8, LANES), jnp.float32)
        for k in range(planes):
            x = turn(ends[k * 8 : k * 8 + 8], 4 * k - (8 * c + 2), 1)
            packed = jnp.where(within(lane, 4 * k, 4), x, packed)
        out.append(packed)
    return out


def ends_kernel(
    halves, state_in, tall_in, low, high, after, state, tall, ends_base, ends_sec, inner,
    tile_fk, tile_w, tile_acc, packed,
):
    del state_in, tall_in, after
    planes, rows = tall.shape[2] - 1, state.shape[2] - 2 * PAD
    every = planes + 1
    half = lax.axis_index("ij")
    low_wall, high_wall = half == 0, half == halves - 1
    low_flag, high_flag = jnp.where(low_wall, 1, 0), jnp.where(high_wall, 1, 0)
    sub, lane = rows_of((8, LANES)), lanes_of((8, LANES))
    top = PAD + rows

    @pl.when(low_wall)
    def _():
        for c in range(CH):
            for k in range(every):
                for n in range(2):
                    x = tall[0, c, k, 4 + n : 5 + n]
                    tall[0, c, k, 3 - n : 4 - n] = -x if 1 <= c <= 3 and k < planes else x

    @pl.when(jnp.logical_not(low_wall))
    def _():
        for c in range(CH):
            for k in range(every):
                tall[0, c, k, 0:4] = low[c, 4 * k : 4 * k + 4]

    @pl.when(high_wall)
    def _():
        for c in range(CH):
            for k in range(every):
                for n in range(2):
                    tall[1, c, k, 4 + n : 5 + n] = tall[1, c, k, 3 - n : 4 - n]

    @pl.when(jnp.logical_not(high_wall))
    def _():
        for c in range(CH):
            for k in range(every):
                tall[1, c, k, 4:8] = high[c, 4 * k : 4 * k + 4]

    for c, x in enumerate(pack_ends(tall, every)):
        ends_base[c] = x
    for c in range(CH):
        state[c, planes, PAD - 4 : PAD] = tall[0, c, planes, 0:4]
        state[c, planes, top : top + 4] = tall[1, c, planes, 4:8]
    mets = [metric_terms([tall[s, c, planes] for c in range(CH)]) for s in range(2)]

    def done(c, s, k, x):
        tall[s, c, k] = x
        if s == 0:
            sign = -1.0 if 1 <= c <= 3 else 1.0
            wall = sign * jnp.where(sub == 2, turn(x, -3, 0), turn(x, -1, 0))
            x = jnp.where((sub < 4) & (low_flag == 1), wall, x)
        else:
            wall = jnp.where(sub == 4, turn(x, 1, 0), turn(x, 3, 0))
            x = jnp.where((sub >= 4) & (high_flag == 1), wall, x)
        start = PAD - 2 if s == 0 else top - 2
        state[c, k, start : start + 4] = x[2:6]

    tile_stage(
        planes, lambda c, s, k: tall[s, c, k], mets, lambda *_: along(0), along(1),
        (tile_fk, tile_w, tile_acc), done,
    )
    for c, x in enumerate(pack_ends(tall, planes)):
        ends_sec[c] = x

    if rows < LANES:
        packed[...] = jnp.zeros(packed.shape, jnp.float32)

    def pack(n):
        at = pl.ds(n + PAD, 8)
        for c in range(CH):
            packs = turn(state[c, planes, at], 12 * planes + 6, 1)
            for k in range(planes):
                x = turn(state[c, k, at], 12 * k + 6, 1)
                packs = jnp.where(within(lane, 12 * k, 12), x, packs)
            packed[c, pl.ds(n, 8)] = packs

    chunks(rows // 8, pack, unroll=2)
    for c in range(CH):
        inner[c] = packed[c].T[0 : inner.shape[1]]


def second_kernel(
    state_in, dens, mom, en, state, fields, mets, fi, w, fk, acc, sems
):
    del state_in
    planes, rows = fields.shape[1:3]
    pairs = [(dens.at[0], fields.at[0]), (mom.at[0], fields.at[1:4]), (en.at[0], fields.at[4])]
    copies = copy_all(pairs, sems)

    def get(c, k, r):
        return state[c, k, pl.ds(r, 8)]

    def fluxes(n):
        at = pl.ds(n, 8)
        for j, x in enumerate(metric_terms([state[c, planes, at] for c in range(CH)])):
            mets[j, at] = x
        flux_chunk(get, mets, fi, w, fk, acc, n)

    def emit(c, k, r, val):
        x = 0.5 * (fields[c, k, pl.ds(r - PAD, 8)] + (get(c, k, r) + val))
        state[c, k, pl.ds(r, 8)] = x

    chunks(rows // 8 + 2, fluxes, unroll=2)
    wait_all(copies)
    chunks(rows // 8, lambda n: sum_chunk(mets, fi, w, fk, acc, n + PAD, emit), unroll=2)


def beyond(packed, f, k, rows):
    base = 28 * f + 4 * k
    low = roll_by(packed, LANES - 2 - base)
    top = rows % LANES
    high = low if top == 0 else roll_by(packed, top - 2 - base)
    lane = lanes_of(packed.shape)

    def at(x, o):
        if o < 0:
            x = jnp.where(lane >= LANES + o, low, x)
        else:
            x = jnp.where(within(lane, top, o), high, x)
        return turn(x, -o, 1)

    return at


def last_kernel(
    halves, rows, planes, own, ends_base, ends_sec, inner, got, out,
    next_dens, next_mom, next_en,
    base, sec, fk, ws, acc, turned, back, full, sems,
):
    half = lax.axis_index("ij")
    low_wall, high_wall = half == 0, half == halves - 1
    sub, lane = rows_of((8, LANES)), lanes_of((8, LANES))

    def mix(f, mine, others):
        return jnp.where((sub < 4) == (f == 1), mine, others)

    others = [jnp.zeros((8, LANES), jnp.float32)] * CH
    for k in range(planes + 1):
        start = DEPTH * k * PASSED
        for f in range(2):

            def ghost(row):
                x = got[pl.ds(start + row, 8, stride=PASSED)]
                return x if f == 1 else turn(x, 4, 0)

            arrived = ghost(2 * CH)
            to = 28 * f + 4 * k
            for c in range(CH):
                base[c, f, k] = mix(f, own[c, k * 8 : k * 8 + 8], ghost(f * CH + c))
                moved = turn(arrived, to - 4 * CH * f - 4 * c, 1)
                others[c] = jnp.where(within(lane, to, 4), moved, others[c])

    low_lanes = lane < 28
    twice = [jnp.where(low_lanes, ends_base[c], turn(ends_base[c], 28, 1)) for c in range(CH)]
    ends = [jnp.where(low_lanes == (sub >= 4), twice[c], others[c]) for c in range(CH)]
    slot = jnp.where(low_lanes, lane, lane - 28)

    def spread(x):
        y = x
        for k in range(planes):
            y = jnp.where(within(slot, 4 * k, 4), turn(x, 4 * (k - planes), 1), y)
        return y

    vax, vay, vbx, vby, niv, _, cw, _ = [spread(x) for x in metric_terms(ends)]
    wrapped = [spread(x) for x in metric_terms(twice)[2:4]]

    def keep(c, f, k, val):
        sec[c, f, k] = val

    def stage(held, ends, gx, gy):
        mets = [metric_terms([held[c, f, planes] for c in range(CH)]) for f in range(2)]
        w, p, h = point(ends)
        rims = (flux(ends, w, p, h, gx, gy), w)
        tile_stage(
            planes,
            lambda c, f, k: held[c, f, k],
            mets,
            lambda kind, c, f, k: beyond(rims[kind][c], f, k, rows),
            along(0),
            (fk, ws, acc),
            keep,
        )

    stage(base, ends, vax, vay)

    def move(k, source):
        for c in range(CH):
            at = 12 * k
            mine = jnp.where(sub < 4, inner[c, at : at + 8], inner[c, at + 4 : at + 12])
            for f in range(2):
                sec[c, f, k] = mix(f, mine, turn(source[c, f, k], 2 if f == 1 else -2, 0))

    for k in range(planes):
        move(k, sec)
    move(planes, base)

    def shifted(x):
        return jnp.where(low_lanes, turn(x, -2, 0), turn(x, 2, 0))

    w1, p1, h1 = point(ends)
    w0, p0, h0 = point(twice)
    new, old = flux(ends, w1, p1, h1, vbx, vby), flux(twice, w0, p0, h0, *wrapped)
    at_j = along(0)
    touched = within(sub, jnp.where(low_lanes, 4, 2), 2)
    second = []
    for c in range(CH):
        add = niv * slope(new[c] - old[c], at_j)
        if c > 0:
            add = add + cw * curve(w1[c - 1] - w0[c - 1], at_j)
        x = jnp.where(low_lanes, ends_sec[c], turn(ends_sec[c], 28, 1))
        second.append(shifted(x + jnp.where(touched, add, 0.0)))
    walled = low_wall | high_wall

    for k in range(planes):
        for f in range(2):
            to = 28 * f + 4 * k
            first = jnp.where(walled, jnp.where(low_wall, to, to + 2), -8)
            shift = jnp.where(low_wall, (to - 1) % LANES, (to + 3 - rows) % LANES)
            next_shift = jnp.where(low_wall, (to + 1) % LANES, (to + 5 - rows) % LANES)
            for c in range(CH):
                x = sec[c, f, k]
                one, two = pltpu.roll(x, shift, 1), pltpu.roll(x, next_shift, 1)
                x = jnp.where(lane == first, one, two)
                if 1 <= c <= 3:
                    x = jnp.where(low_wall, -1.0, 1.0) * x
                second[c] = jnp.where(within(lane, first, 2), x, second[c])
    stage(sec, second, shifted(vax), shifted(vay))

    per = LANES // 8

    for k in range(planes):
        for c in range(CH):
            x = jnp.where(sub < 4, turn(sec[c, 1, k], -2, 0), turn(sec[c, 0, k], 2, 0))
            at = (c * planes + k) * 8
            turned[at : at + 8] = 0.5 * (own[c, k * 8 : k * 8 + 8] + x)
    for n in range(turned.shape[0] // LANES):
        back[n] = turned[n * LANES : (n + 1) * LANES].T
    inside = within(lane, 4, LANES - 8)
    size = max(8, rows // PIECES)

    def leave(start):
        at = pl.ds(start, size)
        targets = [next_dens.at[0, :, at], next_en.at[0, :, at], next_mom.at[0, :, :, at]]
        sources = [full.at[0, :, at], full.at[4, :, at], full.at[1:4, :, at]]
        first = 3 * (start // size)
        return [
            pltpu.make_async_copy(src, dst, sems.at[first + n])
            for n, (src, dst) in enumerate(zip(sources, targets))
        ]

    def merge(r):
        at = pl.ds(r, 8)
        for c in range(CH):
            for k in range(planes):
                index = c * planes + k
                moved = turn(back[index // per, at], LANES - 4 - 8 * (index % per), 1)
                full[c, k, at] = jnp.where(inside, out[c, k, pl.ds(r + PAD, 8)], moved)

        @pl.when(lax.rem(r + 8, size) == 0)
        def _():
            for copy in leave(pl.multiple_of(r + 8 - size, 8)):
                copy.start()

    chunks(rows // 8, merge, unroll=2)
    for n in range(rows // size):
        wait_all(leave(n * size))


def local(mesh_shape, density, momentum, energy, metrics, volume, placed, neighbour, face, orient):
    halves = mesh_shape["ij"]
    blocks = mesh_shape["blk"]
    planes, rows = density.shape[1], density.shape[2]
    every = planes + 1
    fields = (density, momentum, energy, metrics, volume)
    neighbour, face, orient = neighbour.T, face.T, orient.T
    vmem = pl.BlockSpec(memory_space=pltpu.VMEM)
    smem = pl.BlockSpec(memory_space=pltpu.SMEM)
    hbm = pl.BlockSpec(memory_space=pltpu.HBM)
    anywhere = pl.BlockSpec(memory_space=pl.ANY)

    def call(kernel, name, outs, ins, out_specs, scratch, cost=None, alias=None):
        run = pl.pallas_call(
            kernel,
            out_shape=[
                held(x) if spec is vmem else far(x) if spec is hbm else x
                for x, spec in zip(outs, out_specs)
            ],
            in_specs=ins,
            out_specs=out_specs,
            scratch_shapes=scratch,
            compiler_params=pltpu.CompilerParams(vmem_limit_bytes=VMEM_MIB * 1024 * 1024),
            cost_estimate=cost,
            input_output_aliases=alias or {},
            name=name,
        )

        def keep(*operands):
            return run(
                *[
                    x
                    if spec not in (vmem, hbm)
                    else pltpu.with_memory_space_constraint(x, spec.memory_space)
                    for x, spec in zip(operands, ins)
                ]
            )

        return keep

    def shape(*dims):
        return jax.ShapeDtypeStruct(dims, jnp.float32)

    def held(x):
        return pltpu.VMEM(x.shape, x.dtype)

    def far(x):
        return pltpu.HBM(x.shape, x.dtype)

    def table(x):
        return pltpu.SMEM(x.shape, jnp.int32)

    def sems(count):
        return pltpu.SemaphoreType.DMA((count,))

    devices = blocks * halves
    sent, passed = shape(devices * SENT, LANES), shape(devices * PASSED, LANES)
    strip, rim = shape(CH, 64, LANES), shape(CH, 8, LANES)
    edge = shape(CH, 4 * every, LANES)
    edges = 1 if halves == 2 else 2
    square = held(shape(CH, LANES, LANES))
    tall = rows + 2 * PAD
    whole = shape(CH, every, tall, LANES)
    rows_about = shape(2, CH, every, 8, LANES)
    to_send, own, about, state, *halo = call(
        functools.partial(cut_kernel, halves),
        "cut",
        [sent, strip, rows_about, whole] + [edge] * edges,
        [hbm] * 8,
        [hbm] + [vmem] * (3 + edges),
        [
            held(sent),
            square,
            held(shape(CH * 64, LANES)),
            table(placed),
            table(face),
            table(orient),
            sems(5 * PIECES),
            sems(3),
            sems(1),
        ],
    )(*fields, placed, face, orient)

    def swap(x):
        x = x.reshape(devices, x.shape[0] // devices, 1, LANES)
        x = lax.all_to_all(x, ("blk", "ij"), 0, 0, tiled=True)
        return x.reshape(x.shape[0] * x.shape[1], LANES)

    if edges == 1:
        below = above = lax.ppermute(halo[0], "ij", [(0, 1), (1, 0)])
    else:
        below = lax.ppermute(halo[1], "ij", [(i, i + 1) for i in range(halves - 1)])
        above = lax.ppermute(halo[0], "ij", [(i + 1, i) for i in range(halves - 1)])
    got = swap(to_send)

    padded = held(shape(CH, planes, tall, LANES))
    stage = [
        held(shape(8, tall, LANES)),
        padded,
        held(shape(4, planes, tall, LANES)),
        padded,
        padded,
    ]
    work = planes * rows * LANES
    cost = pl.CostEstimate(flops=300 * work, bytes_accessed=150 * work, transcendentals=work)
    route = jax.ShapeDtypeStruct((2 * blocks,), jnp.int32)
    state, route_out = call(
        first_kernel,
        "first_section",
        [whole, route],
        [vmem] + [hbm] * 4,
        [vmem, smem],
        stage + [table(x) for x in (placed, neighbour, face, orient, placed)] + [sems(4)],
        cost,
        {0: 0},
    )(state, placed, neighbour, face, orient)
    (relayed,) = call(
        functools.partial(relay_kernel, halves, rows, planes, devices),
        "relay",
        [passed],
        [anywhere, anywhere, vmem],
        [hbm],
        [
            held(passed),
            held(shape(devices * 16, LANES)),
            held(shape(devices * 16, LANES)),
            held(shape(devices * 2, LANES)),
            table(route),
            sems(2),
        ],
    )(route_out, below, got)
    ghosts = swap(relayed)
    tiles = held(shape(CH, 2, every, 8, LANES))
    state, _, ends_base, ends_sec, inner = call(
        functools.partial(ends_kernel, halves),
        "ends",
        [whole, rows_about, rim, rim, shape(CH, 12 * every + 4, LANES)],
        [vmem] * 4 + [hbm],
        [vmem] * 5,
        [tiles] * 3 + [square],
        cost,
        {0: 0, 1: 1},
    )(state, about, below, above, relayed)
    (state,) = call(
        second_kernel,
        "second_section",
        [whole],
        [vmem] + [hbm] * 3,
        [vmem],
        [held(shape(CH, planes, rows, LANES))] + stage + [sems(3)],
        cost,
        {0: 0},
    )(state, density, momentum, energy)
    flat = -(-CH * planes * 8 // LANES)
    return call(
        functools.partial(last_kernel, halves, rows, planes),
        "strips",
        [shape(*density.shape), shape(*momentum.shape), shape(*energy.shape)],
        [vmem] * 6,
        [hbm] * 3,
        [tiles] * 5
        + [
            held(shape(flat * LANES, LANES)),
            held(shape(flat, LANES, LANES)),
            held(shape(CH, planes, rows, LANES)),
            sems(3 * PIECES),
        ],
    )(own, ends_base, ends_sec, inner, ghosts, state)


def solution(mesh):
    return jax.shard_map(
        functools.partial(local, dict(mesh.shape)),
        mesh=mesh,
        in_specs=(
            P("blk", None, "ij", None),
            P("blk", None, None, "ij", None),
            P("blk", None, "ij", None),
            P("blk", None, "ij", None),
            P("blk", "ij", None),
            P(),
            P(),
            P(),
            P(),
        ),
        out_specs=(
            P("blk", None, "ij", None),
            P("blk", None, None, "ij", None),
            P("blk", None, "ij", None),
        ),
        check_vma=False,
    )
```

```python
import functools

import jax
import jax.numpy as jnp
from jax import lax
from jax.experimental import pallas as pl
from jax.experimental.pallas import tpu as pltpu
from jax.sharding import PartitionSpec as P

pressure_factor = 0.4
viscosity = 0.05
time_step = 0.03
unit = time_step / 12.0

LANES = 128
PAD = 8
PIECES = 4
DEPTH = 4
CH = 5
VMEM_MIB = 32
SENT = 2 * CH
PASSED = 2 * CH + 1
FIRST = 4


def turn(x, shift, axis):
    shift = shift % x.shape[axis]
    return x if shift == 0 else pltpu.roll(x, shift, axis)


def lanes_of(shape):
    return lax.broadcasted_iota(jnp.int32, shape, len(shape) - 1)


def rows_of(shape):
    return lax.broadcasted_iota(jnp.int32, shape, len(shape) - 2)


def point(f):
    rho, m1, m2, m3, e = f
    r = 1.0 / rho
    u1, u2, u3 = m1 * r, m2 * r, m3 * r
    kin = 0.5 * (m1 * u1 + m2 * u2 + m3 * u3)
    p = pressure_factor * (e - kin)
    return (u1, u2, u3, (kin + 2.0 * p) * r), p, e + p


def metric_terms(m):
    ax, ay, bx, by, v = m
    kv = viscosity * unit
    rw = kv * (ax * ax + ay * ay)
    cw = kv * (bx * bx + by * by)
    return v * ax, v * ay, v * bx, v * by, -unit / v, rw, cw, 30.0 * (rw + cw + kv)


def flux(f, w, p, h, gx, gy):
    rho, m1, m2, m3, _ = f
    u = gx * w[0] + gy * w[1]
    return (rho * u, m1 * u + gx * p, m2 * u + gy * p, m3 * u, h * u)


def flux_planes(f, w, p, h):
    u3 = w[2]
    return (f[3], f[1] * u3, f[2] * u3, f[3] * u3 + p, h * u3)


def slope(x, at):
    return 8.0 * (at(x, 1) - at(x, -1)) - (at(x, 2) - at(x, -2))


def curve(x, at):
    return 16.0 * (at(x, 1) + at(x, -1)) - (at(x, 2) + at(x, -2))


def along(axis):
    return lambda x, o: turn(x, -o, axis)


def within(lane, start, size):
    return (lane >= start) & (lane < start + size)


def roll_by(x, shift, axis=1):
    size = x.shape[axis]
    return pltpu.roll(x, lax.rem(shift + 4 * size, size), axis)


def across(x):
    if x.shape[0] < LANES:
        x = jnp.concatenate([x, jnp.zeros((LANES - x.shape[0], LANES), jnp.float32)], axis=0)
    return x.T


def loop(count, body, unroll=1):
    def step(n, _):
        body(n)
        return 0

    lax.fori_loop(0, count, step, 0, unroll=unroll)


def copy_all(pairs, sems, first=0):
    copies = [
        pltpu.make_async_copy(src, dst, sems.at[first + n]) for n, (src, dst) in enumerate(pairs)
    ]
    for copy in copies:
        copy.start()
    return copies


def state_pairs(fields, state, planes, start, size):
    dens, mom, en, met, vol = fields
    at, to = pl.ds(start, size), pl.ds(start + PAD, size)
    return [
        (dens.at[0, :, at], state.at[0, 0:planes, to]),
        (mom.at[0, :, :, at], state.at[1:4, 0:planes, to]),
        (en.at[0, :, at], state.at[4, 0:planes, to]),
        (met.at[0, :, at], state.at[0:4, planes, to]),
        (vol.at[0, at], state.at[4, planes, to]),
    ]


def arrive_in_pieces(fields, state, sems):
    planes, rows = fields[0].shape[1], fields[0].shape[2]
    size = max(8, rows // PIECES)
    for n in range(rows // size):
        copy_all(state_pairs(fields, state, planes, n * size, size), sems, 5 * n)

    def expect(start):
        @pl.when(lax.rem(start, size) == 0)
        def _():
            for n, (src, dst) in enumerate(state_pairs(fields, state, planes, start, size)):
                pltpu.make_async_copy(src, dst, sems.at[5 * (start // size) + n]).wait()

    return expect


def wait_all(copies):
    for copy in copies:
        copy.wait()


def tile_stage(planes, load, mets, shift_i, shift_j, hold, done):
    kv = viscosity * unit
    fk, ws, acc = hold

    def spread(k):
        for s in range(2):
            vax, vay, vbx, vby, niv, rw, cw, tw = mets[s]
            x = [load(c, s, k) for c in range(CH)]
            w, p, h = point(x)
            fi, fj = flux(x, w, p, h, vax, vay), flux(x, w, p, h, vbx, vby)
            for c in range(CH):
                val = niv * (slope(fi[c], shift_i(0, c, s, k)) + slope(fj[c], shift_j))
                if c > 0:
                    v = w[c - 1]
                    val = val + (
                        rw * curve(v, shift_i(1, c - 1, s, k)) + cw * curve(v, shift_j) - tw * v
                    )
                    ws[c - 1, s, k] = v
                acc[c, s, k] = x[c] + val
            for c, v in enumerate(flux_planes(x, w, p, h)):
                fk[c, s, k] = v

    def gather(k):
        at = {o: lax.rem(k + o + planes, planes) for o in (-2, -1, 0, 1, 2)}
        for s in range(2):
            for c in range(CH):
                val = acc[c, s, k] - unit * slope(0, lambda _, o: fk[c, s, at[o]])
                if c > 0:
                    val = val + kv * curve(0, lambda _, o: ws[c - 1, s, at[o]])
                done(c, s, k, val)

    loop(planes, spread, unroll=3)
    loop(planes, gather, unroll=3)


def cut_kernel(
    halves, dens, mom, en, met, vol, placed_at, face_at, orient_at, send, own, tall, state, *rest
):
    edges, rest = rest[: 1 if halves == 2 else 2], rest[1 if halves == 2 else 2 :]
    packed, strips, placed, face, orient, sems, table_sems = rest
    tables = copy_all(
        [(placed_at, placed), (face_at, face), (orient_at, orient)], table_sems
    )
    planes, rows = dens.shape[1], dens.shape[2]
    expect = arrive_in_pieces((dens, mom, en, met, vol), state, sems)
    half = lax.axis_index("ij")
    lane = lanes_of((8, LANES))
    if rows < LANES:
        packed[...] = jnp.zeros(packed.shape, jnp.float32)
    def pack(r):
        expect(r)
        for c in range(CH):
            packs = jnp.zeros((8, LANES), jnp.float32)
            for k in range(planes + 1):
                x = turn(state[c, k, pl.ds(r + PAD, 8)], 8 * k + 4, 1)
                packs = jnp.where(within(lane, 8 * k, 8), x, packs)
            packed[c, pl.ds(r, 8)] = packs

    chunks(rows // 8, pack, unroll=2)

    def cut_ends(k):
        for c in range(CH):
            low, high = state[c, k, PAD : PAD + 4], state[c, k, PAD + rows - 4 : PAD + rows]
            tall[0, c, k, 4:8] = low
            tall[1, c, k, 0:4] = high
            if len(edges) == 1:
                edges[0][c, k * 4 : k * 4 + 4] = jnp.where(half == 0, high, low)
            else:
                edges[0][c, k * 4 : k * 4 + 4] = low
                edges[1][c, k * 4 : k * 4 + 4] = high

    for k in range(planes + 1):
        cut_ends(k)

    wait_all(tables)
    block = placed[lax.axis_index("blk")]
    row = rows_of((64, LANES))
    high_side = row % 8 < 4
    mirror = jnp.where(
        rows_of((LANES, LANES)) + lanes_of((LANES, LANES)) == rows - 1, 1.0, 0.0
    )
    flip = [jnp.where(orient[f, block] == 1, -1.0, 1.0) for f in range(2)]
    same = [jnp.where(face[f, block] == f, -1.0, 1.0) for f in range(2)]
    rising = [face[f, block] == 1 for f in range(2)]
    turned = jnp.where(high_side, flip[1], flip[0])
    facing = jnp.where(high_side, same[1], same[0])

    def orient_strip(c):
        strip = packed[c].T[0:64]
        own[c] = strip
        back = jnp.dot(
            strip,
            mirror,
            precision=lax.Precision.HIGHEST,
            preferred_element_type=jnp.float32,
        )
        moved = jnp.where(turned < 0.0, back, strip)
        sign = jnp.where(c < 2, turned, jnp.where(c < 4, facing, 1.0))
        moved = jnp.where(row >= planes * 8, moved * sign, moved)
        strips[pl.ds(pl.multiple_of(c * 64, 64), 64)] = moved

    loop(CH, orient_strip, unroll=CH)

    def put(n):
        k, e = n >> 2, n & 3
        at = (FIRST + n) * SENT
        low = k * 8 + 4 + jnp.where(rising[0], e, 3 - e)
        high = k * 8 + jnp.where(rising[1], 3 - e, e)
        send[pl.ds(at, CH)] = strips[pl.ds(low, CH, stride=64)]
        send[pl.ds(at + CH, CH)] = strips[pl.ds(high, CH, stride=64)]

    loop(DEPTH * (planes + 1), put, unroll=4)


def relay_kernel(
    halves, rows, planes, devices, route_at, halo, held_got, send,
    below, above, signs, route, sems,
):
    del halo
    wait_all(copy_all([(route_at, route)], sems))
    me = lax.axis_index("blk") * halves + lax.axis_index("ij")
    is_field = (me >= FIRST) & (me < FIRST + DEPTH * planes)

    def pass_on(slot):
        for f in range(2):
            code = route[2 * slot + f]
            partner, side, turned = code >> 2, (code >> 1) & 1, code & 1
            sign = jnp.where(turned == 1, -1.0, 1.0)

            def piece(h):
                h = jnp.where(turned == 1, halves - 1 - h, h)
                return held_got[pl.ds((partner * halves + h) * SENT + side * CH, CH)]

            pieces = [piece(h) for h in range(halves)]
            for half in range(halves):
                at = slot * halves + half
                send[pl.ds(at * PASSED + f * CH, CH)] = pieces[half]
                below[pl.ds((f * devices + at) * 8, CH)] = pieces[max(half - 1, 0)]
                above[pl.ds((f * devices + at) * 8, CH)] = pieces[min(half + 1, halves - 1)]
                signs[pl.ds(f * devices + at, 1)] = jnp.full((1, LANES), sign, jnp.float32)

    loop(devices // halves, pass_on, unroll=4)
    count = 2 * devices
    lane = lanes_of((count, LANES))
    half = rows_of((count, LANES)) % halves
    sign = signs[...]
    ends = jnp.zeros((count, LANES), jnp.float32)
    for c in range(CH):
        low, high = below[pl.ds(c, count, stride=8)], above[pl.ds(c, count, stride=8)]
        at = 4 * c
        low_wall = jnp.where(lane == at, turn(low, at - 1, 1), turn(low, at + 1, 1))
        high_wall = jnp.where(
            lane == at + 2, turn(high, at + 3 - rows, 1), turn(high, at + 5 - rows, 1)
        )
        if 1 <= c <= 3:
            low_wall = jnp.where(is_field, -sign * low_wall, low_wall)
            high_wall = jnp.where(is_field, sign * high_wall, high_wall)
        low = jnp.where(half == 0, low_wall, turn(low, at + 2 - rows, 1))
        high = jnp.where(half == halves - 1, high_wall, turn(high, at + 2, 1))
        ends = jnp.where(within(lane, at, 2), low, jnp.where(within(lane, at + 2, 2), high, ends))
    send[pl.ds(2 * CH, devices, stride=PASSED)] = ends[0:devices] + turn(
        ends[devices:], 4 * CH, 1
    )


def flux_chunk(get, mets, fi, w, fk, acc, r):
    rows = pl.ds(r, 8)
    vax, vay, vbx, vby, niv, rw, cw, tw = [mets[j, rows] for j in range(8)]
    at_j = along(1)
    for k in range(fi.shape[1]):
        f = [get(c, k, r) for c in range(CH)]
        wk, p, h = point(f)
        for c, x in enumerate(flux(f, wk, p, h, vax, vay)):
            fi[c, k, rows] = x
        for c in range(4):
            w[c, k, rows] = wk[c]
        fj = flux(f, wk, p, h, vbx, vby)
        for c in range(CH):
            val = niv * slope(fj[c], at_j)
            if c > 0:
                val = val + (cw * curve(wk[c - 1], at_j) - tw * wk[c - 1])
            acc[c, k, rows] = val
        for c, x in enumerate(flux_planes(f, wk, p, h)):
            fk[c, k, rows] = x


def sum_chunk(mets, fi, w, fk, acc, r, emit):
    planes = fi.shape[1]
    kv = viscosity * unit
    rows = pl.ds(r, 8)
    niv, rw = mets[4, rows], mets[5, rows]
    for c in range(CH):
        t = [fk[c, k, rows] for k in range(planes)]
        x = [w[c - 1, k, rows] for k in range(planes)] if c > 0 else None
        for k in range(planes):

            def near(v, o):
                return v[(k + o) % planes]

            def at_i(v, o):
                return v[pl.ds(r + o, 8)]

            val = acc[c, k, rows] + niv * slope(fi.at[c, k], at_i) - unit * slope(t, near)
            if c > 0:
                val = val + (rw * curve(w.at[c - 1, k], at_i) + kv * curve(x, near))
            emit(c, k, r, val)


def chunks(count, body, unroll=1):
    def step(n, _):
        body(pl.multiple_of(n * 8, 8))
        return 0

    lax.fori_loop(0, count, step, 0, unroll=unroll)


def first_kernel(
    state_in, placed_at, neighbour_at, face_at, orient_at, state, route,
    mets, fi, w, fk, acc, placed, neighbour, face, orient, where_is, sems,
):
    del state_in
    planes, rows = fi.shape[1], fi.shape[2] - 2 * PAD
    pairs = zip((placed_at, neighbour_at, face_at, orient_at), (placed, neighbour, face, orient))
    tables = copy_all(list(pairs), sems)
    count = rows // 8
    blocks = placed.shape[0]
    share = -(-blocks // count)

    def slots(n):
        return [jnp.minimum((n // 8) * share + i, blocks - 1) for i in range(share)]

    def get(c, k, r):
        return state[c, k, pl.ds(r, 8)]

    def fluxes(n):
        at = pl.ds(n + PAD, 8)
        for j, x in enumerate(metric_terms([state[c, planes, at] for c in range(CH)])):
            mets[j, at] = x
        flux_chunk(get, mets, fi, w, fk, acc, n + PAD)

    def emit(c, k, r, val):
        state[c, k, pl.ds(r, 8)] = get(c, k, r) + val

    def sums(n):
        for slot in slots(n):
            block = placed[slot]
            for f in range(2):
                partner = where_is[neighbour[f, block]]
                route[2 * slot + f] = partner * 4 + face[f, block] * 2 + orient[f, block]
        sum_chunk(mets, fi, w, fk, acc, n + PAD, emit)

    def note(slot):
        where_is[placed[slot]] = slot

    chunks(count, fluxes, unroll=2)
    wait_all(tables)
    loop(blocks, note, unroll=8)
    chunks(count, sums, unroll=2)


def pack_ends(tall, planes):
    sub, lane = rows_of((8, LANES)), lanes_of((8, LANES))
    stacked = []
    for c in range(CH):
        packed = jnp.zeros((8, LANES), jnp.float32)
        for k in range(planes):
            x = turn(jnp.where(sub < 4, tall[0, c, k], tall[1, c, k]), 8 * k + 4, 1)
            packed = jnp.where(within(lane, 8 * k, 8), x, packed)
        stacked.append(packed)
    ends = across(jnp.concatenate(stacked, axis=0))
    out = []
    for c in range(CH):
        packed = jnp.zeros((8, LANES), jnp.float32)
        for k in range(planes):
            x = turn(ends[k * 8 : k * 8 + 8], 4 * k - (8 * c + 2), 1)
            packed = jnp.where(within(lane, 4 * k, 4), x, packed)
        out.append(packed)
    return out


def second_kernel(
    halves, state_in, tall_in, low, high, dens, mom, en, after,
    state, tall, ends_base, ends_sec, inner,
    tile_fk, tile_w, tile_acc, packed, base, mets, fi, w, fk, acc, sems,
):
    del state_in, tall_in, after
    pairs = [(dens.at[0], base.at[0]), (mom.at[0], base.at[1:4]), (en.at[0], base.at[4])]
    copies = copy_all(pairs, sems)
    planes, rows = tall.shape[2] - 1, state.shape[2] - 2 * PAD
    every = planes + 1
    half = lax.axis_index("ij")
    low_wall, high_wall = half == 0, half == halves - 1
    low_flag, high_flag = jnp.where(low_wall, 1, 0), jnp.where(high_wall, 1, 0)
    sub, lane = rows_of((8, LANES)), lanes_of((8, LANES))
    top = PAD + rows

    @pl.when(low_wall)
    def _():
        for c in range(CH):
            for k in range(every):
                for n in range(2):
                    x = tall[0, c, k, 4 + n : 5 + n]
                    tall[0, c, k, 3 - n : 4 - n] = -x if 1 <= c <= 3 and k < planes else x

    @pl.when(jnp.logical_not(low_wall))
    def _():
        for c in range(CH):
            for k in range(every):
                tall[0, c, k, 0:4] = low[c, 4 * k : 4 * k + 4]

    @pl.when(high_wall)
    def _():
        for c in range(CH):
            for k in range(every):
                for n in range(2):
                    tall[1, c, k, 4 + n : 5 + n] = tall[1, c, k, 3 - n : 4 - n]

    @pl.when(jnp.logical_not(high_wall))
    def _():
        for c in range(CH):
            for k in range(every):
                tall[1, c, k, 4:8] = high[c, 4 * k : 4 * k + 4]

    for c, x in enumerate(pack_ends(tall, every)):
        ends_base[c] = x
    for c in range(CH):
        state[c, planes, PAD - 4 : PAD] = tall[0, c, planes, 0:4]
        state[c, planes, top : top + 4] = tall[1, c, planes, 4:8]
    tall_mets = [metric_terms([tall[s, c, planes] for c in range(CH)]) for s in range(2)]

    def done(c, s, k, x):
        tall[s, c, k] = x
        if s == 0:
            sign = -1.0 if 1 <= c <= 3 else 1.0
            wall = sign * jnp.where(sub == 2, turn(x, -3, 0), turn(x, -1, 0))
            x = jnp.where((sub < 4) & (low_flag == 1), wall, x)
        else:
            wall = jnp.where(sub == 4, turn(x, 1, 0), turn(x, 3, 0))
            x = jnp.where((sub >= 4) & (high_flag == 1), wall, x)
        start = PAD - 2 if s == 0 else top - 2
        state[c, k, start : start + 4] = x[2:6]

    tile_stage(
        planes, lambda c, s, k: tall[s, c, k], tall_mets, lambda *_: along(0), along(1),
        (tile_fk, tile_w, tile_acc), done,
    )
    for c, x in enumerate(pack_ends(tall, planes)):
        ends_sec[c] = x

    if rows < LANES:
        packed[...] = jnp.zeros(packed.shape, jnp.float32)

    def pack(n):
        at = pl.ds(n + PAD, 8)
        for c in range(CH):
            packs = turn(state[c, planes, at], 12 * planes + 6, 1)
            for k in range(planes):
                x = turn(state[c, k, at], 12 * k + 6, 1)
                packs = jnp.where(within(lane, 12 * k, 12), x, packs)
            packed[c, pl.ds(n, 8)] = packs

    chunks(rows // 8, pack, unroll=2)
    for c in range(CH):
        inner[c] = packed[c].T[0 : inner.shape[1]]

    def get(c, k, r):
        return state[c, k, pl.ds(r, 8)]

    def fluxes(n):
        at = pl.ds(n, 8)
        for j, x in enumerate(metric_terms([state[c, planes, at] for c in range(CH)])):
            mets[j, at] = x
        flux_chunk(get, mets, fi, w, fk, acc, n)

    def emit(c, k, r, val):
        x = 0.5 * (base[c, k, pl.ds(r - PAD, 8)] + (get(c, k, r) + val))
        state[c, k, pl.ds(r, 8)] = x

    chunks(rows // 8 + 2, fluxes, unroll=2)
    wait_all(copies)
    chunks(rows // 8, lambda n: sum_chunk(mets, fi, w, fk, acc, n + PAD, emit), unroll=2)


def beyond(packed, f, k, rows):
    base = 28 * f + 4 * k
    low = roll_by(packed, LANES - 2 - base)
    top = rows % LANES
    high = low if top == 0 else roll_by(packed, top - 2 - base)
    lane = lanes_of(packed.shape)

    def at(x, o):
        if o < 0:
            x = jnp.where(lane >= LANES + o, low, x)
        else:
            x = jnp.where(within(lane, top, o), high, x)
        return turn(x, -o, 1)

    return at


def last_kernel(
    halves, rows, planes, own, ends_base, ends_sec, inner, got, out,
    next_dens, next_mom, next_en,
    base, sec, fk, ws, acc, turned, back, full, sems,
):
    half = lax.axis_index("ij")
    low_wall, high_wall = half == 0, half == halves - 1
    sub, lane = rows_of((8, LANES)), lanes_of((8, LANES))

    def mix(f, mine, others):
        return jnp.where((sub < 4) == (f == 1), mine, others)

    others = [jnp.zeros((8, LANES), jnp.float32)] * CH
    for k in range(planes + 1):
        start = DEPTH * k * PASSED
        for f in range(2):

            def ghost(row):
                x = got[pl.ds(start + row, 8, stride=PASSED)]
                return x if f == 1 else turn(x, 4, 0)

            arrived = ghost(2 * CH)
            to = 28 * f + 4 * k
            for c in range(CH):
                base[c, f, k] = mix(f, own[c, k * 8 : k * 8 + 8], ghost(f * CH + c))
                moved = turn(arrived, to - 4 * CH * f - 4 * c, 1)
                others[c] = jnp.where(within(lane, to, 4), moved, others[c])

    low_lanes = lane < 28
    twice = [jnp.where(low_lanes, ends_base[c], turn(ends_base[c], 28, 1)) for c in range(CH)]
    ends = [jnp.where(low_lanes == (sub >= 4), twice[c], others[c]) for c in range(CH)]
    slot = jnp.where(low_lanes, lane, lane - 28)

    def spread(x):
        y = x
        for k in range(planes):
            y = jnp.where(within(slot, 4 * k, 4), turn(x, 4 * (k - planes), 1), y)
        return y

    vax, vay, vbx, vby, niv, _, cw, _ = [spread(x) for x in metric_terms(ends)]
    wrapped = [spread(x) for x in metric_terms(twice)[2:4]]

    def keep(c, f, k, val):
        sec[c, f, k] = val

    def stage(held, ends, gx, gy):
        mets = [metric_terms([held[c, f, planes] for c in range(CH)]) for f in range(2)]
        w, p, h = point(ends)
        rims = (flux(ends, w, p, h, gx, gy), w)
        tile_stage(
            planes,
            lambda c, f, k: held[c, f, k],
            mets,
            lambda kind, c, f, k: beyond(rims[kind][c], f, k, rows),
            along(0),
            (fk, ws, acc),
            keep,
        )

    stage(base, ends, vax, vay)

    def move(k, source):
        for c in range(CH):
            at = 12 * k
            mine = jnp.where(sub < 4, inner[c, at : at + 8], inner[c, at + 4 : at + 12])
            for f in range(2):
                sec[c, f, k] = mix(f, mine, turn(source[c, f, k], 2 if f == 1 else -2, 0))

    for k in range(planes):
        move(k, sec)
    move(planes, base)

    def shifted(x):
        return jnp.where(low_lanes, turn(x, -2, 0), turn(x, 2, 0))

    w1, p1, h1 = point(ends)
    w0, p0, h0 = point(twice)
    new, old = flux(ends, w1, p1, h1, vbx, vby), flux(twice, w0, p0, h0, *wrapped)
    at_j = along(0)
    touched = within(sub, jnp.where(low_lanes, 4, 2), 2)
    second = []
    for c in range(CH):
        add = niv * slope(new[c] - old[c], at_j)
        if c > 0:
            add = add + cw * curve(w1[c - 1] - w0[c - 1], at_j)
        x = jnp.where(low_lanes, ends_sec[c], turn(ends_sec[c], 28, 1))
        second.append(shifted(x + jnp.where(touched, add, 0.0)))
    walled = low_wall | high_wall

    for k in range(planes):
        for f in range(2):
            to = 28 * f + 4 * k
            first = jnp.where(walled, jnp.where(low_wall, to, to + 2), -8)
            shift = jnp.where(low_wall, (to - 1) % LANES, (to + 3 - rows) % LANES)
            next_shift = jnp.where(low_wall, (to + 1) % LANES, (to + 5 - rows) % LANES)
            for c in range(CH):
                x = sec[c, f, k]
                one, two = pltpu.roll(x, shift, 1), pltpu.roll(x, next_shift, 1)
                x = jnp.where(lane == first, one, two)
                if 1 <= c <= 3:
                    x = jnp.where(low_wall, -1.0, 1.0) * x
                second[c] = jnp.where(within(lane, first, 2), x, second[c])
    stage(sec, second, shifted(vax), shifted(vay))

    per = LANES // 8

    for k in range(planes):
        for c in range(CH):
            x = jnp.where(sub < 4, turn(sec[c, 1, k], -2, 0), turn(sec[c, 0, k], 2, 0))
            at = (c * planes + k) * 8
            turned[at : at + 8] = 0.5 * (own[c, k * 8 : k * 8 + 8] + x)
    for n in range(turned.shape[0] // LANES):
        back[n] = turned[n * LANES : (n + 1) * LANES].T
    inside = within(lane, 4, LANES - 8)
    size = max(8, rows // PIECES)

    def leave(start):
        at = pl.ds(start, size)
        targets = [next_dens.at[0, :, at], next_en.at[0, :, at], next_mom.at[0, :, :, at]]
        sources = [full.at[0, :, at], full.at[4, :, at], full.at[1:4, :, at]]
        first = 3 * (start // size)
        return [
            pltpu.make_async_copy(src, dst, sems.at[first + n])
            for n, (src, dst) in enumerate(zip(sources, targets))
        ]

    def merge(r):
        at = pl.ds(r, 8)
        for c in range(CH):
            for k in range(planes):
                index = c * planes + k
                moved = turn(back[index // per, at], LANES - 4 - 8 * (index % per), 1)
                full[c, k, at] = jnp.where(inside, out[c, k, pl.ds(r + PAD, 8)], moved)

        @pl.when(lax.rem(r + 8, size) == 0)
        def _():
            for copy in leave(pl.multiple_of(r + 8 - size, 8)):
                copy.start()

    chunks(rows // 8, merge, unroll=2)
    for n in range(rows // size):
        wait_all(leave(n * size))


def local(mesh_shape, density, momentum, energy, metrics, volume, placed, neighbour, face, orient):
    halves = mesh_shape["ij"]
    blocks = mesh_shape["blk"]
    planes, rows = density.shape[1], density.shape[2]
    every = planes + 1
    fields = (density, momentum, energy, metrics, volume)
    neighbour, face, orient = neighbour.T, face.T, orient.T
    vmem = pl.BlockSpec(memory_space=pltpu.VMEM)
    smem = pl.BlockSpec(memory_space=pltpu.SMEM)
    hbm = pl.BlockSpec(memory_space=pltpu.HBM)
    anywhere = pl.BlockSpec(memory_space=pl.ANY)

    def call(kernel, name, outs, ins, out_specs, scratch, cost=None, alias=None):
        run = pl.pallas_call(
            kernel,
            out_shape=[
                held(x) if spec is vmem else far(x) if spec is hbm else x
                for x, spec in zip(outs, out_specs)
            ],
            in_specs=ins,
            out_specs=out_specs,
            scratch_shapes=scratch,
            compiler_params=pltpu.CompilerParams(vmem_limit_bytes=VMEM_MIB * 1024 * 1024),
            cost_estimate=cost,
            input_output_aliases=alias or {},
            name=name,
        )

        def keep(*operands):
            return run(
                *[
                    x
                    if spec not in (vmem, hbm)
                    else pltpu.with_memory_space_constraint(x, spec.memory_space)
                    for x, spec in zip(operands, ins)
                ]
            )

        return keep

    def shape(*dims):
        return jax.ShapeDtypeStruct(dims, jnp.float32)

    def held(x):
        return pltpu.VMEM(x.shape, x.dtype)

    def far(x):
        return pltpu.HBM(x.shape, x.dtype)

    def table(x):
        return pltpu.SMEM(x.shape, jnp.int32)

    def sems(count):
        return pltpu.SemaphoreType.DMA((count,))

    devices = blocks * halves
    sent, passed = shape(devices * SENT, LANES), shape(devices * PASSED, LANES)
    strip, rim = shape(CH, 64, LANES), shape(CH, 8, LANES)
    edge = shape(CH, 4 * every, LANES)
    edges = 1 if halves == 2 else 2
    square = held(shape(CH, LANES, LANES))
    tall = rows + 2 * PAD
    whole = shape(CH, every, tall, LANES)
    rows_about = shape(2, CH, every, 8, LANES)
    to_send, own, about, state, *halo = call(
        functools.partial(cut_kernel, halves),
        "cut",
        [sent, strip, rows_about, whole] + [edge] * edges,
        [hbm] * 8,
        [vmem] * (4 + edges),
        [
            square,
            held(shape(CH * 64, LANES)),
            table(placed),
            table(face),
            table(orient),
            sems(5 * PIECES),
            sems(3),
        ],
    )(*fields, placed, face, orient)

    def swap(x):
        shape = x.shape
        x = x.reshape(devices, 1, x.shape[0] * LANES // devices)
        x = lax.all_to_all(x, ("blk", "ij"), 0, 0, tiled=True)
        return x.reshape(shape)

    if edges == 1:
        below = above = lax.ppermute(halo[0], "ij", [(0, 1), (1, 0)])
    else:
        below = lax.ppermute(halo[1], "ij", [(i, i + 1) for i in range(halves - 1)])
        above = lax.ppermute(halo[0], "ij", [(i + 1, i) for i in range(halves - 1)])
    got = swap(to_send)

    padded = held(shape(CH, planes, tall, LANES))
    stage = [
        held(shape(8, tall, LANES)),
        padded,
        held(shape(4, planes, tall, LANES)),
        padded,
        padded,
    ]
    work = planes * rows * LANES
    cost = pl.CostEstimate(flops=300 * work, bytes_accessed=150 * work, transcendentals=work)
    route = jax.ShapeDtypeStruct((2 * blocks,), jnp.int32)
    state, route_out = call(
        first_kernel,
        "first_section",
        [whole, route],
        [vmem] + [hbm] * 4,
        [vmem, smem],
        stage + [table(x) for x in (placed, neighbour, face, orient, placed)] + [sems(4)],
        cost,
        {0: 0},
    )(state, placed, neighbour, face, orient)
    (relayed,) = call(
        functools.partial(relay_kernel, halves, rows, planes, devices),
        "relay",
        [passed],
        [anywhere, anywhere, vmem],
        [vmem],
        [
            held(shape(devices * 16, LANES)),
            held(shape(devices * 16, LANES)),
            held(shape(devices * 2, LANES)),
            table(route),
            sems(1),
        ],
    )(route_out, below, got)
    ghosts = swap(relayed)
    tiles = held(shape(CH, 2, every, 8, LANES))
    state, _, ends_base, ends_sec, inner = call(
        functools.partial(second_kernel, halves),
        "second_section",
        [whole, rows_about, rim, rim, shape(CH, 12 * every + 4, LANES)],
        [vmem] * 4 + [hbm] * 3 + [anywhere],
        [vmem] * 5,
        [tiles] * 3 + [square, held(shape(CH, planes, rows, LANES))] + stage + [sems(3)],
        cost,
        {0: 0, 1: 1},
    )(state, about, below, above, density, momentum, energy, relayed)
    flat = -(-CH * planes * 8 // LANES)
    return call(
        functools.partial(last_kernel, halves, rows, planes),
        "strips",
        [shape(*density.shape), shape(*momentum.shape), shape(*energy.shape)],
        [vmem] * 6,
        [hbm] * 3,
        [tiles] * 5
        + [
            held(shape(flat * LANES, LANES)),
            held(shape(flat, LANES, LANES)),
            held(shape(CH, planes, rows, LANES)),
            sems(3 * PIECES),
        ],
    )(own, ends_base, ends_sec, inner, ghosts, state)


def solution(mesh):
    return jax.shard_map(
        functools.partial(local, dict(mesh.shape)),
        mesh=mesh,
        in_specs=(
            P("blk", None, "ij", None),
            P("blk", None, None, "ij", None),
            P("blk", None, "ij", None),
            P("blk", None, "ij", None),
            P("blk", "ij", None),
            P(),
            P(),
            P(),
            P(),
        ),
        out_specs=(
            P("blk", None, "ij", None),
            P("blk", None, None, "ij", None),
            P("blk", None, "ij", None),
        ),
        check_vma=False,
    )
```

```python
import functools

import jax
import jax.numpy as jnp
from jax import lax
from jax.experimental import pallas as pl
from jax.experimental.pallas import tpu as pltpu
from jax.sharding import PartitionSpec as P

pressure_factor = 0.4
viscosity = 0.05
time_step = 0.03
unit = time_step / 12.0

LANES = 128
PAD = 8
PIECES = 4
DEPTH = 4
CH = 5
VMEM_MIB = 32
SENT = 2 * CH
PASSED = 2 * CH + 1
FIRST = 4


def turn(x, shift, axis):
    shift = shift % x.shape[axis]
    return x if shift == 0 else pltpu.roll(x, shift, axis)


def lanes_of(shape):
    return lax.broadcasted_iota(jnp.int32, shape, len(shape) - 1)


def rows_of(shape):
    return lax.broadcasted_iota(jnp.int32, shape, len(shape) - 2)


def point(f):
    rho, m1, m2, m3, e = f
    r = 1.0 / rho
    u1, u2, u3 = m1 * r, m2 * r, m3 * r
    kin = 0.5 * (m1 * u1 + m2 * u2 + m3 * u3)
    p = pressure_factor * (e - kin)
    return (u1, u2, u3, (kin + 2.0 * p) * r), p, e + p


def metric_terms(m):
    ax, ay, bx, by, v = m
    kv = viscosity * unit
    rw = kv * (ax * ax + ay * ay)
    cw = kv * (bx * bx + by * by)
    return v * ax, v * ay, v * bx, v * by, -unit / v, rw, cw, 30.0 * (rw + cw + kv)


def flux(f, w, p, h, gx, gy):
    rho, m1, m2, m3, _ = f
    u = gx * w[0] + gy * w[1]
    return (rho * u, m1 * u + gx * p, m2 * u + gy * p, m3 * u, h * u)


def flux_planes(f, w, p, h):
    u3 = w[2]
    return (f[3], f[1] * u3, f[2] * u3, f[3] * u3 + p, h * u3)


def slope(x, at):
    return 8.0 * (at(x, 1) - at(x, -1)) - (at(x, 2) - at(x, -2))


def curve(x, at):
    return 16.0 * (at(x, 1) + at(x, -1)) - (at(x, 2) + at(x, -2))


def along(axis):
    return lambda x, o: turn(x, -o, axis)


def within(lane, start, size):
    return (lane >= start) & (lane < start + size)


def roll_by(x, shift, axis=1):
    size = x.shape[axis]
    return pltpu.roll(x, lax.rem(shift + 4 * size, size), axis)


def across(x):
    if x.shape[0] < LANES:
        x = jnp.concatenate([x, jnp.zeros((LANES - x.shape[0], LANES), jnp.float32)], axis=0)
    return x.T


def loop(count, body, unroll=1):
    def step(n, _):
        body(n)
        return 0

    lax.fori_loop(0, count, step, 0, unroll=unroll)


def copy_all(pairs, sems, first=0):
    copies = [
        pltpu.make_async_copy(src, dst, sems.at[first + n]) for n, (src, dst) in enumerate(pairs)
    ]
    for copy in copies:
        copy.start()
    return copies


def state_pairs(fields, state, planes, start, size):
    dens, mom, en, met, vol = fields
    at, to = pl.ds(start, size), pl.ds(start + PAD, size)
    return [
        (dens.at[0, :, at], state.at[0, 0:planes, to]),
        (mom.at[0, :, :, at], state.at[1:4, 0:planes, to]),
        (en.at[0, :, at], state.at[4, 0:planes, to]),
        (met.at[0, :, at], state.at[0:4, planes, to]),
        (vol.at[0, at], state.at[4, planes, to]),
    ]


def arrive_in_pieces(fields, state, sems):
    planes, rows = fields[0].shape[1], fields[0].shape[2]
    size = max(8, rows // PIECES)
    for n in range(rows // size):
        copy_all(state_pairs(fields, state, planes, n * size, size), sems, 5 * n)

    def expect(start):
        @pl.when(lax.rem(start, size) == 0)
        def _():
            for n, (src, dst) in enumerate(state_pairs(fields, state, planes, start, size)):
                pltpu.make_async_copy(src, dst, sems.at[5 * (start // size) + n]).wait()

    return expect


def wait_all(copies):
    for copy in copies:
        copy.wait()


def tile_stage(planes, load, mets, shift_i, shift_j, hold, done):
    kv = viscosity * unit
    fk, ws, acc = hold

    def spread(k):
        for s in range(2):
            vax, vay, vbx, vby, niv, rw, cw, tw = mets[s]
            x = [load(c, s, k) for c in range(CH)]
            w, p, h = point(x)
            fi, fj = flux(x, w, p, h, vax, vay), flux(x, w, p, h, vbx, vby)
            for c in range(CH):
                val = niv * (slope(fi[c], shift_i(0, c, s, k)) + slope(fj[c], shift_j))
                if c > 0:
                    v = w[c - 1]
                    val = val + (
                        rw * curve(v, shift_i(1, c - 1, s, k)) + cw * curve(v, shift_j) - tw * v
                    )
                    ws[c - 1, s, k] = v
                acc[c, s, k] = x[c] + val
            for c, v in enumerate(flux_planes(x, w, p, h)):
                fk[c, s, k] = v

    def gather(k):
        at = {o: lax.rem(k + o + planes, planes) for o in (-2, -1, 0, 1, 2)}
        for s in range(2):
            for c in range(CH):
                val = acc[c, s, k] - unit * slope(0, lambda _, o: fk[c, s, at[o]])
                if c > 0:
                    val = val + kv * curve(0, lambda _, o: ws[c - 1, s, at[o]])
                done(c, s, k, val)

    loop(planes, spread)
    loop(planes, gather)


def cut_kernel(
    halves, dens, mom, en, met, vol, placed_at, face_at, orient_at, send, own, tall, state, *rest
):
    edges, rest = rest[: 1 if halves == 2 else 2], rest[1 if halves == 2 else 2 :]
    held_send, packed, strips, placed, face, orient, sems, table_sems, out_sems = rest
    tables = copy_all(
        [(placed_at, placed), (face_at, face), (orient_at, orient)], table_sems
    )
    planes, rows = dens.shape[1], dens.shape[2]
    expect = arrive_in_pieces((dens, mom, en, met, vol), state, sems)
    half = lax.axis_index("ij")
    lane = lanes_of((8, LANES))
    if rows < LANES:
        packed[...] = jnp.zeros(packed.shape, jnp.float32)
    def pack(r):
        expect(r)
        for c in range(CH):
            packs = jnp.zeros((8, LANES), jnp.float32)
            for k in range(planes + 1):
                x = turn(state[c, k, pl.ds(r + PAD, 8)], 8 * k + 4, 1)
                packs = jnp.where(within(lane, 8 * k, 8), x, packs)
            packed[c, pl.ds(r, 8)] = packs

    chunks(rows // 8, pack, unroll=2)

    def cut_ends(k):
        for c in range(CH):
            low, high = state[c, k, PAD : PAD + 4], state[c, k, PAD + rows - 4 : PAD + rows]
            tall[0, c, k, 4:8] = low
            tall[1, c, k, 0:4] = high
            if len(edges) == 1:
                edges[0][c, k * 4 : k * 4 + 4] = jnp.where(half == 0, high, low)
            else:
                edges[0][c, k * 4 : k * 4 + 4] = low
                edges[1][c, k * 4 : k * 4 + 4] = high

    for k in range(planes + 1):
        cut_ends(k)

    wait_all(tables)
    block = placed[lax.axis_index("blk")]
    row = rows_of((64, LANES))
    high_side = row % 8 < 4
    mirror = jnp.where(
        rows_of((LANES, LANES)) + lanes_of((LANES, LANES)) == rows - 1, 1.0, 0.0
    )
    flip = [jnp.where(orient[f, block] == 1, -1.0, 1.0) for f in range(2)]
    same = [jnp.where(face[f, block] == f, -1.0, 1.0) for f in range(2)]
    rising = [face[f, block] == 1 for f in range(2)]
    turned = jnp.where(high_side, flip[1], flip[0])
    facing = jnp.where(high_side, same[1], same[0])

    def orient_strip(c):
        strip = packed[c].T[0:64]
        own[c] = strip
        back = jnp.dot(
            strip,
            mirror,
            precision=lax.Precision.HIGHEST,
            preferred_element_type=jnp.float32,
        )
        moved = jnp.where(turned < 0.0, back, strip)
        sign = jnp.where(c < 2, turned, jnp.where(c < 4, facing, 1.0))
        moved = jnp.where(row >= planes * 8, moved * sign, moved)
        strips[pl.ds(pl.multiple_of(c * 64, 64), 64)] = moved

    loop(CH, orient_strip, unroll=CH)

    def put(n):
        k, e = n >> 2, n & 3
        at = (FIRST + n) * SENT
        low = k * 8 + 4 + jnp.where(rising[0], e, 3 - e)
        high = k * 8 + jnp.where(rising[1], 3 - e, e)
        held_send[pl.ds(at, CH)] = strips[pl.ds(low, CH, stride=64)]
        held_send[pl.ds(at + CH, CH)] = strips[pl.ds(high, CH, stride=64)]

    loop(DEPTH * (planes + 1), put, unroll=4)
    wait_all(copy_all([(held_send, send)], out_sems))


def relay_kernel(
    halves, rows, planes, devices, route_at, halo, held_got, send,
    held_send, below, above, signs, route, sems,
):
    del halo
    wait_all(copy_all([(route_at, route)], sems, 1))
    me = lax.axis_index("blk") * halves + lax.axis_index("ij")
    is_field = (me >= FIRST) & (me < FIRST + DEPTH * planes)

    def pass_on(slot):
        for f in range(2):
            code = route[2 * slot + f]
            partner, side, turned = code >> 2, (code >> 1) & 1, code & 1
            sign = jnp.where(turned == 1, -1.0, 1.0)

            def piece(h):
                h = jnp.where(turned == 1, halves - 1 - h, h)
                return held_got[pl.ds((partner * halves + h) * SENT + side * CH, CH)]

            pieces = [piece(h) for h in range(halves)]
            for half in range(halves):
                at = slot * halves + half
                held_send[pl.ds(at * PASSED + f * CH, CH)] = pieces[half]
                below[pl.ds((f * devices + at) * 8, CH)] = pieces[max(half - 1, 0)]
                above[pl.ds((f * devices + at) * 8, CH)] = pieces[min(half + 1, halves - 1)]
                signs[pl.ds(f * devices + at, 1)] = jnp.full((1, LANES), sign, jnp.float32)

    loop(devices // halves, pass_on, unroll=4)
    count = 2 * devices
    lane = lanes_of((count, LANES))
    half = rows_of((count, LANES)) % halves
    sign = signs[...]
    ends = jnp.zeros((count, LANES), jnp.float32)
    for c in range(CH):
        low, high = below[pl.ds(c, count, stride=8)], above[pl.ds(c, count, stride=8)]
        at = 4 * c
        low_wall = jnp.where(lane == at, turn(low, at - 1, 1), turn(low, at + 1, 1))
        high_wall = jnp.where(
            lane == at + 2, turn(high, at + 3 - rows, 1), turn(high, at + 5 - rows, 1)
        )
        if 1 <= c <= 3:
            low_wall = jnp.where(is_field, -sign * low_wall, low_wall)
            high_wall = jnp.where(is_field, sign * high_wall, high_wall)
        low = jnp.where(half == 0, low_wall, turn(low, at + 2 - rows, 1))
        high = jnp.where(half == halves - 1, high_wall, turn(high, at + 2, 1))
        ends = jnp.where(within(lane, at, 2), low, jnp.where(within(lane, at + 2, 2), high, ends))
    held_send[pl.ds(2 * CH, devices, stride=PASSED)] = ends[0:devices] + turn(
        ends[devices:], 4 * CH, 1
    )
    wait_all(copy_all([(held_send, send)], sems))


def flux_chunk(get, mets, fi, w, fk, acc, r):
    rows = pl.ds(r, 8)
    vax, vay, vbx, vby, niv, rw, cw, tw = [mets[j, rows] for j in range(8)]
    at_j = along(1)
    for k in range(fi.shape[1]):
        f = [get(c, k, r) for c in range(CH)]
        wk, p, h = point(f)
        for c, x in enumerate(flux(f, wk, p, h, vax, vay)):
            fi[c, k, rows] = x
        for c in range(4):
            w[c, k, rows] = wk[c]
        fj = flux(f, wk, p, h, vbx, vby)
        for c in range(CH):
            val = niv * slope(fj[c], at_j)
            if c > 0:
                val = val + (cw * curve(wk[c - 1], at_j) - tw * wk[c - 1])
            acc[c, k, rows] = val
        for c, x in enumerate(flux_planes(f, wk, p, h)):
            fk[c, k, rows] = x


def sum_chunk(mets, fi, w, fk, acc, r, emit):
    planes = fi.shape[1]
    kv = viscosity * unit
    rows = pl.ds(r, 8)
    niv, rw = mets[4, rows], mets[5, rows]
    for c in range(CH):
        t = [fk[c, k, rows] for k in range(planes)]
        x = [w[c - 1, k, rows] for k in range(planes)] if c > 0 else None
        for k in range(planes):

            def near(v, o):
                return v[(k + o) % planes]

            def at_i(v, o):
                return v[pl.ds(r + o, 8)]

            val = acc[c, k, rows] + niv * slope(fi.at[c, k], at_i) - unit * slope(t, near)
            if c > 0:
                val = val + (rw * curve(w.at[c - 1, k], at_i) + kv * curve(x, near))
            emit(c, k, r, val)


def chunks(count, body, unroll=1):
    def step(n, _):
        body(pl.multiple_of(n * 8, 8))
        return 0

    lax.fori_loop(0, count, step, 0, unroll=unroll)


def first_kernel(
    state_in, placed_at, neighbour_at, face_at, orient_at, state, route,
    mets, fi, w, fk, acc, placed, neighbour, face, orient, where_is, sems,
):
    del state_in
    planes, rows = fi.shape[1], fi.shape[2] - 2 * PAD
    pairs = zip((placed_at, neighbour_at, face_at, orient_at), (placed, neighbour, face, orient))
    tables = copy_all(list(pairs), sems)
    count = rows // 8
    blocks = placed.shape[0]
    share = -(-blocks // count)

    def slots(n):
        return [jnp.minimum((n // 8) * share + i, blocks - 1) for i in range(share)]

    def get(c, k, r):
        return state[c, k, pl.ds(r, 8)]

    def fluxes(n):
        at = pl.ds(n + PAD, 8)
        for j, x in enumerate(metric_terms([state[c, planes, at] for c in range(CH)])):
            mets[j, at] = x
        flux_chunk(get, mets, fi, w, fk, acc, n + PAD)

    def emit(c, k, r, val):
        state[c, k, pl.ds(r, 8)] = get(c, k, r) + val

    def sums(n):
        for slot in slots(n):
            block = placed[slot]
            for f in range(2):
                partner = where_is[neighbour[f, block]]
                route[2 * slot + f] = partner * 4 + face[f, block] * 2 + orient[f, block]
        sum_chunk(mets, fi, w, fk, acc, n + PAD, emit)

    def note(slot):
        where_is[placed[slot]] = slot

    chunks(count, fluxes, unroll=2)
    wait_all(tables)
    loop(blocks, note, unroll=8)
    chunks(count, sums, unroll=2)


def pack_ends(tall, planes):
    sub, lane = rows_of((8, LANES)), lanes_of((8, LANES))
    stacked = []
    for c in range(CH):
        packed = jnp.zeros((8, LANES), jnp.float32)
        for k in range(planes):
            x = turn(jnp.where(sub < 4, tall[0, c, k], tall[1, c, k]), 8 * k + 4, 1)
            packed = jnp.where(within(lane, 8 * k, 8), x, packed)
        stacked.append(packed)
    ends = across(jnp.concatenate(stacked, axis=0))
    out = []
    for c in range(CH):
        packed = jnp.zeros((8, LANES), jnp.float32)
        for k in range(planes):
            x = turn(ends[k * 8 : k * 8 + 8], 4 * k - (8 * c + 2), 1)
            packed = jnp.where(within(lane, 4 * k, 4), x, packed)
        out.append(packed)
    return out


def ends_kernel(
    halves, state_in, tall_in, low, high, after, state, tall, ends_base, ends_sec, inner,
    tile_fk, tile_w, tile_acc, packed, rims, sems,
):
    del state_in, tall_in, after
    planes, rows = tall.shape[2] - 1, state.shape[2] - 2 * PAD
    every = planes + 1
    half = lax.axis_index("ij")
    low_wall, high_wall = half == 0, half == halves - 1
    low_flag, high_flag = jnp.where(low_wall, 1, 0), jnp.where(high_wall, 1, 0)
    sub, lane = rows_of((8, LANES)), lanes_of((8, LANES))
    top = PAD + rows

    @pl.when(low_wall)
    def _():
        for c in range(CH):
            for k in range(every):
                for n in range(2):
                    x = tall[0, c, k, 4 + n : 5 + n]
                    tall[0, c, k, 3 - n : 4 - n] = -x if 1 <= c <= 3 and k < planes else x

    @pl.when(jnp.logical_not(low_wall))
    def _():
        for c in range(CH):
            for k in range(every):
                tall[0, c, k, 0:4] = low[c, 4 * k : 4 * k + 4]

    @pl.when(high_wall)
    def _():
        for c in range(CH):
            for k in range(every):
                for n in range(2):
                    tall[1, c, k, 4 + n : 5 + n] = tall[1, c, k, 3 - n : 4 - n]

    @pl.when(jnp.logical_not(high_wall))
    def _():
        for c in range(CH):
            for k in range(every):
                tall[1, c, k, 4:8] = high[c, 4 * k : 4 * k + 4]

    for c, x in enumerate(pack_ends(tall, every)):
        ends_base[c] = x
    for c in range(CH):
        state[c, planes, PAD - 4 : PAD] = tall[0, c, planes, 0:4]
        state[c, planes, top : top + 4] = tall[1, c, planes, 4:8]
    mets = [metric_terms([tall[s, c, planes] for c in range(CH)]) for s in range(2)]

    def done(c, s, k, x):
        tall[s, c, k] = x
        if s == 0:
            sign = -1.0 if 1 <= c <= 3 else 1.0
            wall = sign * jnp.where(sub == 2, turn(x, -3, 0), turn(x, -1, 0))
            x = jnp.where((sub < 4) & (low_flag == 1), wall, x)
        else:
            wall = jnp.where(sub == 4, turn(x, 1, 0), turn(x, 3, 0))
            x = jnp.where((sub >= 4) & (high_flag == 1), wall, x)
        start = PAD - 2 if s == 0 else top - 2
        state[c, k, start : start + 4] = x[2:6]

    tile_stage(
        planes, lambda c, s, k: tall[s, c, k], mets, lambda *_: along(0), along(1),
        (tile_fk, tile_w, tile_acc), done,
    )
    for c, x in enumerate(pack_ends(tall, planes)):
        rims[c] = x
    leaving = copy_all([(rims, ends_sec)], sems)

    if rows < LANES:
        packed[...] = jnp.zeros(packed.shape, jnp.float32)

    def pack(n):
        at = pl.ds(n + PAD, 8)
        for c in range(CH):
            packs = turn(state[c, planes, at], 12 * planes + 6, 1)
            for k in range(planes):
                x = turn(state[c, k, at], 12 * k + 6, 1)
                packs = jnp.where(within(lane, 12 * k, 12), x, packs)
            packed[c, pl.ds(n, 8)] = packs

    chunks(rows // 8, pack, unroll=2)
    for c in range(CH):
        inner[c] = packed[c].T[0 : inner.shape[1]]
    wait_all(leaving)


def second_kernel(
    state_in, dens, mom, en, state, fields, mets, fi, w, fk, acc, sems
):
    del state_in
    planes, rows = fields.shape[1:3]
    pairs = [(dens.at[0], fields.at[0]), (mom.at[0], fields.at[1:4]), (en.at[0], fields.at[4])]
    copies = copy_all(pairs, sems)

    def get(c, k, r):
        return state[c, k, pl.ds(r, 8)]

    def fluxes(n):
        at = pl.ds(n, 8)
        for j, x in enumerate(metric_terms([state[c, planes, at] for c in range(CH)])):
            mets[j, at] = x
        flux_chunk(get, mets, fi, w, fk, acc, n)

    def emit(c, k, r, val):
        x = 0.5 * (fields[c, k, pl.ds(r - PAD, 8)] + (get(c, k, r) + val))
        state[c, k, pl.ds(r, 8)] = x

    chunks(rows // 8 + 2, fluxes, unroll=2)
    wait_all(copies)
    chunks(rows // 8, lambda n: sum_chunk(mets, fi, w, fk, acc, n + PAD, emit), unroll=2)


def beyond(packed, f, k, rows):
    base = 28 * f + 4 * k
    low = roll_by(packed, LANES - 2 - base)
    top = rows % LANES
    high = low if top == 0 else roll_by(packed, top - 2 - base)
    lane = lanes_of(packed.shape)

    def at(x, o):
        if o < 0:
            x = jnp.where(lane >= LANES + o, low, x)
        else:
            x = jnp.where(within(lane, top, o), high, x)
        return turn(x, -o, 1)

    return at


def last_kernel(
    halves, rows, planes, own, ends_base, ends_sec_at, inner, got, out,
    next_dens, next_mom, next_en,
    base, sec, fk, ws, acc, turned, back, full, ends_sec, sems,
):
    late = copy_all([(ends_sec_at, ends_sec)], sems, 3 * PIECES)
    half = lax.axis_index("ij")
    low_wall, high_wall = half == 0, half == halves - 1
    sub, lane = rows_of((8, LANES)), lanes_of((8, LANES))

    def mix(f, mine, others):
        return jnp.where((sub < 4) == (f == 1), mine, others)

    others = [jnp.zeros((8, LANES), jnp.float32)] * CH
    for k in range(planes + 1):
        start = DEPTH * k * PASSED
        for f in range(2):

            def ghost(row):
                x = got[pl.ds(start + row, 8, stride=PASSED)]
                return x if f == 1 else turn(x, 4, 0)

            arrived = ghost(2 * CH)
            to = 28 * f + 4 * k
            for c in range(CH):
                base[c, f, k] = mix(f, own[c, k * 8 : k * 8 + 8], ghost(f * CH + c))
                moved = turn(arrived, to - 4 * CH * f - 4 * c, 1)
                others[c] = jnp.where(within(lane, to, 4), moved, others[c])

    low_lanes = lane < 28
    twice = [jnp.where(low_lanes, ends_base[c], turn(ends_base[c], 28, 1)) for c in range(CH)]
    ends = [jnp.where(low_lanes == (sub >= 4), twice[c], others[c]) for c in range(CH)]
    slot = jnp.where(low_lanes, lane, lane - 28)

    def spread(x):
        y = x
        for k in range(planes):
            y = jnp.where(within(slot, 4 * k, 4), turn(x, 4 * (k - planes), 1), y)
        return y

    vax, vay, vbx, vby, niv, _, cw, _ = [spread(x) for x in metric_terms(ends)]
    wrapped = [spread(x) for x in metric_terms(twice)[2:4]]

    def keep(c, f, k, val):
        sec[c, f, k] = val

    def stage(held, ends, gx, gy):
        mets = [metric_terms([held[c, f, planes] for c in range(CH)]) for f in range(2)]
        w, p, h = point(ends)
        rims = (flux(ends, w, p, h, gx, gy), w)
        tile_stage(
            planes,
            lambda c, f, k: held[c, f, k],
            mets,
            lambda kind, c, f, k: beyond(rims[kind][c], f, k, rows),
            along(0),
            (fk, ws, acc),
            keep,
        )

    stage(base, ends, vax, vay)
    wait_all(late)

    def move(k, source):
        for c in range(CH):
            at = 12 * k
            mine = jnp.where(sub < 4, inner[c, at : at + 8], inner[c, at + 4 : at + 12])
            for f in range(2):
                sec[c, f, k] = mix(f, mine, turn(source[c, f, k], 2 if f == 1 else -2, 0))

    for k in range(planes):
        move(k, sec)
    move(planes, base)

    def shifted(x):
        return jnp.where(low_lanes, turn(x, -2, 0), turn(x, 2, 0))

    w1, p1, h1 = point(ends)
    w0, p0, h0 = point(twice)
    new, old = flux(ends, w1, p1, h1, vbx, vby), flux(twice, w0, p0, h0, *wrapped)
    at_j = along(0)
    touched = within(sub, jnp.where(low_lanes, 4, 2), 2)
    second = []
    for c in range(CH):
        add = niv * slope(new[c] - old[c], at_j)
        if c > 0:
            add = add + cw * curve(w1[c - 1] - w0[c - 1], at_j)
        x = jnp.where(low_lanes, ends_sec[c], turn(ends_sec[c], 28, 1))
        second.append(shifted(x + jnp.where(touched, add, 0.0)))
    walled = low_wall | high_wall

    for k in range(planes):
        for f in range(2):
            to = 28 * f + 4 * k
            first = jnp.where(walled, jnp.where(low_wall, to, to + 2), -8)
            shift = jnp.where(low_wall, (to - 1) % LANES, (to + 3 - rows) % LANES)
            next_shift = jnp.where(low_wall, (to + 1) % LANES, (to + 5 - rows) % LANES)
            for c in range(CH):
                x = sec[c, f, k]
                one, two = pltpu.roll(x, shift, 1), pltpu.roll(x, next_shift, 1)
                x = jnp.where(lane == first, one, two)
                if 1 <= c <= 3:
                    x = jnp.where(low_wall, -1.0, 1.0) * x
                second[c] = jnp.where(within(lane, first, 2), x, second[c])
    stage(sec, second, shifted(vax), shifted(vay))

    per = LANES // 8

    for k in range(planes):
        for c in range(CH):
            x = jnp.where(sub < 4, turn(sec[c, 1, k], -2, 0), turn(sec[c, 0, k], 2, 0))
            at = (c * planes + k) * 8
            turned[at : at + 8] = 0.5 * (own[c, k * 8 : k * 8 + 8] + x)
    for n in range(turned.shape[0] // LANES):
        back[n] = turned[n * LANES : (n + 1) * LANES].T
    inside = within(lane, 4, LANES - 8)
    size = max(8, rows // PIECES)

    def leave(start):
        at = pl.ds(start, size)
        targets = [next_dens.at[0, :, at], next_en.at[0, :, at], next_mom.at[0, :, :, at]]
        sources = [full.at[0, :, at], full.at[4, :, at], full.at[1:4, :, at]]
        first = 3 * (start // size)
        return [
            pltpu.make_async_copy(src, dst, sems.at[first + n])
            for n, (src, dst) in enumerate(zip(sources, targets))
        ]

    def merge(r):
        at = pl.ds(r, 8)
        for c in range(CH):
            for k in range(planes):
                index = c * planes + k
                moved = turn(back[index // per, at], LANES - 4 - 8 * (index % per), 1)
                full[c, k, at] = jnp.where(inside, out[c, k, pl.ds(r + PAD, 8)], moved)

        @pl.when(lax.rem(r + 8, size) == 0)
        def _():
            for copy in leave(pl.multiple_of(r + 8 - size, 8)):
                copy.start()

    chunks(rows // 8, merge, unroll=2)
    for n in range(rows // size):
        wait_all(leave(n * size))


def local(mesh_shape, density, momentum, energy, metrics, volume, placed, neighbour, face, orient):
    halves = mesh_shape["ij"]
    blocks = mesh_shape["blk"]
    planes, rows = density.shape[1], density.shape[2]
    every = planes + 1
    fields = (density, momentum, energy, metrics, volume)
    neighbour, face, orient = neighbour.T, face.T, orient.T
    vmem = pl.BlockSpec(memory_space=pltpu.VMEM)
    smem = pl.BlockSpec(memory_space=pltpu.SMEM)
    hbm = pl.BlockSpec(memory_space=pltpu.HBM)
    anywhere = pl.BlockSpec(memory_space=pl.ANY)

    def call(kernel, name, outs, ins, out_specs, scratch, cost=None, alias=None):
        run = pl.pallas_call(
            kernel,
            out_shape=[
                held(x) if spec is vmem else far(x) if spec is hbm else x
                for x, spec in zip(outs, out_specs)
            ],
            in_specs=ins,
            out_specs=out_specs,
            scratch_shapes=scratch,
            compiler_params=pltpu.CompilerParams(vmem_limit_bytes=VMEM_MIB * 1024 * 1024),
            cost_estimate=cost,
            input_output_aliases=alias or {},
            name=name,
        )

        def keep(*operands):
            return run(
                *[
                    x
                    if spec not in (vmem, hbm)
                    else pltpu.with_memory_space_constraint(x, spec.memory_space)
                    for x, spec in zip(operands, ins)
                ]
            )

        return keep

    def shape(*dims):
        return jax.ShapeDtypeStruct(dims, jnp.float32)

    def held(x):
        return pltpu.VMEM(x.shape, x.dtype)

    def far(x):
        return pltpu.HBM(x.shape, x.dtype)

    def table(x):
        return pltpu.SMEM(x.shape, jnp.int32)

    def sems(count):
        return pltpu.SemaphoreType.DMA((count,))

    devices = blocks * halves
    sent, passed = shape(devices * SENT, LANES), shape(devices * PASSED, LANES)
    strip, rim = shape(CH, 64, LANES), shape(CH, 8, LANES)
    edge = shape(CH, 4 * every, LANES)
    edges = 1 if halves == 2 else 2
    square = held(shape(CH, LANES, LANES))
    tall = rows + 2 * PAD
    whole = shape(CH, every, tall, LANES)
    rows_about = shape(2, CH, every, 8, LANES)
    to_send, own, about, state, *halo = call(
        functools.partial(cut_kernel, halves),
        "cut",
        [sent, strip, rows_about, whole] + [edge] * edges,
        [hbm] * 8,
        [hbm] + [vmem] * (3 + edges),
        [
            held(sent),
            square,
            held(shape(CH * 64, LANES)),
            table(placed),
            table(face),
            table(orient),
            sems(5 * PIECES),
            sems(3),
            sems(1),
        ],
    )(*fields, placed, face, orient)

    def swap(x):
        x = x.reshape(devices, x.shape[0] // devices, 1, LANES)
        x = lax.all_to_all(x, ("blk", "ij"), 0, 0, tiled=True)
        return x.reshape(x.shape[0] * x.shape[1], LANES)

    if edges == 1:
        below = above = lax.ppermute(halo[0], "ij", [(0, 1), (1, 0)])
    else:
        below = lax.ppermute(halo[1], "ij", [(i, i + 1) for i in range(halves - 1)])
        above = lax.ppermute(halo[0], "ij", [(i + 1, i) for i in range(halves - 1)])
    got = swap(to_send)

    padded = held(shape(CH, planes, tall, LANES))
    stage = [
        held(shape(8, tall, LANES)),
        padded,
        held(shape(4, planes, tall, LANES)),
        padded,
        padded,
    ]
    work = planes * rows * LANES
    cost = pl.CostEstimate(flops=300 * work, bytes_accessed=150 * work, transcendentals=work)
    route = jax.ShapeDtypeStruct((2 * blocks,), jnp.int32)
    state, route_out = call(
        first_kernel,
        "first_section",
        [whole, route],
        [vmem] + [hbm] * 4,
        [vmem, smem],
        stage + [table(x) for x in (placed, neighbour, face, orient, placed)] + [sems(4)],
        cost,
        {0: 0},
    )(state, placed, neighbour, face, orient)
    (relayed,) = call(
        functools.partial(relay_kernel, halves, rows, planes, devices),
        "relay",
        [passed],
        [anywhere, anywhere, vmem],
        [hbm],
        [
            held(passed),
            held(shape(devices * 16, LANES)),
            held(shape(devices * 16, LANES)),
            held(shape(devices * 2, LANES)),
            table(route),
            sems(2),
        ],
    )(route_out, below, got)
    ghosts = swap(relayed)
    tiles = held(shape(CH, 2, every, 8, LANES))
    state, _, ends_base, ends_sec, inner = call(
        functools.partial(ends_kernel, halves),
        "ends",
        [whole, rows_about, rim, rim, shape(CH, 12 * every + 4, LANES)],
        [vmem] * 4 + [hbm],
        [vmem] * 3 + [hbm, vmem],
        [tiles] * 3 + [square, held(rim), sems(1)],
        cost,
        {0: 0, 1: 1},
    )(state, about, below, above, relayed)
    (state,) = call(
        second_kernel,
        "second_section",
        [whole],
        [vmem] + [hbm] * 3,
        [vmem],
        [held(shape(CH, planes, rows, LANES))] + stage + [sems(3)],
        cost,
        {0: 0},
    )(state, density, momentum, energy)
    flat = -(-CH * planes * 8 // LANES)
    return call(
        functools.partial(last_kernel, halves, rows, planes),
        "strips",
        [shape(*density.shape), shape(*momentum.shape), shape(*energy.shape)],
        [vmem] * 2 + [hbm] + [vmem] * 3,
        [hbm] * 3,
        [tiles] * 5
        + [
            held(shape(flat * LANES, LANES)),
            held(shape(flat, LANES, LANES)),
            held(shape(CH, planes, rows, LANES)),
            held(rim),
            sems(3 * PIECES + 1),
        ],
    )(own, ends_base, ends_sec, inner, ghosts, state)


def solution(mesh):
    return jax.shard_map(
        functools.partial(local, dict(mesh.shape)),
        mesh=mesh,
        in_specs=(
            P("blk", None, "ij", None),
            P("blk", None, None, "ij", None),
            P("blk", None, "ij", None),
            P("blk", None, "ij", None),
            P("blk", "ij", None),
            P(),
            P(),
            P(),
            P(),
        ),
        out_specs=(
            P("blk", None, "ij", None),
            P("blk", None, None, "ij", None),
            P("blk", None, "ij", None),
        ),
        check_vma=False,
    )
```

```python
import functools

import jax
import jax.numpy as jnp
from jax import lax
from jax.experimental import pallas as pl
from jax.experimental.pallas import tpu as pltpu
from jax.sharding import PartitionSpec as P

pressure_factor = 0.4
viscosity = 0.05
time_step = 0.03
unit = time_step / 12.0

LANES = 128
PAD = 8
PIECES = 4
DEPTH = 4
CH = 5
VMEM_MIB = 32
SENT = 2 * CH
PASSED = 2 * CH + 1
FIRST = 4


def turn(x, shift, axis):
    shift = shift % x.shape[axis]
    return x if shift == 0 else pltpu.roll(x, shift, axis)


def lanes_of(shape):
    return lax.broadcasted_iota(jnp.int32, shape, len(shape) - 1)


def rows_of(shape):
    return lax.broadcasted_iota(jnp.int32, shape, len(shape) - 2)


def point(f):
    rho, m1, m2, m3, e = f
    r = 1.0 / rho
    u1, u2, u3 = m1 * r, m2 * r, m3 * r
    kin = 0.5 * (m1 * u1 + m2 * u2 + m3 * u3)
    p = pressure_factor * (e - kin)
    return (u1, u2, u3, (kin + 2.0 * p) * r), p, e + p


def metric_terms(m):
    ax, ay, bx, by, v = m
    kv = viscosity * unit
    rw = kv * (ax * ax + ay * ay)
    cw = kv * (bx * bx + by * by)
    return v * ax, v * ay, v * bx, v * by, -unit / v, rw, cw, 30.0 * (rw + cw + kv)


def flux(f, w, p, h, gx, gy):
    rho, m1, m2, m3, _ = f
    u = gx * w[0] + gy * w[1]
    return (rho * u, m1 * u + gx * p, m2 * u + gy * p, m3 * u, h * u)


def flux_planes(f, w, p, h):
    u3 = w[2]
    return (f[3], f[1] * u3, f[2] * u3, f[3] * u3 + p, h * u3)


def slope(x, at):
    return 8.0 * (at(x, 1) - at(x, -1)) - (at(x, 2) - at(x, -2))


def curve(x, at):
    return 16.0 * (at(x, 1) + at(x, -1)) - (at(x, 2) + at(x, -2))


def along(axis):
    return lambda x, o: turn(x, -o, axis)


def within(lane, start, size):
    return (lane >= start) & (lane < start + size)


def roll_by(x, shift, axis=1):
    size = x.shape[axis]
    return pltpu.roll(x, lax.rem(shift + 4 * size, size), axis)


def across(x):
    if x.shape[0] < LANES:
        x = jnp.concatenate([x, jnp.zeros((LANES - x.shape[0], LANES), jnp.float32)], axis=0)
    return x.T


def loop(count, body, unroll=1):
    def step(n, _):
        body(n)
        return 0

    lax.fori_loop(0, count, step, 0, unroll=unroll)


def copy_all(pairs, sems, first=0):
    copies = [
        pltpu.make_async_copy(src, dst, sems.at[first + n]) for n, (src, dst) in enumerate(pairs)
    ]
    for copy in copies:
        copy.start()
    return copies


def state_pairs(fields, state, planes, start, size):
    dens, mom, en, met, vol = fields
    at, to = pl.ds(start, size), pl.ds(start + PAD, size)
    return [
        (dens.at[0, :, at], state.at[0, 0:planes, to]),
        (mom.at[0, :, :, at], state.at[1:4, 0:planes, to]),
        (en.at[0, :, at], state.at[4, 0:planes, to]),
        (met.at[0, :, at], state.at[0:4, planes, to]),
        (vol.at[0, at], state.at[4, planes, to]),
    ]


def arrive_in_pieces(fields, state, sems):
    planes, rows = fields[0].shape[1], fields[0].shape[2]
    size = max(8, rows // PIECES)
    for n in range(rows // size):
        copy_all(state_pairs(fields, state, planes, n * size, size), sems, 5 * n)

    def expect(start):
        @pl.when(lax.rem(start, size) == 0)
        def _():
            for n, (src, dst) in enumerate(state_pairs(fields, state, planes, start, size)):
                pltpu.make_async_copy(src, dst, sems.at[5 * (start // size) + n]).wait()

    return expect


def wait_all(copies):
    for copy in copies:
        copy.wait()


def tile_stage(planes, load, mets, shift_i, shift_j, hold, done):
    kv = viscosity * unit
    fk, ws, acc = hold

    def spread(k):
        for s in range(2):
            vax, vay, vbx, vby, niv, rw, cw, tw = mets[s]
            x = [load(c, s, k) for c in range(CH)]
            w, p, h = point(x)
            fi, fj = flux(x, w, p, h, vax, vay), flux(x, w, p, h, vbx, vby)
            for c in range(CH):
                val = niv * (slope(fi[c], shift_i(0, c, s, k)) + slope(fj[c], shift_j))
                if c > 0:
                    v = w[c - 1]
                    val = val + (
                        rw * curve(v, shift_i(1, c - 1, s, k)) + cw * curve(v, shift_j) - tw * v
                    )
                    ws[c - 1, s, k] = v
                acc[c, s, k] = x[c] + val
            for c, v in enumerate(flux_planes(x, w, p, h)):
                fk[c, s, k] = v

    def gather(k):
        at = {o: lax.rem(k + o + planes, planes) for o in (-2, -1, 0, 1, 2)}
        for s in range(2):
            for c in range(CH):
                val = acc[c, s, k] - unit * slope(0, lambda _, o: fk[c, s, at[o]])
                if c > 0:
                    val = val + kv * curve(0, lambda _, o: ws[c - 1, s, at[o]])
                done(c, s, k, val)

    loop(planes, spread)
    loop(planes, gather)


def cut_kernel(
    halves, dens, mom, en, met, vol, placed_at, face_at, orient_at, send, own, tall, state, *rest
):
    edges, rest = rest[: 1 if halves == 2 else 2], rest[1 if halves == 2 else 2 :]
    held_send, packed, strips, placed, face, orient, sems, table_sems, out_sems = rest
    tables = copy_all(
        [(placed_at, placed), (face_at, face), (orient_at, orient)], table_sems
    )
    planes, rows = dens.shape[1], dens.shape[2]
    expect = arrive_in_pieces((dens, mom, en, met, vol), state, sems)
    half = lax.axis_index("ij")
    lane = lanes_of((8, LANES))
    if rows < LANES:
        packed[...] = jnp.zeros(packed.shape, jnp.float32)
    def pack(r):
        expect(r)
        for c in range(CH):
            packs = jnp.zeros((8, LANES), jnp.float32)
            for k in range(planes + 1):
                x = turn(state[c, k, pl.ds(r + PAD, 8)], 8 * k + 4, 1)
                packs = jnp.where(within(lane, 8 * k, 8), x, packs)
            packed[c, pl.ds(r, 8)] = packs

    chunks(rows // 8, pack, unroll=2)

    def cut_ends(k):
        for c in range(CH):
            low, high = state[c, k, PAD : PAD + 4], state[c, k, PAD + rows - 4 : PAD + rows]
            tall[0, c, k, 4:8] = low
            tall[1, c, k, 0:4] = high
            if len(edges) == 1:
                edges[0][c, k * 4 : k * 4 + 4] = jnp.where(half == 0, high, low)
            else:
                edges[0][c, k * 4 : k * 4 + 4] = low
                edges[1][c, k * 4 : k * 4 + 4] = high

    for k in range(planes + 1):
        cut_ends(k)

    wait_all(tables)
    block = placed[lax.axis_index("blk")]
    row = rows_of((64, LANES))
    high_side = row % 8 < 4
    mirror = jnp.where(
        rows_of((LANES, LANES)) + lanes_of((LANES, LANES)) == rows - 1, 1.0, 0.0
    )
    flip = [jnp.where(orient[f, block] == 1, -1.0, 1.0) for f in range(2)]
    same = [jnp.where(face[f, block] == f, -1.0, 1.0) for f in range(2)]
    rising = [face[f, block] == 1 for f in range(2)]
    turned = jnp.where(high_side, flip[1], flip[0])
    facing = jnp.where(high_side, same[1], same[0])

    def orient_strip(c):
        strip = packed[c].T[0:64]
        own[c] = strip
        back = jnp.dot(
            strip,
            mirror,
            precision=lax.Precision.HIGHEST,
            preferred_element_type=jnp.float32,
        )
        moved = jnp.where(turned < 0.0, back, strip)
        sign = jnp.where(c < 2, turned, jnp.where(c < 4, facing, 1.0))
        moved = jnp.where(row >= planes * 8, moved * sign, moved)
        strips[pl.ds(pl.multiple_of(c * 64, 64), 64)] = moved

    loop(CH, orient_strip, unroll=CH)

    def put(n):
        k, e = n >> 2, n & 3
        at = (FIRST + n) * SENT
        low = k * 8 + 4 + jnp.where(rising[0], e, 3 - e)
        high = k * 8 + jnp.where(rising[1], 3 - e, e)
        held_send[pl.ds(at, CH)] = strips[pl.ds(low, CH, stride=64)]
        held_send[pl.ds(at + CH, CH)] = strips[pl.ds(high, CH, stride=64)]

    loop(DEPTH * (planes + 1), put, unroll=4)
    wait_all(copy_all([(held_send, send)], out_sems))


def relay_kernel(
    halves, rows, planes, devices, route_at, halo, held_got, send,
    held_send, below, above, signs, route, sems,
):
    del halo
    wait_all(copy_all([(route_at, route)], sems, 1))
    me = lax.axis_index("blk") * halves + lax.axis_index("ij")
    is_field = (me >= FIRST) & (me < FIRST + DEPTH * planes)

    def pass_on(slot):
        for f in range(2):
            code = route[2 * slot + f]
            partner, side, turned = code >> 2, (code >> 1) & 1, code & 1
            sign = jnp.where(turned == 1, -1.0, 1.0)

            def piece(h):
                h = jnp.where(turned == 1, halves - 1 - h, h)
                return held_got[pl.ds((partner * halves + h) * SENT + side * CH, CH)]

            pieces = [piece(h) for h in range(halves)]
            for half in range(halves):
                at = slot * halves + half
                held_send[pl.ds(at * PASSED + f * CH, CH)] = pieces[half]
                below[pl.ds((f * devices + at) * 8, CH)] = pieces[max(half - 1, 0)]
                above[pl.ds((f * devices + at) * 8, CH)] = pieces[min(half + 1, halves - 1)]
                signs[pl.ds(f * devices + at, 1)] = jnp.full((1, LANES), sign, jnp.float32)

    loop(devices // halves, pass_on, unroll=4)
    count = 2 * devices
    lane = lanes_of((count, LANES))
    half = rows_of((count, LANES)) % halves
    sign = signs[...]
    ends = jnp.zeros((count, LANES), jnp.float32)
    for c in range(CH):
        low, high = below[pl.ds(c, count, stride=8)], above[pl.ds(c, count, stride=8)]
        at = 4 * c
        low_wall = jnp.where(lane == at, turn(low, at - 1, 1), turn(low, at + 1, 1))
        high_wall = jnp.where(
            lane == at + 2, turn(high, at + 3 - rows, 1), turn(high, at + 5 - rows, 1)
        )
        if 1 <= c <= 3:
            low_wall = jnp.where(is_field, -sign * low_wall, low_wall)
            high_wall = jnp.where(is_field, sign * high_wall, high_wall)
        low = jnp.where(half == 0, low_wall, turn(low, at + 2 - rows, 1))
        high = jnp.where(half == halves - 1, high_wall, turn(high, at + 2, 1))
        ends = jnp.where(within(lane, at, 2), low, jnp.where(within(lane, at + 2, 2), high, ends))
    held_send[pl.ds(2 * CH, devices, stride=PASSED)] = ends[0:devices] + turn(
        ends[devices:], 4 * CH, 1
    )
    wait_all(copy_all([(held_send, send)], sems))


def flux_chunk(get, mets, fi, w, fk, acc, r):
    rows = pl.ds(r, 8)
    vax, vay, vbx, vby, niv, rw, cw, tw = [mets[j, rows] for j in range(8)]
    at_j = along(1)
    for k in range(fi.shape[1]):
        f = [get(c, k, r) for c in range(CH)]
        wk, p, h = point(f)
        for c, x in enumerate(flux(f, wk, p, h, vax, vay)):
            fi[c, k, rows] = x
        for c in range(4):
            w[c, k, rows] = wk[c]
        fj = flux(f, wk, p, h, vbx, vby)
        for c in range(CH):
            val = niv * slope(fj[c], at_j)
            if c > 0:
                val = val + (cw * curve(wk[c - 1], at_j) - tw * wk[c - 1])
            acc[c, k, rows] = val
        for c, x in enumerate(flux_planes(f, wk, p, h)):
            fk[c, k, rows] = x


def sum_chunk(mets, fi, w, fk, acc, r, emit):
    planes = fi.shape[1]
    kv = viscosity * unit
    rows = pl.ds(r, 8)
    niv, rw = mets[4, rows], mets[5, rows]
    for c in range(CH):
        t = [fk[c, k, rows] for k in range(planes)]
        x = [w[c - 1, k, rows] for k in range(planes)] if c > 0 else None
        for k in range(planes):

            def near(v, o):
                return v[(k + o) % planes]

            def at_i(v, o):
                return v[pl.ds(r + o, 8)]

            val = acc[c, k, rows] + niv * slope(fi.at[c, k], at_i) - unit * slope(t, near)
            if c > 0:
                val = val + (rw * curve(w.at[c - 1, k], at_i) + kv * curve(x, near))
            emit(c, k, r, val)


def chunks(count, body, unroll=1):
    def step(n, _):
        body(pl.multiple_of(n * 8, 8))
        return 0

    lax.fori_loop(0, count, step, 0, unroll=unroll)


def first_kernel(
    state_in, placed_at, neighbour_at, face_at, orient_at, state, route,
    mets, fi, w, fk, acc, placed, neighbour, face, orient, where_is, sems,
):
    del state_in
    planes, rows = fi.shape[1], fi.shape[2] - 2 * PAD
    pairs = zip((placed_at, neighbour_at, face_at, orient_at), (placed, neighbour, face, orient))
    tables = copy_all(list(pairs), sems)
    count = rows // 8
    blocks = placed.shape[0]
    share = -(-blocks // count)

    def slots(n):
        return [jnp.minimum((n // 8) * share + i, blocks - 1) for i in range(share)]

    def get(c, k, r):
        return state[c, k, pl.ds(r, 8)]

    def fluxes(n):
        at = pl.ds(n + PAD, 8)
        for j, x in enumerate(metric_terms([state[c, planes, at] for c in range(CH)])):
            mets[j, at] = x
        flux_chunk(get, mets, fi, w, fk, acc, n + PAD)

    def emit(c, k, r, val):
        state[c, k, pl.ds(r, 8)] = get(c, k, r) + val

    def sums(n):
        for slot in slots(n):
            block = placed[slot]
            for f in range(2):
                partner = where_is[neighbour[f, block]]
                route[2 * slot + f] = partner * 4 + face[f, block] * 2 + orient[f, block]
        sum_chunk(mets, fi, w, fk, acc, n + PAD, emit)

    def note(slot):
        where_is[placed[slot]] = slot

    chunks(count, fluxes, unroll=2)
    wait_all(tables)
    loop(blocks, note, unroll=8)
    chunks(count, sums, unroll=2)


def pack_ends(tall, planes):
    sub, lane = rows_of((8, LANES)), lanes_of((8, LANES))
    stacked = []
    for c in range(CH):
        packed = jnp.zeros((8, LANES), jnp.float32)
        for k in range(planes):
            x = turn(jnp.where(sub < 4, tall[0, c, k], tall[1, c, k]), 8 * k + 4, 1)
            packed = jnp.where(within(lane, 8 * k, 8), x, packed)
        stacked.append(packed)
    ends = across(jnp.concatenate(stacked, axis=0))
    out = []
    for c in range(CH):
        packed = jnp.zeros((8, LANES), jnp.float32)
        for k in range(planes):
            x = turn(ends[k * 8 : k * 8 + 8], 4 * k - (8 * c + 2), 1)
            packed = jnp.where(within(lane, 4 * k, 4), x, packed)
        out.append(packed)
    return out


def ends_kernel(
    halves, state_in, tall_in, low, high, after, state, tall, ends_base, ends_sec, inner,
    tile_fk, tile_w, tile_acc, packed, rims, sems,
):
    del state_in, tall_in, after
    planes, rows = tall.shape[2] - 1, state.shape[2] - 2 * PAD
    every = planes + 1
    half = lax.axis_index("ij")
    low_wall, high_wall = half == 0, half == halves - 1
    low_flag, high_flag = jnp.where(low_wall, 1, 0), jnp.where(high_wall, 1, 0)
    sub, lane = rows_of((8, LANES)), lanes_of((8, LANES))
    top = PAD + rows

    @pl.when(low_wall)
    def _():
        for c in range(CH):
            for k in range(every):
                for n in range(2):
                    x = tall[0, c, k, 4 + n : 5 + n]
                    tall[0, c, k, 3 - n : 4 - n] = -x if 1 <= c <= 3 and k < planes else x

    @pl.when(jnp.logical_not(low_wall))
    def _():
        for c in range(CH):
            for k in range(every):
                tall[0, c, k, 0:4] = low[c, 4 * k : 4 * k + 4]

    @pl.when(high_wall)
    def _():
        for c in range(CH):
            for k in range(every):
                for n in range(2):
                    tall[1, c, k, 4 + n : 5 + n] = tall[1, c, k, 3 - n : 4 - n]

    @pl.when(jnp.logical_not(high_wall))
    def _():
        for c in range(CH):
            for k in range(every):
                tall[1, c, k, 4:8] = high[c, 4 * k : 4 * k + 4]

    for c, x in enumerate(pack_ends(tall, every)):
        ends_base[c] = x
    for c in range(CH):
        state[c, planes, PAD - 4 : PAD] = tall[0, c, planes, 0:4]
        state[c, planes, top : top + 4] = tall[1, c, planes, 4:8]
    mets = [metric_terms([tall[s, c, planes] for c in range(CH)]) for s in range(2)]

    def done(c, s, k, x):
        tall[s, c, k] = x
        if s == 0:
            sign = -1.0 if 1 <= c <= 3 else 1.0
            wall = sign * jnp.where(sub == 2, turn(x, -3, 0), turn(x, -1, 0))
            x = jnp.where((sub < 4) & (low_flag == 1), wall, x)
        else:
            wall = jnp.where(sub == 4, turn(x, 1, 0), turn(x, 3, 0))
            x = jnp.where((sub >= 4) & (high_flag == 1), wall, x)
        start = PAD - 2 if s == 0 else top - 2
        state[c, k, start : start + 4] = x[2:6]

    tile_stage(
        planes, lambda c, s, k: tall[s, c, k], mets, lambda *_: along(0), along(1),
        (tile_fk, tile_w, tile_acc), done,
    )
    for c, x in enumerate(pack_ends(tall, planes)):
        rims[c] = x
    leaving = copy_all([(rims, ends_sec)], sems)

    if rows < LANES:
        packed[...] = jnp.zeros(packed.shape, jnp.float32)

    def pack(n):
        at = pl.ds(n + PAD, 8)
        for c in range(CH):
            packs = turn(state[c, planes, at], 12 * planes + 6, 1)
            for k in range(planes):
                x = turn(state[c, k, at], 12 * k + 6, 1)
                packs = jnp.where(within(lane, 12 * k, 12), x, packs)
            packed[c, pl.ds(n, 8)] = packs

    chunks(rows // 8, pack, unroll=2)
    for c in range(CH):
        inner[c] = packed[c].T[0 : inner.shape[1]]
    wait_all(leaving)


def second_kernel(
    state_in, dens, mom, en, state, fields, mets, fi, w, fk, acc, sems
):
    del state_in
    planes, rows = fields.shape[1:3]
    pairs = [(dens.at[0], fields.at[0]), (mom.at[0], fields.at[1:4]), (en.at[0], fields.at[4])]
    copies = copy_all(pairs, sems)

    def get(c, k, r):
        return state[c, k, pl.ds(r, 8)]

    def fluxes(n):
        at = pl.ds(n, 8)
        for j, x in enumerate(metric_terms([state[c, planes, at] for c in range(CH)])):
            mets[j, at] = x
        flux_chunk(get, mets, fi, w, fk, acc, n)

    def emit(c, k, r, val):
        x = 0.5 * (fields[c, k, pl.ds(r - PAD, 8)] + (get(c, k, r) + val))
        state[c, k, pl.ds(r, 8)] = x

    chunks(rows // 8 + 2, fluxes, unroll=2)
    wait_all(copies)
    chunks(rows // 8, lambda n: sum_chunk(mets, fi, w, fk, acc, n + PAD, emit), unroll=2)


def beyond(low, rows):
    top = rows % LANES
    high = low if top == 0 else turn(low, top, 1)
    lane = lanes_of(low.shape)

    def at(x, o):
        if o < 0:
            x = jnp.where(lane >= LANES + o, low, x)
        else:
            x = jnp.where(within(lane, top, o), high, x)
        return turn(x, -o, 1)

    return at


def last_kernel(
    halves, rows, planes, own, ends_base, ends_sec_at, inner, got, out,
    next_dens, next_mom, next_en,
    base, sec, fk, ws, acc, rims, turned, back, full, ends_sec, sems,
):
    late = copy_all([(ends_sec_at, ends_sec)], sems, 3 * PIECES)
    half = lax.axis_index("ij")
    low_wall, high_wall = half == 0, half == halves - 1
    sub, lane = rows_of((8, LANES)), lanes_of((8, LANES))

    def mix(f, mine, others):
        return jnp.where((sub < 4) == (f == 1), mine, others)

    others = [jnp.zeros((8, LANES), jnp.float32)] * CH
    for k in range(planes + 1):
        start = DEPTH * k * PASSED
        for f in range(2):

            def ghost(row):
                x = got[pl.ds(start + row, 8, stride=PASSED)]
                return x if f == 1 else turn(x, 4, 0)

            arrived = ghost(2 * CH)
            to = 28 * f + 4 * k
            for c in range(CH):
                base[c, f, k] = mix(f, own[c, k * 8 : k * 8 + 8], ghost(f * CH + c))
                moved = turn(arrived, to - 4 * CH * f - 4 * c, 1)
                others[c] = jnp.where(within(lane, to, 4), moved, others[c])

    low_lanes = lane < 28
    twice = [jnp.where(low_lanes, ends_base[c], turn(ends_base[c], 28, 1)) for c in range(CH)]
    ends = [jnp.where(low_lanes == (sub >= 4), twice[c], others[c]) for c in range(CH)]
    slot = jnp.where(low_lanes, lane, lane - 28)

    def spread(x):
        y = x
        for k in range(planes):
            y = jnp.where(within(slot, 4 * k, 4), turn(x, 4 * (k - planes), 1), y)
        return y

    vax, vay, vbx, vby, niv, _, cw, _ = [spread(x) for x in metric_terms(ends)]
    wrapped = [spread(x) for x in metric_terms(twice)[2:4]]

    def keep(c, f, k, val):
        sec[c, f, k] = val

    def stage(held, ends, gx, gy):
        mets = [metric_terms([held[c, f, planes] for c in range(CH)]) for f in range(2)]
        w, p, h = point(ends)
        for n, x in enumerate((*flux(ends, w, p, h, gx, gy), *w)):
            for f in range(2):
                for k in range(planes):
                    rims[n, f, k] = turn(x, LANES - 2 - (28 * f + 4 * k), 1)
        tile_stage(
            planes,
            lambda c, f, k: held[c, f, k],
            mets,
            lambda kind, c, f, k: beyond(rims[CH * kind + c, f, k], rows),
            along(0),
            (fk, ws, acc),
            keep,
        )

    stage(base, ends, vax, vay)
    wait_all(late)

    def move(k, source):
        for c in range(CH):
            at = 12 * k
            mine = jnp.where(sub < 4, inner[c, at : at + 8], inner[c, at + 4 : at + 12])
            for f in range(2):
                sec[c, f, k] = mix(f, mine, turn(source[c, f, k], 2 if f == 1 else -2, 0))

    for k in range(planes):
        move(k, sec)
    move(planes, base)

    def shifted(x):
        return jnp.where(low_lanes, turn(x, -2, 0), turn(x, 2, 0))

    w1, p1, h1 = point(ends)
    w0, p0, h0 = point(twice)
    new, old = flux(ends, w1, p1, h1, vbx, vby), flux(twice, w0, p0, h0, *wrapped)
    at_j = along(0)
    touched = within(sub, jnp.where(low_lanes, 4, 2), 2)
    second = []
    for c in range(CH):
        add = niv * slope(new[c] - old[c], at_j)
        if c > 0:
            add = add + cw * curve(w1[c - 1] - w0[c - 1], at_j)
        x = jnp.where(low_lanes, ends_sec[c], turn(ends_sec[c], 28, 1))
        second.append(shifted(x + jnp.where(touched, add, 0.0)))

    def mirror(at_low):
        def reflect(*second):
            second = list(second)
            for k in range(planes):
                for f in range(2):
                    to = 28 * f + 4 * k + (0 if at_low else 2)
                    shift = to - 1 if at_low else to + 1 - rows
                    for c in range(CH):
                        x = sec[c, f, k]
                        x = jnp.where(lane == to, turn(x, shift, 1), turn(x, shift + 2, 1))
                        if at_low and 1 <= c <= 3:
                            x = -x
                        second[c] = jnp.where(within(lane, to, 2), x, second[c])
            return tuple(second)

        return reflect

    def leave(*second):
        return second

    second = lax.cond(low_wall, mirror(True), leave, *second)
    second = lax.cond(high_wall, mirror(False), leave, *second)
    stage(sec, second, shifted(vax), shifted(vay))

    per = LANES // 8

    for k in range(planes):
        for c in range(CH):
            x = jnp.where(sub < 4, turn(sec[c, 1, k], -2, 0), turn(sec[c, 0, k], 2, 0))
            at = (c * planes + k) * 8
            turned[at : at + 8] = 0.5 * (own[c, k * 8 : k * 8 + 8] + x)
    for n in range(turned.shape[0] // LANES):
        back[n] = turned[n * LANES : (n + 1) * LANES].T
    inside = within(lane, 4, LANES - 8)
    size = max(8, rows // PIECES)

    def leave(start):
        at = pl.ds(start, size)
        targets = [next_dens.at[0, :, at], next_en.at[0, :, at], next_mom.at[0, :, :, at]]
        sources = [full.at[0, :, at], full.at[4, :, at], full.at[1:4, :, at]]
        first = 3 * (start // size)
        return [
            pltpu.make_async_copy(src, dst, sems.at[first + n])
            for n, (src, dst) in enumerate(zip(sources, targets))
        ]

    def merge(r):
        at = pl.ds(r, 8)
        for c in range(CH):
            for k in range(planes):
                index = c * planes + k
                moved = turn(back[index // per, at], LANES - 4 - 8 * (index % per), 1)
                full[c, k, at] = jnp.where(inside, out[c, k, pl.ds(r + PAD, 8)], moved)

        @pl.when(lax.rem(r + 8, size) == 0)
        def _():
            for copy in leave(pl.multiple_of(r + 8 - size, 8)):
                copy.start()

    chunks(rows // 8, merge, unroll=2)
    for n in range(rows // size):
        wait_all(leave(n * size))


def local(mesh_shape, density, momentum, energy, metrics, volume, placed, neighbour, face, orient):
    halves = mesh_shape["ij"]
    blocks = mesh_shape["blk"]
    planes, rows = density.shape[1], density.shape[2]
    every = planes + 1
    fields = (density, momentum, energy, metrics, volume)
    neighbour, face, orient = neighbour.T, face.T, orient.T
    vmem = pl.BlockSpec(memory_space=pltpu.VMEM)
    smem = pl.BlockSpec(memory_space=pltpu.SMEM)
    hbm = pl.BlockSpec(memory_space=pltpu.HBM)
    anywhere = pl.BlockSpec(memory_space=pl.ANY)

    def call(kernel, name, outs, ins, out_specs, scratch, cost=None, alias=None):
        run = pl.pallas_call(
            kernel,
            out_shape=[
                held(x) if spec is vmem else far(x) if spec is hbm else x
                for x, spec in zip(outs, out_specs)
            ],
            in_specs=ins,
            out_specs=out_specs,
            scratch_shapes=scratch,
            compiler_params=pltpu.CompilerParams(vmem_limit_bytes=VMEM_MIB * 1024 * 1024),
            cost_estimate=cost,
            input_output_aliases=alias or {},
            name=name,
        )

        def keep(*operands):
            return run(
                *[
                    x
                    if spec not in (vmem, hbm)
                    else pltpu.with_memory_space_constraint(x, spec.memory_space)
                    for x, spec in zip(operands, ins)
                ]
            )

        return keep

    def shape(*dims):
        return jax.ShapeDtypeStruct(dims, jnp.float32)

    def held(x):
        return pltpu.VMEM(x.shape, x.dtype)

    def far(x):
        return pltpu.HBM(x.shape, x.dtype)

    def table(x):
        return pltpu.SMEM(x.shape, jnp.int32)

    def sems(count):
        return pltpu.SemaphoreType.DMA((count,))

    devices = blocks * halves
    sent, passed = shape(devices * SENT, LANES), shape(devices * PASSED, LANES)
    strip, rim = shape(CH, 64, LANES), shape(CH, 8, LANES)
    edge = shape(CH, 4 * every, LANES)
    edges = 1 if halves == 2 else 2
    square = held(shape(CH, LANES, LANES))
    tall = rows + 2 * PAD
    whole = shape(CH, every, tall, LANES)
    rows_about = shape(2, CH, every, 8, LANES)
    to_send, own, about, state, *halo = call(
        functools.partial(cut_kernel, halves),
        "cut",
        [sent, strip, rows_about, whole] + [edge] * edges,
        [hbm] * 8,
        [hbm] + [vmem] * (3 + edges),
        [
            held(sent),
            square,
            held(shape(CH * 64, LANES)),
            table(placed),
            table(face),
            table(orient),
            sems(5 * PIECES),
            sems(3),
            sems(1),
        ],
    )(*fields, placed, face, orient)

    def swap(x):
        x = x.reshape(devices, x.shape[0] // devices, 1, LANES)
        x = lax.all_to_all(x, ("blk", "ij"), 0, 0, tiled=True)
        return x.reshape(x.shape[0] * x.shape[1], LANES)

    if edges == 1:
        below = above = lax.ppermute(halo[0], "ij", [(0, 1), (1, 0)])
    else:
        below = lax.ppermute(halo[1], "ij", [(i, i + 1) for i in range(halves - 1)])
        above = lax.ppermute(halo[0], "ij", [(i + 1, i) for i in range(halves - 1)])
    got = swap(to_send)

    padded = held(shape(CH, planes, tall, LANES))
    stage = [
        held(shape(8, tall, LANES)),
        padded,
        held(shape(4, planes, tall, LANES)),
        padded,
        padded,
    ]
    work = planes * rows * LANES
    cost = pl.CostEstimate(flops=300 * work, bytes_accessed=150 * work, transcendentals=work)
    route = jax.ShapeDtypeStruct((2 * blocks,), jnp.int32)
    state, route_out = call(
        first_kernel,
        "first_section",
        [whole, route],
        [vmem] + [hbm] * 4,
        [vmem, smem],
        stage + [table(x) for x in (placed, neighbour, face, orient, placed)] + [sems(4)],
        cost,
        {0: 0},
    )(state, placed, neighbour, face, orient)
    (relayed,) = call(
        functools.partial(relay_kernel, halves, rows, planes, devices),
        "relay",
        [passed],
        [anywhere, anywhere, vmem],
        [hbm],
        [
            held(passed),
            held(shape(devices * 16, LANES)),
            held(shape(devices * 16, LANES)),
            held(shape(devices * 2, LANES)),
            table(route),
            sems(2),
        ],
    )(route_out, below, got)
    ghosts = swap(relayed)
    tiles = held(shape(CH, 2, every, 8, LANES))
    state, _, ends_base, ends_sec, inner = call(
        functools.partial(ends_kernel, halves),
        "ends",
        [whole, rows_about, rim, rim, shape(CH, 12 * every + 4, LANES)],
        [vmem] * 4 + [hbm],
        [vmem] * 3 + [hbm, vmem],
        [tiles] * 3 + [square, held(rim), sems(1)],
        cost,
        {0: 0, 1: 1},
    )(state, about, below, above, relayed)
    (state,) = call(
        second_kernel,
        "second_section",
        [whole],
        [vmem] + [hbm] * 3,
        [vmem],
        [held(shape(CH, planes, rows, LANES))] + stage + [sems(3)],
        cost,
        {0: 0},
    )(state, density, momentum, energy)
    flat = -(-CH * planes * 8 // LANES)
    return call(
        functools.partial(last_kernel, halves, rows, planes),
        "strips",
        [shape(*density.shape), shape(*momentum.shape), shape(*energy.shape)],
        [vmem] * 2 + [hbm] + [vmem] * 3,
        [hbm] * 3,
        [tiles] * 5
        + [
            held(shape(CH + 4, 2, planes, 8, LANES)),
            held(shape(flat * LANES, LANES)),
            held(shape(flat, LANES, LANES)),
            held(shape(CH, planes, rows, LANES)),
            held(rim),
            sems(3 * PIECES + 1),
        ],
    )(own, ends_base, ends_sec, inner, ghosts, state)


def solution(mesh):
    return jax.shard_map(
        functools.partial(local, dict(mesh.shape)),
        mesh=mesh,
        in_specs=(
            P("blk", None, "ij", None),
            P("blk", None, None, "ij", None),
            P("blk", None, "ij", None),
            P("blk", None, "ij", None),
            P("blk", "ij", None),
            P(),
            P(),
            P(),
            P(),
        ),
        out_specs=(
            P("blk", None, "ij", None),
            P("blk", None, None, "ij", None),
            P("blk", None, "ij", None),
        ),
        check_vma=False,
    )
```

```python
import functools

import jax
import jax.numpy as jnp
from jax import lax
from jax.experimental import pallas as pl
from jax.experimental.pallas import tpu as pltpu
from jax.sharding import PartitionSpec as P

pressure_factor = 0.4
viscosity = 0.05
time_step = 0.03
unit = time_step / 12.0

LANES = 128
PAD = 8
PIECES = 4
DEPTH = 4
CH = 5
VMEM_MIB = 32
SENT = 2 * CH
PASSED = 2 * CH + 1
FIRST = 4


def turn(x, shift, axis):
    shift = shift % x.shape[axis]
    return x if shift == 0 else pltpu.roll(x, shift, axis)


def lanes_of(shape):
    return lax.broadcasted_iota(jnp.int32, shape, len(shape) - 1)


def rows_of(shape):
    return lax.broadcasted_iota(jnp.int32, shape, len(shape) - 2)


def point(f):
    rho, m1, m2, m3, e = f
    r = 1.0 / rho
    u1, u2, u3 = m1 * r, m2 * r, m3 * r
    kin = 0.5 * (m1 * u1 + m2 * u2 + m3 * u3)
    p = pressure_factor * (e - kin)
    return (u1, u2, u3, (kin + 2.0 * p) * r), p, e + p


def metric_terms(m):
    ax, ay, bx, by, v = m
    kv = viscosity * unit
    rw = kv * (ax * ax + ay * ay)
    cw = kv * (bx * bx + by * by)
    return v * ax, v * ay, v * bx, v * by, -unit / v, rw, cw, 30.0 * (rw + kv) + 28.0 * cw


def flux(f, w, p, h, gx, gy):
    rho, m1, m2, m3, _ = f
    u = gx * w[0] + gy * w[1]
    return (rho * u, m1 * u + gx * p, m2 * u + gy * p, m3 * u, h * u)


def flux_planes(f, w, p, h):
    u3 = w[2]
    return (f[3], f[1] * u3, f[2] * u3, f[3] * u3 + p, h * u3)


def slope(x, at):
    return 8.0 * (at(x, 1) - at(x, -1)) - (at(x, 2) - at(x, -2))


def curve(x, at):
    return 16.0 * (at(x, 1) + at(x, -1)) - (at(x, 2) + at(x, -2))


def turned_slope(x, axis):
    ahead = turn(x, -2, axis) - x
    return 8.0 * turn(ahead, 1, axis) - (ahead + turn(ahead, 2, axis))


def turned_curve(x, axis):
    ahead = turn(x, -2, axis) + x
    return 16.0 * turn(ahead, 1, axis) - (ahead + turn(ahead, 2, axis))


def along(axis):
    return lambda x, o: turn(x, -o, axis)


def within(lane, start, size):
    return (lane >= start) & (lane < start + size)


def roll_by(x, shift, axis=1):
    size = x.shape[axis]
    return pltpu.roll(x, lax.rem(shift + 4 * size, size), axis)


def across(x):
    if x.shape[0] < LANES:
        x = jnp.concatenate([x, jnp.zeros((LANES - x.shape[0], LANES), jnp.float32)], axis=0)
    return x.T


def loop(count, body, unroll=1):
    def step(n, _):
        body(n)
        return 0

    lax.fori_loop(0, count, step, 0, unroll=unroll)


def copy_all(pairs, sems, first=0):
    copies = [
        pltpu.make_async_copy(src, dst, sems.at[first + n]) for n, (src, dst) in enumerate(pairs)
    ]
    for copy in copies:
        copy.start()
    return copies


def state_pairs(fields, state, planes, start, size):
    dens, mom, en, met, vol = fields
    at, to = pl.ds(start, size), pl.ds(start + PAD, size)
    return [
        (dens.at[0, :, at], state.at[0, 0:planes, to]),
        (mom.at[0, :, :, at], state.at[1:4, 0:planes, to]),
        (en.at[0, :, at], state.at[4, 0:planes, to]),
        (met.at[0, :, at], state.at[0:4, planes, to]),
        (vol.at[0, at], state.at[4, planes, to]),
    ]


def arrive_in_pieces(fields, state, sems):
    planes, rows = fields[0].shape[1], fields[0].shape[2]
    size = max(8, rows // PIECES)
    for n in range(rows // size):
        copy_all(state_pairs(fields, state, planes, n * size, size), sems, 5 * n)

    def expect(start):
        @pl.when(lax.rem(start, size) == 0)
        def _():
            for n, (src, dst) in enumerate(state_pairs(fields, state, planes, start, size)):
                pltpu.make_async_copy(src, dst, sems.at[5 * (start // size) + n]).wait()

    return expect


def wait_all(copies):
    for copy in copies:
        copy.wait()


def tile_stage(planes, load, mets, shift_i, axis_j, hold, done):
    kv = viscosity * unit
    fk, ws, acc = hold

    def spread(k):
        for s in range(2):
            vax, vay, vbx, vby, niv, rw, cw, tw = mets[s]
            x = [load(c, s, k) for c in range(CH)]
            w, p, h = point(x)
            fi, fj = flux(x, w, p, h, vax, vay), flux(x, w, p, h, vbx, vby)
            for c in range(CH):
                val = niv * (slope(fi[c], shift_i(0, c, s, k)) + turned_slope(fj[c], axis_j))
                if c > 0:
                    v = w[c - 1]
                    val = val + (
                        rw * curve(v, shift_i(1, c - 1, s, k)) + cw * turned_curve(v, axis_j) - tw * v
                    )
                    ws[c - 1, s, k] = v
                acc[c, s, k] = x[c] + val
            for c, v in enumerate(flux_planes(x, w, p, h)):
                fk[c, s, k] = v

    def gather(k):
        at = {o: lax.rem(k + o + planes, planes) for o in (-2, -1, 0, 1, 2)}
        for s in range(2):
            for c in range(CH):
                val = acc[c, s, k] - unit * slope(0, lambda _, o: fk[c, s, at[o]])
                if c > 0:
                    val = val + kv * curve(0, lambda _, o: ws[c - 1, s, at[o]])
                done(c, s, k, val)

    loop(planes, spread)
    loop(planes, gather)


def cut_kernel(
    halves, dens, mom, en, met, vol, placed_at, face_at, orient_at, send, own, tall, state, *rest
):
    edges, rest = rest[: 1 if halves == 2 else 2], rest[1 if halves == 2 else 2 :]
    held_send, packed, strips, placed, face, orient, sems, table_sems, out_sems = rest
    tables = copy_all(
        [(placed_at, placed), (face_at, face), (orient_at, orient)], table_sems
    )
    planes, rows = dens.shape[1], dens.shape[2]
    expect = arrive_in_pieces((dens, mom, en, met, vol), state, sems)
    half = lax.axis_index("ij")
    lane = lanes_of((8, LANES))
    if rows < LANES:
        packed[...] = jnp.zeros(packed.shape, jnp.float32)
    def pack(r):
        expect(r)
        for c in range(CH):
            packs = jnp.zeros((8, LANES), jnp.float32)
            for k in range(planes + 1):
                x = turn(state[c, k, pl.ds(r + PAD, 8)], 8 * k + 4, 1)
                packs = jnp.where(within(lane, 8 * k, 8), x, packs)
            packed[c, pl.ds(r, 8)] = packs

    chunks(rows // 8, pack, unroll=2)

    def cut_ends(k):
        for c in range(CH):
            low, high = state[c, k, PAD : PAD + 4], state[c, k, PAD + rows - 4 : PAD + rows]
            tall[0, c, k, 4:8] = low
            tall[1, c, k, 0:4] = high
            if len(edges) == 1:
                edges[0][c, k * 4 : k * 4 + 4] = jnp.where(half == 0, high, low)
            else:
                edges[0][c, k * 4 : k * 4 + 4] = low
                edges[1][c, k * 4 : k * 4 + 4] = high

    for k in range(planes + 1):
        cut_ends(k)

    wait_all(tables)
    block = placed[lax.axis_index("blk")]
    row = rows_of((64, LANES))
    high_side = row % 8 < 4
    mirror = jnp.where(
        rows_of((LANES, LANES)) + lanes_of((LANES, LANES)) == rows - 1, 1.0, 0.0
    ).astype(jnp.bfloat16)
    flip = [jnp.where(orient[f, block] == 1, -1.0, 1.0) for f in range(2)]
    same = [jnp.where(face[f, block] == f, -1.0, 1.0) for f in range(2)]
    rising = [face[f, block] == 1 for f in range(2)]
    turned = jnp.where(high_side, flip[1], flip[0])
    facing = jnp.where(high_side, same[1], same[0])

    def orient_strip(c):
        strip = packed[c].T[0:64]
        own[c] = strip
        rest, parts = strip, []
        for _ in range(3):
            parts.append(rest.astype(jnp.bfloat16))
            rest = rest - parts[-1].astype(jnp.float32)
        back = jnp.dot(
            jnp.concatenate(parts, axis=0), mirror, preferred_element_type=jnp.float32
        )
        back = back[0:64] + (back[64:128] + back[128:192])
        moved = jnp.where(turned < 0.0, back, strip)
        sign = jnp.where(c < 2, turned, jnp.where(c < 4, facing, 1.0))
        moved = jnp.where(row >= planes * 8, moved * sign, moved)
        strips[pl.ds(pl.multiple_of(c * 64, 64), 64)] = moved

    loop(CH, orient_strip, unroll=CH)

    def put(n):
        k, e = n >> 2, n & 3
        at = (FIRST + n) * SENT
        low = k * 8 + 4 + jnp.where(rising[0], e, 3 - e)
        high = k * 8 + jnp.where(rising[1], 3 - e, e)
        held_send[pl.ds(at, CH)] = strips[pl.ds(low, CH, stride=64)]
        held_send[pl.ds(at + CH, CH)] = strips[pl.ds(high, CH, stride=64)]

    loop(DEPTH * (planes + 1), put, unroll=4)
    wait_all(copy_all([(held_send, send)], out_sems))


def relay_kernel(
    halves, rows, planes, devices, route_at, halo, held_got, send,
    held_send, below, above, signs, route, sems,
):
    del halo
    wait_all(copy_all([(route_at, route)], sems, 1))
    me = lax.axis_index("blk") * halves + lax.axis_index("ij")
    is_field = (me >= FIRST) & (me < FIRST + DEPTH * planes)

    def pass_on(slot):
        for f in range(2):
            code = route[2 * slot + f]
            partner, side, turned = code >> 2, (code >> 1) & 1, code & 1
            sign = jnp.where(turned == 1, -1.0, 1.0)

            def piece(h):
                h = jnp.where(turned == 1, halves - 1 - h, h)
                return held_got[pl.ds((partner * halves + h) * SENT + side * CH, CH)]

            pieces = [piece(h) for h in range(halves)]
            for half in range(halves):
                at = slot * halves + half
                held_send[pl.ds(at * PASSED + f * CH, CH)] = pieces[half]
                below[pl.ds((f * devices + at) * 8, CH)] = pieces[max(half - 1, 0)]
                above[pl.ds((f * devices + at) * 8, CH)] = pieces[min(half + 1, halves - 1)]
                signs[pl.ds(f * devices + at, 1)] = jnp.full((1, LANES), sign, jnp.float32)

    loop(devices // halves, pass_on, unroll=4)
    count = 2 * devices
    lane = lanes_of((count, LANES))
    half = rows_of((count, LANES)) % halves
    sign = signs[...]
    ends = jnp.zeros((count, LANES), jnp.float32)
    for c in range(CH):
        low, high = below[pl.ds(c, count, stride=8)], above[pl.ds(c, count, stride=8)]
        at = 4 * c
        low_wall = jnp.where(lane == at, turn(low, at - 1, 1), turn(low, at + 1, 1))
        high_wall = jnp.where(
            lane == at + 2, turn(high, at + 3 - rows, 1), turn(high, at + 5 - rows, 1)
        )
        if 1 <= c <= 3:
            low_wall = jnp.where(is_field, -sign * low_wall, low_wall)
            high_wall = jnp.where(is_field, sign * high_wall, high_wall)
        low = jnp.where(half == 0, low_wall, turn(low, at + 2 - rows, 1))
        high = jnp.where(half == halves - 1, high_wall, turn(high, at + 2, 1))
        ends = jnp.where(within(lane, at, 2), low, jnp.where(within(lane, at + 2, 2), high, ends))
    held_send[pl.ds(2 * CH, devices, stride=PASSED)] = ends[0:devices] + turn(
        ends[devices:], 4 * CH, 1
    )
    wait_all(copy_all([(held_send, send)], sems))


def flux_chunk(get, mets, fi, w, fk, acc, r):
    rows = pl.ds(r, 8)
    vax, vay, vbx, vby, niv, rw, cw, tw = [mets[j, rows] for j in range(8)]
    for k in range(fi.shape[1]):
        f = [get(c, k, r) for c in range(CH)]
        wk, p, h = point(f)
        for c, x in enumerate(flux(f, wk, p, h, vax, vay)):
            fi[c, k, rows] = x
        for c in range(4):
            w[c, k, rows] = wk[c]
        fj = flux(f, wk, p, h, vbx, vby)
        for c in range(CH):
            val = niv * turned_slope(fj[c], 1)
            if c > 0:
                val = val + (cw * turned_curve(wk[c - 1], 1) - tw * wk[c - 1])
            acc[c, k, rows] = val
        for c, x in enumerate(flux_planes(f, wk, p, h)):
            fk[c, k, rows] = x


def sum_chunk(mets, fi, w, fk, acc, r, emit):
    planes = fi.shape[1]
    kv = viscosity * unit
    rows = pl.ds(r, 8)
    niv, rw = mets[4, rows], mets[5, rows]
    for c in range(CH):
        t = [fk[c, k, rows] for k in range(planes)]
        x = [w[c - 1, k, rows] for k in range(planes)] if c > 0 else None
        for k in range(planes):

            def near(v, o):
                return v[(k + o) % planes]

            def at_i(v, o):
                return v[pl.ds(r + o, 8)]

            val = acc[c, k, rows] + niv * slope(fi.at[c, k], at_i) - unit * slope(t, near)
            if c > 0:
                val = val + (rw * curve(w.at[c - 1, k], at_i) + kv * curve(x, near))
            emit(c, k, r, val)


def chunks(count, body, unroll=1):
    def step(n, _):
        body(pl.multiple_of(n * 8, 8))
        return 0

    lax.fori_loop(0, count, step, 0, unroll=unroll)


def first_kernel(
    state_in, placed_at, neighbour_at, face_at, orient_at, state, route,
    mets, fi, w, fk, acc, placed, neighbour, face, orient, where_is, sems,
):
    del state_in
    planes, rows = fi.shape[1], fi.shape[2] - 2 * PAD
    pairs = zip((placed_at, neighbour_at, face_at, orient_at), (placed, neighbour, face, orient))
    tables = copy_all(list(pairs), sems)
    count = rows // 8
    blocks = placed.shape[0]
    share = -(-blocks // count)

    def slots(n):
        return [jnp.minimum((n // 8) * share + i, blocks - 1) for i in range(share)]

    def get(c, k, r):
        return state[c, k, pl.ds(r, 8)]

    def fluxes(n):
        at = pl.ds(n + PAD, 8)
        for j, x in enumerate(metric_terms([state[c, planes, at] for c in range(CH)])):
            mets[j, at] = x
        flux_chunk(get, mets, fi, w, fk, acc, n + PAD)

    def emit(c, k, r, val):
        state[c, k, pl.ds(r, 8)] = get(c, k, r) + val

    def sums(n):
        for slot in slots(n):
            block = placed[slot]
            for f in range(2):
                partner = where_is[neighbour[f, block]]
                route[2 * slot + f] = partner * 4 + face[f, block] * 2 + orient[f, block]
        sum_chunk(mets, fi, w, fk, acc, n + PAD, emit)

    def note(slot):
        where_is[placed[slot]] = slot

    chunks(count, fluxes, unroll=2)
    wait_all(tables)
    loop(blocks, note, unroll=8)
    chunks(count, sums, unroll=2)


def pack_ends(tall, planes):
    sub, lane = rows_of((8, LANES)), lanes_of((8, LANES))
    stacked = []
    for c in range(CH):
        packed = jnp.zeros((8, LANES), jnp.float32)
        for k in range(planes):
            x = turn(jnp.where(sub < 4, tall[0, c, k], tall[1, c, k]), 8 * k + 4, 1)
            packed = jnp.where(within(lane, 8 * k, 8), x, packed)
        stacked.append(packed)
    ends = across(jnp.concatenate(stacked, axis=0))
    out = []
    for c in range(CH):
        packed = jnp.zeros((8, LANES), jnp.float32)
        for k in range(planes):
            x = turn(ends[k * 8 : k * 8 + 8], 4 * k - (8 * c + 2), 1)
            packed = jnp.where(within(lane, 4 * k, 4), x, packed)
        out.append(packed)
    return out


def ends_kernel(
    halves, state_in, tall_in, low, high, after, state, tall, ends_base, ends_sec, inner,
    tile_fk, tile_w, tile_acc, packed, rims, sems,
):
    del state_in, tall_in, after
    planes, rows = tall.shape[2] - 1, state.shape[2] - 2 * PAD
    every = planes + 1
    half = lax.axis_index("ij")
    low_wall, high_wall = half == 0, half == halves - 1
    low_flag, high_flag = jnp.where(low_wall, 1, 0), jnp.where(high_wall, 1, 0)
    sub, lane = rows_of((8, LANES)), lanes_of((8, LANES))
    top = PAD + rows

    @pl.when(low_wall)
    def _():
        for c in range(CH):
            for k in range(every):
                for n in range(2):
                    x = tall[0, c, k, 4 + n : 5 + n]
                    tall[0, c, k, 3 - n : 4 - n] = -x if 1 <= c <= 3 and k < planes else x

    @pl.when(jnp.logical_not(low_wall))
    def _():
        for c in range(CH):
            for k in range(every):
                tall[0, c, k, 0:4] = low[c, 4 * k : 4 * k + 4]

    @pl.when(high_wall)
    def _():
        for c in range(CH):
            for k in range(every):
                for n in range(2):
                    tall[1, c, k, 4 + n : 5 + n] = tall[1, c, k, 3 - n : 4 - n]

    @pl.when(jnp.logical_not(high_wall))
    def _():
        for c in range(CH):
            for k in range(every):
                tall[1, c, k, 4:8] = high[c, 4 * k : 4 * k + 4]

    for c, x in enumerate(pack_ends(tall, every)):
        ends_base[c] = x
    for c in range(CH):
        state[c, planes, PAD - 4 : PAD] = tall[0, c, planes, 0:4]
        state[c, planes, top : top + 4] = tall[1, c, planes, 4:8]
    mets = [metric_terms([tall[s, c, planes] for c in range(CH)]) for s in range(2)]

    def done(c, s, k, x):
        tall[s, c, k] = x
        if s == 0:
            sign = -1.0 if 1 <= c <= 3 else 1.0
            wall = sign * jnp.where(sub == 2, turn(x, -3, 0), turn(x, -1, 0))
            x = jnp.where((sub < 4) & (low_flag == 1), wall, x)
        else:
            wall = jnp.where(sub == 4, turn(x, 1, 0), turn(x, 3, 0))
            x = jnp.where((sub >= 4) & (high_flag == 1), wall, x)
        start = PAD - 2 if s == 0 else top - 2
        state[c, k, start : start + 4] = x[2:6]

    tile_stage(
        planes, lambda c, s, k: tall[s, c, k], mets, lambda *_: along(0), 1,
        (tile_fk, tile_w, tile_acc), done,
    )
    for c, x in enumerate(pack_ends(tall, planes)):
        rims[c] = x
    leaving = copy_all([(rims, ends_sec)], sems)

    if rows < LANES:
        packed[...] = jnp.zeros(packed.shape, jnp.float32)

    def pack(n):
        at = pl.ds(n + PAD, 8)
        for c in range(CH):
            packs = turn(state[c, planes, at], 12 * planes + 6, 1)
            for k in range(planes):
                x = turn(state[c, k, at], 12 * k + 6, 1)
                packs = jnp.where(within(lane, 12 * k, 12), x, packs)
            packed[c, pl.ds(n, 8)] = packs

    chunks(rows // 8, pack, unroll=2)
    for c in range(CH):
        inner[c] = packed[c].T[0 : inner.shape[1]]
    wait_all(leaving)


def second_kernel(
    state_in, dens, mom, en, state, fields, mets, fi, w, fk, acc, sems
):
    del state_in
    planes, rows = fields.shape[1:3]
    pairs = [(dens.at[0], fields.at[0]), (mom.at[0], fields.at[1:4]), (en.at[0], fields.at[4])]
    copies = copy_all(pairs, sems)

    def get(c, k, r):
        return state[c, k, pl.ds(r, 8)]

    def fluxes(n):
        at = pl.ds(n, 8)
        for j, x in enumerate(metric_terms([state[c, planes, at] for c in range(CH)])):
            mets[j, at] = x
        flux_chunk(get, mets, fi, w, fk, acc, n)

    def emit(c, k, r, val):
        x = 0.5 * (fields[c, k, pl.ds(r - PAD, 8)] + (get(c, k, r) + val))
        state[c, k, pl.ds(r, 8)] = x

    chunks(rows // 8 + 2, fluxes, unroll=2)
    wait_all(copies)
    chunks(rows // 8, lambda n: sum_chunk(mets, fi, w, fk, acc, n + PAD, emit), unroll=2)


def beyond(low, rows):
    top = rows % LANES
    high = low if top == 0 else turn(low, top, 1)
    lane = lanes_of(low.shape)

    def at(x, o):
        if o < 0:
            x = jnp.where(lane >= LANES + o, low, x)
        else:
            x = jnp.where(within(lane, top, o), high, x)
        return turn(x, -o, 1)

    return at


def last_kernel(
    halves, rows, planes, own, ends_base, ends_sec_at, inner, got, out,
    next_dens, next_mom, next_en,
    base, sec, fk, ws, acc, rims, turned, back, full, ends_sec, sems,
):
    late = copy_all([(ends_sec_at, ends_sec)], sems, 3 * PIECES)
    half = lax.axis_index("ij")
    low_wall, high_wall = half == 0, half == halves - 1
    sub, lane = rows_of((8, LANES)), lanes_of((8, LANES))

    def mix(f, mine, others):
        return jnp.where((sub < 4) == (f == 1), mine, others)

    others = [jnp.zeros((8, LANES), jnp.float32)] * CH
    for k in range(planes + 1):
        start = DEPTH * k * PASSED
        for f in range(2):

            def ghost(row):
                x = got[pl.ds(start + row, 8, stride=PASSED)]
                return x if f == 1 else turn(x, 4, 0)

            arrived = ghost(2 * CH)
            to = 28 * f + 4 * k
            for c in range(CH):
                base[c, f, k] = mix(f, own[c, k * 8 : k * 8 + 8], ghost(f * CH + c))
                moved = turn(arrived, to - 4 * CH * f - 4 * c, 1)
                others[c] = jnp.where(within(lane, to, 4), moved, others[c])

    low_lanes = lane < 28
    twice = [jnp.where(low_lanes, ends_base[c], turn(ends_base[c], 28, 1)) for c in range(CH)]
    ends = [jnp.where(low_lanes == (sub >= 4), twice[c], others[c]) for c in range(CH)]
    slot = jnp.where(low_lanes, lane, lane - 28)

    def spread(x):
        y = x
        for k in range(planes):
            y = jnp.where(within(slot, 4 * k, 4), turn(x, 4 * (k - planes), 1), y)
        return y

    vax, vay, vbx, vby, niv, _, cw, _ = [spread(x) for x in metric_terms(ends)]
    wrapped = [spread(x) for x in metric_terms(twice)[2:4]]

    def keep(c, f, k, val):
        sec[c, f, k] = val

    def stage(held, ends, gx, gy):
        mets = [metric_terms([held[c, f, planes] for c in range(CH)]) for f in range(2)]
        w, p, h = point(ends)
        for n, x in enumerate((*flux(ends, w, p, h, gx, gy), *w)):
            for f in range(2):
                for k in range(planes):
                    rims[n, f, k] = turn(x, LANES - 2 - (28 * f + 4 * k), 1)
        tile_stage(
            planes,
            lambda c, f, k: held[c, f, k],
            mets,
            lambda kind, c, f, k: beyond(rims[CH * kind + c, f, k], rows),
            0,
            (fk, ws, acc),
            keep,
        )

    stage(base, ends, vax, vay)
    wait_all(late)

    def move(k, source):
        for c in range(CH):
            at = 12 * k
            mine = jnp.where(sub < 4, inner[c, at : at + 8], inner[c, at + 4 : at + 12])
            for f in range(2):
                sec[c, f, k] = mix(f, mine, turn(source[c, f, k], 2 if f == 1 else -2, 0))

    for k in range(planes):
        move(k, sec)
    move(planes, base)

    def shifted(x):
        return jnp.where(low_lanes, turn(x, -2, 0), turn(x, 2, 0))

    w1, p1, h1 = point(ends)
    w0, p0, h0 = point(twice)
    new, old = flux(ends, w1, p1, h1, vbx, vby), flux(twice, w0, p0, h0, *wrapped)
    at_j = along(0)
    touched = within(sub, jnp.where(low_lanes, 4, 2), 2)
    second = []
    for c in range(CH):
        add = niv * slope(new[c] - old[c], at_j)
        if c > 0:
            add = add + cw * curve(w1[c - 1] - w0[c - 1], at_j)
        x = jnp.where(low_lanes, ends_sec[c], turn(ends_sec[c], 28, 1))
        second.append(shifted(x + jnp.where(touched, add, 0.0)))

    def mirror(at_low):
        def reflect(*second):
            second = list(second)
            for k in range(planes):
                for f in range(2):
                    to = 28 * f + 4 * k + (0 if at_low else 2)
                    shift = to - 1 if at_low else to + 1 - rows
                    for c in range(CH):
                        x = sec[c, f, k]
                        x = jnp.where(lane == to, turn(x, shift, 1), turn(x, shift + 2, 1))
                        if at_low and 1 <= c <= 3:
                            x = -x
                        second[c] = jnp.where(within(lane, to, 2), x, second[c])
            return tuple(second)

        return reflect

    def leave(*second):
        return second

    second = lax.cond(low_wall, mirror(True), leave, *second)
    second = lax.cond(high_wall, mirror(False), leave, *second)
    stage(sec, second, shifted(vax), shifted(vay))

    per = LANES // 8

    for k in range(planes):
        for c in range(CH):
            x = jnp.where(sub < 4, turn(sec[c, 1, k], -2, 0), turn(sec[c, 0, k], 2, 0))
            at = (c * planes + k) * 8
            turned[at : at + 8] = 0.5 * (own[c, k * 8 : k * 8 + 8] + x)
    for n in range(turned.shape[0] // LANES):
        back[n] = turned[n * LANES : (n + 1) * LANES].T
    inside = within(lane, 4, LANES - 8)
    size = max(8, rows // PIECES)

    def leave(start):
        at = pl.ds(start, size)
        targets = [next_dens.at[0, :, at], next_en.at[0, :, at], next_mom.at[0, :, :, at]]
        sources = [full.at[0, :, at], full.at[4, :, at], full.at[1:4, :, at]]
        first = 3 * (start // size)
        return [
            pltpu.make_async_copy(src, dst, sems.at[first + n])
            for n, (src, dst) in enumerate(zip(sources, targets))
        ]

    def merge(r):
        at = pl.ds(r, 8)
        for c in range(CH):
            for k in range(planes):
                index = c * planes + k
                moved = turn(back[index // per, at], LANES - 4 - 8 * (index % per), 1)
                full[c, k, at] = jnp.where(inside, out[c, k, pl.ds(r + PAD, 8)], moved)

        @pl.when(lax.rem(r + 8, size) == 0)
        def _():
            for copy in leave(pl.multiple_of(r + 8 - size, 8)):
                copy.start()

    chunks(rows // 8, merge, unroll=2)
    for n in range(rows // size):
        wait_all(leave(n * size))


def local(mesh_shape, density, momentum, energy, metrics, volume, placed, neighbour, face, orient):
    halves = mesh_shape["ij"]
    blocks = mesh_shape["blk"]
    planes, rows = density.shape[1], density.shape[2]
    every = planes + 1
    fields = (density, momentum, energy, metrics, volume)
    neighbour, face, orient = neighbour.T, face.T, orient.T
    vmem = pl.BlockSpec(memory_space=pltpu.VMEM)
    smem = pl.BlockSpec(memory_space=pltpu.SMEM)
    hbm = pl.BlockSpec(memory_space=pltpu.HBM)
    anywhere = pl.BlockSpec(memory_space=pl.ANY)

    def call(kernel, name, outs, ins, out_specs, scratch, cost=None, alias=None):
        run = pl.pallas_call(
            kernel,
            out_shape=[
                held(x) if spec is vmem else far(x) if spec is hbm else x
                for x, spec in zip(outs, out_specs)
            ],
            in_specs=ins,
            out_specs=out_specs,
            scratch_shapes=scratch,
            compiler_params=pltpu.CompilerParams(vmem_limit_bytes=VMEM_MIB * 1024 * 1024),
            cost_estimate=cost,
            input_output_aliases=alias or {},
            name=name,
        )

        def keep(*operands):
            return run(
                *[
                    x
                    if spec not in (vmem, hbm)
                    else pltpu.with_memory_space_constraint(x, spec.memory_space)
                    for x, spec in zip(operands, ins)
                ]
            )

        return keep

    def shape(*dims):
        return jax.ShapeDtypeStruct(dims, jnp.float32)

    def held(x):
        return pltpu.VMEM(x.shape, x.dtype)

    def far(x):
        return pltpu.HBM(x.shape, x.dtype)

    def table(x):
        return pltpu.SMEM(x.shape, jnp.int32)

    def sems(count):
        return pltpu.SemaphoreType.DMA((count,))

    devices = blocks * halves
    sent, passed = shape(devices * SENT, LANES), shape(devices * PASSED, LANES)
    strip, rim = shape(CH, 64, LANES), shape(CH, 8, LANES)
    edge = shape(CH, 4 * every, LANES)
    edges = 1 if halves == 2 else 2
    square = held(shape(CH, LANES, LANES))
    tall = rows + 2 * PAD
    whole = shape(CH, every, tall, LANES)
    rows_about = shape(2, CH, every, 8, LANES)
    to_send, own, about, state, *halo = call(
        functools.partial(cut_kernel, halves),
        "cut",
        [sent, strip, rows_about, whole] + [edge] * edges,
        [hbm] * 8,
        [hbm] + [vmem] * (3 + edges),
        [
            held(sent),
            square,
            held(shape(CH * 64, LANES)),
            table(placed),
            table(face),
            table(orient),
            sems(5 * PIECES),
            sems(3),
            sems(1),
        ],
    )(*fields, placed, face, orient)

    def swap(x):
        x = x.reshape(devices, x.shape[0] // devices, 1, LANES)
        x = lax.all_to_all(x, ("blk", "ij"), 0, 0, tiled=True)
        return x.reshape(x.shape[0] * x.shape[1], LANES)

    if edges == 1:
        below = above = lax.ppermute(halo[0], "ij", [(0, 1), (1, 0)])
    else:
        below = lax.ppermute(halo[1], "ij", [(i, i + 1) for i in range(halves - 1)])
        above = lax.ppermute(halo[0], "ij", [(i + 1, i) for i in range(halves - 1)])
    got = swap(to_send)

    padded = held(shape(CH, planes, tall, LANES))
    stage = [
        held(shape(8, tall, LANES)),
        padded,
        held(shape(4, planes, tall, LANES)),
        padded,
        padded,
    ]
    work = planes * rows * LANES
    cost = pl.CostEstimate(flops=300 * work, bytes_accessed=150 * work, transcendentals=work)
    route = jax.ShapeDtypeStruct((2 * blocks,), jnp.int32)
    state, route_out = call(
        first_kernel,
        "first_section",
        [whole, route],
        [vmem] + [hbm] * 4,
        [vmem, smem],
        stage + [table(x) for x in (placed, neighbour, face, orient, placed)] + [sems(4)],
        cost,
        {0: 0},
    )(state, placed, neighbour, face, orient)
    (relayed,) = call(
        functools.partial(relay_kernel, halves, rows, planes, devices),
        "relay",
        [passed],
        [anywhere, anywhere, vmem],
        [hbm],
        [
            held(passed),
            held(shape(devices * 16, LANES)),
            held(shape(devices * 16, LANES)),
            held(shape(devices * 2, LANES)),
            table(route),
            sems(2),
        ],
    )(route_out, below, got)
    ghosts = swap(relayed)
    tiles = held(shape(CH, 2, every, 8, LANES))
    state, _, ends_base, ends_sec, inner = call(
        functools.partial(ends_kernel, halves),
        "ends",
        [whole, rows_about, rim, rim, shape(CH, 12 * every + 4, LANES)],
        [vmem] * 4 + [hbm],
        [vmem] * 3 + [hbm, vmem],
        [tiles] * 3 + [square, held(rim), sems(1)],
        cost,
        {0: 0, 1: 1},
    )(state, about, below, above, relayed)
    (state,) = call(
        second_kernel,
        "second_section",
        [whole],
        [vmem] + [hbm] * 3,
        [vmem],
        [held(shape(CH, planes, rows, LANES))] + stage + [sems(3)],
        cost,
        {0: 0},
    )(state, density, momentum, energy)
    flat = -(-CH * planes * 8 // LANES)
    return call(
        functools.partial(last_kernel, halves, rows, planes),
        "strips",
        [shape(*density.shape), shape(*momentum.shape), shape(*energy.shape)],
        [vmem] * 2 + [hbm] + [vmem] * 3,
        [hbm] * 3,
        [tiles] * 5
        + [
            held(shape(CH + 4, 2, planes, 8, LANES)),
            held(shape(flat * LANES, LANES)),
            held(shape(flat, LANES, LANES)),
            held(shape(CH, planes, rows, LANES)),
            held(rim),
            sems(3 * PIECES + 1),
        ],
    )(own, ends_base, ends_sec, inner, ghosts, state)


def solution(mesh):
    return jax.shard_map(
        functools.partial(local, dict(mesh.shape)),
        mesh=mesh,
        in_specs=(
            P("blk", None, "ij", None),
            P("blk", None, None, "ij", None),
            P("blk", None, "ij", None),
            P("blk", None, "ij", None),
            P("blk", "ij", None),
            P(),
            P(),
            P(),
            P(),
        ),
        out_specs=(
            P("blk", None, "ij", None),
            P("blk", None, None, "ij", None),
            P("blk", None, "ij", None),
        ),
        check_vma=False,
    )
```

```python
import functools

import jax
import jax.numpy as jnp
from jax import lax
from jax.experimental import pallas as pl
from jax.experimental.pallas import tpu as pltpu
from jax.sharding import PartitionSpec as P

pressure_factor = 0.4
viscosity = 0.05
time_step = 0.03
unit = time_step / 12.0

LANES = 128
PAD = 8
PIECES = 8
DEPTH = 4
CH = 5
VMEM_MIB = 32
SENT = 2 * CH
PASSED = 2 * CH + 1
FIRST = 4


def turn(x, shift, axis):
    shift = shift % x.shape[axis]
    return x if shift == 0 else pltpu.roll(x, shift, axis)


def lanes_of(shape):
    return lax.broadcasted_iota(jnp.int32, shape, len(shape) - 1)


def rows_of(shape):
    return lax.broadcasted_iota(jnp.int32, shape, len(shape) - 2)


def point(f):
    rho, m1, m2, m3, e = f
    r = 1.0 / rho
    u1, u2, u3 = m1 * r, m2 * r, m3 * r
    kin = 0.5 * (m1 * u1 + m2 * u2 + m3 * u3)
    p = pressure_factor * (e - kin)
    return (u1, u2, u3, (kin + 2.0 * p) * r), p, e + p


def metric_terms(m):
    ax, ay, bx, by, v = m
    kv = viscosity * unit
    rw = kv * (ax * ax + ay * ay)
    cw = kv * (bx * bx + by * by)
    return v * ax, v * ay, v * bx, v * by, -unit / v, rw, cw, 30.0 * (rw + cw + kv)


def flux(f, w, p, h, gx, gy):
    rho, m1, m2, m3, _ = f
    u = gx * w[0] + gy * w[1]
    return (rho * u, m1 * u + gx * p, m2 * u + gy * p, m3 * u, h * u)


def flux_planes(f, w, p, h):
    u3 = w[2]
    return (f[3], f[1] * u3, f[2] * u3, f[3] * u3 + p, h * u3)


def slope(x, at):
    return 8.0 * (at(x, 1) - at(x, -1)) - (at(x, 2) - at(x, -2))


def curve(x, at):
    return 16.0 * (at(x, 1) + at(x, -1)) - (at(x, 2) + at(x, -2))


def along(axis):
    return lambda x, o: turn(x, -o, axis)


def within(lane, start, size):
    return (lane >= start) & (lane < start + size)


def roll_by(x, shift, axis=1):
    size = x.shape[axis]
    return pltpu.roll(x, lax.rem(shift + 4 * size, size), axis)


def across(x):
    if x.shape[0] < LANES:
        x = jnp.concatenate([x, jnp.zeros((LANES - x.shape[0], LANES), jnp.float32)], axis=0)
    return x.T


def loop(count, body, unroll=1):
    def step(n, _):
        body(n)
        return 0

    lax.fori_loop(0, count, step, 0, unroll=unroll)


def copy_all(pairs, sems, first=0):
    copies = [
        pltpu.make_async_copy(src, dst, sems.at[first + n]) for n, (src, dst) in enumerate(pairs)
    ]
    for copy in copies:
        copy.start()
    return copies


def state_pairs(fields, state, planes, start, size):
    dens, mom, en, met, vol = fields
    at, to = pl.ds(start, size), pl.ds(start + PAD, size)
    return [
        (dens.at[0, :, at], state.at[0, 0:planes, to]),
        (mom.at[0, :, :, at], state.at[1:4, 0:planes, to]),
        (en.at[0, :, at], state.at[4, 0:planes, to]),
        (met.at[0, :, at], state.at[0:4, planes, to]),
        (vol.at[0, at], state.at[4, planes, to]),
    ]


def arrive_in_pieces(fields, state, sems):
    planes, rows = fields[0].shape[1], fields[0].shape[2]
    size = max(8, rows // PIECES)
    for n in range(rows // size):
        copy_all(state_pairs(fields, state, planes, n * size, size), sems, 5 * n)

    def expect(start):
        @pl.when(lax.rem(start, size) == 0)
        def _():
            for n, (src, dst) in enumerate(state_pairs(fields, state, planes, start, size)):
                pltpu.make_async_copy(src, dst, sems.at[5 * (start // size) + n]).wait()

    return expect


def wait_all(copies):
    for copy in copies:
        copy.wait()


def tile_stage(planes, load, mets, shift_i, shift_j, hold, done):
    kv = viscosity * unit
    fk, ws, acc = hold

    def spread(k):
        for s in range(2):
            vax, vay, vbx, vby, niv, rw, cw, tw = mets[s]
            x = [load(c, s, k) for c in range(CH)]
            w, p, h = point(x)
            fi, fj = flux(x, w, p, h, vax, vay), flux(x, w, p, h, vbx, vby)
            for c in range(CH):
                val = niv * (slope(fi[c], shift_i(0, c, s, k)) + slope(fj[c], shift_j))
                if c > 0:
                    v = w[c - 1]
                    val = val + (
                        rw * curve(v, shift_i(1, c - 1, s, k)) + cw * curve(v, shift_j) - tw * v
                    )
                    ws[c - 1, s, k] = v
                acc[c, s, k] = x[c] + val
            for c, v in enumerate(flux_planes(x, w, p, h)):
                fk[c, s, k] = v

    def gather(k):
        at = {o: lax.rem(k + o + planes, planes) for o in (-2, -1, 0, 1, 2)}
        for s in range(2):
            for c in range(CH):
                val = acc[c, s, k] - unit * slope(0, lambda _, o: fk[c, s, at[o]])
                if c > 0:
                    val = val + kv * curve(0, lambda _, o: ws[c - 1, s, at[o]])
                done(c, s, k, val)

    loop(planes, spread)
    loop(planes, gather)


def cut_kernel(
    halves, dens, mom, en, met, vol, placed_at, face_at, orient_at, send, own, tall, state, *rest
):
    edges, rest = rest[: 1 if halves == 2 else 2], rest[1 if halves == 2 else 2 :]
    held_send, packed, strips, placed, face, orient, sems, table_sems, out_sems = rest
    tables = copy_all(
        [(placed_at, placed), (face_at, face), (orient_at, orient)], table_sems
    )
    planes, rows = dens.shape[1], dens.shape[2]
    expect = arrive_in_pieces((dens, mom, en, met, vol), state, sems)
    half = lax.axis_index("ij")
    lane = lanes_of((8, LANES))
    if rows < LANES:
        packed[...] = jnp.zeros(packed.shape, jnp.float32)
    def pack(r):
        expect(r)
        for c in range(CH):
            packs = jnp.zeros((8, LANES), jnp.float32)
            for k in range(planes + 1):
                x = turn(state[c, k, pl.ds(r + PAD, 8)], 8 * k + 4, 1)
                packs = jnp.where(within(lane, 8 * k, 8), x, packs)
            packed[c, pl.ds(r, 8)] = packs

    chunks(rows // 8, pack, unroll=2)

    def cut_ends(k):
        for c in range(CH):
            low, high = state[c, k, PAD : PAD + 4], state[c, k, PAD + rows - 4 : PAD + rows]
            tall[0, c, k, 4:8] = low
            tall[1, c, k, 0:4] = high
            if len(edges) == 1:
                edges[0][c, k * 4 : k * 4 + 4] = jnp.where(half == 0, high, low)
            else:
                edges[0][c, k * 4 : k * 4 + 4] = low
                edges[1][c, k * 4 : k * 4 + 4] = high

    for k in range(planes + 1):
        cut_ends(k)

    wait_all(tables)
    block = placed[lax.axis_index("blk")]
    row = rows_of((64, LANES))
    high_side = row % 8 < 4
    mirror = jnp.where(
        rows_of((LANES, LANES)) + lanes_of((LANES, LANES)) == rows - 1, 1.0, 0.0
    ).astype(jnp.bfloat16)
    flip = [jnp.where(orient[f, block] == 1, -1.0, 1.0) for f in range(2)]
    same = [jnp.where(face[f, block] == f, -1.0, 1.0) for f in range(2)]
    rising = [face[f, block] == 1 for f in range(2)]
    turned = jnp.where(high_side, flip[1], flip[0])
    facing = jnp.where(high_side, same[1], same[0])

    def orient_strip(c):
        strip = packed[c].T[0:64]
        own[c] = strip
        rest, parts = strip, []
        for _ in range(3):
            parts.append(rest.astype(jnp.bfloat16))
            rest = rest - parts[-1].astype(jnp.float32)
        back = jnp.dot(
            jnp.concatenate(parts, axis=0), mirror, preferred_element_type=jnp.float32
        )
        back = back[0:64] + (back[64:128] + back[128:192])
        moved = jnp.where(turned < 0.0, back, strip)
        sign = jnp.where(c < 2, turned, jnp.where(c < 4, facing, 1.0))
        moved = jnp.where(row >= planes * 8, moved * sign, moved)
        strips[pl.ds(pl.multiple_of(c * 64, 64), 64)] = moved

    loop(CH, orient_strip, unroll=CH)

    def put(n):
        k, e = n >> 2, n & 3
        at = (FIRST + n) * SENT
        low = k * 8 + 4 + jnp.where(rising[0], e, 3 - e)
        high = k * 8 + jnp.where(rising[1], 3 - e, e)
        held_send[pl.ds(at, CH)] = strips[pl.ds(low, CH, stride=64)]
        held_send[pl.ds(at + CH, CH)] = strips[pl.ds(high, CH, stride=64)]

    loop(DEPTH * (planes + 1), put, unroll=4)
    wait_all(copy_all([(held_send, send)], out_sems))


def relay_kernel(
    halves, rows, planes, devices, route_at, halo, held_got, send,
    held_send, below, above, signs, route, sems,
):
    del halo
    wait_all(copy_all([(route_at, route)], sems, 1))
    me = lax.axis_index("blk") * halves + lax.axis_index("ij")
    is_field = (me >= FIRST) & (me < FIRST + DEPTH * planes)

    def pass_on(slot):
        for f in range(2):
            code = route[2 * slot + f]
            partner, side, turned = code >> 2, (code >> 1) & 1, code & 1
            sign = jnp.where(turned == 1, -1.0, 1.0)

            def piece(h):
                h = jnp.where(turned == 1, halves - 1 - h, h)
                return held_got[pl.ds((partner * halves + h) * SENT + side * CH, CH)]

            pieces = [piece(h) for h in range(halves)]
            for half in range(halves):
                at = slot * halves + half
                held_send[pl.ds(at * PASSED + f * CH, CH)] = pieces[half]
                below[pl.ds((f * devices + at) * 8, CH)] = pieces[max(half - 1, 0)]
                above[pl.ds((f * devices + at) * 8, CH)] = pieces[min(half + 1, halves - 1)]
                signs[pl.ds(f * devices + at, 1)] = jnp.full((1, LANES), sign, jnp.float32)

    loop(devices // halves, pass_on, unroll=4)
    count = 2 * devices
    lane = lanes_of((count, LANES))
    half = rows_of((count, LANES)) % halves
    sign = signs[...]
    ends = jnp.zeros((count, LANES), jnp.float32)
    for c in range(CH):
        low, high = below[pl.ds(c, count, stride=8)], above[pl.ds(c, count, stride=8)]
        at = 4 * c
        low_wall = jnp.where(lane == at, turn(low, at - 1, 1), turn(low, at + 1, 1))
        high_wall = jnp.where(
            lane == at + 2, turn(high, at + 3 - rows, 1), turn(high, at + 5 - rows, 1)
        )
        if 1 <= c <= 3:
            low_wall = jnp.where(is_field, -sign * low_wall, low_wall)
            high_wall = jnp.where(is_field, sign * high_wall, high_wall)
        low = jnp.where(half == 0, low_wall, turn(low, at + 2 - rows, 1))
        high = jnp.where(half == halves - 1, high_wall, turn(high, at + 2, 1))
        ends = jnp.where(within(lane, at, 2), low, jnp.where(within(lane, at + 2, 2), high, ends))
    held_send[pl.ds(2 * CH, devices, stride=PASSED)] = ends[0:devices] + turn(
        ends[devices:], 4 * CH, 1
    )
    wait_all(copy_all([(held_send, send)], sems))


def flux_chunk(get, mets, fi, w, fk, acc, r):
    rows = pl.ds(r, 8)
    vax, vay, vbx, vby, niv, rw, cw, tw = [mets[j, rows] for j in range(8)]
    at_j = along(1)
    for k in range(fi.shape[1]):
        f = [get(c, k, r) for c in range(CH)]
        wk, p, h = point(f)
        for c, x in enumerate(flux(f, wk, p, h, vax, vay)):
            fi[c, k, rows] = x
        for c in range(4):
            w[c, k, rows] = wk[c]
        fj = flux(f, wk, p, h, vbx, vby)
        for c in range(CH):
            val = niv * slope(fj[c], at_j)
            if c > 0:
                val = val + (cw * curve(wk[c - 1], at_j) - tw * wk[c - 1])
            acc[c, k, rows] = val
        for c, x in enumerate(flux_planes(f, wk, p, h)):
            fk[c, k, rows] = x


def sum_chunk(mets, fi, w, fk, acc, r, emit):
    planes = fi.shape[1]
    kv = viscosity * unit
    rows = pl.ds(r, 8)
    niv, rw = mets[4, rows], mets[5, rows]
    for c in range(CH):
        t = [fk[c, k, rows] for k in range(planes)]
        x = [w[c - 1, k, rows] for k in range(planes)] if c > 0 else None
        for k in range(planes):

            def near(v, o):
                return v[(k + o) % planes]

            def at_i(v, o):
                return v[pl.ds(r + o, 8)]

            val = acc[c, k, rows] + niv * slope(fi.at[c, k], at_i) - unit * slope(t, near)
            if c > 0:
                val = val + (rw * curve(w.at[c - 1, k], at_i) + kv * curve(x, near))
            emit(c, k, r, val)


def chunks(count, body, unroll=1):
    def step(n, _):
        body(pl.multiple_of(n * 8, 8))
        return 0

    lax.fori_loop(0, count, step, 0, unroll=unroll)


def first_kernel(
    state_in, placed_at, neighbour_at, face_at, orient_at, state, route,
    mets, fi, w, fk, acc, placed, neighbour, face, orient, where_is, sems,
):
    del state_in
    planes, rows = fi.shape[1], fi.shape[2] - 2 * PAD
    pairs = zip((placed_at, neighbour_at, face_at, orient_at), (placed, neighbour, face, orient))
    tables = copy_all(list(pairs), sems)
    count = rows // 8
    blocks = placed.shape[0]
    share = -(-blocks // count)

    def slots(n):
        return [jnp.minimum((n // 8) * share + i, blocks - 1) for i in range(share)]

    def get(c, k, r):
        return state[c, k, pl.ds(r, 8)]

    def fluxes(n):
        at = pl.ds(n + PAD, 8)
        for j, x in enumerate(metric_terms([state[c, planes, at] for c in range(CH)])):
            mets[j, at] = x
        flux_chunk(get, mets, fi, w, fk, acc, n + PAD)

    def emit(c, k, r, val):
        state[c, k, pl.ds(r, 8)] = get(c, k, r) + val

    def sums(n):
        for slot in slots(n):
            block = placed[slot]
            for f in range(2):
                partner = where_is[neighbour[f, block]]
                route[2 * slot + f] = partner * 4 + face[f, block] * 2 + orient[f, block]
        sum_chunk(mets, fi, w, fk, acc, n + PAD, emit)

    def note(slot):
        where_is[placed[slot]] = slot

    chunks(count, fluxes, unroll=2)
    wait_all(tables)
    loop(blocks, note, unroll=8)
    chunks(count, sums)


def pack_ends(tall, planes):
    sub, lane = rows_of((8, LANES)), lanes_of((8, LANES))
    stacked = []
    for c in range(CH):
        packed = jnp.zeros((8, LANES), jnp.float32)
        for k in range(planes):
            x = turn(jnp.where(sub < 4, tall[0, c, k], tall[1, c, k]), 8 * k + 4, 1)
            packed = jnp.where(within(lane, 8 * k, 8), x, packed)
        stacked.append(packed)
    ends = across(jnp.concatenate(stacked, axis=0))
    out = []
    for c in range(CH):
        packed = jnp.zeros((8, LANES), jnp.float32)
        for k in range(planes):
            x = turn(ends[k * 8 : k * 8 + 8], 4 * k - (8 * c + 2), 1)
            packed = jnp.where(within(lane, 4 * k, 4), x, packed)
        out.append(packed)
    return out


def ends_kernel(
    halves, state_in, tall_in, low, high, after, state, tall, ends_base, ends_sec, inner,
    tile_fk, tile_w, tile_acc, packed, rims, sems,
):
    del state_in, tall_in, after
    planes, rows = tall.shape[2] - 1, state.shape[2] - 2 * PAD
    every = planes + 1
    half = lax.axis_index("ij")
    low_wall, high_wall = half == 0, half == halves - 1
    low_flag, high_flag = jnp.where(low_wall, 1, 0), jnp.where(high_wall, 1, 0)
    sub, lane = rows_of((8, LANES)), lanes_of((8, LANES))
    top = PAD + rows

    @pl.when(low_wall)
    def _():
        for c in range(CH):
            for k in range(every):
                for n in range(2):
                    x = tall[0, c, k, 4 + n : 5 + n]
                    tall[0, c, k, 3 - n : 4 - n] = -x if 1 <= c <= 3 and k < planes else x

    @pl.when(jnp.logical_not(low_wall))
    def _():
        for c in range(CH):
            for k in range(every):
                tall[0, c, k, 0:4] = low[c, 4 * k : 4 * k + 4]

    @pl.when(high_wall)
    def _():
        for c in range(CH):
            for k in range(every):
                for n in range(2):
                    tall[1, c, k, 4 + n : 5 + n] = tall[1, c, k, 3 - n : 4 - n]

    @pl.when(jnp.logical_not(high_wall))
    def _():
        for c in range(CH):
            for k in range(every):
                tall[1, c, k, 4:8] = high[c, 4 * k : 4 * k + 4]

    for c, x in enumerate(pack_ends(tall, every)):
        ends_base[c] = x
    for c in range(CH):
        state[c, planes, PAD - 4 : PAD] = tall[0, c, planes, 0:4]
        state[c, planes, top : top + 4] = tall[1, c, planes, 4:8]
    mets = [metric_terms([tall[s, c, planes] for c in range(CH)]) for s in range(2)]

    def done(c, s, k, x):
        tall[s, c, k] = x
        if s == 0:
            sign = -1.0 if 1 <= c <= 3 else 1.0
            wall = sign * jnp.where(sub == 2, turn(x, -3, 0), turn(x, -1, 0))
            x = jnp.where((sub < 4) & (low_flag == 1), wall, x)
        else:
            wall = jnp.where(sub == 4, turn(x, 1, 0), turn(x, 3, 0))
            x = jnp.where((sub >= 4) & (high_flag == 1), wall, x)
        start = PAD - 2 if s == 0 else top - 2
        state[c, k, start : start + 4] = x[2:6]

    tile_stage(
        planes, lambda c, s, k: tall[s, c, k], mets, lambda *_: along(0), along(1),
        (tile_fk, tile_w, tile_acc), done,
    )
    for c, x in enumerate(pack_ends(tall, planes)):
        rims[c] = x
    leaving = copy_all([(rims, ends_sec)], sems)

    if rows < LANES:
        packed[...] = jnp.zeros(packed.shape, jnp.float32)

    def pack(n):
        at = pl.ds(n + PAD, 8)
        for c in range(CH):
            packs = turn(state[c, planes, at], 12 * planes + 6, 1)
            for k in range(planes):
                x = turn(state[c, k, at], 12 * k + 6, 1)
                packs = jnp.where(within(lane, 12 * k, 12), x, packs)
            packed[c, pl.ds(n, 8)] = packs

    chunks(rows // 8, pack, unroll=2)
    for c in range(CH):
        inner[c] = packed[c].T[0 : inner.shape[1]]
    wait_all(leaving)


def second_kernel(
    state_in, dens, mom, en, state, fields, mets, fi, w, fk, acc, sems
):
    del state_in
    planes, rows = fields.shape[1:3]
    pairs = [(dens.at[0], fields.at[0]), (mom.at[0], fields.at[1:4]), (en.at[0], fields.at[4])]
    copies = copy_all(pairs, sems)

    def get(c, k, r):
        return state[c, k, pl.ds(r, 8)]

    def fluxes(n):
        at = pl.ds(n, 8)
        for j, x in enumerate(metric_terms([state[c, planes, at] for c in range(CH)])):
            mets[j, at] = x
        flux_chunk(get, mets, fi, w, fk, acc, n)

    def emit(c, k, r, val):
        x = 0.5 * (fields[c, k, pl.ds(r - PAD, 8)] + (get(c, k, r) + val))
        state[c, k, pl.ds(r, 8)] = x

    chunks(rows // 8 + 2, fluxes, unroll=2)
    wait_all(copies)
    chunks(rows // 8, lambda n: sum_chunk(mets, fi, w, fk, acc, n + PAD, emit))


def beyond(low, rows):
    top = rows % LANES
    high = low if top == 0 else turn(low, top, 1)
    lane = lanes_of(low.shape)

    def at(x, o):
        if o < 0:
            x = jnp.where(lane >= LANES + o, low, x)
        else:
            x = jnp.where(within(lane, top, o), high, x)
        return turn(x, -o, 1)

    return at


def last_kernel(
    halves, rows, planes, own, ends_base, ends_sec_at, inner, got, out,
    next_dens, next_mom, next_en,
    base, sec, fk, ws, acc, rims, turned, back, full, ends_sec, sems,
):
    late = copy_all([(ends_sec_at, ends_sec)], sems, 3 * PIECES)
    half = lax.axis_index("ij")
    low_wall, high_wall = half == 0, half == halves - 1
    sub, lane = rows_of((8, LANES)), lanes_of((8, LANES))

    def mix(f, mine, others):
        return jnp.where((sub < 4) == (f == 1), mine, others)

    others = [jnp.zeros((8, LANES), jnp.float32)] * CH
    for k in range(planes + 1):
        start = DEPTH * k * PASSED
        for f in range(2):

            def ghost(row):
                x = got[pl.ds(start + row, 8, stride=PASSED)]
                return x if f == 1 else turn(x, 4, 0)

            arrived = ghost(2 * CH)
            to = 28 * f + 4 * k
            for c in range(CH):
                base[c, f, k] = mix(f, own[c, k * 8 : k * 8 + 8], ghost(f * CH + c))
                moved = turn(arrived, to - 4 * CH * f - 4 * c, 1)
                others[c] = jnp.where(within(lane, to, 4), moved, others[c])

    low_lanes = lane < 28
    twice = [jnp.where(low_lanes, ends_base[c], turn(ends_base[c], 28, 1)) for c in range(CH)]
    ends = [jnp.where(low_lanes == (sub >= 4), twice[c], others[c]) for c in range(CH)]
    slot = jnp.where(low_lanes, lane, lane - 28)

    def spread(x):
        y = x
        for k in range(planes):
            y = jnp.where(within(slot, 4 * k, 4), turn(x, 4 * (k - planes), 1), y)
        return y

    vax, vay, vbx, vby, niv, _, cw, _ = [spread(x) for x in metric_terms(ends)]
    wrapped = [spread(x) for x in metric_terms(twice)[2:4]]

    def keep(c, f, k, val):
        sec[c, f, k] = val

    def stage(held, ends, gx, gy):
        mets = [metric_terms([held[c, f, planes] for c in range(CH)]) for f in range(2)]
        w, p, h = point(ends)
        for n, x in enumerate((*flux(ends, w, p, h, gx, gy), *w)):
            for f in range(2):
                for k in range(planes):
                    rims[n, f, k] = turn(x, LANES - 2 - (28 * f + 4 * k), 1)
        tile_stage(
            planes,
            lambda c, f, k: held[c, f, k],
            mets,
            lambda kind, c, f, k: beyond(rims[CH * kind + c, f, k], rows),
            along(0),
            (fk, ws, acc),
            keep,
        )

    stage(base, ends, vax, vay)
    wait_all(late)

    def move(k, source):
        for c in range(CH):
            at = 12 * k
            mine = jnp.where(sub < 4, inner[c, at : at + 8], inner[c, at + 4 : at + 12])
            for f in range(2):
                sec[c, f, k] = mix(f, mine, turn(source[c, f, k], 2 if f == 1 else -2, 0))

    for k in range(planes):
        move(k, sec)
    move(planes, base)

    def shifted(x):
        return jnp.where(low_lanes, turn(x, -2, 0), turn(x, 2, 0))

    w1, p1, h1 = point(ends)
    w0, p0, h0 = point(twice)
    new, old = flux(ends, w1, p1, h1, vbx, vby), flux(twice, w0, p0, h0, *wrapped)
    at_j = along(0)
    touched = within(sub, jnp.where(low_lanes, 4, 2), 2)
    second = []
    for c in range(CH):
        add = niv * slope(new[c] - old[c], at_j)
        if c > 0:
            add = add + cw * curve(w1[c - 1] - w0[c - 1], at_j)
        x = jnp.where(low_lanes, ends_sec[c], turn(ends_sec[c], 28, 1))
        second.append(shifted(x + jnp.where(touched, add, 0.0)))

    def mirror(at_low):
        def reflect(*second):
            second = list(second)
            for k in range(planes):
                for f in range(2):
                    to = 28 * f + 4 * k + (0 if at_low else 2)
                    shift = to - 1 if at_low else to + 1 - rows
                    for c in range(CH):
                        x = sec[c, f, k]
                        x = jnp.where(lane == to, turn(x, shift, 1), turn(x, shift + 2, 1))
                        if at_low and 1 <= c <= 3:
                            x = -x
                        second[c] = jnp.where(within(lane, to, 2), x, second[c])
            return tuple(second)

        return reflect

    def leave(*second):
        return second

    second = lax.cond(low_wall, mirror(True), leave, *second)
    second = lax.cond(high_wall, mirror(False), leave, *second)
    stage(sec, second, shifted(vax), shifted(vay))

    per = LANES // 8

    for k in range(planes):
        for c in range(CH):
            x = jnp.where(sub < 4, turn(sec[c, 1, k], -2, 0), turn(sec[c, 0, k], 2, 0))
            at = (c * planes + k) * 8
            turned[at : at + 8] = 0.5 * (own[c, k * 8 : k * 8 + 8] + x)
    for n in range(turned.shape[0] // LANES):
        back[n] = turned[n * LANES : (n + 1) * LANES].T
    inside = within(lane, 4, LANES - 8)
    size = max(8, rows // PIECES)

    def leave(start):
        at = pl.ds(start, size)
        targets = [next_dens.at[0, :, at], next_en.at[0, :, at], next_mom.at[0, :, :, at]]
        sources = [full.at[0, :, at], full.at[4, :, at], full.at[1:4, :, at]]
        first = 3 * (start // size)
        return [
            pltpu.make_async_copy(src, dst, sems.at[first + n])
            for n, (src, dst) in enumerate(zip(sources, targets))
        ]

    def merge(r):
        at = pl.ds(r, 8)
        for c in range(CH):
            for k in range(planes):
                index = c * planes + k
                moved = turn(back[index // per, at], LANES - 4 - 8 * (index % per), 1)
                full[c, k, at] = jnp.where(inside, out[c, k, pl.ds(r + PAD, 8)], moved)

        @pl.when(lax.rem(r + 8, size) == 0)
        def _():
            for copy in leave(pl.multiple_of(r + 8 - size, 8)):
                copy.start()

    chunks(rows // 8, merge, unroll=2)
    for n in range(rows // size):
        wait_all(leave(n * size))


def local(mesh_shape, density, momentum, energy, metrics, volume, placed, neighbour, face, orient):
    halves = mesh_shape["ij"]
    blocks = mesh_shape["blk"]
    planes, rows = density.shape[1], density.shape[2]
    every = planes + 1
    fields = (density, momentum, energy, metrics, volume)
    neighbour, face, orient = neighbour.T, face.T, orient.T
    vmem = pl.BlockSpec(memory_space=pltpu.VMEM)
    smem = pl.BlockSpec(memory_space=pltpu.SMEM)
    hbm = pl.BlockSpec(memory_space=pltpu.HBM)
    anywhere = pl.BlockSpec(memory_space=pl.ANY)

    def call(kernel, name, outs, ins, out_specs, scratch, cost=None, alias=None):
        run = pl.pallas_call(
            kernel,
            out_shape=[
                held(x) if spec is vmem else far(x) if spec is hbm else x
                for x, spec in zip(outs, out_specs)
            ],
            in_specs=ins,
            out_specs=out_specs,
            scratch_shapes=scratch,
            compiler_params=pltpu.CompilerParams(vmem_limit_bytes=VMEM_MIB * 1024 * 1024),
            cost_estimate=cost,
            input_output_aliases=alias or {},
            name=name,
        )

        def keep(*operands):
            return run(
                *[
                    x
                    if spec not in (vmem, hbm)
                    else pltpu.with_memory_space_constraint(x, spec.memory_space)
                    for x, spec in zip(operands, ins)
                ]
            )

        return keep

    def shape(*dims):
        return jax.ShapeDtypeStruct(dims, jnp.float32)

    def held(x):
        return pltpu.VMEM(x.shape, x.dtype)

    def far(x):
        return pltpu.HBM(x.shape, x.dtype)

    def table(x):
        return pltpu.SMEM(x.shape, jnp.int32)

    def sems(count):
        return pltpu.SemaphoreType.DMA((count,))

    devices = blocks * halves
    sent, passed = shape(devices * SENT, LANES), shape(devices * PASSED, LANES)
    strip, rim = shape(CH, 64, LANES), shape(CH, 8, LANES)
    edge = shape(CH, 4 * every, LANES)
    edges = 1 if halves == 2 else 2
    square = held(shape(CH, LANES, LANES))
    tall = rows + 2 * PAD
    whole = shape(CH, every, tall, LANES)
    rows_about = shape(2, CH, every, 8, LANES)
    to_send, own, about, state, *halo = call(
        functools.partial(cut_kernel, halves),
        "cut",
        [sent, strip, rows_about, whole] + [edge] * edges,
        [hbm] * 8,
        [hbm] + [vmem] * (3 + edges),
        [
            held(sent),
            square,
            held(shape(CH * 64, LANES)),
            table(placed),
            table(face),
            table(orient),
            sems(5 * PIECES),
            sems(3),
            sems(1),
        ],
    )(*fields, placed, face, orient)

    def swap(x):
        x = x.reshape(devices, x.shape[0] // devices, 1, LANES)
        x = lax.all_to_all(x, ("blk", "ij"), 0, 0, tiled=True)
        return x.reshape(x.shape[0] * x.shape[1], LANES)

    if edges == 1:
        below = above = lax.ppermute(halo[0], "ij", [(0, 1), (1, 0)])
    else:
        below = lax.ppermute(halo[1], "ij", [(i, i + 1) for i in range(halves - 1)])
        above = lax.ppermute(halo[0], "ij", [(i + 1, i) for i in range(halves - 1)])
    got = swap(to_send)

    padded = held(shape(CH, planes, tall, LANES))
    stage = [
        held(shape(8, tall, LANES)),
        padded,
        held(shape(4, planes, tall, LANES)),
        padded,
        padded,
    ]
    work = planes * rows * LANES
    cost = pl.CostEstimate(flops=300 * work, bytes_accessed=150 * work, transcendentals=work)
    route = jax.ShapeDtypeStruct((2 * blocks,), jnp.int32)
    state, route_out = call(
        first_kernel,
        "first_section",
        [whole, route],
        [vmem] + [hbm] * 4,
        [vmem, smem],
        stage + [table(x) for x in (placed, neighbour, face, orient, placed)] + [sems(4)],
        cost,
        {0: 0},
    )(state, placed, neighbour, face, orient)
    (relayed,) = call(
        functools.partial(relay_kernel, halves, rows, planes, devices),
        "relay",
        [passed],
        [anywhere, anywhere, vmem],
        [hbm],
        [
            held(passed),
            held(shape(devices * 16, LANES)),
            held(shape(devices * 16, LANES)),
            held(shape(devices * 2, LANES)),
            table(route),
            sems(2),
        ],
    )(route_out, below, got)
    ghosts = swap(relayed)
    tiles = held(shape(CH, 2, every, 8, LANES))
    state, _, ends_base, ends_sec, inner = call(
        functools.partial(ends_kernel, halves),
        "ends",
        [whole, rows_about, rim, rim, shape(CH, 12 * every + 4, LANES)],
        [vmem] * 4 + [hbm],
        [vmem] * 3 + [hbm, vmem],
        [tiles] * 3 + [square, held(rim), sems(1)],
        cost,
        {0: 0, 1: 1},
    )(state, about, below, above, relayed)
    (state,) = call(
        second_kernel,
        "second_section",
        [whole],
        [vmem] + [hbm] * 3,
        [vmem],
        [held(shape(CH, planes, rows, LANES))] + stage + [sems(3)],
        cost,
        {0: 0},
    )(state, density, momentum, energy)
    flat = -(-CH * planes * 8 // LANES)
    return call(
        functools.partial(last_kernel, halves, rows, planes),
        "strips",
        [shape(*density.shape), shape(*momentum.shape), shape(*energy.shape)],
        [vmem] * 2 + [hbm] + [vmem] * 3,
        [hbm] * 3,
        [tiles] * 5
        + [
            held(shape(CH + 4, 2, planes, 8, LANES)),
            held(shape(flat * LANES, LANES)),
            held(shape(flat, LANES, LANES)),
            held(shape(CH, planes, rows, LANES)),
            held(rim),
            sems(3 * PIECES + 1),
        ],
    )(own, ends_base, ends_sec, inner, ghosts, state)


def solution(mesh):
    return jax.shard_map(
        functools.partial(local, dict(mesh.shape)),
        mesh=mesh,
        in_specs=(
            P("blk", None, "ij", None),
            P("blk", None, None, "ij", None),
            P("blk", None, "ij", None),
            P("blk", None, "ij", None),
            P("blk", "ij", None),
            P(),
            P(),
            P(),
            P(),
        ),
        out_specs=(
            P("blk", None, "ij", None),
            P("blk", None, None, "ij", None),
            P("blk", None, "ij", None),
        ),
        check_vma=False,
    )
```

```python
import functools

import jax
import jax.numpy as jnp
from jax import lax
from jax.experimental import pallas as pl
from jax.experimental.pallas import tpu as pltpu
from jax.sharding import PartitionSpec as P

pressure_factor = 0.4
viscosity = 0.05
time_step = 0.03
unit = time_step / 12.0

LANES = 128
PAD = 8
PIECES = 4
DEPTH = 4
CH = 5
VMEM_MIB = 32
SENT = 2 * CH
PASSED = 2 * CH + 1
FIRST = 4


def turn(x, shift, axis):
    shift = shift % x.shape[axis]
    return x if shift == 0 else pltpu.roll(x, shift, axis)


def lanes_of(shape):
    return lax.broadcasted_iota(jnp.int32, shape, len(shape) - 1)


def rows_of(shape):
    return lax.broadcasted_iota(jnp.int32, shape, len(shape) - 2)


def point(f):
    rho, m1, m2, m3, e = f
    r = 1.0 / rho
    u1, u2, u3 = m1 * r, m2 * r, m3 * r
    kin = 0.5 * (m1 * u1 + m2 * u2 + m3 * u3)
    p = pressure_factor * (e - kin)
    return (u1, u2, u3, (kin + 2.0 * p) * r), p, e + p


def metric_terms(m):
    ax, ay, bx, by, v = m
    kv = viscosity * unit
    rw = kv * (ax * ax + ay * ay)
    cw = kv * (bx * bx + by * by)
    return v * ax, v * ay, v * bx, v * by, -unit / v, rw, cw, 30.0 * (rw + cw + kv)


def flux(f, w, p, h, gx, gy):
    rho, m1, m2, m3, _ = f
    u = gx * w[0] + gy * w[1]
    return (rho * u, m1 * u + gx * p, m2 * u + gy * p, m3 * u, h * u)


def flux_planes(f, w, p, h):
    u3 = w[2]
    return (f[3], f[1] * u3, f[2] * u3, f[3] * u3 + p, h * u3)


def slope(x, at):
    return 8.0 * (at(x, 1) - at(x, -1)) - (at(x, 2) - at(x, -2))


def curve(x, at):
    return 16.0 * (at(x, 1) + at(x, -1)) - (at(x, 2) + at(x, -2))


def along(axis):
    return lambda x, o: turn(x, -o, axis)


def within(lane, start, size):
    return (lane >= start) & (lane < start + size)


def roll_by(x, shift, axis=1):
    size = x.shape[axis]
    return pltpu.roll(x, lax.rem(shift + 4 * size, size), axis)


def across(x):
    if x.shape[0] < LANES:
        x = jnp.concatenate([x, jnp.zeros((LANES - x.shape[0], LANES), jnp.float32)], axis=0)
    return x.T


def loop(count, body, unroll=1):
    def step(n, _):
        body(n)
        return 0

    lax.fori_loop(0, count, step, 0, unroll=unroll)


def copy_all(pairs, sems, first=0):
    copies = [
        pltpu.make_async_copy(src, dst, sems.at[first + n]) for n, (src, dst) in enumerate(pairs)
    ]
    for copy in copies:
        copy.start()
    return copies


def state_pairs(fields, state, planes, start, size):
    dens, mom, en, met, vol = fields
    at, to = pl.ds(start, size), pl.ds(start + PAD, size)
    return [
        (dens.at[0, :, at], state.at[0, 0:planes, to]),
        (mom.at[0, :, :, at], state.at[1:4, 0:planes, to]),
        (en.at[0, :, at], state.at[4, 0:planes, to]),
        (met.at[0, :, at], state.at[0:4, planes, to]),
        (vol.at[0, at], state.at[4, planes, to]),
    ]


def arrive_in_pieces(fields, state, sems):
    planes, rows = fields[0].shape[1], fields[0].shape[2]
    size = max(8, rows // PIECES)
    for n in range(rows // size):
        copy_all(state_pairs(fields, state, planes, n * size, size), sems, 5 * n)

    def expect(start):
        @pl.when(lax.rem(start, size) == 0)
        def _():
            for n, (src, dst) in enumerate(state_pairs(fields, state, planes, start, size)):
                pltpu.make_async_copy(src, dst, sems.at[5 * (start // size) + n]).wait()

    return expect


def wait_all(copies):
    for copy in copies:
        copy.wait()


def tile_stage(planes, load, mets, shift_i, shift_j, hold, done):
    kv = viscosity * unit
    fk, ws, acc = hold

    def spread(k):
        for s in range(2):
            vax, vay, vbx, vby, niv, rw, cw, tw = mets[s]
            x = [load(c, s, k) for c in range(CH)]
            w, p, h = point(x)
            fi, fj = flux(x, w, p, h, vax, vay), flux(x, w, p, h, vbx, vby)
            for c in range(CH):
                val = niv * (slope(fi[c], shift_i(0, c, s, k)) + slope(fj[c], shift_j))
                if c > 0:
                    v = w[c - 1]
                    val = val + (
                        rw * curve(v, shift_i(1, c - 1, s, k)) + cw * curve(v, shift_j) - tw * v
                    )
                    ws[c - 1, s, k] = v
                acc[c, s, k] = x[c] + val
            for c, v in enumerate(flux_planes(x, w, p, h)):
                fk[c, s, k] = v

    def gather(k):
        at = {o: lax.rem(k + o + planes, planes) for o in (-2, -1, 0, 1, 2)}
        for s in range(2):
            for c in range(CH):
                val = acc[c, s, k] - unit * slope(0, lambda _, o: fk[c, s, at[o]])
                if c > 0:
                    val = val + kv * curve(0, lambda _, o: ws[c - 1, s, at[o]])
                done(c, s, k, val)

    loop(planes, spread)
    loop(planes, gather)


def cut_kernel(
    halves, dens, mom, en, met, vol, placed_at, face_at, orient_at, send, own, tall, state, *rest
):
    edges, rest = rest[: 1 if halves == 2 else 2], rest[1 if halves == 2 else 2 :]
    held_send, packed, strips, placed, face, orient, sems, table_sems, out_sems = rest
    tables = copy_all(
        [(placed_at, placed), (face_at, face), (orient_at, orient)], table_sems
    )
    planes, rows = dens.shape[1], dens.shape[2]
    expect = arrive_in_pieces((dens, mom, en, met, vol), state, sems)
    half = lax.axis_index("ij")
    lane = lanes_of((8, LANES))
    if rows < LANES:
        packed[...] = jnp.zeros(packed.shape, jnp.float32)
    def pack(r):
        expect(r)
        for c in range(CH):
            packs = jnp.zeros((8, LANES), jnp.float32)
            for k in range(planes + 1):
                x = turn(state[c, k, pl.ds(r + PAD, 8)], 8 * k + 4, 1)
                packs = jnp.where(within(lane, 8 * k, 8), x, packs)
            packed[c, pl.ds(r, 8)] = packs

    chunks(rows // 8, pack, unroll=2)

    def cut_ends(k):
        for c in range(CH):
            low, high = state[c, k, PAD : PAD + 4], state[c, k, PAD + rows - 4 : PAD + rows]
            tall[0, c, k, 4:8] = low
            tall[1, c, k, 0:4] = high
            if len(edges) == 1:
                edges[0][c, k * 4 : k * 4 + 4] = jnp.where(half == 0, high, low)
            else:
                edges[0][c, k * 4 : k * 4 + 4] = low
                edges[1][c, k * 4 : k * 4 + 4] = high

    for k in range(planes + 1):
        cut_ends(k)

    wait_all(tables)
    block = placed[lax.axis_index("blk")]
    row = rows_of((64, LANES))
    high_side = row % 8 < 4
    mirror = jnp.where(
        rows_of((LANES, LANES)) + lanes_of((LANES, LANES)) == rows - 1, 1.0, 0.0
    ).astype(jnp.bfloat16)
    flip = [jnp.where(orient[f, block] == 1, -1.0, 1.0) for f in range(2)]
    same = [jnp.where(face[f, block] == f, -1.0, 1.0) for f in range(2)]
    rising = [face[f, block] == 1 for f in range(2)]
    turned = jnp.where(high_side, flip[1], flip[0])
    facing = jnp.where(high_side, same[1], same[0])

    def orient_strip(c):
        strip = packed[c].T[0:64]
        own[c] = strip
        rest, parts = strip, []
        for _ in range(3):
            parts.append(rest.astype(jnp.bfloat16))
            rest = rest - parts[-1].astype(jnp.float32)
        back = jnp.dot(
            jnp.concatenate(parts, axis=0), mirror, preferred_element_type=jnp.float32
        )
        back = back[0:64] + (back[64:128] + back[128:192])
        moved = jnp.where(turned < 0.0, back, strip)
        sign = jnp.where(c < 2, turned, jnp.where(c < 4, facing, 1.0))
        moved = jnp.where(row >= planes * 8, moved * sign, moved)
        strips[pl.ds(pl.multiple_of(c * 64, 64), 64)] = moved

    loop(CH, orient_strip, unroll=CH)

    def put(n):
        k, e = n >> 2, n & 3
        at = (FIRST + n) * SENT
        low = k * 8 + 4 + jnp.where(rising[0], e, 3 - e)
        high = k * 8 + jnp.where(rising[1], 3 - e, e)
        held_send[pl.ds(at, CH)] = strips[pl.ds(low, CH, stride=64)]
        held_send[pl.ds(at + CH, CH)] = strips[pl.ds(high, CH, stride=64)]

    loop(DEPTH * (planes + 1), put, unroll=4)
    wait_all(copy_all([(held_send, send)], out_sems))


def relay_kernel(
    halves, rows, planes, devices, route_at, halo, held_got, send,
    held_send, below, above, signs, route, sems,
):
    del halo
    wait_all(copy_all([(route_at, route)], sems, 1))
    me = lax.axis_index("blk") * halves + lax.axis_index("ij")
    is_field = (me >= FIRST) & (me < FIRST + DEPTH * planes)

    def pass_on(slot):
        for f in range(2):
            code = route[2 * slot + f]
            partner, side, turned = code >> 2, (code >> 1) & 1, code & 1
            sign = jnp.where(turned == 1, -1.0, 1.0)

            def piece(h):
                h = jnp.where(turned == 1, halves - 1 - h, h)
                return held_got[pl.ds((partner * halves + h) * SENT + side * CH, CH)]

            pieces = [piece(h) for h in range(halves)]
            for half in range(halves):
                at = slot * halves + half
                held_send[pl.ds(at * PASSED + f * CH, CH)] = pieces[half]
                below[pl.ds((f * devices + at) * 8, CH)] = pieces[max(half - 1, 0)]
                above[pl.ds((f * devices + at) * 8, CH)] = pieces[min(half + 1, halves - 1)]
                signs[pl.ds(f * devices + at, 1)] = jnp.full((1, LANES), sign, jnp.float32)

    loop(devices // halves, pass_on, unroll=4)
    count = 2 * devices
    lane = lanes_of((count, LANES))
    half = rows_of((count, LANES)) % halves
    sign = signs[...]
    ends = jnp.zeros((count, LANES), jnp.float32)
    for c in range(CH):
        low, high = below[pl.ds(c, count, stride=8)], above[pl.ds(c, count, stride=8)]
        at = 4 * c
        low_wall = jnp.where(lane == at, turn(low, at - 1, 1), turn(low, at + 1, 1))
        high_wall = jnp.where(
            lane == at + 2, turn(high, at + 3 - rows, 1), turn(high, at + 5 - rows, 1)
        )
        if 1 <= c <= 3:
            low_wall = jnp.where(is_field, -sign * low_wall, low_wall)
            high_wall = jnp.where(is_field, sign * high_wall, high_wall)
        low = jnp.where(half == 0, low_wall, turn(low, at + 2 - rows, 1))
        high = jnp.where(half == halves - 1, high_wall, turn(high, at + 2, 1))
        ends = jnp.where(within(lane, at, 2), low, jnp.where(within(lane, at + 2, 2), high, ends))
    held_send[pl.ds(2 * CH, devices, stride=PASSED)] = ends[0:devices] + turn(
        ends[devices:], 4 * CH, 1
    )
    wait_all(copy_all([(held_send, send)], sems))


def flux_chunk(get, mets, fi, w, fk, acc, r):
    rows = pl.ds(r, 8)
    vax, vay, vbx, vby, niv, rw, cw, tw = [mets[j, rows] for j in range(8)]
    at_j = along(1)
    for k in range(fi.shape[1]):
        f = [get(c, k, r) for c in range(CH)]
        wk, p, h = point(f)
        for c, x in enumerate(flux(f, wk, p, h, vax, vay)):
            fi[c, k, rows] = x
        for c in range(4):
            w[c, k, rows] = wk[c]
        fj = flux(f, wk, p, h, vbx, vby)
        for c in range(CH):
            val = niv * slope(fj[c], at_j)
            if c > 0:
                val = val + (cw * curve(wk[c - 1], at_j) - tw * wk[c - 1])
            acc[c, k, rows] = f[c] + val
        for c, x in enumerate(flux_planes(f, wk, p, h)):
            if c > 0:
                fk[c - 1, k, rows] = x


def sum_chunk(get, mets, fi, w, fk, acc, r, emit):
    planes = fi.shape[1]
    kv = viscosity * unit
    rows = pl.ds(r, 8)
    niv, rw = mets[4, rows], mets[5, rows]
    for c in range(CH):
        t = [fk[c - 1, k, rows] if c > 0 else get(3, k, r) for k in range(planes)]
        x = [w[c - 1, k, rows] for k in range(planes)] if c > 0 else None
        for k in range(planes):

            def near(v, o):
                return v[(k + o) % planes]

            def at_i(v, o):
                return v[pl.ds(r + o, 8)]

            val = acc[c, k, rows] + niv * slope(fi.at[c, k], at_i) - unit * slope(t, near)
            if c > 0:
                val = val + (rw * curve(w.at[c - 1, k], at_i) + kv * curve(x, near))
            emit(c, k, r, val)


def chunks(count, body, unroll=1):
    def step(n, _):
        body(pl.multiple_of(n * 8, 8))
        return 0

    lax.fori_loop(0, count, step, 0, unroll=unroll)


def first_kernel(
    state_in, placed_at, neighbour_at, face_at, orient_at, state, route,
    mets, fi, w, fk, acc, placed, neighbour, face, orient, where_is, sems,
):
    del state_in
    planes, rows = fi.shape[1], fi.shape[2] - 2 * PAD
    pairs = zip((placed_at, neighbour_at, face_at, orient_at), (placed, neighbour, face, orient))
    tables = copy_all(list(pairs), sems)
    count = rows // 8
    blocks = placed.shape[0]
    share = -(-blocks // count)

    def slots(n):
        return [jnp.minimum((n // 8) * share + i, blocks - 1) for i in range(share)]

    def get(c, k, r):
        return state[c, k, pl.ds(r, 8)]

    def fluxes(n):
        at = pl.ds(n + PAD, 8)
        for j, x in enumerate(metric_terms([state[c, planes, at] for c in range(CH)])):
            mets[j, at] = x
        flux_chunk(get, mets, fi, w, fk, acc, n + PAD)

    def emit(c, k, r, val):
        state[c, k, pl.ds(r, 8)] = val

    def sums(n):
        for slot in slots(n):
            block = placed[slot]
            for f in range(2):
                partner = where_is[neighbour[f, block]]
                route[2 * slot + f] = partner * 4 + face[f, block] * 2 + orient[f, block]
        sum_chunk(get, mets, fi, w, fk, acc, n + PAD, emit)

    def note(slot):
        where_is[placed[slot]] = slot

    chunks(count, fluxes, unroll=2)
    wait_all(tables)
    loop(blocks, note, unroll=8)
    chunks(count, sums, unroll=2)


def pack_ends(tall, planes):
    sub, lane = rows_of((8, LANES)), lanes_of((8, LANES))
    stacked = []
    for c in range(CH):
        packed = jnp.zeros((8, LANES), jnp.float32)
        for k in range(planes):
            x = turn(jnp.where(sub < 4, tall[0, c, k], tall[1, c, k]), 8 * k + 4, 1)
            packed = jnp.where(within(lane, 8 * k, 8), x, packed)
        stacked.append(packed)
    ends = across(jnp.concatenate(stacked, axis=0))
    out = []
    for c in range(CH):
        packed = jnp.zeros((8, LANES), jnp.float32)
        for k in range(planes):
            x = turn(ends[k * 8 : k * 8 + 8], 4 * k - (8 * c + 2), 1)
            packed = jnp.where(within(lane, 4 * k, 4), x, packed)
        out.append(packed)
    return out


def ends_kernel(
    halves, state_in, tall_in, low, high, after, state, tall, ends_base, ends_sec, inner,
    tile_fk, tile_w, tile_acc, packed, rims, sems,
):
    del state_in, tall_in, after
    planes, rows = tall.shape[2] - 1, state.shape[2] - 2 * PAD
    every = planes + 1
    half = lax.axis_index("ij")
    low_wall, high_wall = half == 0, half == halves - 1
    low_flag, high_flag = jnp.where(low_wall, 1, 0), jnp.where(high_wall, 1, 0)
    sub, lane = rows_of((8, LANES)), lanes_of((8, LANES))
    top = PAD + rows

    @pl.when(low_wall)
    def _():
        for c in range(CH):
            for k in range(every):
                for n in range(2):
                    x = tall[0, c, k, 4 + n : 5 + n]
                    tall[0, c, k, 3 - n : 4 - n] = -x if 1 <= c <= 3 and k < planes else x

    @pl.when(jnp.logical_not(low_wall))
    def _():
        for c in range(CH):
            for k in range(every):
                tall[0, c, k, 0:4] = low[c, 4 * k : 4 * k + 4]

    @pl.when(high_wall)
    def _():
        for c in range(CH):
            for k in range(every):
                for n in range(2):
                    tall[1, c, k, 4 + n : 5 + n] = tall[1, c, k, 3 - n : 4 - n]

    @pl.when(jnp.logical_not(high_wall))
    def _():
        for c in range(CH):
            for k in range(every):
                tall[1, c, k, 4:8] = high[c, 4 * k : 4 * k + 4]

    for c, x in enumerate(pack_ends(tall, every)):
        ends_base[c] = x
    for c in range(CH):
        state[c, planes, PAD - 4 : PAD] = tall[0, c, planes, 0:4]
        state[c, planes, top : top + 4] = tall[1, c, planes, 4:8]
    mets = [metric_terms([tall[s, c, planes] for c in range(CH)]) for s in range(2)]

    def done(c, s, k, x):
        tall[s, c, k] = x
        if s == 0:
            sign = -1.0 if 1 <= c <= 3 else 1.0
            wall = sign * jnp.where(sub == 2, turn(x, -3, 0), turn(x, -1, 0))
            x = jnp.where((sub < 4) & (low_flag == 1), wall, x)
        else:
            wall = jnp.where(sub == 4, turn(x, 1, 0), turn(x, 3, 0))
            x = jnp.where((sub >= 4) & (high_flag == 1), wall, x)
        start = PAD - 2 if s == 0 else top - 2
        state[c, k, start : start + 4] = x[2:6]

    tile_stage(
        planes, lambda c, s, k: tall[s, c, k], mets, lambda *_: along(0), along(1),
        (tile_fk, tile_w, tile_acc), done,
    )
    for c, x in enumerate(pack_ends(tall, planes)):
        rims[c] = x
    leaving = copy_all([(rims, ends_sec)], sems)

    if rows < LANES:
        packed[...] = jnp.zeros(packed.shape, jnp.float32)

    def pack(n):
        at = pl.ds(n + PAD, 8)
        for c in range(CH):
            packs = turn(state[c, planes, at], 12 * planes + 6, 1)
            for k in range(planes):
                x = turn(state[c, k, at], 12 * k + 6, 1)
                packs = jnp.where(within(lane, 12 * k, 12), x, packs)
            packed[c, pl.ds(n, 8)] = packs

    chunks(rows // 8, pack, unroll=2)
    for c in range(CH):
        inner[c] = packed[c].T[0 : inner.shape[1]]
    wait_all(leaving)


def second_kernel(
    state_in, dens, mom, en, state, fields, mets, fi, w, fk, acc, sems
):
    del state_in
    planes, rows = fields.shape[1:3]
    pairs = [(dens.at[0], fields.at[0]), (mom.at[0], fields.at[1:4]), (en.at[0], fields.at[4])]
    copies = copy_all(pairs, sems)

    def get(c, k, r):
        return state[c, k, pl.ds(r, 8)]

    def fluxes(n):
        at = pl.ds(n, 8)
        for j, x in enumerate(metric_terms([state[c, planes, at] for c in range(CH)])):
            mets[j, at] = x
        flux_chunk(get, mets, fi, w, fk, acc, n)

    def emit(c, k, r, val):
        x = 0.5 * (fields[c, k, pl.ds(r - PAD, 8)] + val)
        state[c, k, pl.ds(r, 8)] = x

    chunks(rows // 8 + 2, fluxes, unroll=2)
    wait_all(copies)
    chunks(rows // 8, lambda n: sum_chunk(get, mets, fi, w, fk, acc, n + PAD, emit), unroll=2)


def beyond(low, rows):
    top = rows % LANES
    high = low if top == 0 else turn(low, top, 1)
    lane = lanes_of(low.shape)

    def at(x, o):
        if o < 0:
            x = jnp.where(lane >= LANES + o, low, x)
        else:
            x = jnp.where(within(lane, top, o), high, x)
        return turn(x, -o, 1)

    return at


def last_kernel(
    halves, rows, planes, own, ends_base, ends_sec_at, inner, got, out,
    next_dens, next_mom, next_en,
    base, sec, fk, ws, acc, rims, turned, back, full, ends_sec, sems,
):
    late = copy_all([(ends_sec_at, ends_sec)], sems, 3 * PIECES)
    half = lax.axis_index("ij")
    low_wall, high_wall = half == 0, half == halves - 1
    sub, lane = rows_of((8, LANES)), lanes_of((8, LANES))

    def mix(f, mine, others):
        return jnp.where((sub < 4) == (f == 1), mine, others)

    others = [jnp.zeros((8, LANES), jnp.float32)] * CH
    for k in range(planes + 1):
        start = DEPTH * k * PASSED
        for f in range(2):

            def ghost(row):
                x = got[pl.ds(start + row, 8, stride=PASSED)]
                return x if f == 1 else turn(x, 4, 0)

            arrived = ghost(2 * CH)
            to = 28 * f + 4 * k
            for c in range(CH):
                base[c, f, k] = mix(f, own[c, k * 8 : k * 8 + 8], ghost(f * CH + c))
                moved = turn(arrived, to - 4 * CH * f - 4 * c, 1)
                others[c] = jnp.where(within(lane, to, 4), moved, others[c])

    low_lanes = lane < 28
    twice = [jnp.where(low_lanes, ends_base[c], turn(ends_base[c], 28, 1)) for c in range(CH)]
    ends = [jnp.where(low_lanes == (sub >= 4), twice[c], others[c]) for c in range(CH)]
    slot = jnp.where(low_lanes, lane, lane - 28)

    def spread(x):
        y = x
        for k in range(planes):
            y = jnp.where(within(slot, 4 * k, 4), turn(x, 4 * (k - planes), 1), y)
        return y

    vax, vay, vbx, vby, niv, _, cw, _ = [spread(x) for x in metric_terms(ends)]
    wrapped = [spread(x) for x in metric_terms(twice)[2:4]]

    def keep(c, f, k, val):
        sec[c, f, k] = val

    def stage(held, ends, gx, gy):
        mets = [metric_terms([held[c, f, planes] for c in range(CH)]) for f in range(2)]
        w, p, h = point(ends)
        for n, x in enumerate((*flux(ends, w, p, h, gx, gy), *w)):
            for f in range(2):
                for k in range(planes):
                    rims[n, f, k] = turn(x, LANES - 2 - (28 * f + 4 * k), 1)
        tile_stage(
            planes,
            lambda c, f, k: held[c, f, k],
            mets,
            lambda kind, c, f, k: beyond(rims[CH * kind + c, f, k], rows),
            along(0),
            (fk, ws, acc),
            keep,
        )

    stage(base, ends, vax, vay)
    wait_all(late)

    def move(k, source):
        for c in range(CH):
            at = 12 * k
            mine = jnp.where(sub < 4, inner[c, at : at + 8], inner[c, at + 4 : at + 12])
            for f in range(2):
                sec[c, f, k] = mix(f, mine, turn(source[c, f, k], 2 if f == 1 else -2, 0))

    for k in range(planes):
        move(k, sec)
    move(planes, base)

    def shifted(x):
        return jnp.where(low_lanes, turn(x, -2, 0), turn(x, 2, 0))

    w1, p1, h1 = point(ends)
    w0, p0, h0 = point(twice)
    new, old = flux(ends, w1, p1, h1, vbx, vby), flux(twice, w0, p0, h0, *wrapped)
    at_j = along(0)
    touched = within(sub, jnp.where(low_lanes, 4, 2), 2)
    second = []
    for c in range(CH):
        add = niv * slope(new[c] - old[c], at_j)
        if c > 0:
            add = add + cw * curve(w1[c - 1] - w0[c - 1], at_j)
        x = jnp.where(low_lanes, ends_sec[c], turn(ends_sec[c], 28, 1))
        second.append(shifted(x + jnp.where(touched, add, 0.0)))

    def mirror(at_low):
        def reflect(*second):
            second = list(second)
            for k in range(planes):
                for f in range(2):
                    to = 28 * f + 4 * k + (0 if at_low else 2)
                    shift = to - 1 if at_low else to + 1 - rows
                    for c in range(CH):
                        x = sec[c, f, k]
                        x = jnp.where(lane == to, turn(x, shift, 1), turn(x, shift + 2, 1))
                        if at_low and 1 <= c <= 3:
                            x = -x
                        second[c] = jnp.where(within(lane, to, 2), x, second[c])
            return tuple(second)

        return reflect

    def leave(*second):
        return second

    second = lax.cond(low_wall, mirror(True), leave, *second)
    second = lax.cond(high_wall, mirror(False), leave, *second)
    stage(sec, second, shifted(vax), shifted(vay))

    per = LANES // 8

    for k in range(planes):
        for c in range(CH):
            x = jnp.where(sub < 4, turn(sec[c, 1, k], -2, 0), turn(sec[c, 0, k], 2, 0))
            at = (c * planes + k) * 8
            turned[at : at + 8] = 0.5 * (own[c, k * 8 : k * 8 + 8] + x)
    for n in range(turned.shape[0] // LANES):
        back[n] = turned[n * LANES : (n + 1) * LANES].T
    inside = within(lane, 4, LANES - 8)
    size = max(8, rows // PIECES)

    def leave(start):
        at = pl.ds(start, size)
        targets = [next_dens.at[0, :, at], next_en.at[0, :, at], next_mom.at[0, :, :, at]]
        sources = [full.at[0, :, at], full.at[4, :, at], full.at[1:4, :, at]]
        first = 3 * (start // size)
        return [
            pltpu.make_async_copy(src, dst, sems.at[first + n])
            for n, (src, dst) in enumerate(zip(sources, targets))
        ]

    def merge(r):
        at = pl.ds(r, 8)
        for c in range(CH):
            for k in range(planes):
                index = c * planes + k
                moved = turn(back[index // per, at], LANES - 4 - 8 * (index % per), 1)
                full[c, k, at] = jnp.where(inside, out[c, k, pl.ds(r + PAD, 8)], moved)

        @pl.when(lax.rem(r + 8, size) == 0)
        def _():
            for copy in leave(pl.multiple_of(r + 8 - size, 8)):
                copy.start()

    chunks(rows // 8, merge, unroll=2)
    for n in range(rows // size):
        wait_all(leave(n * size))


def local(mesh_shape, density, momentum, energy, metrics, volume, placed, neighbour, face, orient):
    halves = mesh_shape["ij"]
    blocks = mesh_shape["blk"]
    planes, rows = density.shape[1], density.shape[2]
    every = planes + 1
    fields = (density, momentum, energy, metrics, volume)
    neighbour, face, orient = neighbour.T, face.T, orient.T
    vmem = pl.BlockSpec(memory_space=pltpu.VMEM)
    smem = pl.BlockSpec(memory_space=pltpu.SMEM)
    hbm = pl.BlockSpec(memory_space=pltpu.HBM)
    anywhere = pl.BlockSpec(memory_space=pl.ANY)

    def call(kernel, name, outs, ins, out_specs, scratch, cost=None, alias=None):
        run = pl.pallas_call(
            kernel,
            out_shape=[
                held(x) if spec is vmem else far(x) if spec is hbm else x
                for x, spec in zip(outs, out_specs)
            ],
            in_specs=ins,
            out_specs=out_specs,
            scratch_shapes=scratch,
            compiler_params=pltpu.CompilerParams(vmem_limit_bytes=VMEM_MIB * 1024 * 1024),
            cost_estimate=cost,
            input_output_aliases=alias or {},
            name=name,
        )

        def keep(*operands):
            return run(
                *[
                    x
                    if spec not in (vmem, hbm)
                    else pltpu.with_memory_space_constraint(x, spec.memory_space)
                    for x, spec in zip(operands, ins)
                ]
            )

        return keep

    def shape(*dims):
        return jax.ShapeDtypeStruct(dims, jnp.float32)

    def held(x):
        return pltpu.VMEM(x.shape, x.dtype)

    def far(x):
        return pltpu.HBM(x.shape, x.dtype)

    def table(x):
        return pltpu.SMEM(x.shape, jnp.int32)

    def sems(count):
        return pltpu.SemaphoreType.DMA((count,))

    devices = blocks * halves
    sent, passed = shape(devices * SENT, LANES), shape(devices * PASSED, LANES)
    strip, rim = shape(CH, 64, LANES), shape(CH, 8, LANES)
    edge = shape(CH, 4 * every, LANES)
    edges = 1 if halves == 2 else 2
    square = held(shape(CH, LANES, LANES))
    tall = rows + 2 * PAD
    whole = shape(CH, every, tall, LANES)
    rows_about = shape(2, CH, every, 8, LANES)
    to_send, own, about, state, *halo = call(
        functools.partial(cut_kernel, halves),
        "cut",
        [sent, strip, rows_about, whole] + [edge] * edges,
        [hbm] * 8,
        [hbm] + [vmem] * (3 + edges),
        [
            held(sent),
            square,
            held(shape(CH * 64, LANES)),
            table(placed),
            table(face),
            table(orient),
            sems(5 * PIECES),
            sems(3),
            sems(1),
        ],
    )(*fields, placed, face, orient)

    def swap(x):
        x = x.reshape(devices, x.shape[0] // devices, 1, LANES)
        x = lax.all_to_all(x, ("blk", "ij"), 0, 0, tiled=True)
        return x.reshape(x.shape[0] * x.shape[1], LANES)

    if edges == 1:
        below = above = lax.ppermute(halo[0], "ij", [(0, 1), (1, 0)])
    else:
        below = lax.ppermute(halo[1], "ij", [(i, i + 1) for i in range(halves - 1)])
        above = lax.ppermute(halo[0], "ij", [(i + 1, i) for i in range(halves - 1)])
    got = swap(to_send)

    padded = held(shape(CH, planes, tall, LANES))
    stage = [
        held(shape(8, tall, LANES)),
        padded,
        held(shape(4, planes, tall, LANES)),
        held(shape(4, planes, tall, LANES)),
        padded,
    ]
    work = planes * rows * LANES
    cost = pl.CostEstimate(flops=300 * work, bytes_accessed=150 * work, transcendentals=work)
    route = jax.ShapeDtypeStruct((2 * blocks,), jnp.int32)
    state, route_out = call(
        first_kernel,
        "first_section",
        [whole, route],
        [vmem] + [hbm] * 4,
        [vmem, smem],
        stage + [table(x) for x in (placed, neighbour, face, orient, placed)] + [sems(4)],
        cost,
        {0: 0},
    )(state, placed, neighbour, face, orient)
    (relayed,) = call(
        functools.partial(relay_kernel, halves, rows, planes, devices),
        "relay",
        [passed],
        [anywhere, anywhere, vmem],
        [hbm],
        [
            held(passed),
            held(shape(devices * 16, LANES)),
            held(shape(devices * 16, LANES)),
            held(shape(devices * 2, LANES)),
            table(route),
            sems(2),
        ],
    )(route_out, below, got)
    ghosts = swap(relayed)
    tiles = held(shape(CH, 2, every, 8, LANES))
    state, _, ends_base, ends_sec, inner = call(
        functools.partial(ends_kernel, halves),
        "ends",
        [whole, rows_about, rim, rim, shape(CH, 12 * every + 4, LANES)],
        [vmem] * 4 + [hbm],
        [vmem] * 3 + [hbm, vmem],
        [tiles] * 3 + [square, held(rim), sems(1)],
        cost,
        {0: 0, 1: 1},
    )(state, about, below, above, relayed)
    (state,) = call(
        second_kernel,
        "second_section",
        [whole],
        [vmem] + [hbm] * 3,
        [vmem],
        [held(shape(CH, planes, rows, LANES))] + stage + [sems(3)],
        cost,
        {0: 0},
    )(state, density, momentum, energy)
    flat = -(-CH * planes * 8 // LANES)
    return call(
        functools.partial(last_kernel, halves, rows, planes),
        "strips",
        [shape(*density.shape), shape(*momentum.shape), shape(*energy.shape)],
        [vmem] * 2 + [hbm] + [vmem] * 3,
        [hbm] * 3,
        [tiles] * 5
        + [
            held(shape(CH + 4, 2, planes, 8, LANES)),
            held(shape(flat * LANES, LANES)),
            held(shape(flat, LANES, LANES)),
            held(shape(CH, planes, rows, LANES)),
            held(rim),
            sems(3 * PIECES + 1),
        ],
    )(own, ends_base, ends_sec, inner, ghosts, state)


def solution(mesh):
    return jax.shard_map(
        functools.partial(local, dict(mesh.shape)),
        mesh=mesh,
        in_specs=(
            P("blk", None, "ij", None),
            P("blk", None, None, "ij", None),
            P("blk", None, "ij", None),
            P("blk", None, "ij", None),
            P("blk", "ij", None),
            P(),
            P(),
            P(),
            P(),
        ),
        out_specs=(
            P("blk", None, "ij", None),
            P("blk", None, None, "ij", None),
            P("blk", None, "ij", None),
        ),
        check_vma=False,
    )
```
